32 devices in a mesh: grp: 2 (over y), tile: 4 (over z), var: 4 (over x, core).
Axes of the slice: x: 2, y: 2, z: 4, core: 2. Of those that a mesh axis runs over, the one named last changes fastest.
Arguments:
- control: float32 [8, 128, 2048], P('var', ('grp', 'tile')), parts along dimension 1, may hold values from -6 to 6
- diffusivity: float32 [2, 128, 2048], P(None, ('grp', 'tile')), parts along dimension 1, may hold values from 0.05 to 0.95
- land_mask: int32 [128, 2048], P(('grp', 'tile')), parts along dimension 0, may hold values 0 or 1
- panel_tile: int32 [1024, 1], P(('grp', 'tile')), parts along dimension 0, may hold values from 0 to 3; in each aligned block of 128 rows (0 to 127, 128 to 255, ...) at most 64 rows name the same one
- panel_row: int32 [1024], P(('grp', 'tile')), parts along dimension 0, may hold values from 0 to 15
- panel_cols: int32 [1024, 128], P(('grp', 'tile')), parts along dimension 0, may hold values from 0 to 2047
- obs_values: float32 [1024, 128], P(('grp', 'tile')), parts along dimension 0, may hold values from -6 to 6
- obs_weights: float32 [1024, 128], P(('grp', 'tile')), parts along dimension 0, may hold values from 0.5 to 4
- panel_sensor: int32 [1024], P(('grp', 'tile')), parts along dimension 0, may hold values from 0 to 1
- sensitivity: float32 [2, 8], replicated, may hold values from 0.2 to 1
- cross_factor: float32 [8, 8], replicated, may hold values from -0.45 to 2
Outputs:
- gradient: float32 [8, 128, 2048], P('var', ('grp', 'tile')), parts along dimension 1
The draws below stay inside these ranges and needn't reach their ends.
There are 2 independent parts, one for each index of `grp`. The reference program is written for one: setup_inputs(seed, part) draws one part's arguments, and reference() takes and returns one part's arrays. A program takes and returns all parts, laid end to end along the dimension named above; an argument that names none is the same for every part. Nothing has to cross between parts.
Inputs may be any that keep to these rules, and one draw needn't show every extreme that they name: `panel_tile`: among the 128 panels held by one tile index, at most 64 name the same tile.
All inputs are finite; a program needn't handle non-finite values. No bound on the sum of `land_mask` on one device may be relied on, other than what follows from the above.
Results may differ from the reference program's by a relative error of at most 0.00014.
Values sent between devices are 32-bit elements; how exact they have to be, the bound alone decides.
No kernel may reach another device: no remote copies, remote signals or barrier semaphores. Data moves between devices by JAX's collectives and lax.ppermute only.
A program may use at most 128 MiB of HBM per device.

```python
import math
import jax
import jax.numpy as jnp
import numpy as np
from jax import lax

NV = 8
ROWS_DEV = 16
COLS = 2048
PASSES = 10
PANELS_DEV = 128
PANEL_W = 128
SENSORS = 2
ROWS = 64
PANELS = 512
CAP = 64
N_TILE = 4


def draw_cross_factor(key, part):
    key_diag, key_off = jax.random.split(key)
    diag_part = jax.random.uniform(key_diag, (NV, NV), jnp.float32, 1.0, 1.5)
    off_part = jax.random.uniform(key_off, (NV, NV), jnp.float32, -0.3, 0.3)
    identity = jnp.eye(NV, dtype=jnp.float32)
    return identity * diag_part + (1.0 - identity) * off_part


def place_ends(drawn, key, low, largest):
    shape = drawn.shape
    index_at = [jax.random.randint(jax.random.fold_in(key, axis), (), 0, shape[axis]) for axis in range(len(shape))]
    drawn = drawn.at[tuple(index_at)].set(low)
    longest = shape.index(max(shape))
    index_at[longest] = (index_at[longest] + 1) % shape[longest]
    return drawn.at[tuple(index_at)].set(largest)


def steps_of(rng, extent, cuts, smallest, high):
    gain, own = 1.0, jax.random.fold_in(rng, 6)
    for dim, parts in cuts:
        draws = jnp.exp(jax.random.uniform(jax.random.fold_in(own, dim), (parts,), jnp.float32, smallest / len(cuts), high / len(cuts)))
        gain = gain * jnp.repeat(draws, extent[dim] // parts).reshape([-1 if axis == dim else 1 for axis in range(len(extent))])
    return gain


def deal_out(rng, own, number, rows, count, top, limit, slope):
    order = jax.random.permutation(rng, count)
    heavy_load, ordinary = portions_of(count, rows * top, limit, slope, True), portions_of(count, rows * top, limit, slope, False)
    places = jnp.arange(count)

    def named(tallies, rotation):
        used = int((tallies > 0).sum())
        fixed = max(1, used // 4)
        shifted = fixed + (places - fixed + rotation * (used - fixed)) % max(1, count - fixed)
        return jnp.zeros((count,), jnp.int32).at[order[jnp.where(places < fixed, places, shifted)]].set(jnp.asarray(tallies, jnp.int32))

    tallies = jnp.where(number % 4 == 0, named(heavy_load, number // 4), named(ordinary, number - number // 4 - 1))
    mixed = jax.random.permutation(jax.random.fold_in(own, 3), count)
    source_of, receiver = mixed[0:count // 2 * 2:2], mixed[1:count // 2 * 2:2]
    slack = jnp.minimum(tallies[source_of] - 1, limit - tallies[receiver]) // 2
    slack = jnp.where((source_of == order[0]) | (receiver == order[0]) | (tallies[receiver] == 0), 0, jnp.maximum(slack, 0))
    shifted = jax.random.randint(jax.random.fold_in(own, 4), (count // 2,), 0, 1 << 20) % (slack + 1)
    tallies = tallies.at[source_of].add(-shifted).at[receiver].add(shifted)
    members = jnp.searchsorted(jnp.cumsum(tallies), jnp.arange(rows * top), side="right").astype(jnp.int32)
    listing = members.reshape(top, rows).T
    listing = listing[jax.random.permutation(jax.random.fold_in(own, 1), rows)]
    rotation = jax.random.randint(jax.random.fold_in(own, 2), (rows, 1), 0, top)
    return jnp.take_along_axis(listing, (jnp.arange(top)[None, :] + rotation) % top, axis=1)


def portions_of(count, total, most, lean, full):
    portions = [(1 << 20) // math.isqrt(rank ** lean) + 1 for rank in range(1, count + 1)]
    largest = most if full else min(most, max(-(-total // count), total * portions[0] // sum(portions)))
    least = 1 if total - largest >= count - 1 else 0
    holding, rest = [largest] + [least] * (count - 1), total - largest - least * (count - 1)
    while rest > 0:
        movable = [i for i in range(1, count) if holding[i] < largest] or [i for i in range(1, count) if holding[i] < most]
        pool, remaining = sum([portions[i] for i in movable]), rest
        for i in movable:
            addition = min(most - holding[i], max(1, remaining * portions[i] // pool), rest)
            holding[i] = holding[i] + addition
            rest = rest - addition
    return np.array(holding)


def centred(rng, shape, scale, limit, cuts=(), kind=jnp.bfloat16):
    level = steps_of(rng, shape, cuts, -0.22, 0.18) if cuts else 1.0
    entries = jax.random.normal(rng, shape, jnp.float32) * scale * level
    return jnp.minimum(jnp.maximum(entries, -limit), limit).astype(kind)


def setup_inputs(seed: int = 0, part: int = 0) -> dict:
    keys = jax.random.split(jax.random.key(seed), 12)
    part_splits = jax.random.split(jax.random.fold_in(keys[11], part), 12)
    control = centred(part_splits[0], (NV, ROWS, COLS), 1.0, 6.0, ((0, 4), (1, 4)), jnp.float32)
    diffusivity = jnp.clip(jnp.exp(math.log(0.95) - 2.944439 * jax.random.uniform(part_splits[1], (2, ROWS, COLS), jnp.float32) ** steps_of(part_splits[1], (2, ROWS, COLS), ((1, 4),), -0.2, 0.2)), 0.05, 0.95)
    land_mask = place_ends((jax.random.randint(part_splits[2], (ROWS, COLS), 0, 4) < 3).astype(jnp.int32), jax.random.fold_in(part_splits[2], 1), 0, 1)
    panel_tile_keys = jax.random.split(jax.random.fold_in(part_splits[3], 1), PANELS // PANELS_DEV)
    panel_tile_turns = jax.random.permutation(jax.random.fold_in(part_splits[3], 3), PANELS // PANELS_DEV)
    panel_tile = jax.vmap(lambda own, number: deal_out(jax.random.fold_in(part_splits[3], 2), own, number, PANELS_DEV, N_TILE, 1, CAP, 2))(panel_tile_keys, panel_tile_turns).reshape((PANELS, 1))
    panel_row = place_ends(jax.random.randint(part_splits[4], (PANELS,), 0, ROWS_DEV), jax.random.fold_in(part_splits[4], 1), 0, ROWS_DEV - 1).astype(jnp.int32)
    panel_cols = place_ends(jax.random.randint(part_splits[5], (PANELS, PANEL_W), 0, COLS), jax.random.fold_in(part_splits[5], 1), 0, COLS - 1).astype(jnp.int32)
    obs_values = centred(part_splits[6], (PANELS, PANEL_W), 1.0, 6.0, ((0, 4),), jnp.float32)
    obs_weights = jnp.clip(jnp.exp(math.log(4.0) - 2.0794415 * jax.random.uniform(part_splits[7], (PANELS, PANEL_W), jnp.float32) ** steps_of(part_splits[7], (PANELS, PANEL_W), ((0, 4),), -0.2, 0.2)), 0.5, 4.0)
    panel_sensor = place_ends(jax.random.randint(part_splits[8], (PANELS,), 0, SENSORS), jax.random.fold_in(part_splits[8], 1), 0, SENSORS - 1).astype(jnp.int32)
    sensitivity = jnp.clip(jax.random.uniform(keys[9], (SENSORS, NV), jnp.float32, 0.2, 1.0), 0.2, 1.0)
    cross_factor = draw_cross_factor(jax.random.fold_in(keys[11], 71), part)
    return {"control": control, "diffusivity": diffusivity, "land_mask": land_mask, "panel_tile": panel_tile, "panel_row": panel_row, "panel_cols": panel_cols, "obs_values": obs_values, "obs_weights": obs_weights, "panel_sensor": panel_sensor, "sensitivity": sensitivity, "cross_factor": cross_factor}


def one_pass(values, row_kappa, col_kappa):
    row_pad = jnp.pad(row_kappa, ((1, 1), (0, 0)))
    col_pad = jnp.pad(col_kappa, ((0, 0), (1, 1)))
    face_up = 0.125 * (row_kappa + row_pad[:-2])
    face_down = 0.125 * (row_kappa + row_pad[2:])
    face_left = 0.125 * (col_kappa + col_pad[:, :-2])
    face_right = 0.125 * (col_kappa + col_pad[:, 2:])
    vals_rows = jnp.pad(values, ((0, 0), (1, 1), (0, 0)))
    vals_cols = jnp.pad(values, ((0, 0), (0, 0), (1, 1)))
    return (values - face_up * (values - vals_rows[:, :-2]) - face_down * (values - vals_rows[:, 2:])
            - face_left * (values - vals_cols[:, :, :-2]) - face_right * (values - vals_cols[:, :, 2:]))


def diffuse_all(values, diffusivity):
    def advance(index, current):
        return one_pass(current, diffusivity[0], diffusivity[1])
    return lax.fori_loop(0, PASSES, advance, values)


def reference(control, diffusivity, land_mask, panel_tile, panel_row, panel_cols, obs_values, obs_weights, panel_sensor, sensitivity, cross_factor):
    highest = lax.Precision.HIGHEST
    smooth = diffuse_all(control, diffusivity)
    state = jnp.einsum("uv,vrc->urc", cross_factor, smooth, precision=highest)
    grid_row = (panel_tile[:, 0] * ROWS_DEV + panel_row).astype(jnp.int32)
    cell_index = (grid_row[:, None] * COLS + panel_cols).astype(jnp.int32)
    panel_sens = sensitivity[panel_sensor]
    state_flat = state.reshape(NV, -1)
    picked = state_flat[:, cell_index]
    model_obs = jnp.sum(panel_sens.T[:, :, None] * picked, axis=0)
    usable = land_mask.reshape(-1)[cell_index].astype(jnp.float32)
    misfit = obs_weights * usable * (model_obs - obs_values)
    spread = panel_sens.T[:, :, None] * misfit[None]
    adjoint = jnp.zeros((NV, ROWS_DEV * N_TILE * COLS), jnp.float32)
    adjoint = adjoint.at[:, cell_index.reshape(-1)].add(spread.reshape(NV, -1))
    adjoint = adjoint.reshape(NV, ROWS_DEV * N_TILE, COLS)
    pulled = jnp.einsum("uv,urc->vrc", cross_factor, adjoint, precision=highest)
    return control + diffuse_all(pulled, diffusivity)
```

```python
import functools

import jax
import jax.numpy as jnp
from jax import lax
from jax.experimental import pallas as pl
from jax.experimental.pallas import tpu as pltpu
from jax.sharding import PartitionSpec as P

PASSES = 10
LANES = 128
GROUP = 8
VMEM = pl.BlockSpec(memory_space=pltpu.VMEM)
SMEM = pl.BlockSpec(memory_space=pltpu.SMEM)
F32 = jnp.float32


def call(body, outs, ins, scratch=(), limit=16, cost=None):
    return pl.pallas_call(
        body,
        out_shape=outs,
        in_specs=ins,
        out_specs=[VMEM] * len(outs),
        scratch_shapes=list(scratch),
        compiler_params=pltpu.CompilerParams(vmem_limit_bytes=limit << 20),
        cost_estimate=cost,
    )


def cost(cycles):
    return pl.CostEstimate(flops=cycles * 4096, bytes_accessed=cycles * 1024, transcendentals=0)


def response(sens_ref, factor_ref, sensor, variable):
    total = sens_ref[sensor, 0] * factor_ref[0, variable]
    for u in range(1, factor_ref.shape[0]):
        total = total + sens_ref[sensor, u] * factor_ref[u, variable]
    return total


def combine_kernel(pos_ref, sens_ref, factor_ref, control_ref, own_ref, other_ref):
    var_dev = control_ref.shape[0]
    pos = pos_ref[0]
    core = pos % 2
    for sensor, out_ref in ((1 - core, other_ref), (core, own_ref)):
        total = None
        for v in range(var_dev):
            term = response(sens_ref, factor_ref, sensor, pos * var_dev + v) * control_ref[v]
            total = term if total is None else total + term
        out_ref[...] = total


def pack_kernel(slots, pos_ref, tile_ref, row_ref, sensor_ref, value_ref, weight_ref, cols_ref,
                send_ref, cells_ref, count_ref):
    tiles = send_ref.shape[0]
    panels, width = value_ref.shape
    core = pos_ref[0] % 2
    cells_ref[...] = cols_ref[...].astype(F32)
    send_ref[...] = jnp.zeros(send_ref.shape, F32)
    for t in range(tiles):
        count_ref[t] = 0
    pad_tiles = -(-tiles // 8) * 8
    sub = lax.broadcasted_iota(jnp.int32, (pad_tiles, LANES), 0)
    lane = lax.broadcasted_iota(jnp.int32, (pad_tiles, LANES), 1)

    def place(p, meta):
        t = tile_ref[p]
        keep = sensor_ref[p] == core
        slot = count_ref[t]
        count_ref[t] = slot + keep.astype(jnp.int32)
        trash = 3 * slots + 7
        for part, ref in enumerate((value_ref, weight_ref, cells_ref)):
            at = jnp.where(keep, part * slots + slot, trash)
            send_ref[t, pl.ds(at, 1), :] = ref[pl.ds(p, 1), :]
        where = jnp.where(keep, slot, LANES)
        return jnp.where((sub == t) & (lane == where), row_ref[p].astype(F32), meta)

    meta = lax.fori_loop(0, panels, place, jnp.zeros((pad_tiles, LANES), F32), unroll=4)
    for t in range(tiles):
        meta = jnp.where((sub == t) & (lane == slots), count_ref[t].astype(F32), meta)
    for t in range(tiles):
        send_ref[t, pl.ds(3 * slots, 1), :] = meta[t : t + 1]


def pieces(values):
    top = values.astype(jnp.bfloat16).astype(F32)
    return top, values - top


def scatter_kernel(slots, got_ref, meta_ref, weight_out, value_out, acc_ref):
    tiles = got_ref.shape[0]
    rows, width_cols = weight_out.shape
    blocks = width_cols // LANES
    acc_ref[...] = jnp.zeros(acc_ref.shape, F32)
    block_ids = lax.broadcasted_iota(jnp.int32, (blocks, LANES), 0)
    lane_ids = lax.broadcasted_iota(jnp.int32, (LANES, LANES), 0)
    sub = lax.broadcasted_iota(jnp.int32, (GROUP, LANES), 0)

    def source(s, carry):
        count = meta_ref[s, slots]

        def group(g, carry):
            base = pl.multiple_of(g * GROUP, GROUP)
            value = got_ref[s, pl.ds(base, GROUP), :]
            weight = got_ref[s, pl.ds(slots + base, GROUP), :]
            cell = got_ref[s, pl.ds(2 * slots + base, GROUP), :].astype(jnp.int32)
            weight = jnp.where(sub + base < count, weight, 0.0)
            parts = pieces(weight) + pieces(weight * value)
            low = cell % LANES
            high = cell // LANES
            for k in range(GROUP):
                in_block = block_ids == high[k : k + 1]
                left = jnp.concatenate(
                    [jnp.where(in_block, parts[i][k : k + 1], 0.0) for i in (0, 2, 1, 3)], axis=0
                ).astype(jnp.bfloat16)
                right = jnp.where(lane_ids == low[k : k + 1], 1.0, 0.0).astype(jnp.bfloat16)
                both = lax.dot_general(
                    left, right, (((1,), (1,)), ((), ())), preferred_element_type=F32
                )
                row = meta_ref[s, base + k]
                at = pl.ds(pl.multiple_of(row * 2 * blocks, 2 * blocks), 2 * blocks)
                acc_ref[at, :] += both[: 2 * blocks] + both[2 * blocks :]
            return carry

        return lax.fori_loop(0, (count + GROUP - 1) // GROUP, group, carry)

    lax.fori_loop(0, tiles, source, 0)
    for b in range(blocks):
        at = slice(b * LANES, (b + 1) * LANES)
        weight_out[:, at] = acc_ref[pl.ds(b, rows, stride=2 * blocks), :]
        value_out[:, at] = acc_ref[pl.ds(blocks + b, rows, stride=2 * blocks), :]


def edges_kernel(first_ref, second_ref, kappa_ref, total_ref, head_ref, tail_ref):
    rows = first_ref.shape[0]
    margin = head_ref.shape[1]
    total_ref[...] = first_ref[...] + second_ref[...]
    head_ref[0] = total_ref[:margin]
    tail_ref[0] = total_ref[rows - margin :]
    for i in range(2):
        head_ref[1 + i] = kappa_ref[i, :margin]
        tail_ref[1 + i] = kappa_ref[i, rows - margin :]


def ring_rows(rows, margin):
    return -(-(rows + 2 * margin) // 8) * 8


def lay_ring(ref, own, below, above):
    rows, margin, total = own.shape[0], below.shape[0], ref.shape[0]
    ref[rows:total] = jnp.zeros((total - rows, ref.shape[1]), F32)
    ref[:rows] = own
    ref[rows : rows + margin] = below
    ref[total - margin :] = above


def block(ref, j):
    return ref[:, j * LANES : (j + 1) * LANES]


def sideways(ref, j, blocks):
    here = block(ref, j)
    shape = here.shape
    lane = lax.broadcasted_iota(jnp.int32, shape, 1)
    left = pltpu.roll(here, 1, 1)
    right = pltpu.roll(here, LANES - 1, 1)
    before = pltpu.roll(block(ref, j - 1), 1, 1) if j else jnp.zeros(shape, F32)
    after = pltpu.roll(block(ref, j + 1), LANES - 1, 1) if j + 1 < blocks else jnp.zeros(shape, F32)
    return jnp.where(lane == 0, before, left), jnp.where(lane == LANES - 1, after, right)


def face_weights(coef_ref, row_ref, col_ref, rows, margin, has_above, has_below):
    total, width = row_ref.shape
    blocks = width // LANES
    r = lax.broadcasted_iota(jnp.int32, (total, LANES), 0)
    inside = (
        (r < rows)
        | ((r < rows + margin) & has_below)
        | ((r >= total - margin) & has_above)
    )
    scale = jnp.where(inside, 0.125, 0.0)
    unit = jnp.where(inside, 1.0, 0.0)
    for j in range(blocks):
        at = slice(j * LANES, (j + 1) * LANES)
        k_row, k_col = block(row_ref, j), block(col_ref, j)
        k_left, k_right = sideways(col_ref, j, blocks)
        up = scale * (k_row + pltpu.roll(k_row, 1, 0))
        down = scale * (k_row + pltpu.roll(k_row, total - 1, 0))
        left = scale * (k_col + k_left)
        right = scale * (k_col + k_right)
        coef_ref[0, :, at] = unit - up - down - left - right
        coef_ref[1, :, at] = up
        coef_ref[2, :, at] = down
        coef_ref[3, :, at] = left
        coef_ref[4, :, at] = right


def one_pass(source_ref, target_ref, coef_ref):
    total, width = source_ref.shape
    blocks = width // LANES
    for j in range(blocks):
        at = slice(j * LANES, (j + 1) * LANES)
        here = source_ref[:, at]
        left, right = sideways(source_ref, j, blocks)
        target_ref[:, at] = (
            coef_ref[0, :, at] * here
            + coef_ref[1, :, at] * pltpu.roll(here, 1, 0)
            + coef_ref[2, :, at] * pltpu.roll(here, total - 1, 0)
            + coef_ref[3, :, at] * left
            + coef_ref[4, :, at] * right
        )


def diffuse(one_ref, two_ref, coef_ref):
    def twice(index, carry):
        one_pass(one_ref, two_ref, coef_ref)
        one_pass(two_ref, one_ref, coef_ref)
        return carry

    lax.fori_loop(0, PASSES // 2, twice, 0)


def analyse_kernel(tiles, pos_ref, own_ref, above_ref, below_ref, kappa_ref, mask_ref, weight_ref,
                   value_ref, coef_ref, adjoint_ref, head_ref, tail_ref, one_ref, two_ref):
    rows, margin = own_ref.shape[0], above_ref.shape[1]
    lay_ring(one_ref, kappa_ref[0], below_ref[1], above_ref[1])
    lay_ring(two_ref, kappa_ref[1], below_ref[2], above_ref[2])
    tile = pos_ref[1]
    face_weights(coef_ref, one_ref, two_ref, rows, margin, tile > 0, tile + 1 < tiles)
    lay_ring(one_ref, own_ref[...], below_ref[0], above_ref[0])
    diffuse(one_ref, two_ref, coef_ref)
    adjoint_ref[...] = mask_ref[...].astype(F32) * (
        weight_ref[...] * one_ref[:rows] - value_ref[...]
    )
    head_ref[...] = adjoint_ref[:margin]
    tail_ref[...] = adjoint_ref[rows - margin :]


def spread_kernel(own_ref, above_ref, below_ref, coef_ref, out_ref, one_ref, two_ref):
    lay_ring(one_ref, own_ref[...], below_ref[...], above_ref[...])
    diffuse(one_ref, two_ref, coef_ref)
    out_ref[...] = one_ref[: out_ref.shape[0]]


def result_kernel(pos_ref, sens_ref, factor_ref, control_ref, own_ref, other_ref, out_ref):
    var_dev = control_ref.shape[0]
    pos = pos_ref[0]
    core = pos % 2
    for v in range(var_dev):
        mine = response(sens_ref, factor_ref, core, pos * var_dev + v)
        theirs = response(sens_ref, factor_ref, 1 - core, pos * var_dev + v)
        out_ref[v] = control_ref[v] + mine * own_ref[...] + theirs * other_ref[...]


def swap(values, axis, bit):
    count = lax.axis_size(axis)
    return lax.ppermute(values, axis, [(i, i ^ bit) for i in range(count)])


def neighbours(head, tail):
    count = lax.axis_size("tile")
    above = lax.ppermute(tail, "tile", [(i, i + 1) for i in range(count - 1)])
    below = lax.ppermute(head, "tile", [(i + 1, i) for i in range(count - 1)])
    return above, below


def local(control, diffusivity, land_mask, panel_tile, panel_row, panel_cols, obs_values,
          obs_weights, panel_sensor, sensitivity, cross_factor):
    var_dev, rows, width = control.shape
    tiles, members = lax.axis_size("tile"), lax.axis_size("var")
    panels, panel_width = panel_cols.shape
    slots = 2 * panels // tiles
    blocks = width // LANES
    margin = PASSES
    total = ring_rows(rows, margin)
    field = jax.ShapeDtypeStruct((rows, width), F32)
    edge = jax.ShapeDtypeStruct((margin, width), F32)
    edge3 = jax.ShapeDtypeStruct((3, margin, width), F32)
    pos = jnp.stack([lax.axis_index("var"), lax.axis_index("tile")]).astype(jnp.int32)

    own, other = call(combine_kernel, [field, field], [SMEM] * 3 + [VMEM], cost=cost(1000))(
        pos, sensitivity, cross_factor, control
    )
    (send,) = call(
        functools.partial(pack_kernel, slots),
        [jax.ShapeDtypeStruct((tiles, 3 * slots + 8, panel_width), F32)],
        [SMEM] * 4 + [VMEM] * 3,
        [pltpu.VMEM((panels, panel_width), F32), pltpu.SMEM((tiles,), jnp.int32)],
        cost=cost(3000),
    )(pos, panel_tile.reshape(-1), panel_row, panel_sensor, obs_values, obs_weights, panel_cols)
    got = lax.all_to_all(send, "tile", split_axis=0, concat_axis=0, tiled=True)

    part = own + swap(other, "var", 1)
    bit = 2
    while 2 * bit < members:
        part = part + swap(part, "var", bit)
        bit *= 2
    smooth_in, head, tail = call(
        edges_kernel, [field, edge3, edge3], [VMEM] * 3, cost=cost(1000)
    )(part, swap(part, "var", bit), diffusivity)
    above, below = neighbours(head, tail)

    weight_sum, value_sum = call(
        functools.partial(scatter_kernel, slots),
        [field, field],
        [VMEM, SMEM],
        [pltpu.VMEM((rows * 2 * blocks, LANES), F32)],
        cost=cost(10000),
    )(got, got[:, 3 * slots].astype(jnp.int32))

    ring = pltpu.VMEM((total, width), F32)
    coef, adjoint, head, tail = call(
        functools.partial(analyse_kernel, tiles),
        [jax.ShapeDtypeStruct((5, total, width), F32), field, edge, edge],
        [SMEM] + [VMEM] * 7,
        [ring, ring],
        cost=cost(5000),
    )(pos, smooth_in, above, below, diffusivity, land_mask, weight_sum, value_sum)
    above, below = neighbours(head, tail)
    (mine,) = call(spread_kernel, [field], [VMEM] * 4, [ring, ring], cost=cost(4000))(
        adjoint, above, below, coef
    )
    (out,) = call(
        result_kernel,
        [jax.ShapeDtypeStruct(control.shape, F32)],
        [SMEM] * 3 + [VMEM] * 3,
        cost=cost(1000),
    )(pos, sensitivity, cross_factor, control, mine, swap(mine, "var", 1))
    return out


def solution(mesh):
    return jax.shard_map(
        local,
        mesh=mesh,
        in_specs=(
            P("var", ("grp", "tile"), None),
            P(None, ("grp", "tile"), None),
            P(("grp", "tile"), None),
            P(("grp", "tile"), None),
            P(("grp", "tile")),
            P(("grp", "tile"), None),
            P(("grp", "tile"), None),
            P(("grp", "tile"), None),
            P(("grp", "tile")),
            P(),
            P(),
        ),
        out_specs=P("var", ("grp", "tile"), None),
        check_vma=False,
    )
```

```python
import functools

import jax
import jax.numpy as jnp
from jax import lax
from jax.experimental import pallas as pl
from jax.experimental.pallas import tpu as pltpu
from jax.sharding import PartitionSpec as P

PASSES = 10
LANES = 128
GROUP = 8
VMEM = pl.BlockSpec(memory_space=pltpu.VMEM)
SMEM = pl.BlockSpec(memory_space=pltpu.SMEM)
HBM = pl.BlockSpec(memory_space=pltpu.HBM)
F32 = jnp.float32


def call(body, outs, ins, scratch=(), limit=16, cost=None):
    return pl.pallas_call(
        body,
        out_shape=outs,
        in_specs=ins,
        out_specs=[VMEM] * len(outs),
        scratch_shapes=list(scratch),
        compiler_params=pltpu.CompilerParams(vmem_limit_bytes=limit << 20),
        cost_estimate=cost,
    )


def cost(cycles):
    return pl.CostEstimate(flops=cycles * 4096, bytes_accessed=cycles * 1024, transcendentals=0)


def response(sens_ref, factor_ref, sensor, variable):
    total = sens_ref[sensor, 0] * factor_ref[0, variable]
    for u in range(1, factor_ref.shape[0]):
        total = total + sens_ref[sensor, u] * factor_ref[u, variable]
    return total


def first_kernel(slots, margin, pos_ref, sens_hbm, factor_hbm, control_hbm, kappa_hbm, tile_hbm, row_hbm,
                 sensor_hbm, value_hbm, weight_hbm, cols_hbm, *refs):
    outs, refs = refs[:4], refs[4:]
    own_ref, other_ref, even_ref, odd_ref = outs
    tiles = len(refs) - 13
    chunk_refs, refs = refs[:tiles], refs[tiles:]
    (sens_ref, factor_ref, control_ref, kappa_ref, tile_ref, row_ref, sensor_ref, value_ref, weight_ref,
     cols_ref, send_ref, count_ref, sems) = refs
    pairs = (
        (sens_hbm, sens_ref), (factor_hbm, factor_ref), (control_hbm, control_ref),
        (kappa_hbm, kappa_ref), (tile_hbm, tile_ref), (row_hbm, row_ref), (sensor_hbm, sensor_ref),
        (value_hbm, value_ref), (weight_hbm, weight_ref), (cols_hbm, cols_ref),
    )
    copies = [pltpu.make_async_copy(src, dst, sems.at[i]) for i, (src, dst) in enumerate(pairs)]
    for copy in copies:
        copy.start()
    send_ref[...] = jnp.zeros(send_ref.shape, F32)
    for t in range(tiles):
        count_ref[t] = 0
    for copy in copies:
        copy.wait()

    pos, mine = pos_ref[0], pos_ref[1]
    core = pos % 2
    var_dev = control_ref.shape[0]
    for sensor, out_ref in ((1 - core, other_ref), (core, own_ref)):
        total = None
        for v in range(var_dev):
            term = response(sens_ref, factor_ref, sensor, pos * var_dev + v) * control_ref[v]
            total = term if total is None else total + term
        out_ref[...] = total
    for i in range(2):
        pack_edges(even_ref.at[i], odd_ref.at[i], kappa_ref[i], margin, mine % 2 == 0)

    panels = value_ref.shape[0]
    pad_tiles = -(-tiles // 8) * 8
    sub = lax.broadcasted_iota(jnp.int32, (pad_tiles, LANES), 0)
    lane = lax.broadcasted_iota(jnp.int32, (pad_tiles, LANES), 1)

    def place(p, meta):
        t = tile_ref[p]
        keep = sensor_ref[p] == core
        slot = count_ref[t]
        count_ref[t] = slot + keep.astype(jnp.int32)
        trash = 3 * slots + 7
        rows = (value_ref[pl.ds(p, 1), :], weight_ref[pl.ds(p, 1), :], cols_ref[pl.ds(p, 1), :].astype(F32))
        for part, row in enumerate(rows):
            send_ref[t, pl.ds(jnp.where(keep, part * slots + slot, trash), 1), :] = row
        where = jnp.where(keep, slot, LANES)
        return jnp.where((sub == t) & (lane == where), row_ref[p].astype(F32), meta)

    meta = lax.fori_loop(0, panels, place, jnp.zeros((pad_tiles, LANES), F32), unroll=4)
    for t in range(tiles):
        meta = jnp.where((sub == t) & (lane == slots), count_ref[t].astype(F32), meta)
    for t in range(tiles):
        send_ref[t, pl.ds(3 * slots, 1), :] = meta[t : t + 1]
    for d in range(tiles):
        chunk_refs[d][...] = send_ref[mine ^ d]


def pieces(values):
    top = values.astype(jnp.bfloat16).astype(F32)
    return top, values - top


def scatter_kernel(slots, meta_ref, *refs):
    got_refs, (weight_out, value_out, acc_ref) = refs[:-3], refs[-3:]
    rows, width_cols = weight_out.shape
    blocks = width_cols // LANES
    acc_ref[...] = jnp.zeros(acc_ref.shape, F32)
    block_ids = lax.broadcasted_iota(jnp.int32, (blocks, LANES), 0)
    lane_ids = lax.broadcasted_iota(jnp.int32, (LANES, LANES), 0)
    sub = lax.broadcasted_iota(jnp.int32, (GROUP, LANES), 0)

    def source(s, got_ref):
        count = meta_ref[s, slots]

        def group(g, carry):
            base = pl.multiple_of(g * GROUP, GROUP)
            value = got_ref[pl.ds(base, GROUP), :]
            weight = got_ref[pl.ds(slots + base, GROUP), :]
            cell = got_ref[pl.ds(2 * slots + base, GROUP), :].astype(jnp.int32)
            weight = jnp.where(sub + base < count, weight, 0.0)
            parts = pieces(weight) + pieces(weight * value)
            low = cell % LANES
            high = cell // LANES
            for k in range(GROUP):
                in_block = block_ids == high[k : k + 1]
                left = jnp.concatenate(
                    [jnp.where(in_block, parts[i][k : k + 1], 0.0) for i in (0, 2, 1, 3)], axis=0
                ).astype(jnp.bfloat16)
                right = jnp.where(lane_ids == low[k : k + 1], 1.0, 0.0).astype(jnp.bfloat16)
                both = lax.dot_general(
                    left, right, (((1,), (1,)), ((), ())), preferred_element_type=F32
                )
                row = meta_ref[s, base + k]
                at = pl.ds(pl.multiple_of(row * 2 * blocks, 2 * blocks), 2 * blocks)
                acc_ref[at, :] += both[: 2 * blocks] + both[2 * blocks :]
            return carry

        lax.fori_loop(0, (count + GROUP - 1) // GROUP, group, 0)

    for s, got_ref in enumerate(got_refs):
        source(s, got_ref)
    for b in range(blocks):
        at = slice(b * LANES, (b + 1) * LANES)
        weight_out[:, at] = acc_ref[pl.ds(b, rows, stride=2 * blocks), :]
        value_out[:, at] = acc_ref[pl.ds(blocks + b, rows, stride=2 * blocks), :]


def pack_edges(even_ref, odd_ref, rows_value, margin, even):
    rows, width = rows_value.shape
    for b in range(width // LANES):
        at = slice(b * LANES, (b + 1) * LANES)
        head, tail = rows_value[:margin, at], rows_value[rows - margin :, at]
        even_ref[b * margin : (b + 1) * margin] = jnp.where(even, tail, head)
        odd_ref[b * margin : (b + 1) * margin] = jnp.where(even, head, tail)


def edges_kernel(margin, pos_ref, first_ref, second_ref, total_ref, even_ref, odd_ref):
    total = first_ref[...] + second_ref[...]
    total_ref[...] = total
    pack_edges(even_ref, odd_ref, total, margin, pos_ref[1] % 2 == 0)


def ring_rows(rows, margin):
    return -(-(rows + 2 * margin) // 8) * 8


def lay_ring(ref, own, from_even, from_odd, margin, even):
    rows, total = own.shape[0], ref.shape[0]
    ref[rows:total] = jnp.zeros((total - rows, ref.shape[1]), F32)
    ref[:rows] = own
    for b in range(ref.shape[1] // LANES):
        at = slice(b * LANES, (b + 1) * LANES)
        one, two = (m[b * margin : (b + 1) * margin] for m in (from_even, from_odd))
        ref[rows : rows + margin, at] = jnp.where(even, one, two)
        ref[total - margin :, at] = jnp.where(even, two, one)


def block(ref, j):
    return ref[:, j * LANES : (j + 1) * LANES]


def sideways(blocks):
    shape = blocks[0].shape
    lane = lax.broadcasted_iota(jnp.int32, shape, 1)
    zero = jnp.zeros(shape, F32)
    ahead = [pltpu.roll(x, 1, 1) for x in blocks]
    back = [pltpu.roll(x, LANES - 1, 1) for x in blocks]
    for j, here in enumerate(blocks):
        before = ahead[j - 1] if j else zero
        after = back[j + 1] if j + 1 < len(blocks) else zero
        yield here, jnp.where(lane == 0, before, ahead[j]), jnp.where(lane == LANES - 1, after, back[j])


def face_weights(coef_ref, row_ref, col_ref, rows, margin, has_above, has_below):
    total, width = row_ref.shape
    blocks = width // LANES
    r = lax.broadcasted_iota(jnp.int32, (total, LANES), 0)
    inside = (
        (r < rows)
        | ((r < rows + margin) & has_below)
        | ((r >= total - margin) & has_above)
    )
    scale = jnp.where(inside, 0.125, 0.0)
    unit = jnp.where(inside, 1.0, 0.0)
    columns = [block(col_ref, j) for j in range(blocks)]
    for j, (k_col, k_left, k_right) in enumerate(sideways(columns)):
        at = slice(j * LANES, (j + 1) * LANES)
        k_row = block(row_ref, j)
        up = scale * (k_row + pltpu.roll(k_row, 1, 0))
        down = scale * (k_row + pltpu.roll(k_row, total - 1, 0))
        left = scale * (k_col + k_left)
        right = scale * (k_col + k_right)
        coef_ref[0, :, at] = unit - up - down - left - right
        coef_ref[1, :, at] = up
        coef_ref[2, :, at] = down
        coef_ref[3, :, at] = left
        coef_ref[4, :, at] = right


def one_pass(source_ref, target_ref, coef_ref, spans, keep):
    width = source_ref.shape[1]

    def read(ref, *lead, at):
        got = [ref[(*lead, span, at)] for span in spans]
        return jnp.concatenate(got, axis=0) if len(got) > 1 else got[0]

    sections = [slice(j * LANES, (j + 1) * LANES) for j in range(width // LANES)]
    fields = [read(source_ref, at=at) for at in sections]
    total = fields[0].shape[0]
    for at, (here, left, right) in zip(sections, sideways(fields)):
        new = (
            read(coef_ref, 0, at=at) * here
            + read(coef_ref, 1, at=at) * pltpu.roll(here, 1, 0)
            + read(coef_ref, 2, at=at) * pltpu.roll(here, total - 1, 0)
            + read(coef_ref, 3, at=at) * left
            + read(coef_ref, 4, at=at) * right
        )
        start = 0
        for span in spans[:keep]:
            size = span.stop - span.start
            target_ref[span, at] = new[start : start + size]
            start += size


def diffuse(one_ref, two_ref, coef_ref, rows, margin):
    total = one_ref.shape[0]
    wide = [slice(0, total)]
    inner = margin // 8 * 8
    narrow = [slice(0, rows), slice(rows, rows + inner), slice(total - inner, total)]
    first = (margin - inner + 1) // 2

    def twice(spans, index, carry):
        one_pass(one_ref, two_ref, coef_ref, spans, len(spans))
        one_pass(two_ref, one_ref, coef_ref, spans, len(spans))
        return carry

    for i in range(first):
        twice(wide, i, 0)
    lax.fori_loop(0, PASSES // 2 - first - 1, functools.partial(twice, narrow), 0)
    one_pass(one_ref, two_ref, coef_ref, narrow, 3)
    one_pass(two_ref, one_ref, coef_ref, narrow, 1)


def analyse_kernel(tiles, margin, pos_ref, own_ref, even_ref, odd_ref, kappa_ref, kappa_even_ref,
                   kappa_odd_ref, mask_ref, weight_ref, value_ref, coef_ref, adjoint_ref, even_out,
                   odd_out, one_ref, two_ref):
    rows = own_ref.shape[0]
    tile = pos_ref[1]
    even = tile % 2 == 0
    lay_ring(one_ref, kappa_ref[0], kappa_even_ref.at[0], kappa_odd_ref.at[0], margin, even)
    lay_ring(two_ref, kappa_ref[1], kappa_even_ref.at[1], kappa_odd_ref.at[1], margin, even)
    face_weights(coef_ref, one_ref, two_ref, rows, margin, tile > 0, tile + 1 < tiles)
    lay_ring(one_ref, own_ref[...], even_ref, odd_ref, margin, even)
    diffuse(one_ref, two_ref, coef_ref, rows, margin)
    adjoint = mask_ref[...].astype(F32) * (weight_ref[...] * one_ref[:rows] - value_ref[...])
    adjoint_ref[...] = adjoint
    pack_edges(even_out, odd_out, adjoint, margin, even)


def spread_kernel(margin, pos_ref, own_ref, even_ref, odd_ref, coef_ref, out_ref, one_ref, two_ref):
    rows = own_ref.shape[0]
    lay_ring(one_ref, own_ref[...], even_ref, odd_ref, margin, pos_ref[1] % 2 == 0)
    diffuse(one_ref, two_ref, coef_ref, rows, margin)
    out_ref[...] = one_ref[:rows]


def result_kernel(pos_ref, sens_ref, factor_ref, control_ref, own_ref, other_ref, out_ref):
    var_dev = control_ref.shape[0]
    pos = pos_ref[0]
    core = pos % 2
    for v in range(var_dev):
        mine = response(sens_ref, factor_ref, core, pos * var_dev + v)
        theirs = response(sens_ref, factor_ref, 1 - core, pos * var_dev + v)
        out_ref[v] = control_ref[v] + mine * own_ref[...] + theirs * other_ref[...]


def swap(values, axis, bit):
    count = lax.axis_size(axis)
    return lax.ppermute(values, axis, [(i, i ^ bit) for i in range(count)])


def swap_edges(even, odd):
    count = lax.axis_size("tile")
    later = [(i, i + 1) for i in range(1, count - 1, 2)]
    later += [(b, a) for a, b in later]
    return swap(even, "tile", 1), lax.ppermute(odd, "tile", later)


def local(control, diffusivity, land_mask, panel_tile, panel_row, panel_cols, obs_values,
          obs_weights, panel_sensor, sensitivity, cross_factor):
    rows, width = control.shape[1:]
    tiles, members = lax.axis_size("tile"), lax.axis_size("var")
    panels, panel_width = panel_cols.shape
    slots = 2 * panels // tiles
    blocks = width // LANES
    margin = PASSES
    total = ring_rows(rows, margin)
    field = jax.ShapeDtypeStruct((rows, width), F32)
    edge = jax.ShapeDtypeStruct((margin * blocks, LANES), F32)
    edge2 = jax.ShapeDtypeStruct((2, margin * blocks, LANES), F32)
    chunk = jax.ShapeDtypeStruct((3 * slots + 8, panel_width), F32)
    pos = jnp.stack([lax.axis_index("var"), lax.axis_index("tile")]).astype(jnp.int32)

    own, other, kappa_even, kappa_odd, *chunks = call(
        functools.partial(first_kernel, slots, margin),
        [field, field, edge2, edge2] + [chunk] * tiles,
        [SMEM] + [HBM] * 10,
        [
            pltpu.SMEM(sensitivity.shape, F32),
            pltpu.SMEM(cross_factor.shape, F32),
            pltpu.VMEM(control.shape, F32),
            pltpu.VMEM(diffusivity.shape, F32),
            pltpu.SMEM((panels,), jnp.int32),
            pltpu.SMEM((panels,), jnp.int32),
            pltpu.SMEM((panels,), jnp.int32),
            pltpu.VMEM(obs_values.shape, F32),
            pltpu.VMEM(obs_weights.shape, F32),
            pltpu.VMEM(panel_cols.shape, jnp.int32),
            pltpu.VMEM((tiles, *chunk.shape), F32),
            pltpu.SMEM((tiles,), jnp.int32),
            pltpu.SemaphoreType.DMA((10,)),
        ],
        cost=cost(4000),
    )(pos, sensitivity, cross_factor, control, diffusivity, panel_tile.reshape(-1), panel_row,
      panel_sensor, obs_values, obs_weights, panel_cols)

    part = own + swap(other, "var", 1)
    got = [chunks[0]] + [swap(chunks[d], "tile", d) for d in range(1, tiles)]
    kappa_even, kappa_odd = swap_edges(kappa_even, kappa_odd)
    bit = 2
    while 2 * bit < members:
        part = part + swap(part, "var", bit)
        bit *= 2
    smooth_in, even, odd = call(
        functools.partial(edges_kernel, margin),
        [field, edge, edge],
        [SMEM] + [VMEM] * 2,
        cost=cost(500),
    )(pos, part, swap(part, "var", bit))
    even, odd = swap_edges(even, odd)

    meta = jnp.stack([g[3 * slots] for g in got]).astype(jnp.int32)
    weight_sum, value_sum = call(
        functools.partial(scatter_kernel, slots),
        [field, field],
        [SMEM] + [VMEM] * tiles,
        [pltpu.VMEM((rows * 2 * blocks, LANES), F32)],
        cost=cost(10000),
    )(meta, *got)

    ring = pltpu.VMEM((total, width), F32)
    coef, adjoint, even, odd = call(
        functools.partial(analyse_kernel, tiles, margin),
        [jax.ShapeDtypeStruct((5, total, width), F32), field, edge, edge],
        [SMEM] + [VMEM] * 9,
        [ring, ring],
        cost=cost(5000),
    )(pos, smooth_in, even, odd, diffusivity, kappa_even, kappa_odd, land_mask, weight_sum, value_sum)
    even, odd = swap_edges(even, odd)
    (mine,) = call(
        functools.partial(spread_kernel, margin),
        [field],
        [SMEM] + [VMEM] * 4,
        [ring, ring],
        cost=cost(4000),
    )(pos, adjoint, even, odd, coef)
    (out,) = call(
        result_kernel,
        [jax.ShapeDtypeStruct(control.shape, F32)],
        [SMEM] * 3 + [VMEM] * 3,
        cost=cost(1000),
    )(pos, sensitivity, cross_factor, control, mine, swap(mine, "var", 1))
    return out


def solution(mesh):
    return jax.shard_map(
        local,
        mesh=mesh,
        in_specs=(
            P("var", ("grp", "tile"), None),
            P(None, ("grp", "tile"), None),
            P(("grp", "tile"), None),
            P(("grp", "tile"), None),
            P(("grp", "tile")),
            P(("grp", "tile"), None),
            P(("grp", "tile"), None),
            P(("grp", "tile"), None),
            P(("grp", "tile")),
            P(),
            P(),
        ),
        out_specs=P("var", ("grp", "tile"), None),
        check_vma=False,
    )
```

```python
import functools

import jax
import jax.numpy as jnp
from jax import lax
from jax.experimental import pallas as pl
from jax.experimental.pallas import tpu as pltpu
from jax.sharding import PartitionSpec as P

PASSES = 10
LANES = 128
GROUP = 8
VMEM = pl.BlockSpec(memory_space=pltpu.VMEM)
SMEM = pl.BlockSpec(memory_space=pltpu.SMEM)
HBM = pl.BlockSpec(memory_space=pltpu.HBM)
F32 = jnp.float32


def call(body, outs, ins, scratch=(), limit=16, cost=None):
    return pl.pallas_call(
        body,
        out_shape=outs,
        in_specs=ins,
        out_specs=[VMEM] * len(outs),
        scratch_shapes=list(scratch),
        compiler_params=pltpu.CompilerParams(vmem_limit_bytes=limit << 20),
        cost_estimate=cost,
    )


def cost(cycles):
    return pl.CostEstimate(flops=cycles * 4096, bytes_accessed=cycles * 1024, transcendentals=0)


def response(sens_ref, factor_ref, sensor, variable):
    total = sens_ref[sensor, 0] * factor_ref[0, variable]
    for u in range(1, factor_ref.shape[0]):
        total = total + sens_ref[sensor, u] * factor_ref[u, variable]
    return total


def first_kernel(slots, margin, pos_ref, sens_hbm, factor_hbm, control_hbm, kappa_hbm, tile_hbm, row_hbm,
                 sensor_hbm, value_hbm, weight_hbm, cols_hbm, *refs):
    outs, refs = refs[:4], refs[4:]
    own_ref, other_ref, even_ref, odd_ref = outs
    tiles = len(refs) - 13
    chunk_refs, refs = refs[:tiles], refs[tiles:]
    (sens_ref, factor_ref, control_ref, kappa_ref, tile_ref, row_ref, sensor_ref, value_ref, weight_ref,
     cols_ref, send_ref, count_ref, sems) = refs
    pairs = (
        (sens_hbm, sens_ref), (factor_hbm, factor_ref), (control_hbm, control_ref),
        (kappa_hbm, kappa_ref), (tile_hbm, tile_ref), (row_hbm, row_ref), (sensor_hbm, sensor_ref),
        (value_hbm, value_ref), (weight_hbm, weight_ref), (cols_hbm, cols_ref),
    )
    copies = [pltpu.make_async_copy(src, dst, sems.at[i]) for i, (src, dst) in enumerate(pairs)]
    for copy in copies:
        copy.start()
    send_ref[...] = jnp.zeros(send_ref.shape, F32)
    for t in range(tiles):
        count_ref[t] = 0
    for copy in copies:
        copy.wait()

    pos, mine = pos_ref[0], pos_ref[1]
    core = pos % 2
    var_dev = control_ref.shape[0]
    for sensor, out_ref in ((1 - core, other_ref), (core, own_ref)):
        total = None
        for v in range(var_dev):
            term = response(sens_ref, factor_ref, sensor, pos * var_dev + v) * control_ref[v]
            total = term if total is None else total + term
        out_ref[...] = total
    for i in range(2):
        pack_edges(even_ref.at[i], odd_ref.at[i], kappa_ref[i], margin, mine % 2 == 0)

    panels = value_ref.shape[0]
    pad_tiles = -(-tiles // 8) * 8
    sub = lax.broadcasted_iota(jnp.int32, (pad_tiles, LANES), 0)
    lane = lax.broadcasted_iota(jnp.int32, (pad_tiles, LANES), 1)

    def place(p, meta):
        t = tile_ref[p]
        keep = sensor_ref[p] == core
        slot = count_ref[t]
        count_ref[t] = slot + keep.astype(jnp.int32)
        trash = 3 * slots + 7
        rows = (value_ref[pl.ds(p, 1), :], weight_ref[pl.ds(p, 1), :], cols_ref[pl.ds(p, 1), :].astype(F32))
        for part, row in enumerate(rows):
            send_ref[t, pl.ds(jnp.where(keep, part * slots + slot, trash), 1), :] = row
        where = jnp.where(keep, slot, LANES)
        return jnp.where((sub == t) & (lane == where), row_ref[p].astype(F32), meta)

    meta = lax.fori_loop(0, panels, place, jnp.zeros((pad_tiles, LANES), F32), unroll=4)
    for t in range(tiles):
        meta = jnp.where((sub == t) & (lane == slots), count_ref[t].astype(F32), meta)
    for t in range(tiles):
        send_ref[t, pl.ds(3 * slots, 1), :] = meta[t : t + 1]
    for d in range(tiles):
        chunk_refs[d][...] = send_ref[mine ^ d]


def pieces(values):
    top = values.astype(jnp.bfloat16).astype(F32)
    return top, values - top


def scatter_kernel(slots, *refs):
    got_refs, (weight_out, value_out, acc_ref, meta_ref, sems) = refs[:-5], refs[-5:]
    copies = [
        pltpu.make_async_copy(got_ref.at[pl.ds(3 * slots, 1)], meta_ref.at[pl.ds(s, 1)], sems.at[s])
        for s, got_ref in enumerate(got_refs)
    ]
    for copy in copies:
        copy.start()
    rows, width_cols = weight_out.shape
    blocks = width_cols // LANES
    acc_ref[...] = jnp.zeros(acc_ref.shape, F32)
    block_ids = lax.broadcasted_iota(jnp.int32, (blocks, LANES), 0)
    lane_ids = lax.broadcasted_iota(jnp.int32, (LANES, LANES), 0)
    sub = lax.broadcasted_iota(jnp.int32, (GROUP, LANES), 0)
    for copy in copies:
        copy.wait()

    def source(s, got_ref):
        count = meta_ref[s, slots].astype(jnp.int32)

        def group(g, carry):
            base = pl.multiple_of(g * GROUP, GROUP)
            value = got_ref[pl.ds(base, GROUP), :]
            weight = got_ref[pl.ds(slots + base, GROUP), :]
            cell = got_ref[pl.ds(2 * slots + base, GROUP), :].astype(jnp.int32)
            weight = jnp.where(sub + base < count, weight, 0.0)
            parts = pieces(weight) + pieces(weight * value)
            low = cell % LANES
            high = cell // LANES
            for k in range(GROUP):
                in_block = block_ids == high[k : k + 1]
                left = jnp.concatenate(
                    [jnp.where(in_block, parts[i][k : k + 1], 0.0) for i in (0, 2, 1, 3)], axis=0
                ).astype(jnp.bfloat16)
                right = jnp.where(lane_ids == low[k : k + 1], 1.0, 0.0).astype(jnp.bfloat16)
                both = lax.dot_general(
                    left, right, (((1,), (1,)), ((), ())), preferred_element_type=F32
                )
                row = meta_ref[s, base + k].astype(jnp.int32)
                at = pl.ds(pl.multiple_of(row * 2 * blocks, 2 * blocks), 2 * blocks)
                acc_ref[at, :] += both[: 2 * blocks] + both[2 * blocks :]
            return carry

        lax.fori_loop(0, (count + GROUP - 1) // GROUP, group, 0)

    for s, got_ref in enumerate(got_refs):
        source(s, got_ref)
    for b in range(blocks):
        at = slice(b * LANES, (b + 1) * LANES)
        weight_out[:, at] = acc_ref[pl.ds(b, rows, stride=2 * blocks), :]
        value_out[:, at] = acc_ref[pl.ds(blocks + b, rows, stride=2 * blocks), :]


def pack_edges(even_ref, odd_ref, rows_value, margin, even):
    rows, width = rows_value.shape
    for b in range(width // LANES):
        at = slice(b * LANES, (b + 1) * LANES)
        head, tail = rows_value[:margin, at], rows_value[rows - margin :, at]
        even_ref[b * margin : (b + 1) * margin] = jnp.where(even, tail, head)
        odd_ref[b * margin : (b + 1) * margin] = jnp.where(even, head, tail)


def edges_kernel(margin, pos_ref, first_ref, second_ref, total_ref, even_ref, odd_ref):
    total = first_ref[...] + second_ref[...]
    total_ref[...] = total
    pack_edges(even_ref, odd_ref, total, margin, pos_ref[1] % 2 == 0)


def ring_rows(rows, margin):
    return -(-(rows + 2 * margin) // 8) * 8


def lay_ring(ref, own, from_even, from_odd, margin, even):
    rows, total = own.shape[0], ref.shape[0]
    ref[rows:total] = jnp.zeros((total - rows, ref.shape[1]), F32)
    ref[:rows] = own
    for b in range(ref.shape[1] // LANES):
        at = slice(b * LANES, (b + 1) * LANES)
        one, two = (m[b * margin : (b + 1) * margin] for m in (from_even, from_odd))
        ref[rows : rows + margin, at] = jnp.where(even, one, two)
        ref[total - margin :, at] = jnp.where(even, two, one)


def block(ref, j):
    return ref[:, j * LANES : (j + 1) * LANES]


def sideways(blocks):
    shape = blocks[0].shape
    lane = lax.broadcasted_iota(jnp.int32, shape, 1)
    zero = jnp.zeros(shape, F32)
    ahead = [pltpu.roll(x, 1, 1) for x in blocks]
    back = [pltpu.roll(x, LANES - 1, 1) for x in blocks]
    for j, here in enumerate(blocks):
        before = ahead[j - 1] if j else zero
        after = back[j + 1] if j + 1 < len(blocks) else zero
        yield here, jnp.where(lane == 0, before, ahead[j]), jnp.where(lane == LANES - 1, after, back[j])


def face_weights(coef_ref, row_ref, col_ref, rows, margin, has_above, has_below):
    total, width = row_ref.shape
    blocks = width // LANES
    r = lax.broadcasted_iota(jnp.int32, (total, LANES), 0)
    inside = (
        (r < rows)
        | ((r < rows + margin) & has_below)
        | ((r >= total - margin) & has_above)
    )
    scale = jnp.where(inside, 0.125, 0.0)
    unit = jnp.where(inside, 1.0, 0.0)
    columns = [block(col_ref, j) for j in range(blocks)]
    for j, (k_col, k_left, k_right) in enumerate(sideways(columns)):
        at = slice(j * LANES, (j + 1) * LANES)
        k_row = block(row_ref, j)
        up = scale * (k_row + pltpu.roll(k_row, 1, 0))
        down = scale * (k_row + pltpu.roll(k_row, total - 1, 0))
        left = scale * (k_col + k_left)
        right = scale * (k_col + k_right)
        coef_ref[0, :, at] = unit - up - down - left - right
        coef_ref[1, :, at] = up
        coef_ref[2, :, at] = down
        coef_ref[3, :, at] = left
        coef_ref[4, :, at] = right


def one_pass(source_ref, target_ref, coef_ref, spans, keep):
    width = source_ref.shape[1]

    def read(ref, *lead, at):
        got = [ref[(*lead, span, at)] for span in spans]
        return jnp.concatenate(got, axis=0) if len(got) > 1 else got[0]

    sections = [slice(j * LANES, (j + 1) * LANES) for j in range(width // LANES)]
    fields = [read(source_ref, at=at) for at in sections]
    total = fields[0].shape[0]
    for at, (here, left, right) in zip(sections, sideways(fields)):
        new = (
            read(coef_ref, 0, at=at) * here
            + read(coef_ref, 1, at=at) * pltpu.roll(here, 1, 0)
            + read(coef_ref, 2, at=at) * pltpu.roll(here, total - 1, 0)
            + read(coef_ref, 3, at=at) * left
            + read(coef_ref, 4, at=at) * right
        )
        start = 0
        for span in spans[:keep]:
            size = span.stop - span.start
            target_ref[span, at] = new[start : start + size]
            start += size


def diffuse(one_ref, two_ref, coef_ref, rows, margin):
    total = one_ref.shape[0]
    wide = [slice(0, total)]
    inner = margin // 8 * 8
    narrow = [slice(0, rows), slice(rows, rows + inner), slice(total - inner, total)]
    first = (margin - inner + 1) // 2

    def twice(spans, index, carry):
        one_pass(one_ref, two_ref, coef_ref, spans, len(spans))
        one_pass(two_ref, one_ref, coef_ref, spans, len(spans))
        return carry

    for i in range(first):
        twice(wide, i, 0)
    lax.fori_loop(0, PASSES // 2 - first - 1, functools.partial(twice, narrow), 0)
    one_pass(one_ref, two_ref, coef_ref, narrow, 3)
    one_pass(two_ref, one_ref, coef_ref, narrow, 1)


def analyse_kernel(tiles, margin, pos_ref, own_ref, even_ref, odd_ref, kappa_ref, kappa_even_ref,
                   kappa_odd_ref, mask_ref, weight_ref, value_ref, coef_ref, adjoint_ref, even_out,
                   odd_out, one_ref, two_ref):
    rows = own_ref.shape[0]
    tile = pos_ref[1]
    even = tile % 2 == 0
    lay_ring(one_ref, kappa_ref[0], kappa_even_ref.at[0], kappa_odd_ref.at[0], margin, even)
    lay_ring(two_ref, kappa_ref[1], kappa_even_ref.at[1], kappa_odd_ref.at[1], margin, even)
    face_weights(coef_ref, one_ref, two_ref, rows, margin, tile > 0, tile + 1 < tiles)
    lay_ring(one_ref, own_ref[...], even_ref, odd_ref, margin, even)
    diffuse(one_ref, two_ref, coef_ref, rows, margin)
    adjoint = mask_ref[...].astype(F32) * (weight_ref[...] * one_ref[:rows] - value_ref[...])
    adjoint_ref[...] = adjoint
    pack_edges(even_out, odd_out, adjoint, margin, even)


def spread_kernel(margin, pos_ref, own_ref, even_ref, odd_ref, coef_ref, out_ref, one_ref, two_ref):
    rows = own_ref.shape[0]
    lay_ring(one_ref, own_ref[...], even_ref, odd_ref, margin, pos_ref[1] % 2 == 0)
    diffuse(one_ref, two_ref, coef_ref, rows, margin)
    out_ref[...] = one_ref[:rows]


def result_kernel(pos_ref, sens_ref, factor_ref, control_ref, own_ref, other_ref, out_ref):
    var_dev = control_ref.shape[0]
    pos = pos_ref[0]
    core = pos % 2
    for v in range(var_dev):
        mine = response(sens_ref, factor_ref, core, pos * var_dev + v)
        theirs = response(sens_ref, factor_ref, 1 - core, pos * var_dev + v)
        out_ref[v] = control_ref[v] + mine * own_ref[...] + theirs * other_ref[...]


def swap(values, axis, bit):
    count = lax.axis_size(axis)
    return lax.ppermute(values, axis, [(i, i ^ bit) for i in range(count)])


def swap_edges(even, odd):
    count = lax.axis_size("tile")
    later = [(i, i + 1) for i in range(1, count - 1, 2)]
    later += [(b, a) for a, b in later]
    return swap(even, "tile", 1), lax.ppermute(odd, "tile", later)


def in_hbm(values):
    return pltpu.with_memory_space_constraint(values, pltpu.HBM)


def local(control, diffusivity, land_mask, panel_tile, panel_row, panel_cols, obs_values,
          obs_weights, panel_sensor, sensitivity, cross_factor):
    rows, width = control.shape[1:]
    tiles, members = lax.axis_size("tile"), lax.axis_size("var")
    panels, panel_width = panel_cols.shape
    slots = 2 * panels // tiles
    blocks = width // LANES
    margin = PASSES
    total = ring_rows(rows, margin)
    field = jax.ShapeDtypeStruct((rows, width), F32)
    edge = jax.ShapeDtypeStruct((margin * blocks, LANES), F32)
    edge2 = jax.ShapeDtypeStruct((2, margin * blocks, LANES), F32)
    chunk = jax.ShapeDtypeStruct((3 * slots + 8, panel_width), F32)
    pos = jnp.stack([lax.axis_index("var"), lax.axis_index("tile")]).astype(jnp.int32)

    own, other, kappa_even, kappa_odd, *chunks = call(
        functools.partial(first_kernel, slots, margin),
        [field, field, edge2, edge2] + [chunk] * tiles,
        [SMEM] + [HBM] * 10,
        [
            pltpu.SMEM(sensitivity.shape, F32),
            pltpu.SMEM(cross_factor.shape, F32),
            pltpu.VMEM(control.shape, F32),
            pltpu.VMEM(diffusivity.shape, F32),
            pltpu.SMEM((panels,), jnp.int32),
            pltpu.SMEM((panels,), jnp.int32),
            pltpu.SMEM((panels,), jnp.int32),
            pltpu.VMEM(obs_values.shape, F32),
            pltpu.VMEM(obs_weights.shape, F32),
            pltpu.VMEM(panel_cols.shape, jnp.int32),
            pltpu.VMEM((tiles, *chunk.shape), F32),
            pltpu.SMEM((tiles,), jnp.int32),
            pltpu.SemaphoreType.DMA((10,)),
        ],
        cost=cost(4000),
    )(pos, *(in_hbm(x) for x in (sensitivity, cross_factor, control, diffusivity, panel_tile.reshape(-1),
                                 panel_row, panel_sensor, obs_values, obs_weights, panel_cols)))

    part = own + swap(other, "var", 1)
    got = [chunks[0]] + [swap(chunks[d], "tile", d) for d in range(1, tiles)]
    kappa_even, kappa_odd = swap_edges(kappa_even, kappa_odd)
    bit = 2
    while 2 * bit < members:
        part = part + swap(part, "var", bit)
        bit *= 2
    smooth_in, even, odd = call(
        functools.partial(edges_kernel, margin),
        [field, edge, edge],
        [SMEM] + [VMEM] * 2,
        cost=cost(500),
    )(pos, part, swap(part, "var", bit))
    even, odd = swap_edges(even, odd)

    weight_sum, value_sum = call(
        functools.partial(scatter_kernel, slots),
        [field, field],
        [VMEM] * tiles,
        [
            pltpu.VMEM((rows * 2 * blocks, LANES), F32),
            pltpu.SMEM((tiles, LANES), F32),
            pltpu.SemaphoreType.DMA((tiles,)),
        ],
        cost=cost(10000),
    )(*got)

    ring = pltpu.VMEM((total, width), F32)
    coef, adjoint, even, odd = call(
        functools.partial(analyse_kernel, tiles, margin),
        [jax.ShapeDtypeStruct((5, total, width), F32), field, edge, edge],
        [SMEM] + [VMEM] * 9,
        [ring, ring],
        cost=cost(5000),
    )(pos, smooth_in, even, odd, diffusivity, kappa_even, kappa_odd, land_mask, weight_sum, value_sum)
    even, odd = swap_edges(even, odd)
    (mine,) = call(
        functools.partial(spread_kernel, margin),
        [field],
        [SMEM] + [VMEM] * 4,
        [ring, ring],
        cost=cost(4000),
    )(pos, adjoint, even, odd, coef)
    (out,) = call(
        result_kernel,
        [jax.ShapeDtypeStruct(control.shape, F32)],
        [SMEM] * 3 + [VMEM] * 3,
        cost=cost(1000),
    )(pos, sensitivity, cross_factor, control, mine, swap(mine, "var", 1))
    return out


def solution(mesh):
    return jax.shard_map(
        local,
        mesh=mesh,
        in_specs=(
            P("var", ("grp", "tile"), None),
            P(None, ("grp", "tile"), None),
            P(("grp", "tile"), None),
            P(("grp", "tile"), None),
            P(("grp", "tile")),
            P(("grp", "tile"), None),
            P(("grp", "tile"), None),
            P(("grp", "tile"), None),
            P(("grp", "tile")),
            P(),
            P(),
        ),
        out_specs=P("var", ("grp", "tile"), None),
        check_vma=False,
    )
```

```python
import functools

import jax
import jax.numpy as jnp
from jax import lax
from jax.experimental import pallas as pl
from jax.experimental.pallas import tpu as pltpu
from jax.sharding import PartitionSpec as P

PASSES = 10
LANES = 128
GROUP = 8
VMEM = pl.BlockSpec(memory_space=pltpu.VMEM)
SMEM = pl.BlockSpec(memory_space=pltpu.SMEM)
HBM = pl.BlockSpec(memory_space=pltpu.HBM)
AFTER = pl.BlockSpec(memory_space=pl.ANY)
F32 = jnp.float32


def in_hbm(values):
    return pltpu.with_memory_space_constraint(values, pltpu.HBM)


def call(body, outs, ins, scratch=(), limit=16, cost=None):
    return pl.pallas_call(
        body,
        out_shape=outs,
        in_specs=ins,
        out_specs=[VMEM] * len(outs),
        scratch_shapes=list(scratch),
        compiler_params=pltpu.CompilerParams(vmem_limit_bytes=limit << 20),
        cost_estimate=cost,
    )


def cost(cycles):
    return pl.CostEstimate(flops=cycles * 4096, bytes_accessed=cycles * 1024, transcendentals=0)


def response(sens_ref, factor_ref, sensor, variable):
    total = sens_ref[sensor, 0] * factor_ref[0, variable]
    for u in range(1, factor_ref.shape[0]):
        total = total + sens_ref[sensor, u] * factor_ref[u, variable]
    return total


def fetch(pairs, sems):
    copies = [pltpu.make_async_copy(src, dst, sems.at[i]) for i, (src, dst) in enumerate(pairs)]
    for copy in copies:
        copy.start()
    return copies


def offset_of(member, members, turn):
    return turn * members + member // 2 + (member % 2) * (members // 2)


def first_kernel(slots, members, sens_hbm, factor_hbm, control_hbm, tile_hbm, row_hbm, sensor_hbm,
                 value_hbm, weight_hbm, cols_hbm, own_ref, other_ref, response_ref, *refs):
    chunk_refs = refs[:-10]
    (sens_ref, factor_ref, control_ref, tile_ref, row_ref, sensor_ref, value_ref, weight_ref, cols_ref,
     sems) = refs[-10:]
    pairs = (
        (sens_hbm, sens_ref), (factor_hbm, factor_ref), (control_hbm, control_ref), (tile_hbm, tile_ref),
        (row_hbm, row_ref), (sensor_hbm, sensor_ref), (value_hbm, value_ref), (weight_hbm, weight_ref),
        (cols_hbm, cols_ref),
    )
    copies = [pltpu.make_async_copy(src, dst, sems.at[i]) for i, (src, dst) in enumerate(pairs)]
    for copy in copies:
        copy.start()
    for chunk_ref in chunk_refs:
        chunk_ref[...] = jnp.zeros(chunk_ref.shape, F32)
    for copy in copies:
        copy.wait()

    member, mine = lax.axis_index("var"), lax.axis_index("tile")
    core = member % 2
    var_dev = control_ref.shape[0]
    for which, (sensor, out_ref) in enumerate(((core, own_ref), (1 - core, other_ref))):
        total = None
        for v in range(var_dev):
            scale = response(sens_ref, factor_ref, sensor, member * var_dev + v)
            response_ref[which, v] = jnp.full(response_ref.shape[2:], scale, F32)
            term = scale * control_ref[v]
            total = term if total is None else total + term
        out_ref[...] = total

    panels = value_ref.shape[0]
    sub = lax.broadcasted_iota(jnp.int32, (8, LANES), 0)
    lane = lax.broadcasted_iota(jnp.int32, (8, LANES), 1)
    trash = 3 * slots + 7
    for turn, chunk_ref in enumerate(chunk_refs):
        target = mine ^ offset_of(member, members, turn)

        def place(p, carry):
            slot, meta = carry
            keep = tile_ref[p] == target
            rows = (value_ref[pl.ds(p, 1), :], weight_ref[pl.ds(p, 1), :],
                    cols_ref[pl.ds(p, 1), :].astype(F32))
            for part, row in enumerate(rows):
                chunk_ref[pl.ds(jnp.where(keep, part * slots + slot, trash), 1), :] = row
            facts = jnp.where(sub == 0, row_ref[p], sensor_ref[p]).astype(F32)
            meta = jnp.where(lane == jnp.where(keep, slot, LANES), facts, meta)
            return slot + keep.astype(jnp.int32), meta

        count, meta = lax.fori_loop(
            0, panels, place, (jnp.int32(0), jnp.zeros((8, LANES), F32)), unroll=8
        )
        chunk_ref[3 * slots :] = jnp.where(lane == slots, count.astype(F32), meta)


def pieces(values):
    top = values.astype(jnp.bfloat16).astype(F32)
    return top, values - top


def scatter_kernel(slots, after_ref, *refs):
    got_refs, (own_ref, other_ref, acc_ref, meta_ref, sems) = refs[:-5], refs[-5:]
    copies = [
        pltpu.make_async_copy(ref.at[pl.ds(3 * slots, 8)], meta_ref.at[pl.ds(8 * s, 8)], sems.at[s])
        for s, ref in enumerate(got_refs)
    ]
    for copy in copies:
        copy.start()
    rows, width_cols = own_ref.shape[1:]
    blocks = width_cols // LANES
    acc_ref[...] = jnp.zeros(acc_ref.shape, F32)
    block_ids = lax.broadcasted_iota(jnp.int32, (blocks, LANES), 0)
    lane_ids = lax.broadcasted_iota(jnp.int32, (LANES, LANES), 0)
    sub = lax.broadcasted_iota(jnp.int32, (GROUP, LANES), 0)
    for copy in copies:
        copy.wait()

    def source(s, got_ref):
        count = meta_ref[8 * s, slots].astype(jnp.int32)

        def group(g, carry):
            base = pl.multiple_of(g * GROUP, GROUP)
            value = got_ref[pl.ds(base, GROUP), :]
            weight = got_ref[pl.ds(slots + base, GROUP), :]
            cell = got_ref[pl.ds(2 * slots + base, GROUP), :].astype(jnp.int32)
            weight = jnp.where(sub + base < count, weight, 0.0)
            parts = pieces(weight) + pieces(weight * value)
            low = cell % LANES
            high = cell // LANES
            for k in range(GROUP):
                in_block = block_ids == high[k : k + 1]
                left = jnp.concatenate(
                    [jnp.where(in_block, parts[i][k : k + 1], 0.0) for i in (0, 2, 1, 3)], axis=0
                ).astype(jnp.bfloat16)
                right = jnp.where(lane_ids == low[k : k + 1], 1.0, 0.0).astype(jnp.bfloat16)
                both = lax.dot_general(
                    left, right, (((1,), (1,)), ((), ())), preferred_element_type=F32
                )
                row = meta_ref[8 * s, base + k].astype(jnp.int32)
                sensor = meta_ref[8 * s + 1, base + k].astype(jnp.int32)
                at = pl.multiple_of((sensor * rows + row) * 2 * blocks, 2 * blocks)
                acc_ref[pl.ds(at, 2 * blocks), :] += both[: 2 * blocks] + both[2 * blocks :]
            return carry

        lax.fori_loop(0, (count + GROUP - 1) // GROUP, group, 0)

    for s, got_ref in enumerate(got_refs):
        source(s, got_ref)
    core = lax.axis_index("var") % 2
    for sensor, out_ref in ((core, own_ref), (1 - core, other_ref)):
        start = sensor * rows * 2 * blocks
        for kind in range(2):
            for b in range(blocks):
                out_ref[kind, :, b * LANES : (b + 1) * LANES] = acc_ref[
                    pl.ds(start + kind * blocks + b, rows, stride=2 * blocks), :
                ]


def even_tile():
    return lax.axis_index("tile") % 2 == 0


def pack_edges(even_ref, odd_ref, rows_value, margin):
    rows, width = rows_value.shape
    even = even_tile()
    for b in range(width // LANES):
        at = slice(b * LANES, (b + 1) * LANES)
        head, tail = rows_value[:margin, at], rows_value[rows - margin :, at]
        even_ref[b * margin : (b + 1) * margin] = jnp.where(even, tail, head)
        odd_ref[b * margin : (b + 1) * margin] = jnp.where(even, head, tail)


def edges_kernel(margin, sums_ref, first_ref, second_ref, kappa_ref, total_ref, even_ref, odd_ref,
                 sums_out):
    sums_out[...] = sums_ref[...]
    total = first_ref[...] + second_ref[...]
    total_ref[...] = total
    for i, field in enumerate((total, kappa_ref[0], kappa_ref[1])):
        pack_edges(even_ref.at[i], odd_ref.at[i], field, margin)


def ring_rows(rows, margin):
    return -(-(rows + 2 * margin) // 8) * 8


def lay_ring(ref, own, from_even, from_odd, margin):
    rows, total = own.shape[0], ref.shape[0]
    even = even_tile()
    ref[rows:total] = jnp.zeros((total - rows, ref.shape[1]), F32)
    ref[:rows] = own
    for b in range(ref.shape[1] // LANES):
        at = slice(b * LANES, (b + 1) * LANES)
        one, two = (m[b * margin : (b + 1) * margin] for m in (from_even, from_odd))
        ref[rows : rows + margin, at] = jnp.where(even, one, two)
        ref[total - margin :, at] = jnp.where(even, two, one)


def block(ref, j):
    return ref[:, j * LANES : (j + 1) * LANES]


def sideways(blocks):
    shape = blocks[0].shape
    lane = lax.broadcasted_iota(jnp.int32, shape, 1)
    zero = jnp.zeros(shape, F32)
    ahead = [pltpu.roll(x, 1, 1) for x in blocks]
    back = [pltpu.roll(x, LANES - 1, 1) for x in blocks]
    for j, here in enumerate(blocks):
        before = ahead[j - 1] if j else zero
        after = back[j + 1] if j + 1 < len(blocks) else zero
        yield here, jnp.where(lane == 0, before, ahead[j]), jnp.where(lane == LANES - 1, after, back[j])


def face_weights(coef_ref, row_ref, col_ref, rows, margin, has_above, has_below):
    total, width = row_ref.shape
    blocks = width // LANES
    r = lax.broadcasted_iota(jnp.int32, (total, LANES), 0)
    inside = (
        (r < rows)
        | ((r < rows + margin) & has_below)
        | ((r >= total - margin) & has_above)
    )
    scale = jnp.where(inside, 0.125, 0.0)
    unit = jnp.where(inside, 1.0, 0.0)
    columns = [block(col_ref, j) for j in range(blocks)]
    for j, (k_col, k_left, k_right) in enumerate(sideways(columns)):
        at = slice(j * LANES, (j + 1) * LANES)
        k_row = block(row_ref, j)
        up = scale * (k_row + pltpu.roll(k_row, 1, 0))
        down = scale * (k_row + pltpu.roll(k_row, total - 1, 0))
        left = scale * (k_col + k_left)
        right = scale * (k_col + k_right)
        coef_ref[0, :, at] = unit - up - down - left - right
        coef_ref[1, :, at] = up
        coef_ref[2, :, at] = down
        coef_ref[3, :, at] = left
        coef_ref[4, :, at] = right


def one_pass(source_ref, target_ref, coef_ref, spans, keep):
    width = source_ref.shape[1]

    def read(ref, *lead, at):
        got = [ref[(*lead, span, at)] for span in spans]
        return jnp.concatenate(got, axis=0) if len(got) > 1 else got[0]

    sections = [slice(j * LANES, (j + 1) * LANES) for j in range(width // LANES)]
    fields = [read(source_ref, at=at) for at in sections]
    total = fields[0].shape[0]
    for at, (here, left, right) in zip(sections, sideways(fields)):
        new = (
            read(coef_ref, 0, at=at) * here
            + read(coef_ref, 1, at=at) * pltpu.roll(here, 1, 0)
            + read(coef_ref, 2, at=at) * pltpu.roll(here, total - 1, 0)
            + read(coef_ref, 3, at=at) * left
            + read(coef_ref, 4, at=at) * right
        )
        start = 0
        for span in spans[:keep]:
            size = span.stop - span.start
            target_ref[span, at] = new[start : start + size]
            start += size


def diffuse(one_ref, two_ref, coef_ref, rows, margin):
    total = one_ref.shape[0]
    wide = [slice(0, total)]
    inner = margin // 8 * 8
    narrow = [slice(0, rows), slice(rows, rows + inner), slice(total - inner, total)]
    first = (margin - inner + 1) // 2

    def twice(spans, index, carry):
        one_pass(one_ref, two_ref, coef_ref, spans, len(spans))
        one_pass(two_ref, one_ref, coef_ref, spans, len(spans))
        return carry

    for i in range(first):
        twice(wide, i, 0)
    lax.fori_loop(0, PASSES // 2 - first - 1, functools.partial(twice, narrow), 0)
    one_pass(one_ref, two_ref, coef_ref, narrow, 3)
    one_pass(two_ref, one_ref, coef_ref, narrow, 1)


def smooth_kernel(tiles, margin, own_ref, even_ref, odd_ref, kappa_ref, coef_ref, out_ref, one_ref,
                  two_ref):
    rows = own_ref.shape[0]
    tile = lax.axis_index("tile")
    lay_ring(one_ref, kappa_ref[0], even_ref.at[1], odd_ref.at[1], margin)
    lay_ring(two_ref, kappa_ref[1], even_ref.at[2], odd_ref.at[2], margin)
    face_weights(coef_ref, one_ref, two_ref, rows, margin, tile > 0, tile + 1 < tiles)
    lay_ring(one_ref, own_ref[...], even_ref.at[0], odd_ref.at[0], margin)
    diffuse(one_ref, two_ref, coef_ref, rows, margin)
    out_ref[...] = one_ref[:rows]


def adjoint_kernel(margin, smooth_ref, mask_ref, sums_ref, more_ref, adjoint_ref, even_ref, odd_ref):
    weight = sums_ref[0] + more_ref[0]
    value = sums_ref[1] + more_ref[1]
    adjoint = mask_ref[...].astype(F32) * (weight * smooth_ref[...] - value)
    adjoint_ref[...] = adjoint
    pack_edges(even_ref, odd_ref, adjoint, margin)


def spread_kernel(margin, own_ref, even_ref, odd_ref, coef_ref, out_ref, one_ref, two_ref):
    rows = own_ref.shape[0]
    lay_ring(one_ref, own_ref[...], even_ref, odd_ref, margin)
    diffuse(one_ref, two_ref, coef_ref, rows, margin)
    out_ref[...] = one_ref[:rows]


def result_kernel(response_ref, control_ref, own_ref, other_ref, out_ref):
    for v in range(control_ref.shape[0]):
        mine, theirs = (response_ref[i, v][:1, :1] for i in range(2))
        out_ref[v] = control_ref[v] + mine * own_ref[...] + theirs * other_ref[...]


def swap(values, axis, bit):
    count = lax.axis_size(axis)
    return lax.ppermute(values, axis, [(i, i ^ bit) for i in range(count)])


def swap_edges(even, odd):
    count = lax.axis_size("tile")
    later = [(i, i + 1) for i in range(1, count - 1, 2)]
    later += [(b, a) for a, b in later]
    return swap(even, "tile", 1), lax.ppermute(odd, "tile", later)


def in_hbm(values):
    return pltpu.with_memory_space_constraint(values, pltpu.HBM)


def combine(values, members, first):
    bit = first
    while 2 * bit < members:
        values = values + swap(values, "var", bit)
        bit *= 2
    return values, swap(values, "var", bit)


def deliver(chunk, turn):
    tiles, members = lax.axis_size("tile"), lax.axis_size("var")
    pairs = [
        (t * members + q, (t ^ offset_of(q, members, turn)) * members + q)
        for t in range(tiles)
        for q in range(members)
    ]
    return lax.ppermute(chunk, ("tile", "var"), pairs)


def local(control, diffusivity, land_mask, panel_tile, panel_row, panel_cols, obs_values,
          obs_weights, panel_sensor, sensitivity, cross_factor):
    rows, width = control.shape[1:]
    var_dev = control.shape[0]
    tiles, members = lax.axis_size("tile"), lax.axis_size("var")
    panels, panel_width = panel_cols.shape
    slots = 2 * panels // tiles
    turns = tiles // members
    blocks = width // LANES
    margin = PASSES
    total = ring_rows(rows, margin)
    field = jax.ShapeDtypeStruct((rows, width), F32)
    field2 = jax.ShapeDtypeStruct((2, rows, width), F32)
    edge = jax.ShapeDtypeStruct((margin * blocks, LANES), F32)
    edge3 = jax.ShapeDtypeStruct((3, margin * blocks, LANES), F32)
    chunk = jax.ShapeDtypeStruct((3 * slots + 8, panel_width), F32)
    ints = pltpu.SMEM((panels,), jnp.int32)

    own, other, responses, *chunks = call(
        functools.partial(first_kernel, slots, members),
        [field, field, jax.ShapeDtypeStruct((2, var_dev, 8, LANES), F32)] + [chunk] * turns,
        [HBM] * 9,
        [
            pltpu.SMEM(sensitivity.shape, F32),
            pltpu.SMEM(cross_factor.shape, F32),
            pltpu.VMEM(control.shape, F32),
            ints, ints, ints,
            pltpu.VMEM(obs_values.shape, F32),
            pltpu.VMEM(obs_weights.shape, F32),
            pltpu.VMEM(panel_cols.shape, jnp.int32),
            pltpu.SemaphoreType.DMA((9,)),
        ],
        cost=cost(3000),
    )(*(in_hbm(x) for x in (sensitivity, cross_factor, control, panel_tile.reshape(-1), panel_row,
                            panel_sensor, obs_values, obs_weights, panel_cols)))

    got = [deliver(c, turn) for turn, c in enumerate(chunks)]
    part, more = combine(own + swap(other, "var", 1), members, 2)
    sums, sums_other = call(
        functools.partial(scatter_kernel, slots),
        [field2, field2],
        [AFTER] + [VMEM] * turns,
        [
            pltpu.VMEM((2 * rows * 2 * blocks, LANES), F32),
            pltpu.SMEM((8 * turns, LANES), F32),
            pltpu.SemaphoreType.DMA((turns,)),
        ],
        cost=cost(5000),
    )(part, *got)
    smooth_in, even, odd, sums_other = call(
        functools.partial(edges_kernel, margin),
        [field, edge3, edge3, field2],
        [VMEM] * 4,
        cost=cost(500),
    )(sums_other, part, more, diffusivity)
    even, odd = swap_edges(even, odd)
    sums, more_sums = combine(sums + swap(sums_other, "var", 1), members, 2)

    ring = pltpu.VMEM((total, width), F32)
    coef, smooth = call(
        functools.partial(smooth_kernel, tiles, margin),
        [jax.ShapeDtypeStruct((5, total, width), F32), field],
        [VMEM] * 4,
        [ring, ring],
        cost=cost(5000),
    )(smooth_in, even, odd, diffusivity)
    adjoint, even, odd = call(
        functools.partial(adjoint_kernel, margin), [field, edge, edge], [VMEM] * 4, cost=cost(500)
    )(smooth, land_mask, sums, more_sums)
    even, odd = swap_edges(even, odd)
    (mine,) = call(
        functools.partial(spread_kernel, margin),
        [field],
        [VMEM] * 4,
        [ring, ring],
        cost=cost(4000),
    )(adjoint, even, odd, coef)
    (out,) = call(
        result_kernel,
        [jax.ShapeDtypeStruct(control.shape, F32)],
        [VMEM] * 4,
        cost=cost(1000),
    )(responses, control, mine, swap(mine, "var", 1))
    return out


def solution(mesh):
    return jax.shard_map(
        local,
        mesh=mesh,
        in_specs=(
            P("var", ("grp", "tile"), None),
            P(None, ("grp", "tile"), None),
            P(("grp", "tile"), None),
            P(("grp", "tile"), None),
            P(("grp", "tile")),
            P(("grp", "tile"), None),
            P(("grp", "tile"), None),
            P(("grp", "tile"), None),
            P(("grp", "tile")),
            P(),
            P(),
        ),
        out_specs=P("var", ("grp", "tile"), None),
        check_vma=False,
    )
```

```python
import functools

import jax
import jax.numpy as jnp
from jax import lax
from jax.experimental import pallas as pl
from jax.experimental.pallas import tpu as pltpu
from jax.sharding import PartitionSpec as P

PASSES = 10
LANES = 128
GROUP = 8
VMEM = pl.BlockSpec(memory_space=pltpu.VMEM)
SMEM = pl.BlockSpec(memory_space=pltpu.SMEM)
HBM = pl.BlockSpec(memory_space=pltpu.HBM)
AFTER = pl.BlockSpec(memory_space=pl.ANY)
F32 = jnp.float32


def in_hbm(values):
    return pltpu.with_memory_space_constraint(values, pltpu.HBM)


def call(body, outs, ins, scratch=(), limit=16, cost=None):
    return pl.pallas_call(
        body,
        out_shape=outs,
        in_specs=ins,
        out_specs=[VMEM] * len(outs),
        scratch_shapes=list(scratch),
        compiler_params=pltpu.CompilerParams(vmem_limit_bytes=limit << 20),
        cost_estimate=cost,
    )


def cost(cycles):
    return pl.CostEstimate(flops=cycles * 4096, bytes_accessed=cycles * 1024, transcendentals=0)


def response(sens_ref, factor_ref, sensor, variable):
    total = sens_ref[sensor, 0] * factor_ref[0, variable]
    for u in range(1, factor_ref.shape[0]):
        total = total + sens_ref[sensor, u] * factor_ref[u, variable]
    return total


def fetch(pairs, sems):
    copies = [pltpu.make_async_copy(src, dst, sems.at[i]) for i, (src, dst) in enumerate(pairs)]
    for copy in copies:
        copy.start()
    return copies


def first_kernel(slots, sens_hbm, factor_hbm, control_hbm, kappa_hbm, tile_hbm, row_hbm, sensor_hbm,
                 value_hbm, weight_hbm, cols_hbm, own_ref, other_ref, response_ref, kappa_ref, *refs):
    chunk_refs = refs[:-12]
    (sens_ref, factor_ref, control_ref, tile_ref, row_ref, sensor_ref, value_ref, weight_ref, cols_ref,
     send_ref, count_ref, sems) = refs[-12:]
    pairs = (
        (sens_hbm, sens_ref), (factor_hbm, factor_ref), (control_hbm, control_ref),
        (kappa_hbm, kappa_ref), (tile_hbm, tile_ref), (row_hbm, row_ref), (sensor_hbm, sensor_ref),
        (value_hbm, value_ref), (weight_hbm, weight_ref), (cols_hbm, cols_ref),
    )
    copies = [pltpu.make_async_copy(src, dst, sems.at[i]) for i, (src, dst) in enumerate(pairs)]
    for copy in copies:
        copy.start()
    send_ref[...] = jnp.zeros(send_ref.shape, F32)
    turns = len(chunk_refs)
    for turn in range(turns):
        count_ref[turn] = 0
    for copy in copies:
        copy.wait()

    member, mine = lax.axis_index("var"), lax.axis_index("tile")
    core = member % 2
    var_dev = control_ref.shape[0]
    for which, (sensor, out_ref) in enumerate(((core, own_ref), (1 - core, other_ref))):
        total = None
        for v in range(var_dev):
            scale = response(sens_ref, factor_ref, sensor, member * var_dev + v)
            response_ref[which, v] = jnp.full(response_ref.shape[2:], scale, F32)
            term = scale * control_ref[v]
            total = term if total is None else total + term
        out_ref[...] = total

    panels = value_ref.shape[0]
    sub = lax.broadcasted_iota(jnp.int32, (8 * turns, LANES), 0)
    lane = lax.broadcasted_iota(jnp.int32, (8 * turns, LANES), 1)
    trash = 3 * slots + 7

    def place(p, meta):
        turn = (tile_ref[p] ^ mine) - core * turns
        keep = (turn >= 0) & (turn < turns)
        turn = jnp.where(keep, turn, 0)
        slot = count_ref[turn]
        count_ref[turn] = slot + keep.astype(jnp.int32)
        rows = (value_ref[pl.ds(p, 1), :], weight_ref[pl.ds(p, 1), :], cols_ref[pl.ds(p, 1), :].astype(F32))
        for part, row in enumerate(rows):
            send_ref[turn, pl.ds(jnp.where(keep, part * slots + slot, trash), 1), :] = row
        facts = jnp.where(sub == 8 * turn, row_ref[p], sensor_ref[p]).astype(F32)
        here = (lane == jnp.where(keep, slot, LANES)) & (sub // 8 == turn)
        return jnp.where(here, facts, meta)

    meta = lax.fori_loop(0, panels, place, jnp.zeros((8 * turns, LANES), F32), unroll=8)
    for turn, chunk_ref in enumerate(chunk_refs):
        chunk_ref[: 3 * slots] = send_ref[turn, : 3 * slots]
        facts = meta[8 * turn : 8 * turn + 8]
        chunk_ref[3 * slots :] = jnp.where(lane[:8] == slots, count_ref[turn].astype(F32), facts)


def pieces(values):
    top = values.astype(jnp.bfloat16).astype(F32)
    return top, values - top


def scatter_kernel(slots, after_ref, home_ref, *refs):
    got_refs, (own_ref, other_ref, first_ref, acc_ref, meta_ref, sems) = refs[:-6], refs[-6:]
    core = lax.axis_index("var") % 2
    first_ref[...] = jnp.where(core == 0, home_ref[...], got_refs[0][...])
    got_refs = (first_ref, *got_refs[1:])
    copies = [
        pltpu.make_async_copy(ref.at[pl.ds(3 * slots, 8)], meta_ref.at[pl.ds(8 * s, 8)], sems.at[s])
        for s, ref in enumerate(got_refs)
    ]
    for copy in copies:
        copy.start()
    rows, width_cols = own_ref.shape[1:]
    blocks = width_cols // LANES
    acc_ref[...] = jnp.zeros(acc_ref.shape, F32)
    block_ids = lax.broadcasted_iota(jnp.int32, (blocks, LANES), 0)
    lane_ids = lax.broadcasted_iota(jnp.int32, (LANES, LANES), 0).astype(F32).astype(jnp.bfloat16)
    one, zero = jnp.bfloat16(1), jnp.bfloat16(0)
    sub = lax.broadcasted_iota(jnp.int32, (GROUP, LANES), 0)
    for copy in copies:
        copy.wait()

    def source(s, got_ref):
        count = meta_ref[8 * s, slots].astype(jnp.int32)

        def group(g, carry):
            base = pl.multiple_of(g * GROUP, GROUP)
            value = got_ref[pl.ds(base, GROUP), :]
            weight = got_ref[pl.ds(slots + base, GROUP), :]
            cell = got_ref[pl.ds(2 * slots + base, GROUP), :].astype(jnp.int32)
            weight = jnp.where(sub + base < count, weight, 0.0)
            parts = pieces(weight) + pieces(weight * value)
            low = (cell % LANES).astype(F32)
            high = cell // LANES
            for k in range(GROUP):
                in_block = block_ids == high[k : k + 1]
                left = jnp.concatenate(
                    [jnp.where(in_block, parts[i][k : k + 1], 0.0) for i in (0, 2, 1, 3)], axis=0
                ).astype(jnp.bfloat16)
                column = jnp.broadcast_to(low[k : k + 1], (16, LANES)).astype(jnp.bfloat16)
                right = jnp.where(lane_ids == jnp.concatenate([column] * (LANES // 16), axis=0), one, zero)
                both = lax.dot_general(
                    left, right, (((1,), (1,)), ((), ())), preferred_element_type=F32
                )
                row = meta_ref[8 * s, base + k].astype(jnp.int32)
                sensor = meta_ref[8 * s + 1, base + k].astype(jnp.int32)
                at = pl.multiple_of((sensor * rows + row) * 2 * blocks, 2 * blocks)
                acc_ref[pl.ds(at, 2 * blocks), :] += both[: 2 * blocks] + both[2 * blocks :]
            return carry

        lax.fori_loop(0, (count + GROUP - 1) // GROUP, group, 0)

    for s, got_ref in enumerate(got_refs):
        source(s, got_ref)
    for sensor, out_ref in ((core, own_ref), (1 - core, other_ref)):
        start = sensor * rows * 2 * blocks
        for kind in range(2):
            for b in range(blocks):
                out_ref[kind, :, b * LANES : (b + 1) * LANES] = acc_ref[
                    pl.ds(start + kind * blocks + b, rows, stride=2 * blocks), :
                ]


def even_tile():
    return lax.axis_index("tile") % 2 == 0


def has_above():
    return lax.axis_index("tile") > 0


def has_below():
    return lax.axis_index("tile") + 1 < lax.axis_size("tile")


def pack_edges(even_ref, odd_ref, rows_value, margin):
    rows, width = rows_value.shape
    even = even_tile()
    for b in range(width // LANES):
        at = slice(b * LANES, (b + 1) * LANES)
        head, tail = rows_value[:margin, at], rows_value[rows - margin :, at]
        even_ref[b * margin : (b + 1) * margin] = jnp.where(even, tail, head)
        odd_ref[b * margin : (b + 1) * margin] = jnp.where(even, head, tail)


def edges_kernel(margin, first_ref, second_ref, kappa_ref, *refs):
    total_ref, even_ref, odd_ref = refs[-3:]
    total = first_ref[...] + second_ref[...]
    total_ref[...] = total
    for i, field in enumerate((total, kappa_ref[0], kappa_ref[1])):
        pack_edges(even_ref.at[i], odd_ref.at[i], field, margin)


def ring_rows(rows, margin):
    return -(-(rows + 2 * margin) // 8) * 8


def lay_ring(ref, own, from_even, from_odd, margin):
    rows, total = own.shape[0], ref.shape[0]
    even = even_tile()
    ref[rows:total] = jnp.zeros((total - rows, ref.shape[1]), F32)
    ref[:rows] = own
    for b in range(ref.shape[1] // LANES):
        at = slice(b * LANES, (b + 1) * LANES)
        one, two = (m[b * margin : (b + 1) * margin] for m in (from_even, from_odd))
        ref[rows : rows + margin, at] = jnp.where(has_below(), jnp.where(even, one, two), 0.0)
        ref[total - margin :, at] = jnp.where(has_above(), jnp.where(even, two, one), 0.0)


def block(ref, j):
    return ref[:, j * LANES : (j + 1) * LANES]


def sideways(blocks):
    shape = blocks[0].shape
    lane = lax.broadcasted_iota(jnp.int32, shape, 1)
    zero = jnp.zeros(shape, F32)
    ahead = [pltpu.roll(x, 1, 1) for x in blocks]
    back = [pltpu.roll(x, LANES - 1, 1) for x in blocks]
    for j, here in enumerate(blocks):
        before = ahead[j - 1] if j else zero
        after = back[j + 1] if j + 1 < len(blocks) else zero
        yield here, jnp.where(lane == 0, before, ahead[j]), jnp.where(lane == LANES - 1, after, back[j])


def face_weights(coef_ref, row_ref, col_ref, rows, margin):
    total, width = row_ref.shape
    blocks = width // LANES
    r = lax.broadcasted_iota(jnp.int32, (total, LANES), 0)
    inside = (
        (r < rows)
        | ((r < rows + margin) & has_below())
        | ((r >= total - margin) & has_above())
    )
    scale = jnp.where(inside, 0.125, 0.0)
    unit = jnp.where(inside, 1.0, 0.0)
    columns = [block(col_ref, j) for j in range(blocks)]
    for j, (k_col, k_left, k_right) in enumerate(sideways(columns)):
        at = slice(j * LANES, (j + 1) * LANES)
        k_row = block(row_ref, j)
        up = scale * (k_row + pltpu.roll(k_row, 1, 0))
        down = scale * (k_row + pltpu.roll(k_row, total - 1, 0))
        left = scale * (k_col + k_left)
        right = scale * (k_col + k_right)
        coef_ref[0, :, at] = unit - up - down - left - right
        coef_ref[1, :, at] = up
        coef_ref[2, :, at] = down
        coef_ref[3, :, at] = left
        coef_ref[4, :, at] = right


def one_pass(source_ref, target_ref, coef_ref, spans, keep):
    width = source_ref.shape[1]

    def read(ref, *lead, at):
        got = [ref[(*lead, span, at)] for span in spans]
        return jnp.concatenate(got, axis=0) if len(got) > 1 else got[0]

    sections = [slice(j * LANES, (j + 1) * LANES) for j in range(width // LANES)]
    fields = [read(source_ref, at=at) for at in sections]
    total = fields[0].shape[0]
    for at, (here, left, right) in zip(sections, sideways(fields)):
        new = (
            read(coef_ref, 0, at=at) * here
            + read(coef_ref, 1, at=at) * pltpu.roll(here, 1, 0)
            + read(coef_ref, 2, at=at) * pltpu.roll(here, total - 1, 0)
            + read(coef_ref, 3, at=at) * left
            + read(coef_ref, 4, at=at) * right
        )
        start = 0
        for span in spans[:keep]:
            size = span.stop - span.start
            target_ref[span, at] = new[start : start + size]
            start += size


def diffuse(one_ref, two_ref, coef_ref, rows, margin):
    total = one_ref.shape[0]
    wide = [slice(0, total)]
    inner = margin // 8 * 8
    narrow = [slice(0, rows), slice(rows, rows + inner), slice(total - inner, total)]
    first = (margin - inner + 1) // 2

    def twice(spans, index, carry):
        one_pass(one_ref, two_ref, coef_ref, spans, len(spans))
        one_pass(two_ref, one_ref, coef_ref, spans, len(spans))
        return carry

    for i in range(first):
        twice(wide, i, 0)
    lax.fori_loop(0, PASSES // 2 - first - 1, functools.partial(twice, narrow), 0)
    one_pass(one_ref, two_ref, coef_ref, narrow, 3)
    one_pass(two_ref, one_ref, coef_ref, narrow, 1)


def faces_kernel(margin, even_ref, odd_ref, kappa_ref, sums_ref, coef_ref, sums_out, one_ref, two_ref):
    sums_out[...] = sums_ref[...]
    rows = kappa_ref.shape[1]
    lay_ring(one_ref, kappa_ref[0], even_ref.at[1], odd_ref.at[1], margin)
    lay_ring(two_ref, kappa_ref[1], even_ref.at[2], odd_ref.at[2], margin)
    face_weights(coef_ref, one_ref, two_ref, rows, margin)


def smooth_kernel(margin, own_ref, even_ref, odd_ref, coef_ref, out_ref, one_ref, two_ref):
    rows = own_ref.shape[0]
    lay_ring(one_ref, own_ref[...], even_ref.at[0], odd_ref.at[0], margin)
    diffuse(one_ref, two_ref, coef_ref, rows, margin)
    out_ref[...] = one_ref[:rows]


def adjoint_kernel(margin, smooth_ref, mask_ref, sums_ref, more_ref, adjoint_ref, even_ref, odd_ref):
    weight = sums_ref[0] + more_ref[0]
    value = sums_ref[1] + more_ref[1]
    adjoint = mask_ref[...].astype(F32) * (weight * smooth_ref[...] - value)
    adjoint_ref[...] = adjoint
    pack_edges(even_ref, odd_ref, adjoint, margin)


def spread_kernel(margin, own_ref, even_ref, odd_ref, coef_ref, out_ref, one_ref, two_ref):
    rows = own_ref.shape[0]
    lay_ring(one_ref, own_ref[...], even_ref, odd_ref, margin)
    diffuse(one_ref, two_ref, coef_ref, rows, margin)
    out_ref[...] = one_ref[:rows]


def result_kernel(response_ref, control_ref, own_ref, other_ref, out_ref):
    for v in range(control_ref.shape[0]):
        mine, theirs = (response_ref[i, v][:1, :1] for i in range(2))
        out_ref[v] = control_ref[v] + mine * own_ref[...] + theirs * other_ref[...]


def swap(values, axis, bit):
    count = lax.axis_size(axis)
    return lax.ppermute(values, axis, [(i, i ^ bit) for i in range(count)])


def swap_edges(even, odd):
    tiles, members = lax.axis_size("tile"), lax.axis_size("var")
    pairs = []
    for t in range(tiles):
        other = t + 1 if t % 2 else t - 1
        for q in range(members):
            to = other * members + q if 0 <= other < tiles else t * members + (q ^ 1)
            pairs.append((t * members + q, to))
    return swap(even, "tile", 1), lax.ppermute(odd, ("tile", "var"), pairs)


def combine(values, members, first):
    bit = first
    while 2 * bit < members:
        values = values + swap(values, "var", bit)
        bit *= 2
    return values, swap(values, "var", bit)


def deliver(chunk, turn):
    tiles, members = lax.axis_size("tile"), lax.axis_size("var")
    pairs = []
    for t in range(tiles):
        for q in range(members):
            offset = (q % 2) * (tiles // 2) + turn
            pairs.append((t * members + q, (t ^ max(offset, 1)) * members + q))
    return lax.ppermute(chunk, ("tile", "var"), pairs)


def local(control, diffusivity, land_mask, panel_tile, panel_row, panel_cols, obs_values,
          obs_weights, panel_sensor, sensitivity, cross_factor):
    rows, width = control.shape[1:]
    var_dev = control.shape[0]
    tiles, members = lax.axis_size("tile"), lax.axis_size("var")
    panels, panel_width = panel_cols.shape
    slots = 2 * panels // tiles
    turns = tiles // 2
    blocks = width // LANES
    margin = PASSES
    total = ring_rows(rows, margin)
    field = jax.ShapeDtypeStruct((rows, width), F32)
    field2 = jax.ShapeDtypeStruct((2, rows, width), F32)
    edge = jax.ShapeDtypeStruct((margin * blocks, LANES), F32)
    edge3 = jax.ShapeDtypeStruct((3, margin * blocks, LANES), F32)
    chunk = jax.ShapeDtypeStruct((3 * slots + 8, panel_width), F32)
    ints = pltpu.SMEM((panels,), jnp.int32)

    own, other, responses, kappa, *chunks = call(
        functools.partial(first_kernel, slots),
        [field, field, jax.ShapeDtypeStruct((2, var_dev, 8, LANES), F32), field2] + [chunk] * turns,
        [HBM] * 10,
        [
            pltpu.SMEM(sensitivity.shape, F32),
            pltpu.SMEM(cross_factor.shape, F32),
            pltpu.VMEM(control.shape, F32),
            ints, ints, ints,
            pltpu.VMEM(obs_values.shape, F32),
            pltpu.VMEM(obs_weights.shape, F32),
            pltpu.VMEM(panel_cols.shape, jnp.int32),
            pltpu.VMEM((turns, *chunk.shape), F32),
            pltpu.SMEM((turns,), jnp.int32),
            pltpu.SemaphoreType.DMA((10,)),
        ],
        cost=cost(3000),
    )(*(in_hbm(x) for x in (sensitivity, cross_factor, control, diffusivity, panel_tile.reshape(-1),
                            panel_row, panel_sensor, obs_values, obs_weights, panel_cols)))

    got = [deliver(c, turn) for turn, c in enumerate(chunks)]
    part, more = combine(own + swap(other, "var", 1), members, 2)
    smooth_in, even, odd = call(
        functools.partial(edges_kernel, margin),
        [field, edge3, edge3],
        [VMEM] * 3 + [AFTER] * turns,
        cost=cost(500),
    )(part, more, kappa, *got)
    even, odd = swap_edges(even, odd)
    sums, sums_other = call(
        functools.partial(scatter_kernel, slots),
        [field2, field2],
        [AFTER] + [VMEM] * (turns + 1),
        [
            pltpu.VMEM(chunk.shape, F32),
            pltpu.VMEM((2 * rows * 2 * blocks, LANES), F32),
            pltpu.SMEM((8 * turns, LANES), F32),
            pltpu.SemaphoreType.DMA((turns,)),
        ],
        cost=cost(10000),
    )(smooth_in, chunks[0], *got)
    ring = pltpu.VMEM((total, width), F32)
    coef, sums_other = call(
        functools.partial(faces_kernel, margin),
        [jax.ShapeDtypeStruct((5, total, width), F32), field2],
        [VMEM] * 4,
        [ring, ring],
        cost=cost(1000),
    )(even, odd, kappa, sums_other)
    more_sums = swap(sums_other, "var", 1)
    (smooth,) = call(
        functools.partial(smooth_kernel, margin),
        [field],
        [VMEM] * 4,
        [ring, ring],
        cost=cost(4000),
    )(smooth_in, even, odd, coef)
    adjoint, even, odd = call(
        functools.partial(adjoint_kernel, margin), [field, edge, edge], [VMEM] * 4, cost=cost(500)
    )(smooth, land_mask, sums, more_sums)
    even, odd = swap_edges(even, odd)
    (mine,) = call(
        functools.partial(spread_kernel, margin),
        [field],
        [VMEM] * 4,
        [ring, ring],
        cost=cost(4000),
    )(adjoint, even, odd, coef)
    (out,) = call(
        result_kernel,
        [jax.ShapeDtypeStruct(control.shape, F32)],
        [VMEM] * 4,
        cost=cost(1000),
    )(responses, control, mine, swap(mine, "var", 1))
    return out


def solution(mesh):
    return jax.shard_map(
        local,
        mesh=mesh,
        in_specs=(
            P("var", ("grp", "tile"), None),
            P(None, ("grp", "tile"), None),
            P(("grp", "tile"), None),
            P(("grp", "tile"), None),
            P(("grp", "tile")),
            P(("grp", "tile"), None),
            P(("grp", "tile"), None),
            P(("grp", "tile"), None),
            P(("grp", "tile")),
            P(),
            P(),
        ),
        out_specs=P("var", ("grp", "tile"), None),
        check_vma=False,
    )
```

```python
import functools

import jax
import jax.numpy as jnp
from jax import lax
from jax.experimental import pallas as pl
from jax.experimental.pallas import tpu as pltpu
from jax.sharding import PartitionSpec as P

PASSES = 10
LANES = 128
GROUP = 16
VMEM = pl.BlockSpec(memory_space=pltpu.VMEM)
SMEM = pl.BlockSpec(memory_space=pltpu.SMEM)
HBM = pl.BlockSpec(memory_space=pltpu.HBM)
AFTER = pl.BlockSpec(memory_space=pl.ANY)
F32 = jnp.float32


def in_hbm(values):
    return pltpu.with_memory_space_constraint(values, pltpu.HBM)


def call(body, outs, ins, scratch=(), limit=16, cost=None):
    return pl.pallas_call(
        body,
        out_shape=outs,
        in_specs=ins,
        out_specs=[VMEM] * len(outs),
        scratch_shapes=list(scratch),
        compiler_params=pltpu.CompilerParams(vmem_limit_bytes=limit << 20),
        cost_estimate=cost,
    )


def cost(cycles):
    return pl.CostEstimate(flops=cycles * 4096, bytes_accessed=cycles * 1024, transcendentals=0)


def response(sens_ref, factor_ref, sensor, variable):
    total = sens_ref[sensor, 0] * factor_ref[0, variable]
    for u in range(1, factor_ref.shape[0]):
        total = total + sens_ref[sensor, u] * factor_ref[u, variable]
    return total


def fetch(pairs, sems):
    copies = [pltpu.make_async_copy(src, dst, sems.at[i]) for i, (src, dst) in enumerate(pairs)]
    for copy in copies:
        copy.start()
    return copies


def first_kernel(slots, margin, sens_hbm, factor_hbm, control_hbm, kappa_hbm, tile_hbm, row_hbm, sensor_hbm,
                 value_hbm, weight_hbm, cols_hbm, own_ref, other_ref, response_ref, kappa_ref, even_ref,
                 odd_ref, *refs):
    chunk_refs = refs[:-12]
    (sens_ref, factor_ref, control_ref, tile_ref, row_ref, sensor_ref, value_ref, weight_ref, cols_ref,
     send_ref, count_ref, sems) = refs[-12:]
    pairs = (
        (sens_hbm, sens_ref), (factor_hbm, factor_ref), (control_hbm, control_ref),
        (kappa_hbm, kappa_ref), (tile_hbm, tile_ref), (row_hbm, row_ref), (sensor_hbm, sensor_ref),
        (value_hbm, value_ref), (weight_hbm, weight_ref), (cols_hbm, cols_ref),
    )
    copies = [pltpu.make_async_copy(src, dst, sems.at[i]) for i, (src, dst) in enumerate(pairs)]
    for copy in copies:
        copy.start()
    send_ref[...] = jnp.zeros(send_ref.shape, F32)
    turns = len(chunk_refs)
    for turn in range(turns):
        count_ref[turn] = 0
    for copy in copies:
        copy.wait()

    member, mine = lax.axis_index("var"), lax.axis_index("tile")
    core = member % 2
    var_dev = control_ref.shape[0]
    for which, (sensor, out_ref) in enumerate(((core, own_ref), (1 - core, other_ref))):
        total = None
        for v in range(var_dev):
            scale = response(sens_ref, factor_ref, sensor, member * var_dev + v)
            response_ref[which, v] = jnp.full(response_ref.shape[2:], scale, F32)
            term = scale * control_ref[v]
            total = term if total is None else total + term
        out_ref[...] = total
    for i in range(2):
        pack_edges(even_ref.at[i], odd_ref.at[i], kappa_ref[i], margin)

    panels = value_ref.shape[0]
    sub = lax.broadcasted_iota(jnp.int32, (8 * turns, LANES), 0)
    lane = lax.broadcasted_iota(jnp.int32, (8 * turns, LANES), 1)
    trash = 3 * slots + 7

    def place(p, meta):
        turn = (tile_ref[p] ^ mine) - core * turns
        keep = (turn >= 0) & (turn < turns)
        turn = jnp.where(keep, turn, 0)
        slot = count_ref[turn]
        count_ref[turn] = slot + keep.astype(jnp.int32)
        rows = (value_ref[pl.ds(p, 1), :], weight_ref[pl.ds(p, 1), :], cols_ref[pl.ds(p, 1), :].astype(F32))
        for part, row in enumerate(rows):
            send_ref[turn, pl.ds(jnp.where(keep, part * slots + slot, trash), 1), :] = row
        facts = jnp.where(sub == 8 * turn, row_ref[p], sensor_ref[p]).astype(F32)
        here = (lane == jnp.where(keep, slot, LANES)) & (sub // 8 == turn)
        return jnp.where(here, facts, meta)

    meta = lax.fori_loop(0, panels, place, jnp.zeros((8 * turns, LANES), F32), unroll=8)
    for turn, chunk_ref in enumerate(chunk_refs):
        chunk_ref[: 3 * slots] = send_ref[turn, : 3 * slots]
        facts = meta[8 * turn : 8 * turn + 8]
        chunk_ref[3 * slots :] = jnp.where(lane[:8] == slots, count_ref[turn].astype(F32), facts)


def pieces(values):
    top = values.astype(jnp.bfloat16).astype(F32)
    return top, values - top


def scatter_kernel(slots, after_ref, home_ref, *refs):
    got_refs, (own_ref, other_ref, first_ref, acc_ref, meta_ref, sems) = refs[:-6], refs[-6:]
    core = lax.axis_index("var") % 2
    first_ref[...] = jnp.where(core == 0, home_ref[...], got_refs[0][...])
    got_refs = (first_ref, *got_refs[1:])
    copies = [
        pltpu.make_async_copy(ref.at[pl.ds(3 * slots, 8)], meta_ref.at[pl.ds(8 * s, 8)], sems.at[s])
        for s, ref in enumerate(got_refs)
    ]
    for copy in copies:
        copy.start()
    rows, width_cols = own_ref.shape[1:]
    blocks = width_cols // LANES
    acc_ref[...] = jnp.zeros(acc_ref.shape, F32)
    block_ids = lax.broadcasted_iota(jnp.int32, (blocks, LANES), 0)
    lane_ids = lax.broadcasted_iota(jnp.int32, (LANES, LANES), 0).astype(F32).astype(jnp.bfloat16)
    one, zero = jnp.bfloat16(1), jnp.bfloat16(0)
    sub = lax.broadcasted_iota(jnp.int32, (GROUP, LANES), 0)
    for copy in copies:
        copy.wait()

    def source(s, got_ref):
        count = meta_ref[8 * s, slots].astype(jnp.int32)

        def group(g, carry):
            base = pl.multiple_of(g * GROUP, GROUP)
            value = got_ref[pl.ds(base, GROUP), :]
            weight = got_ref[pl.ds(slots + base, GROUP), :]
            cell = got_ref[pl.ds(2 * slots + base, GROUP), :].astype(jnp.int32)
            weight = jnp.where(sub + base < count, weight, 0.0)
            parts = pieces(weight) + pieces(weight * value)
            low = (cell % LANES).astype(F32)
            high = cell // LANES
            for k in range(GROUP):
                in_block = block_ids == high[k : k + 1]
                left = jnp.concatenate(
                    [jnp.where(in_block, parts[i][k : k + 1], 0.0) for i in (0, 2, 1, 3)], axis=0
                ).astype(jnp.bfloat16)
                column = jnp.broadcast_to(low[k : k + 1], (16, LANES)).astype(jnp.bfloat16)
                right = jnp.where(lane_ids == jnp.concatenate([column] * (LANES // 16), axis=0), one, zero)
                both = lax.dot_general(
                    left, right, (((1,), (1,)), ((), ())), preferred_element_type=F32
                )
                row = meta_ref[8 * s, base + k].astype(jnp.int32)
                sensor = meta_ref[8 * s + 1, base + k].astype(jnp.int32)
                at = pl.multiple_of((sensor * rows + row) * 2 * blocks, 2 * blocks)
                acc_ref[pl.ds(at, 2 * blocks), :] += both[: 2 * blocks] + both[2 * blocks :]
            return carry

        lax.fori_loop(0, (count + GROUP - 1) // GROUP, group, 0)

    for s, got_ref in enumerate(got_refs):
        source(s, got_ref)
    for sensor, out_ref in ((core, own_ref), (1 - core, other_ref)):
        start = sensor * rows * 2 * blocks
        for kind in range(2):
            for b in range(blocks):
                out_ref[kind, :, b * LANES : (b + 1) * LANES] = acc_ref[
                    pl.ds(start + kind * blocks + b, rows, stride=2 * blocks), :
                ]


def even_tile():
    return lax.axis_index("tile") % 2 == 0


def has_above():
    return lax.axis_index("tile") > 0


def has_below():
    return lax.axis_index("tile") + 1 < lax.axis_size("tile")


def pack_edges(even_ref, odd_ref, rows_value, margin):
    rows, width = rows_value.shape
    even = even_tile()
    for b in range(width // LANES):
        at = slice(b * LANES, (b + 1) * LANES)
        head, tail = rows_value[:margin, at], rows_value[rows - margin :, at]
        even_ref[b * margin : (b + 1) * margin] = jnp.where(even, tail, head)
        odd_ref[b * margin : (b + 1) * margin] = jnp.where(even, head, tail)


def edges_kernel(margin, first_ref, second_ref, total_ref, even_ref, odd_ref):
    total = first_ref[...] + second_ref[...]
    total_ref[...] = total
    pack_edges(even_ref, odd_ref, total, margin)


def ring_rows(rows, margin):
    return -(-(rows + 2 * margin) // 8) * 8


def lay_ring(ref, own, from_even, from_odd, margin):
    rows, total = own.shape[0], ref.shape[0]
    even = even_tile()
    ref[rows:total] = jnp.zeros((total - rows, ref.shape[1]), F32)
    ref[:rows] = own
    for b in range(ref.shape[1] // LANES):
        at = slice(b * LANES, (b + 1) * LANES)
        one, two = (m[b * margin : (b + 1) * margin] for m in (from_even, from_odd))
        ref[rows : rows + margin, at] = jnp.where(has_below(), jnp.where(even, one, two), 0.0)
        ref[total - margin :, at] = jnp.where(has_above(), jnp.where(even, two, one), 0.0)


def block(ref, j):
    return ref[:, j * LANES : (j + 1) * LANES]


def sideways(blocks):
    shape = blocks[0].shape
    lane = lax.broadcasted_iota(jnp.int32, shape, 1)
    zero = jnp.zeros(shape, F32)
    ahead = [pltpu.roll(x, 1, 1) for x in blocks]
    back = [pltpu.roll(x, LANES - 1, 1) for x in blocks]
    for j, here in enumerate(blocks):
        before = ahead[j - 1] if j else zero
        after = back[j + 1] if j + 1 < len(blocks) else zero
        yield here, jnp.where(lane == 0, before, ahead[j]), jnp.where(lane == LANES - 1, after, back[j])


def face_weights(coef_ref, row_ref, col_ref, rows, margin):
    total, width = row_ref.shape
    blocks = width // LANES
    r = lax.broadcasted_iota(jnp.int32, (total, LANES), 0)
    inside = (
        (r < rows)
        | ((r < rows + margin) & has_below())
        | ((r >= total - margin) & has_above())
    )
    scale = jnp.where(inside, 0.125, 0.0)
    unit = jnp.where(inside, 1.0, 0.0)
    columns = [block(col_ref, j) for j in range(blocks)]
    for j, (k_col, k_left, k_right) in enumerate(sideways(columns)):
        at = slice(j * LANES, (j + 1) * LANES)
        k_row = block(row_ref, j)
        up = scale * (k_row + pltpu.roll(k_row, 1, 0))
        down = scale * (k_row + pltpu.roll(k_row, total - 1, 0))
        left = scale * (k_col + k_left)
        right = scale * (k_col + k_right)
        coef_ref[0, :, at] = unit - up - down - left - right
        coef_ref[1, :, at] = up
        coef_ref[2, :, at] = down
        coef_ref[3, :, at] = left
        coef_ref[4, :, at] = right


def one_pass(source_ref, target_ref, coef_ref, spans, keep):
    width = source_ref.shape[1]

    def read(ref, *lead, at):
        got = [ref[(*lead, span, at)] for span in spans]
        return jnp.concatenate(got, axis=0) if len(got) > 1 else got[0]

    sections = [slice(j * LANES, (j + 1) * LANES) for j in range(width // LANES)]
    fields = [read(source_ref, at=at) for at in sections]
    total = fields[0].shape[0]
    for at, (here, left, right) in zip(sections, sideways(fields)):
        new = (
            read(coef_ref, 0, at=at) * here
            + read(coef_ref, 1, at=at) * pltpu.roll(here, 1, 0)
            + read(coef_ref, 2, at=at) * pltpu.roll(here, total - 1, 0)
            + read(coef_ref, 3, at=at) * left
            + read(coef_ref, 4, at=at) * right
        )
        start = 0
        for span in spans[:keep]:
            size = span.stop - span.start
            target_ref[span, at] = new[start : start + size]
            start += size


def diffuse(one_ref, two_ref, coef_ref, rows, margin):
    total = one_ref.shape[0]
    wide = [slice(0, total)]
    inner = margin // 8 * 8
    narrow = [slice(0, rows), slice(rows, rows + inner), slice(total - inner, total)]
    first = (margin - inner + 1) // 2

    def twice(spans, index, carry):
        one_pass(one_ref, two_ref, coef_ref, spans, len(spans))
        one_pass(two_ref, one_ref, coef_ref, spans, len(spans))
        return carry

    for i in range(first):
        twice(wide, i, 0)
    lax.fori_loop(0, PASSES // 2 - first - 1, functools.partial(twice, narrow), 0)
    one_pass(one_ref, two_ref, coef_ref, narrow, 3)
    one_pass(two_ref, one_ref, coef_ref, narrow, 1)


def faces_kernel(margin, even_ref, odd_ref, kappa_ref, sums_ref, *refs):
    coef_ref, sums_out, one_ref, two_ref = refs[-4:]
    sums_out[...] = sums_ref[...]
    rows = kappa_ref.shape[1]
    lay_ring(one_ref, kappa_ref[0], even_ref.at[0], odd_ref.at[0], margin)
    lay_ring(two_ref, kappa_ref[1], even_ref.at[1], odd_ref.at[1], margin)
    face_weights(coef_ref, one_ref, two_ref, rows, margin)


def smooth_kernel(margin, own_ref, even_ref, odd_ref, coef_ref, out_ref, one_ref, two_ref):
    rows = own_ref.shape[0]
    lay_ring(one_ref, own_ref[...], even_ref, odd_ref, margin)
    diffuse(one_ref, two_ref, coef_ref, rows, margin)
    out_ref[...] = one_ref[:rows]


def adjoint_kernel(margin, smooth_ref, mask_ref, sums_ref, more_ref, adjoint_ref, even_ref, odd_ref):
    weight = sums_ref[0] + more_ref[0]
    value = sums_ref[1] + more_ref[1]
    adjoint = mask_ref[...].astype(F32) * (weight * smooth_ref[...] - value)
    adjoint_ref[...] = adjoint
    pack_edges(even_ref, odd_ref, adjoint, margin)


def spread_kernel(margin, own_ref, even_ref, odd_ref, coef_ref, out_ref, one_ref, two_ref):
    rows = own_ref.shape[0]
    lay_ring(one_ref, own_ref[...], even_ref, odd_ref, margin)
    diffuse(one_ref, two_ref, coef_ref, rows, margin)
    out_ref[...] = one_ref[:rows]


def result_kernel(response_ref, control_ref, own_ref, other_ref, out_ref):
    for v in range(control_ref.shape[0]):
        mine, theirs = (response_ref[i, v][:1, :1] for i in range(2))
        out_ref[v] = control_ref[v] + mine * own_ref[...] + theirs * other_ref[...]


def swap(values, axis, bit):
    count = lax.axis_size(axis)
    return lax.ppermute(values, axis, [(i, i ^ bit) for i in range(count)])


def swap_edges(even, odd):
    tiles, members = lax.axis_size("tile"), lax.axis_size("var")
    pairs = []
    for t in range(tiles):
        other = t + 1 if t % 2 else t - 1
        for q in range(members):
            to = other * members + q if 0 <= other < tiles else t * members + (q ^ 1)
            pairs.append((t * members + q, to))
    return swap(even, "tile", 1), lax.ppermute(odd, ("tile", "var"), pairs)


def combine(values, members, first):
    bit = first
    while 2 * bit < members:
        values = values + swap(values, "var", bit)
        bit *= 2
    return values, swap(values, "var", bit)


def deliver(chunk, turn):
    tiles, members = lax.axis_size("tile"), lax.axis_size("var")
    pairs = []
    for t in range(tiles):
        for q in range(members):
            offset = (q % 2) * (tiles // 2) + turn
            pairs.append((t * members + q, (t ^ max(offset, 1)) * members + q))
    return lax.ppermute(chunk, ("tile", "var"), pairs)


def local(control, diffusivity, land_mask, panel_tile, panel_row, panel_cols, obs_values,
          obs_weights, panel_sensor, sensitivity, cross_factor):
    rows, width = control.shape[1:]
    var_dev = control.shape[0]
    tiles, members = lax.axis_size("tile"), lax.axis_size("var")
    panels, panel_width = panel_cols.shape
    slots = 2 * panels // tiles
    turns = tiles // 2
    blocks = width // LANES
    margin = PASSES
    total = ring_rows(rows, margin)
    field = jax.ShapeDtypeStruct((rows, width), F32)
    field2 = jax.ShapeDtypeStruct((2, rows, width), F32)
    edge = jax.ShapeDtypeStruct((margin * blocks, LANES), F32)
    edge2 = jax.ShapeDtypeStruct((2, margin * blocks, LANES), F32)
    chunk = jax.ShapeDtypeStruct((3 * slots + 8, panel_width), F32)
    ints = pltpu.SMEM((panels,), jnp.int32)

    own, other, responses, kappa, kappa_even, kappa_odd, *chunks = call(
        functools.partial(first_kernel, slots, margin),
        [field, field, jax.ShapeDtypeStruct((2, var_dev, 8, LANES), F32), field2, edge2, edge2]
        + [chunk] * turns,
        [HBM] * 10,
        [
            pltpu.SMEM(sensitivity.shape, F32),
            pltpu.SMEM(cross_factor.shape, F32),
            pltpu.VMEM(control.shape, F32),
            ints, ints, ints,
            pltpu.VMEM(obs_values.shape, F32),
            pltpu.VMEM(obs_weights.shape, F32),
            pltpu.VMEM(panel_cols.shape, jnp.int32),
            pltpu.VMEM((turns, *chunk.shape), F32),
            pltpu.SMEM((turns,), jnp.int32),
            pltpu.SemaphoreType.DMA((10,)),
        ],
        cost=cost(3000),
    )(*(in_hbm(x) for x in (sensitivity, cross_factor, control, diffusivity, panel_tile.reshape(-1),
                            panel_row, panel_sensor, obs_values, obs_weights, panel_cols)))

    got = [deliver(c, turn) for turn, c in enumerate(chunks)]
    kappa_even, kappa_odd = swap_edges(kappa_even, kappa_odd)
    part, more = combine(own + swap(other, "var", 1), members, 2)
    smooth_in, even, odd = call(
        functools.partial(edges_kernel, margin),
        [field, edge, edge],
        [VMEM] * 2,
        cost=cost(500),
    )(part, more)
    even, odd = swap_edges(even, odd)
    sums, sums_other = call(
        functools.partial(scatter_kernel, slots),
        [field2, field2],
        [AFTER] + [VMEM] * (turns + 1),
        [
            pltpu.VMEM(chunk.shape, F32),
            pltpu.VMEM((2 * rows * 2 * blocks, LANES), F32),
            pltpu.SMEM((8 * turns, LANES), F32),
            pltpu.SemaphoreType.DMA((turns,)),
        ],
        cost=cost(100000),
    )(smooth_in, chunks[0], *got)
    ring = pltpu.VMEM((total, width), F32)
    coef, sums_other = call(
        functools.partial(faces_kernel, margin),
        [jax.ShapeDtypeStruct((5, total, width), F32), field2],
        [VMEM] * 4 + [AFTER] * 2,
        [ring, ring],
        cost=cost(1000),
    )(kappa_even, kappa_odd, kappa, sums_other, even, odd)
    more_sums = swap(sums_other, "var", 1)
    (smooth,) = call(
        functools.partial(smooth_kernel, margin),
        [field],
        [VMEM] * 4,
        [ring, ring],
        cost=cost(4000),
    )(smooth_in, even, odd, coef)
    adjoint, even, odd = call(
        functools.partial(adjoint_kernel, margin), [field, edge, edge], [VMEM] * 4, cost=cost(500)
    )(smooth, land_mask, sums, more_sums)
    even, odd = swap_edges(even, odd)
    (mine,) = call(
        functools.partial(spread_kernel, margin),
        [field],
        [VMEM] * 4,
        [ring, ring],
        cost=cost(4000),
    )(adjoint, even, odd, coef)
    (out,) = call(
        result_kernel,
        [jax.ShapeDtypeStruct(control.shape, F32)],
        [VMEM] * 4,
        cost=cost(1000),
    )(responses, control, mine, swap(mine, "var", 1))
    return out


def solution(mesh):
    return jax.shard_map(
        local,
        mesh=mesh,
        in_specs=(
            P("var", ("grp", "tile"), None),
            P(None, ("grp", "tile"), None),
            P(("grp", "tile"), None),
            P(("grp", "tile"), None),
            P(("grp", "tile")),
            P(("grp", "tile"), None),
            P(("grp", "tile"), None),
            P(("grp", "tile"), None),
            P(("grp", "tile")),
            P(),
            P(),
        ),
        out_specs=P("var", ("grp", "tile"), None),
        check_vma=False,
    )
```

```python
import functools

import jax
import jax.numpy as jnp
from jax import lax
from jax.experimental import pallas as pl
from jax.experimental.pallas import tpu as pltpu
from jax.sharding import PartitionSpec as P

PASSES = 10
LANES = 128
GROUP = 16
VMEM = pl.BlockSpec(memory_space=pltpu.VMEM)
SMEM = pl.BlockSpec(memory_space=pltpu.SMEM)
HBM = pl.BlockSpec(memory_space=pltpu.HBM)
AFTER = pl.BlockSpec(memory_space=pl.ANY)
F32 = jnp.float32


def in_hbm(values):
    return pltpu.with_memory_space_constraint(values, pltpu.HBM)


def call(body, outs, ins, scratch=(), limit=16, cost=None):
    return pl.pallas_call(
        body,
        out_shape=outs,
        in_specs=ins,
        out_specs=[VMEM] * len(outs),
        scratch_shapes=list(scratch),
        compiler_params=pltpu.CompilerParams(vmem_limit_bytes=limit << 20),
        cost_estimate=cost,
    )


def cost(cycles):
    return pl.CostEstimate(flops=cycles * 4096, bytes_accessed=cycles * 1024, transcendentals=0)


def response(sens_ref, factor_ref, sensor, variable):
    total = sens_ref[sensor, 0] * factor_ref[0, variable]
    for u in range(1, factor_ref.shape[0]):
        total = total + sens_ref[sensor, u] * factor_ref[u, variable]
    return total


def fetch(pairs, sems):
    copies = [pltpu.make_async_copy(src, dst, sems.at[i]) for i, (src, dst) in enumerate(pairs)]
    for copy in copies:
        copy.start()
    return copies


def offset_of(member, members, turn):
    return turn * members + member // 2 + (member % 2) * (members // 2)


def first_kernel(slots, margin, sens_hbm, factor_hbm, control_hbm, kappa_hbm, tile_hbm, row_hbm, sensor_hbm,
                 value_hbm, weight_hbm, cols_hbm, own_ref, other_ref, response_ref, kappa_ref, even_ref,
                 odd_ref, *refs):
    chunk_refs = refs[:-12]
    (sens_ref, factor_ref, control_ref, tile_ref, row_ref, sensor_ref, value_ref, weight_ref, cols_ref,
     send_ref, count_ref, sems) = refs[-12:]
    pairs = (
        (sens_hbm, sens_ref), (factor_hbm, factor_ref), (control_hbm, control_ref),
        (kappa_hbm, kappa_ref), (tile_hbm, tile_ref), (row_hbm, row_ref), (sensor_hbm, sensor_ref),
        (value_hbm, value_ref), (weight_hbm, weight_ref), (cols_hbm, cols_ref),
    )
    copies = [pltpu.make_async_copy(src, dst, sems.at[i]) for i, (src, dst) in enumerate(pairs)]
    for copy in copies:
        copy.start()
    send_ref[...] = jnp.zeros(send_ref.shape, F32)
    turns = len(chunk_refs)
    for turn in range(turns):
        count_ref[turn] = 0
    for copy in copies:
        copy.wait()

    member, mine = lax.axis_index("var"), lax.axis_index("tile")
    members = lax.axis_size("var")
    core = member % 2
    var_dev = control_ref.shape[0]
    for which, (sensor, out_ref) in enumerate(((core, own_ref), (1 - core, other_ref))):
        total = None
        for v in range(var_dev):
            scale = response(sens_ref, factor_ref, sensor, member * var_dev + v)
            response_ref[which, v] = jnp.full(response_ref.shape[2:], scale, F32)
            term = scale * control_ref[v]
            total = term if total is None else total + term
        out_ref[...] = total
    pack_edges(even_ref, odd_ref, jnp.where(core == 0, kappa_ref[0], kappa_ref[1]), margin)

    panels = value_ref.shape[0]
    sub = lax.broadcasted_iota(jnp.int32, (8 * turns, LANES), 0)
    lane = lax.broadcasted_iota(jnp.int32, (8 * turns, LANES), 1)
    trash = 3 * slots + 7

    def place(p, meta):
        offset = tile_ref[p] ^ mine
        keep = offset % members == offset_of(member, members, 0)
        turn = offset // members
        slot = count_ref[turn]
        count_ref[turn] = slot + keep.astype(jnp.int32)
        rows = (value_ref[pl.ds(p, 1), :], weight_ref[pl.ds(p, 1), :], cols_ref[pl.ds(p, 1), :].astype(F32))
        for part, row in enumerate(rows):
            send_ref[turn, pl.ds(jnp.where(keep, part * slots + slot, trash), 1), :] = row
        facts = jnp.where(sub == 8 * turn, row_ref[p], sensor_ref[p]).astype(F32)
        here = (lane == jnp.where(keep, slot, LANES)) & (sub // 8 == turn)
        return jnp.where(here, facts, meta)

    meta = lax.fori_loop(0, panels, place, jnp.zeros((8 * turns, LANES), F32), unroll=8)
    for turn, chunk_ref in enumerate(chunk_refs):
        chunk_ref[: 3 * slots] = send_ref[turn, : 3 * slots]
        facts = meta[8 * turn : 8 * turn + 8]
        chunk_ref[3 * slots :] = jnp.where(lane[:8] == slots, count_ref[turn].astype(F32), facts)


def pieces(values):
    top = values.astype(jnp.bfloat16).astype(F32)
    return top, values - top


def scatter_kernel(slots, after_ref, *refs):
    got_refs, (own_ref, other_ref, acc_ref, meta_ref, sems) = refs[:-5], refs[-5:]
    core = lax.axis_index("var") % 2
    copies = [
        pltpu.make_async_copy(ref.at[pl.ds(3 * slots, 8)], meta_ref.at[pl.ds(8 * s, 8)], sems.at[s])
        for s, ref in enumerate(got_refs)
    ]
    for copy in copies:
        copy.start()
    rows, width_cols = own_ref.shape[1:]
    blocks = width_cols // LANES
    acc_ref[...] = jnp.zeros(acc_ref.shape, F32)
    block_ids = lax.broadcasted_iota(jnp.int32, (blocks, LANES), 0)
    lane_ids = lax.broadcasted_iota(jnp.int32, (LANES, LANES), 0).astype(F32).astype(jnp.bfloat16)
    one, zero = jnp.bfloat16(1), jnp.bfloat16(0)
    sub = lax.broadcasted_iota(jnp.int32, (GROUP, LANES), 0)
    for copy in copies:
        copy.wait()

    def source(s, got_ref):
        count = meta_ref[8 * s, slots].astype(jnp.int32)

        def group(g, carry):
            base = pl.multiple_of(g * GROUP, GROUP)
            value = got_ref[pl.ds(base, GROUP), :]
            weight = got_ref[pl.ds(slots + base, GROUP), :]
            cell = got_ref[pl.ds(2 * slots + base, GROUP), :].astype(jnp.int32)
            weight = jnp.where(sub + base < count, weight, 0.0)
            parts = pieces(weight) + pieces(weight * value)
            low = (cell % LANES).astype(F32)
            high = cell // LANES
            for k in range(GROUP):
                in_block = block_ids == high[k : k + 1]
                left = jnp.concatenate(
                    [jnp.where(in_block, parts[i][k : k + 1], 0.0) for i in (0, 2, 1, 3)], axis=0
                ).astype(jnp.bfloat16)
                column = jnp.broadcast_to(low[k : k + 1], (16, LANES)).astype(jnp.bfloat16)
                right = jnp.where(lane_ids == jnp.concatenate([column] * (LANES // 16), axis=0), one, zero)
                both = lax.dot_general(
                    left, right, (((1,), (1,)), ((), ())), preferred_element_type=F32
                )
                row = meta_ref[8 * s, base + k].astype(jnp.int32)
                sensor = meta_ref[8 * s + 1, base + k].astype(jnp.int32)
                at = pl.multiple_of((sensor * rows + row) * 2 * blocks, 2 * blocks)
                acc_ref[pl.ds(at, 2 * blocks), :] += both[: 2 * blocks] + both[2 * blocks :]
            return carry

        lax.fori_loop(0, (count + GROUP - 1) // GROUP, group, 0)

    for s, got_ref in enumerate(got_refs):
        source(s, got_ref)
    for sensor, out_ref in ((core, own_ref), (1 - core, other_ref)):
        start = sensor * rows * 2 * blocks
        for kind in range(2):
            for b in range(blocks):
                out_ref[kind, :, b * LANES : (b + 1) * LANES] = acc_ref[
                    pl.ds(start + kind * blocks + b, rows, stride=2 * blocks), :
                ]


def even_tile():
    return lax.axis_index("tile") % 2 == 0


def has_above():
    return lax.axis_index("tile") > 0


def has_below():
    return lax.axis_index("tile") + 1 < lax.axis_size("tile")


def pack_edges(even_ref, odd_ref, rows_value, margin):
    rows, width = rows_value.shape
    even = even_tile()
    for b in range(width // LANES):
        at = slice(b * LANES, (b + 1) * LANES)
        head, tail = rows_value[:margin, at], rows_value[rows - margin :, at]
        even_ref[b * margin : (b + 1) * margin] = jnp.where(even, tail, head)
        odd_ref[b * margin : (b + 1) * margin] = jnp.where(even, head, tail)


def edges_kernel(margin, first_ref, second_ref, kappa_even_ref, kappa_odd_ref, total_ref, even_ref,
                 odd_ref, kappa_ref):
    kappa_ref[0] = kappa_even_ref[...]
    kappa_ref[1] = kappa_odd_ref[...]
    total = first_ref[...] + second_ref[...]
    total_ref[...] = total
    pack_edges(even_ref, odd_ref, total, margin)


def ring_rows(rows, margin):
    return -(-(rows + 2 * margin) // 8) * 8


def lay_ring(ref, own, from_even, from_odd, margin):
    rows, total = own.shape[0], ref.shape[0]
    even = even_tile()
    ref[rows:total] = jnp.zeros((total - rows, ref.shape[1]), F32)
    ref[:rows] = own
    for b in range(ref.shape[1] // LANES):
        at = slice(b * LANES, (b + 1) * LANES)
        one, two = (m[b * margin : (b + 1) * margin] for m in (from_even, from_odd))
        ref[rows : rows + margin, at] = jnp.where(has_below(), jnp.where(even, one, two), 0.0)
        ref[total - margin :, at] = jnp.where(has_above(), jnp.where(even, two, one), 0.0)


def block(ref, j):
    return ref[:, j * LANES : (j + 1) * LANES]


def sideways(blocks):
    shape = blocks[0].shape
    lane = lax.broadcasted_iota(jnp.int32, shape, 1)
    zero = jnp.zeros(shape, F32)
    ahead = [pltpu.roll(x, 1, 1) for x in blocks]
    back = [pltpu.roll(x, LANES - 1, 1) for x in blocks]
    for j, here in enumerate(blocks):
        before = ahead[j - 1] if j else zero
        after = back[j + 1] if j + 1 < len(blocks) else zero
        yield here, jnp.where(lane == 0, before, ahead[j]), jnp.where(lane == LANES - 1, after, back[j])


def face_weights(coef_ref, row_ref, col_ref, rows, margin):
    total, width = row_ref.shape
    blocks = width // LANES
    r = lax.broadcasted_iota(jnp.int32, (total, LANES), 0)
    inside = (
        (r < rows)
        | ((r < rows + margin) & has_below())
        | ((r >= total - margin) & has_above())
    )
    scale = jnp.where(inside, 0.125, 0.0)
    unit = jnp.where(inside, 1.0, 0.0)
    columns = [block(col_ref, j) for j in range(blocks)]
    for j, (k_col, k_left, k_right) in enumerate(sideways(columns)):
        at = slice(j * LANES, (j + 1) * LANES)
        k_row = block(row_ref, j)
        up = scale * (k_row + pltpu.roll(k_row, 1, 0))
        down = scale * (k_row + pltpu.roll(k_row, total - 1, 0))
        left = scale * (k_col + k_left)
        right = scale * (k_col + k_right)
        coef_ref[0, :, at] = unit - up - down - left - right
        coef_ref[1, :, at] = up
        coef_ref[2, :, at] = down
        coef_ref[3, :, at] = left
        coef_ref[4, :, at] = right


def one_pass(source_ref, target_ref, coef_ref, spans, keep):
    width = source_ref.shape[1]

    def read(ref, *lead, at):
        got = [ref[(*lead, span, at)] for span in spans]
        return jnp.concatenate(got, axis=0) if len(got) > 1 else got[0]

    sections = [slice(j * LANES, (j + 1) * LANES) for j in range(width // LANES)]
    fields = [read(source_ref, at=at) for at in sections]
    total = fields[0].shape[0]
    for at, (here, left, right) in zip(sections, sideways(fields)):
        new = (
            read(coef_ref, 0, at=at) * here
            + read(coef_ref, 1, at=at) * pltpu.roll(here, 1, 0)
            + read(coef_ref, 2, at=at) * pltpu.roll(here, total - 1, 0)
            + read(coef_ref, 3, at=at) * left
            + read(coef_ref, 4, at=at) * right
        )
        start = 0
        for span in spans[:keep]:
            size = span.stop - span.start
            target_ref[span, at] = new[start : start + size]
            start += size


def diffuse(one_ref, two_ref, coef_ref, rows, margin):
    total = one_ref.shape[0]
    wide = [slice(0, total)]
    inner = margin // 8 * 8
    narrow = [slice(0, rows), slice(rows, rows + inner), slice(total - inner, total)]
    first = (margin - inner + 1) // 2

    def twice(spans, index, carry):
        one_pass(one_ref, two_ref, coef_ref, spans, len(spans))
        one_pass(two_ref, one_ref, coef_ref, spans, len(spans))
        return carry

    for i in range(first):
        twice(wide, i, 0)
    lax.fori_loop(0, PASSES // 2 - first - 1, functools.partial(twice, narrow), 0)
    one_pass(one_ref, two_ref, coef_ref, narrow, 3)
    one_pass(two_ref, one_ref, coef_ref, narrow, 1)


def faces_kernel(margin, mine_ref, theirs_ref, kappa_ref, sums_ref, *refs):
    coef_ref, sums_out, one_ref, two_ref = refs[-4:]
    sums_out[...] = sums_ref[...]
    rows = kappa_ref.shape[1]
    core = lax.axis_index("var") % 2
    for i, ring_ref in enumerate((one_ref, two_ref)):
        even, odd = (jnp.where(core == i, mine_ref[j], theirs_ref[j]) for j in range(2))
        lay_ring(ring_ref, kappa_ref[i], even, odd, margin)
    face_weights(coef_ref, one_ref, two_ref, rows, margin)


def smooth_kernel(margin, own_ref, even_ref, odd_ref, coef_ref, out_ref, one_ref, two_ref):
    rows = own_ref.shape[0]
    lay_ring(one_ref, own_ref[...], even_ref, odd_ref, margin)
    diffuse(one_ref, two_ref, coef_ref, rows, margin)
    out_ref[...] = one_ref[:rows]


def adjoint_kernel(margin, smooth_ref, mask_ref, sums_ref, more_ref, adjoint_ref, even_ref, odd_ref):
    weight = sums_ref[0] + more_ref[0]
    value = sums_ref[1] + more_ref[1]
    adjoint = mask_ref[...].astype(F32) * (weight * smooth_ref[...] - value)
    adjoint_ref[...] = adjoint
    pack_edges(even_ref, odd_ref, adjoint, margin)


def spread_kernel(margin, own_ref, even_ref, odd_ref, coef_ref, out_ref, one_ref, two_ref):
    rows = own_ref.shape[0]
    lay_ring(one_ref, own_ref[...], even_ref, odd_ref, margin)
    diffuse(one_ref, two_ref, coef_ref, rows, margin)
    out_ref[...] = one_ref[:rows]


def result_kernel(response_ref, control_ref, own_ref, other_ref, out_ref):
    for v in range(control_ref.shape[0]):
        mine, theirs = (response_ref[i, v][:1, :1] for i in range(2))
        out_ref[v] = control_ref[v] + mine * own_ref[...] + theirs * other_ref[...]


def swap(values, axis, bit):
    count = lax.axis_size(axis)
    return lax.ppermute(values, axis, [(i, i ^ bit) for i in range(count)])


def swap_edges(even, odd):
    tiles, members = lax.axis_size("tile"), lax.axis_size("var")
    pairs = []
    for t in range(tiles):
        other = t + 1 if t % 2 else t - 1
        for q in range(members):
            to = other * members + q if 0 <= other < tiles else t * members + (q ^ 1)
            pairs.append((t * members + q, to))
    return swap(even, "tile", 1), lax.ppermute(odd, ("tile", "var"), pairs)


def combine(values, members, first):
    bit = first
    while 2 * bit < members:
        values = values + swap(values, "var", bit)
        bit *= 2
    return values, swap(values, "var", bit)


def deliver(chunk, turn):
    tiles, members = lax.axis_size("tile"), lax.axis_size("var")
    pairs = []
    for t in range(tiles):
        for q in range(members):
            offset = max(offset_of(q, members, turn), 1)
            pairs.append((t * members + q, (t ^ offset) * members + q))
    return lax.ppermute(chunk, ("tile", "var"), pairs)


def share(chunks):
    bit = 2
    while bit < lax.axis_size("var"):
        chunks = chunks + [swap(c, "var", bit) for c in chunks]
        bit *= 2
    return chunks


def local(control, diffusivity, land_mask, panel_tile, panel_row, panel_cols, obs_values,
          obs_weights, panel_sensor, sensitivity, cross_factor):
    rows, width = control.shape[1:]
    var_dev = control.shape[0]
    tiles, members = lax.axis_size("tile"), lax.axis_size("var")
    panels, panel_width = panel_cols.shape
    slots = 2 * panels // tiles
    turns = tiles // members
    blocks = width // LANES
    margin = PASSES
    total = ring_rows(rows, margin)
    field = jax.ShapeDtypeStruct((rows, width), F32)
    field2 = jax.ShapeDtypeStruct((2, rows, width), F32)
    edge = jax.ShapeDtypeStruct((margin * blocks, LANES), F32)
    chunk = jax.ShapeDtypeStruct((3 * slots + 8, panel_width), F32)
    ints = pltpu.SMEM((panels,), jnp.int32)

    own, other, responses, kappa, kappa_even, kappa_odd, *chunks = call(
        functools.partial(first_kernel, slots, margin),
        [field, field, jax.ShapeDtypeStruct((2, var_dev, 8, LANES), F32), field2, edge, edge]
        + [chunk] * turns,
        [HBM] * 10,
        [
            pltpu.SMEM(sensitivity.shape, F32),
            pltpu.SMEM(cross_factor.shape, F32),
            pltpu.VMEM(control.shape, F32),
            ints, ints, ints,
            pltpu.VMEM(obs_values.shape, F32),
            pltpu.VMEM(obs_weights.shape, F32),
            pltpu.VMEM(panel_cols.shape, jnp.int32),
            pltpu.VMEM((turns, *chunk.shape), F32),
            pltpu.SMEM((turns,), jnp.int32),
            pltpu.SemaphoreType.DMA((10,)),
        ],
        cost=cost(3000),
    )(*(in_hbm(x) for x in (sensitivity, cross_factor, control, diffusivity, panel_tile.reshape(-1),
                            panel_row, panel_sensor, obs_values, obs_weights, panel_cols)))

    got = [deliver(c, turn) for turn, c in enumerate(chunks)]
    got[0] = jnp.where(lax.axis_index("var") == 0, chunks[0], got[0])
    got = share(got)
    kappa_even, kappa_odd = swap_edges(kappa_even, kappa_odd)
    part, more = combine(own + swap(other, "var", 1), members, 2)
    smooth_in, even, odd, kappa_mine = call(
        functools.partial(edges_kernel, margin),
        [field, edge, edge, jax.ShapeDtypeStruct((2, *edge.shape), F32)],
        [VMEM] * 4,
        cost=cost(500),
    )(part, more, kappa_even, kappa_odd)
    kappa_theirs = swap(kappa_mine, "var", 1)
    even, odd = swap_edges(even, odd)
    sums, sums_other = call(
        functools.partial(scatter_kernel, slots),
        [field2, field2],
        [AFTER] + [VMEM] * len(got),
        [
            pltpu.VMEM((2 * rows * 2 * blocks, LANES), F32),
            pltpu.SMEM((8 * len(got), LANES), F32),
            pltpu.SemaphoreType.DMA((len(got),)),
        ],
        cost=cost(100000),
    )(smooth_in, *got)
    ring = pltpu.VMEM((total, width), F32)
    coef, sums_other = call(
        functools.partial(faces_kernel, margin),
        [jax.ShapeDtypeStruct((5, total, width), F32), field2],
        [VMEM] * 4 + [AFTER] * 2,
        [ring, ring],
        cost=cost(1000),
    )(kappa_mine, kappa_theirs, kappa, sums_other, even, odd)
    more_sums = swap(sums_other, "var", 1)
    (smooth,) = call(
        functools.partial(smooth_kernel, margin),
        [field],
        [VMEM] * 4,
        [ring, ring],
        cost=cost(4000),
    )(smooth_in, even, odd, coef)
    adjoint, even, odd = call(
        functools.partial(adjoint_kernel, margin), [field, edge, edge], [VMEM] * 4, cost=cost(500)
    )(smooth, land_mask, sums, more_sums)
    even, odd = swap_edges(even, odd)
    (mine,) = call(
        functools.partial(spread_kernel, margin),
        [field],
        [VMEM] * 4,
        [ring, ring],
        cost=cost(4000),
    )(adjoint, even, odd, coef)
    (out,) = call(
        result_kernel,
        [jax.ShapeDtypeStruct(control.shape, F32)],
        [VMEM] * 4,
        cost=cost(1000),
    )(responses, control, mine, swap(mine, "var", 1))
    return out


def solution(mesh):
    return jax.shard_map(
        local,
        mesh=mesh,
        in_specs=(
            P("var", ("grp", "tile"), None),
            P(None, ("grp", "tile"), None),
            P(("grp", "tile"), None),
            P(("grp", "tile"), None),
            P(("grp", "tile")),
            P(("grp", "tile"), None),
            P(("grp", "tile"), None),
            P(("grp", "tile"), None),
            P(("grp", "tile")),
            P(),
            P(),
        ),
        out_specs=P("var", ("grp", "tile"), None),
        check_vma=False,
    )
```

```python
import functools

import jax
import jax.numpy as jnp
from jax import lax
from jax.experimental import pallas as pl
from jax.experimental.pallas import tpu as pltpu
from jax.sharding import PartitionSpec as P

PASSES = 10
LANES = 128
GROUP = 16
VMEM = pl.BlockSpec(memory_space=pltpu.VMEM)
SMEM = pl.BlockSpec(memory_space=pltpu.SMEM)
HBM = pl.BlockSpec(memory_space=pltpu.HBM)
AFTER = pl.BlockSpec(memory_space=pl.ANY)
F32 = jnp.float32


def in_hbm(values):
    return pltpu.with_memory_space_constraint(values, pltpu.HBM)


def call(body, outs, ins, scratch=(), limit=16, cost=None):
    return pl.pallas_call(
        body,
        out_shape=outs,
        in_specs=ins,
        out_specs=[VMEM] * len(outs),
        scratch_shapes=list(scratch),
        compiler_params=pltpu.CompilerParams(vmem_limit_bytes=limit << 20),
        cost_estimate=cost,
    )


def cost(cycles):
    return pl.CostEstimate(flops=cycles * 4096, bytes_accessed=cycles * 1024, transcendentals=0)


def response(sens_ref, factor_ref, sensor, variable):
    total = sens_ref[sensor, 0] * factor_ref[0, variable]
    for u in range(1, factor_ref.shape[0]):
        total = total + sens_ref[sensor, u] * factor_ref[u, variable]
    return total


def fetch(pairs, sems):
    copies = [pltpu.make_async_copy(src, dst, sems.at[i]) for i, (src, dst) in enumerate(pairs)]
    for copy in copies:
        copy.start()
    return copies


def first_kernel(slots, margin, sens_hbm, factor_hbm, control_hbm, kappa_hbm, tile_hbm, row_hbm, sensor_hbm,
                 value_hbm, weight_hbm, cols_hbm, own_ref, other_ref, response_ref, kappa_ref, even_ref,
                 odd_ref, *refs):
    chunk_refs = refs[:-12]
    (sens_ref, factor_ref, control_ref, tile_ref, row_ref, sensor_ref, value_ref, weight_ref, cols_ref,
     send_ref, count_ref, sems) = refs[-12:]
    pairs = (
        (sens_hbm, sens_ref), (factor_hbm, factor_ref), (control_hbm, control_ref),
        (kappa_hbm, kappa_ref), (tile_hbm, tile_ref), (row_hbm, row_ref), (sensor_hbm, sensor_ref),
        (value_hbm, value_ref), (weight_hbm, weight_ref), (cols_hbm, cols_ref),
    )
    copies = [pltpu.make_async_copy(src, dst, sems.at[i]) for i, (src, dst) in enumerate(pairs)]
    for copy in copies:
        copy.start()
    send_ref[...] = jnp.zeros(send_ref.shape, F32)
    turns = len(chunk_refs)
    for turn in range(turns):
        count_ref[turn] = 0
    for copy in copies:
        copy.wait()

    member, mine = lax.axis_index("var"), lax.axis_index("tile")
    core = member % 2
    var_dev = control_ref.shape[0]
    for which, (sensor, out_ref) in enumerate(((core, own_ref), (1 - core, other_ref))):
        total = None
        for v in range(var_dev):
            scale = response(sens_ref, factor_ref, sensor, member * var_dev + v)
            response_ref[which, v] = jnp.full(response_ref.shape[2:], scale, F32)
            term = scale * control_ref[v]
            total = term if total is None else total + term
        out_ref[...] = total
    pack_edges(even_ref, odd_ref, jnp.where(core == 0, kappa_ref[0], kappa_ref[1]), margin)

    panels = value_ref.shape[0]
    sub = lax.broadcasted_iota(jnp.int32, (8 * turns, LANES), 0)
    lane = lax.broadcasted_iota(jnp.int32, (8 * turns, LANES), 1)
    trash = 3 * slots + 7

    def place(p, meta):
        turn = (tile_ref[p] ^ mine) - core * turns
        keep = (turn >= 0) & (turn < turns)
        turn = jnp.where(keep, turn, 0)
        slot = count_ref[turn]
        count_ref[turn] = slot + keep.astype(jnp.int32)
        rows = (value_ref[pl.ds(p, 1), :], weight_ref[pl.ds(p, 1), :], cols_ref[pl.ds(p, 1), :].astype(F32))
        for part, row in enumerate(rows):
            send_ref[turn, pl.ds(jnp.where(keep, part * slots + slot, trash), 1), :] = row
        facts = jnp.where(sub == 8 * turn, row_ref[p], sensor_ref[p]).astype(F32)
        here = (lane == jnp.where(keep, slot, LANES)) & (sub // 8 == turn)
        return jnp.where(here, facts, meta)

    meta = lax.fori_loop(0, panels, place, jnp.zeros((8 * turns, LANES), F32), unroll=8)
    for turn, chunk_ref in enumerate(chunk_refs):
        chunk_ref[: 3 * slots] = send_ref[turn, : 3 * slots]
        facts = meta[8 * turn : 8 * turn + 8]
        chunk_ref[3 * slots :] = jnp.where(lane[:8] == slots, count_ref[turn].astype(F32), facts)


def pieces(values):
    top = values.astype(jnp.bfloat16).astype(F32)
    return top, values - top


def scatter_kernel(slots, after_ref, home_ref, *refs):
    got_refs, (own_ref, other_ref, first_ref, acc_ref, meta_ref, sems) = refs[:-6], refs[-6:]
    core = lax.axis_index("var") % 2
    first_ref[...] = jnp.where(core == 0, home_ref[...], got_refs[0][...])
    got_refs = (first_ref, *got_refs[1:])
    copies = [
        pltpu.make_async_copy(ref.at[pl.ds(3 * slots, 8)], meta_ref.at[pl.ds(8 * s, 8)], sems.at[s])
        for s, ref in enumerate(got_refs)
    ]
    for copy in copies:
        copy.start()
    rows, width_cols = own_ref.shape[1:]
    blocks = width_cols // LANES
    acc_ref[...] = jnp.zeros(acc_ref.shape, F32)
    block_ids = lax.broadcasted_iota(jnp.int32, (blocks, LANES), 0)
    lane_ids = lax.broadcasted_iota(jnp.int32, (LANES, LANES), 0).astype(F32).astype(jnp.bfloat16)
    one, zero = jnp.bfloat16(1), jnp.bfloat16(0)
    sub = lax.broadcasted_iota(jnp.int32, (GROUP, LANES), 0)
    for copy in copies:
        copy.wait()

    def source(s, got_ref):
        count = meta_ref[8 * s, slots].astype(jnp.int32)

        def group(g, carry):
            base = pl.multiple_of(g * GROUP, GROUP)
            value = got_ref[pl.ds(base, GROUP), :]
            weight = got_ref[pl.ds(slots + base, GROUP), :]
            cell = got_ref[pl.ds(2 * slots + base, GROUP), :].astype(jnp.int32)
            weight = jnp.where(sub + base < count, weight, 0.0)
            parts = pieces(weight) + pieces(weight * value)
            low = (cell % LANES).astype(F32)
            high = cell // LANES
            blank = jnp.zeros((4 * blocks, LANES), jnp.bfloat16)
            for k in range(0, GROUP, 2):
                left, right = [], []
                for i in (k, k + 1):
                    in_block = block_ids == high[i : i + 1]
                    rows_of = [jnp.where(in_block, parts[j][i : i + 1], 0.0) for j in (0, 2, 1, 3)]
                    left.append(jnp.concatenate(rows_of, axis=0).astype(jnp.bfloat16))
                    column = jnp.broadcast_to(low[i : i + 1], (16, LANES)).astype(jnp.bfloat16)
                    column = jnp.concatenate([column] * (LANES // 16), axis=0)
                    right.append(jnp.where(lane_ids == column, one, zero))
                left = jnp.concatenate(
                    [
                        jnp.concatenate([left[0], blank], axis=1),
                        jnp.concatenate([blank, left[1]], axis=1),
                    ],
                    axis=0,
                )
                both = lax.dot_general(
                    left, jnp.concatenate(right, axis=1), (((1,), (1,)), ((), ())),
                    preferred_element_type=F32,
                )
                for i in (0, 1):
                    row = meta_ref[8 * s, base + k + i].astype(jnp.int32)
                    sensor = meta_ref[8 * s + 1, base + k + i].astype(jnp.int32)
                    at = pl.multiple_of((sensor * rows + row) * 2 * blocks, 2 * blocks)
                    mine = both[i * 4 * blocks : (i + 1) * 4 * blocks]
                    acc_ref[pl.ds(at, 2 * blocks), :] += mine[: 2 * blocks] + mine[2 * blocks :]
            return carry

        lax.fori_loop(0, (count + GROUP - 1) // GROUP, group, 0)

    for s, got_ref in enumerate(got_refs):
        source(s, got_ref)
    for sensor, out_ref in ((core, own_ref), (1 - core, other_ref)):
        start = sensor * rows * 2 * blocks
        for kind in range(2):
            for b in range(blocks):
                out_ref[kind, :, b * LANES : (b + 1) * LANES] = acc_ref[
                    pl.ds(start + kind * blocks + b, rows, stride=2 * blocks), :
                ]


def even_tile():
    return lax.axis_index("tile") % 2 == 0


def has_above():
    return lax.axis_index("tile") > 0


def has_below():
    return lax.axis_index("tile") + 1 < lax.axis_size("tile")


def pack_edges(even_ref, odd_ref, rows_value, margin):
    rows, width = rows_value.shape
    even = even_tile()
    for b in range(width // LANES):
        at = slice(b * LANES, (b + 1) * LANES)
        head, tail = rows_value[:margin, at], rows_value[rows - margin :, at]
        even_ref[b * margin : (b + 1) * margin] = jnp.where(even, tail, head)
        odd_ref[b * margin : (b + 1) * margin] = jnp.where(even, head, tail)


def sum_kernel(own_ref, other_ref, kappa_even_ref, kappa_odd_ref, part_ref, kappa_ref):
    kappa_ref[0] = kappa_even_ref[...]
    kappa_ref[1] = kappa_odd_ref[...]
    part_ref[...] = own_ref[...] + other_ref[...]


def edges_kernel(margin, first_ref, second_ref, *refs):
    total_ref, even_ref, odd_ref = refs[-3:]
    total = first_ref[...] + second_ref[...]
    total_ref[...] = total
    pack_edges(even_ref, odd_ref, total, margin)


def ring_rows(rows, margin):
    return -(-(rows + 2 * margin) // 8) * 8


def lay_ring(ref, own, from_even, from_odd, margin):
    rows, total = own.shape[0], ref.shape[0]
    even = even_tile()
    ref[rows:total] = jnp.zeros((total - rows, ref.shape[1]), F32)
    ref[:rows] = own
    for b in range(ref.shape[1] // LANES):
        at = slice(b * LANES, (b + 1) * LANES)
        one, two = (m[b * margin : (b + 1) * margin] for m in (from_even, from_odd))
        ref[rows : rows + margin, at] = jnp.where(has_below(), jnp.where(even, one, two), 0.0)
        ref[total - margin :, at] = jnp.where(has_above(), jnp.where(even, two, one), 0.0)


def block(ref, j):
    return ref[:, j * LANES : (j + 1) * LANES]


def sideways(blocks):
    shape = blocks[0].shape
    lane = lax.broadcasted_iota(jnp.int32, shape, 1)
    zero = jnp.zeros(shape, F32)
    ahead = [pltpu.roll(x, 1, 1) for x in blocks]
    back = [pltpu.roll(x, LANES - 1, 1) for x in blocks]
    for j, here in enumerate(blocks):
        before = ahead[j - 1] if j else zero
        after = back[j + 1] if j + 1 < len(blocks) else zero
        yield here, jnp.where(lane == 0, before, ahead[j]), jnp.where(lane == LANES - 1, after, back[j])


def face_weights(coef_ref, row_ref, col_ref, rows, margin):
    total, width = row_ref.shape
    blocks = width // LANES
    r = lax.broadcasted_iota(jnp.int32, (total, LANES), 0)
    inside = (
        (r < rows)
        | ((r < rows + margin) & has_below())
        | ((r >= total - margin) & has_above())
    )
    scale = jnp.where(inside, 0.125, 0.0)
    unit = jnp.where(inside, 1.0, 0.0)
    columns = [block(col_ref, j) for j in range(blocks)]
    for j, (k_col, k_left, k_right) in enumerate(sideways(columns)):
        at = slice(j * LANES, (j + 1) * LANES)
        k_row = block(row_ref, j)
        up = scale * (k_row + pltpu.roll(k_row, 1, 0))
        down = scale * (k_row + pltpu.roll(k_row, total - 1, 0))
        left = scale * (k_col + k_left)
        right = scale * (k_col + k_right)
        coef_ref[0, :, at] = unit - up - down - left - right
        coef_ref[1, :, at] = up
        coef_ref[2, :, at] = down
        coef_ref[3, :, at] = left
        coef_ref[4, :, at] = right


def one_pass(source_ref, target_ref, coef_ref, spans, keep):
    width = source_ref.shape[1]

    def read(ref, *lead, at):
        got = [ref[(*lead, span, at)] for span in spans]
        return jnp.concatenate(got, axis=0) if len(got) > 1 else got[0]

    sections = [slice(j * LANES, (j + 1) * LANES) for j in range(width // LANES)]
    fields = [read(source_ref, at=at) for at in sections]
    total = fields[0].shape[0]
    for at, (here, left, right) in zip(sections, sideways(fields)):
        new = (
            read(coef_ref, 0, at=at) * here
            + read(coef_ref, 1, at=at) * pltpu.roll(here, 1, 0)
            + read(coef_ref, 2, at=at) * pltpu.roll(here, total - 1, 0)
            + read(coef_ref, 3, at=at) * left
            + read(coef_ref, 4, at=at) * right
        )
        start = 0
        for span in spans[:keep]:
            size = span.stop - span.start
            target_ref[span, at] = new[start : start + size]
            start += size


def diffuse(one_ref, two_ref, coef_ref, rows, margin):
    total = one_ref.shape[0]
    wide = [slice(0, total)]
    inner = margin // 8 * 8
    narrow = [slice(0, rows), slice(rows, rows + inner), slice(total - inner, total)]
    first = (margin - inner + 1) // 2

    def twice(spans, index, carry):
        one_pass(one_ref, two_ref, coef_ref, spans, len(spans))
        one_pass(two_ref, one_ref, coef_ref, spans, len(spans))
        return carry

    for i in range(first):
        twice(wide, i, 0)
    lax.fori_loop(0, PASSES // 2 - first - 1, functools.partial(twice, narrow), 0)
    one_pass(one_ref, two_ref, coef_ref, narrow, 3)
    one_pass(two_ref, one_ref, coef_ref, narrow, 1)


def faces_kernel(margin, mine_ref, theirs_ref, kappa_ref, sums_ref, *refs):
    coef_ref, sums_out, one_ref, two_ref = refs[-4:]
    sums_out[...] = sums_ref[...]
    rows = kappa_ref.shape[1]
    core = lax.axis_index("var") % 2
    for i, ring_ref in enumerate((one_ref, two_ref)):
        even, odd = (jnp.where(core == i, mine_ref[j], theirs_ref[j]) for j in range(2))
        lay_ring(ring_ref, kappa_ref[i], even, odd, margin)
    face_weights(coef_ref, one_ref, two_ref, rows, margin)


def smooth_kernel(margin, own_ref, even_ref, odd_ref, coef_ref, out_ref, one_ref, two_ref):
    rows = own_ref.shape[0]
    lay_ring(one_ref, own_ref[...], even_ref, odd_ref, margin)
    diffuse(one_ref, two_ref, coef_ref, rows, margin)
    out_ref[...] = one_ref[:rows]


def adjoint_kernel(margin, smooth_ref, mask_ref, sums_ref, more_ref, adjoint_ref, even_ref, odd_ref):
    weight = sums_ref[0] + more_ref[0]
    value = sums_ref[1] + more_ref[1]
    adjoint = mask_ref[...].astype(F32) * (weight * smooth_ref[...] - value)
    adjoint_ref[...] = adjoint
    pack_edges(even_ref, odd_ref, adjoint, margin)


def spread_kernel(margin, own_ref, even_ref, odd_ref, coef_ref, out_ref, one_ref, two_ref):
    rows = own_ref.shape[0]
    lay_ring(one_ref, own_ref[...], even_ref, odd_ref, margin)
    diffuse(one_ref, two_ref, coef_ref, rows, margin)
    out_ref[...] = one_ref[:rows]


def result_kernel(response_ref, control_ref, own_ref, other_ref, out_ref):
    for v in range(control_ref.shape[0]):
        mine, theirs = (response_ref[i, v][:1, :1] for i in range(2))
        out_ref[v] = control_ref[v] + mine * own_ref[...] + theirs * other_ref[...]


def swap(values, axis, bit):
    count = lax.axis_size(axis)
    return lax.ppermute(values, axis, [(i, i ^ bit) for i in range(count)])


def swap_edges(even, odd):
    tiles, members = lax.axis_size("tile"), lax.axis_size("var")
    pairs = []
    for t in range(tiles):
        other = t + 1 if t % 2 else t - 1
        for q in range(members):
            to = other * members + q if 0 <= other < tiles else t * members + (q ^ 1)
            pairs.append((t * members + q, to))
    return swap(even, "tile", 1), lax.ppermute(odd, ("tile", "var"), pairs)


def combine(values, members, first):
    bit = first
    while 2 * bit < members:
        values = values + swap(values, "var", bit)
        bit *= 2
    return values, swap(values, "var", bit)


def deliver(chunk, turn):
    tiles, members = lax.axis_size("tile"), lax.axis_size("var")
    pairs = []
    for t in range(tiles):
        for q in range(members):
            offset = (q % 2) * (tiles // 2) + turn
            pairs.append((t * members + q, (t ^ max(offset, 1)) * members + q))
    return lax.ppermute(chunk, ("tile", "var"), pairs)


def local(control, diffusivity, land_mask, panel_tile, panel_row, panel_cols, obs_values,
          obs_weights, panel_sensor, sensitivity, cross_factor):
    rows, width = control.shape[1:]
    var_dev = control.shape[0]
    tiles, members = lax.axis_size("tile"), lax.axis_size("var")
    panels, panel_width = panel_cols.shape
    slots = 2 * panels // tiles
    turns = tiles // 2
    blocks = width // LANES
    margin = PASSES
    total = ring_rows(rows, margin)
    field = jax.ShapeDtypeStruct((rows, width), F32)
    field2 = jax.ShapeDtypeStruct((2, rows, width), F32)
    edge = jax.ShapeDtypeStruct((margin * blocks, LANES), F32)
    edge2 = jax.ShapeDtypeStruct((2, margin * blocks, LANES), F32)
    chunk = jax.ShapeDtypeStruct((3 * slots + 8, panel_width), F32)
    ints = pltpu.SMEM((panels,), jnp.int32)

    own, other, responses, kappa, kappa_even, kappa_odd, *chunks = call(
        functools.partial(first_kernel, slots, margin),
        [field, field, jax.ShapeDtypeStruct((2, var_dev, 8, LANES), F32), field2, edge, edge]
        + [chunk] * turns,
        [HBM] * 10,
        [
            pltpu.SMEM(sensitivity.shape, F32),
            pltpu.SMEM(cross_factor.shape, F32),
            pltpu.VMEM(control.shape, F32),
            ints, ints, ints,
            pltpu.VMEM(obs_values.shape, F32),
            pltpu.VMEM(obs_weights.shape, F32),
            pltpu.VMEM(panel_cols.shape, jnp.int32),
            pltpu.VMEM((turns, *chunk.shape), F32),
            pltpu.SMEM((turns,), jnp.int32),
            pltpu.SemaphoreType.DMA((10,)),
        ],
        cost=cost(3000),
    )(*(in_hbm(x) for x in (sensitivity, cross_factor, control, diffusivity, panel_tile.reshape(-1),
                            panel_row, panel_sensor, obs_values, obs_weights, panel_cols)))

    got = [deliver(c, turn) for turn, c in enumerate(chunks)]
    part, kappa_mine = call(sum_kernel, [field, edge2], [VMEM] * 4, cost=cost(200))(
        own, swap(other, "var", 1), *swap_edges(kappa_even, kappa_odd)
    )
    kappa_theirs = swap(kappa_mine, "var", 1)
    part, more = combine(part, members, 2)
    smooth_in, even, odd = call(
        functools.partial(edges_kernel, margin),
        [field, edge, edge],
        [VMEM] * 2 + [AFTER] * turns,
        cost=cost(500),
    )(part, more, *got)
    even, odd = swap_edges(even, odd)
    sums, sums_other = call(
        functools.partial(scatter_kernel, slots),
        [field2, field2],
        [AFTER] + [VMEM] * (turns + 1),
        [
            pltpu.VMEM(chunk.shape, F32),
            pltpu.VMEM((2 * rows * 2 * blocks, LANES), F32),
            pltpu.SMEM((8 * turns, LANES), F32),
            pltpu.SemaphoreType.DMA((turns,)),
        ],
        cost=cost(100000),
    )(smooth_in, chunks[0], *got)
    ring = pltpu.VMEM((total, width), F32)
    coef, sums_other = call(
        functools.partial(faces_kernel, margin),
        [jax.ShapeDtypeStruct((5, total, width), F32), field2],
        [VMEM] * 4 + [AFTER] * 2,
        [ring, ring],
        cost=cost(1000),
    )(kappa_mine, kappa_theirs, kappa, sums_other, even, odd)
    more_sums = swap(sums_other, "var", 1)
    (smooth,) = call(
        functools.partial(smooth_kernel, margin),
        [field],
        [VMEM] * 4,
        [ring, ring],
        cost=cost(4000),
    )(smooth_in, even, odd, coef)
    adjoint, even, odd = call(
        functools.partial(adjoint_kernel, margin), [field, edge, edge], [VMEM] * 4, cost=cost(500)
    )(smooth, land_mask, sums, more_sums)
    even, odd = swap_edges(even, odd)
    (mine,) = call(
        functools.partial(spread_kernel, margin),
        [field],
        [VMEM] * 4,
        [ring, ring],
        cost=cost(4000),
    )(adjoint, even, odd, coef)
    (out,) = call(
        result_kernel,
        [jax.ShapeDtypeStruct(control.shape, F32)],
        [VMEM] * 4,
        cost=cost(1000),
    )(responses, control, mine, swap(mine, "var", 1))
    return out


def solution(mesh):
    return jax.shard_map(
        local,
        mesh=mesh,
        in_specs=(
            P("var", ("grp", "tile"), None),
            P(None, ("grp", "tile"), None),
            P(("grp", "tile"), None),
            P(("grp", "tile"), None),
            P(("grp", "tile")),
            P(("grp", "tile"), None),
            P(("grp", "tile"), None),
            P(("grp", "tile"), None),
            P(("grp", "tile")),
            P(),
            P(),
        ),
        out_specs=P("var", ("grp", "tile"), None),
        check_vma=False,
    )
```

```python
import functools

import jax
import jax.numpy as jnp
from jax import lax
from jax.experimental import pallas as pl
from jax.experimental.pallas import tpu as pltpu
from jax.sharding import PartitionSpec as P

PASSES = 10
LANES = 128
GROUP = 16
VMEM = pl.BlockSpec(memory_space=pltpu.VMEM)
SMEM = pl.BlockSpec(memory_space=pltpu.SMEM)
HBM = pl.BlockSpec(memory_space=pltpu.HBM)
AFTER = pl.BlockSpec(memory_space=pl.ANY)
F32 = jnp.float32


def in_hbm(values):
    return pltpu.with_memory_space_constraint(values, pltpu.HBM)


def call(body, outs, ins, scratch=(), limit=16, cost=None):
    return pl.pallas_call(
        body,
        out_shape=outs,
        in_specs=ins,
        out_specs=[VMEM] * len(outs),
        scratch_shapes=list(scratch),
        compiler_params=pltpu.CompilerParams(vmem_limit_bytes=limit << 20),
        cost_estimate=cost,
    )


def cost(cycles):
    return pl.CostEstimate(flops=cycles * 4096, bytes_accessed=cycles * 1024, transcendentals=0)


def response(sens_ref, factor_ref, sensor, variable):
    total = sens_ref[sensor, 0] * factor_ref[0, variable]
    for u in range(1, factor_ref.shape[0]):
        total = total + sens_ref[sensor, u] * factor_ref[u, variable]
    return total


def fetch(pairs, sems):
    copies = [pltpu.make_async_copy(src, dst, sems.at[i]) for i, (src, dst) in enumerate(pairs)]
    for copy in copies:
        copy.start()
    return copies


def fetch(pairs, sems):
    copies = [pltpu.make_async_copy(src, dst, sems.at[i]) for i, (src, dst) in enumerate(pairs)]
    for copy in copies:
        copy.start()
    return copies


def first_kernel(sens_hbm, factor_hbm, control_hbm, kappa_hbm, own_ref, other_ref, response_ref, kappa_ref,
                 sens_ref, factor_ref, control_ref, sems):
    copies = fetch(
        ((sens_hbm, sens_ref), (factor_hbm, factor_ref), (control_hbm, control_ref),
         (kappa_hbm, kappa_ref)),
        sems,
    )
    for copy in copies:
        copy.wait()
    member = lax.axis_index("var")
    core = member % 2
    var_dev = control_ref.shape[0]
    for which, (sensor, out_ref) in enumerate(((core, own_ref), (1 - core, other_ref))):
        total = None
        for v in range(var_dev):
            scale = response(sens_ref, factor_ref, sensor, member * var_dev + v)
            response_ref[which, v] = jnp.full(response_ref.shape[2:], scale, F32)
            term = scale * control_ref[v]
            total = term if total is None else total + term
        out_ref[...] = total


def pack_kernel(slots, after_ref, tile_hbm, row_hbm, sensor_hbm, value_hbm, weight_hbm, cols_hbm, send_ref,
                tile_ref, row_ref, sensor_ref, value_ref, weight_ref, cols_ref, count_ref, sems):
    copies = fetch(
        ((tile_hbm, tile_ref), (row_hbm, row_ref), (sensor_hbm, sensor_ref), (value_hbm, value_ref),
         (weight_hbm, weight_ref), (cols_hbm, cols_ref)),
        sems,
    )
    send_ref[...] = jnp.zeros(send_ref.shape, F32)
    tiles = send_ref.shape[0]
    for t in range(tiles):
        count_ref[t] = 0
    for copy in copies:
        copy.wait()
    core = lax.axis_index("var") % 2
    panels = value_ref.shape[0]
    sub = lax.broadcasted_iota(jnp.int32, (8 * tiles, LANES), 0)
    lane = lax.broadcasted_iota(jnp.int32, (8 * tiles, LANES), 1)
    trash = 3 * slots + 7

    def place(p, meta):
        t = tile_ref[p]
        count = count_ref[t]
        count_ref[t] = count + 1
        keep = count % 2 == core
        slot = count // 2
        rows = (value_ref[pl.ds(p, 1), :], weight_ref[pl.ds(p, 1), :], cols_ref[pl.ds(p, 1), :].astype(F32))
        for part, row in enumerate(rows):
            send_ref[t, pl.ds(jnp.where(keep, part * slots + slot, trash), 1), :] = row
        facts = jnp.where(sub == 8 * t, row_ref[p], sensor_ref[p]).astype(F32)
        here = (lane == jnp.where(keep, slot, LANES)) & (sub // 8 == t)
        return jnp.where(here, facts, meta)

    meta = lax.fori_loop(0, panels, place, jnp.zeros((8 * tiles, LANES), F32), unroll=8)
    for t in range(tiles):
        facts = meta[8 * t : 8 * t + 8]
        held = (count_ref[t] + 1 - core) // 2
        send_ref[t, 3 * slots :] = jnp.where(lane[:8] == slots, held.astype(F32), facts)


def relay_kernel(after_ref, in_ref, out_ref):
    out_ref[...] = in_ref[...]


def pieces(values):
    top = values.astype(jnp.bfloat16).astype(F32)
    return top, values - top


def scatter_kernel(slots, after_ref, got_ref, own_ref, other_ref, acc_ref, meta_ref, sems):
    core = lax.axis_index("var") % 2
    got_refs = [got_ref.at[s] for s in range(got_ref.shape[0])]
    copies = [
        pltpu.make_async_copy(ref.at[pl.ds(3 * slots, 8)], meta_ref.at[pl.ds(8 * s, 8)], sems.at[s])
        for s, ref in enumerate(got_refs)
    ]
    for copy in copies:
        copy.start()
    rows, width_cols = own_ref.shape[1:]
    blocks = width_cols // LANES
    acc_ref[...] = jnp.zeros(acc_ref.shape, F32)
    block_ids = lax.broadcasted_iota(jnp.int32, (blocks, LANES), 0)
    lane_ids = lax.broadcasted_iota(jnp.int32, (LANES, LANES), 0).astype(F32).astype(jnp.bfloat16)
    one, zero = jnp.bfloat16(1), jnp.bfloat16(0)
    sub = lax.broadcasted_iota(jnp.int32, (GROUP, LANES), 0)
    for copy in copies:
        copy.wait()

    def source(s, got_ref):
        count = meta_ref[8 * s, slots].astype(jnp.int32)

        def group(g, carry):
            base = pl.multiple_of(g * GROUP, GROUP)
            value = got_ref[pl.ds(base, GROUP), :]
            weight = got_ref[pl.ds(slots + base, GROUP), :]
            cell = got_ref[pl.ds(2 * slots + base, GROUP), :].astype(jnp.int32)
            weight = jnp.where(sub + base < count, weight, 0.0)
            parts = pieces(weight) + pieces(weight * value)
            low = (cell % LANES).astype(F32)
            high = cell // LANES
            blank = jnp.zeros((4 * blocks, LANES), jnp.bfloat16)
            for k in range(0, GROUP, 2):
                left, right = [], []
                for i in (k, k + 1):
                    in_block = block_ids == high[i : i + 1]
                    rows_of = [jnp.where(in_block, parts[j][i : i + 1], 0.0) for j in (0, 2, 1, 3)]
                    left.append(jnp.concatenate(rows_of, axis=0).astype(jnp.bfloat16))
                    column = jnp.broadcast_to(low[i : i + 1], (16, LANES)).astype(jnp.bfloat16)
                    column = jnp.concatenate([column] * (LANES // 16), axis=0)
                    right.append(jnp.where(lane_ids == column, one, zero))
                left = jnp.concatenate(
                    [
                        jnp.concatenate([left[0], blank], axis=1),
                        jnp.concatenate([blank, left[1]], axis=1),
                    ],
                    axis=0,
                )
                both = lax.dot_general(
                    left, jnp.concatenate(right, axis=1), (((1,), (1,)), ((), ())),
                    preferred_element_type=F32,
                )
                for i in (0, 1):
                    row = meta_ref[8 * s, base + k + i].astype(jnp.int32)
                    sensor = meta_ref[8 * s + 1, base + k + i].astype(jnp.int32)
                    at = pl.multiple_of((sensor * rows + row) * 2 * blocks, 2 * blocks)
                    mine = both[i * 4 * blocks : (i + 1) * 4 * blocks]
                    acc_ref[pl.ds(at, 2 * blocks), :] += mine[: 2 * blocks] + mine[2 * blocks :]
            return carry

        lax.fori_loop(0, (count + GROUP - 1) // GROUP, group, 0)

    for s, got_ref in enumerate(got_refs):
        source(s, got_ref)
    for sensor, out_ref in ((core, own_ref), (1 - core, other_ref)):
        start = sensor * rows * 2 * blocks
        for kind in range(2):
            for b in range(blocks):
                out_ref[kind, :, b * LANES : (b + 1) * LANES] = acc_ref[
                    pl.ds(start + kind * blocks + b, rows, stride=2 * blocks), :
                ]


def even_tile():
    return lax.axis_index("tile") % 2 == 0


def has_above():
    return lax.axis_index("tile") > 0


def has_below():
    return lax.axis_index("tile") + 1 < lax.axis_size("tile")


def pack_edges(even_ref, odd_ref, rows_value, margin):
    rows, width = rows_value.shape
    even = even_tile()
    for b in range(width // LANES):
        at = slice(b * LANES, (b + 1) * LANES)
        head, tail = rows_value[:margin, at], rows_value[rows - margin :, at]
        even_ref[b * margin : (b + 1) * margin] = jnp.where(even, tail, head)
        odd_ref[b * margin : (b + 1) * margin] = jnp.where(even, head, tail)


def edges_kernel(margin, first_ref, second_ref, kappa_ref, total_ref, even_ref, odd_ref):
    total = first_ref[...] + second_ref[...]
    total_ref[...] = total
    for i, field in enumerate((total, kappa_ref[0], kappa_ref[1])):
        pack_edges(even_ref.at[i], odd_ref.at[i], field, margin)


def ring_rows(rows, margin):
    return -(-(rows + 2 * margin) // 8) * 8


def lay_ring(ref, own, from_even, from_odd, margin):
    rows, total = own.shape[0], ref.shape[0]
    even = even_tile()
    ref[rows:total] = jnp.zeros((total - rows, ref.shape[1]), F32)
    ref[:rows] = own
    for b in range(ref.shape[1] // LANES):
        at = slice(b * LANES, (b + 1) * LANES)
        one, two = (m[b * margin : (b + 1) * margin] for m in (from_even, from_odd))
        ref[rows : rows + margin, at] = jnp.where(has_below(), jnp.where(even, one, two), 0.0)
        ref[total - margin :, at] = jnp.where(has_above(), jnp.where(even, two, one), 0.0)


def block(ref, j):
    return ref[:, j * LANES : (j + 1) * LANES]


def sideways(blocks):
    shape = blocks[0].shape
    lane = lax.broadcasted_iota(jnp.int32, shape, 1)
    zero = jnp.zeros(shape, F32)
    ahead = [pltpu.roll(x, 1, 1) for x in blocks]
    back = [pltpu.roll(x, LANES - 1, 1) for x in blocks]
    for j, here in enumerate(blocks):
        before = ahead[j - 1] if j else zero
        after = back[j + 1] if j + 1 < len(blocks) else zero
        yield here, jnp.where(lane == 0, before, ahead[j]), jnp.where(lane == LANES - 1, after, back[j])


def face_weights(coef_ref, row_ref, col_ref, rows, margin):
    total, width = row_ref.shape
    blocks = width // LANES
    r = lax.broadcasted_iota(jnp.int32, (total, LANES), 0)
    inside = (
        (r < rows)
        | ((r < rows + margin) & has_below())
        | ((r >= total - margin) & has_above())
    )
    scale = jnp.where(inside, 0.125, 0.0)
    unit = jnp.where(inside, 1.0, 0.0)
    columns = [block(col_ref, j) for j in range(blocks)]
    for j, (k_col, k_left, k_right) in enumerate(sideways(columns)):
        at = slice(j * LANES, (j + 1) * LANES)
        k_row = block(row_ref, j)
        up = scale * (k_row + pltpu.roll(k_row, 1, 0))
        down = scale * (k_row + pltpu.roll(k_row, total - 1, 0))
        left = scale * (k_col + k_left)
        right = scale * (k_col + k_right)
        coef_ref[0, :, at] = unit - up - down - left - right
        coef_ref[1, :, at] = up
        coef_ref[2, :, at] = down
        coef_ref[3, :, at] = left
        coef_ref[4, :, at] = right


def one_pass(source_ref, target_ref, coef_ref, spans, keep):
    width = source_ref.shape[1]

    def read(ref, *lead, at):
        got = [ref[(*lead, span, at)] for span in spans]
        return jnp.concatenate(got, axis=0) if len(got) > 1 else got[0]

    sections = [slice(j * LANES, (j + 1) * LANES) for j in range(width // LANES)]
    fields = [read(source_ref, at=at) for at in sections]
    total = fields[0].shape[0]
    for at, (here, left, right) in zip(sections, sideways(fields)):
        new = (
            read(coef_ref, 0, at=at) * here
            + read(coef_ref, 1, at=at) * pltpu.roll(here, 1, 0)
            + read(coef_ref, 2, at=at) * pltpu.roll(here, total - 1, 0)
            + read(coef_ref, 3, at=at) * left
            + read(coef_ref, 4, at=at) * right
        )
        start = 0
        for span in spans[:keep]:
            size = span.stop - span.start
            target_ref[span, at] = new[start : start + size]
            start += size


def diffuse(one_ref, two_ref, coef_ref, rows, margin):
    total = one_ref.shape[0]
    wide = [slice(0, total)]
    inner = margin // 8 * 8
    narrow = [slice(0, rows), slice(rows, rows + inner), slice(total - inner, total)]
    first = (margin - inner + 1) // 2

    def twice(spans, index, carry):
        one_pass(one_ref, two_ref, coef_ref, spans, len(spans))
        one_pass(two_ref, one_ref, coef_ref, spans, len(spans))
        return carry

    for i in range(first):
        twice(wide, i, 0)
    lax.fori_loop(0, PASSES // 2 - first - 1, functools.partial(twice, narrow), 0)
    one_pass(one_ref, two_ref, coef_ref, narrow, 3)
    one_pass(two_ref, one_ref, coef_ref, narrow, 1)


def faces_kernel(margin, even_ref, odd_ref, kappa_ref, sums_ref, coef_ref, sums_out, one_ref, two_ref):
    sums_out[...] = sums_ref[...]
    rows = kappa_ref.shape[1]
    lay_ring(one_ref, kappa_ref[0], even_ref.at[1], odd_ref.at[1], margin)
    lay_ring(two_ref, kappa_ref[1], even_ref.at[2], odd_ref.at[2], margin)
    face_weights(coef_ref, one_ref, two_ref, rows, margin)


def smooth_kernel(margin, own_ref, even_ref, odd_ref, coef_ref, out_ref, one_ref, two_ref):
    rows = own_ref.shape[0]
    lay_ring(one_ref, own_ref[...], even_ref.at[0], odd_ref.at[0], margin)
    diffuse(one_ref, two_ref, coef_ref, rows, margin)
    out_ref[...] = one_ref[:rows]


def adjoint_kernel(margin, smooth_ref, mask_ref, sums_ref, more_ref, adjoint_ref, even_ref, odd_ref):
    weight = sums_ref[0] + more_ref[0]
    value = sums_ref[1] + more_ref[1]
    adjoint = mask_ref[...].astype(F32) * (weight * smooth_ref[...] - value)
    adjoint_ref[...] = adjoint
    pack_edges(even_ref, odd_ref, adjoint, margin)


def spread_kernel(margin, own_ref, even_ref, odd_ref, coef_ref, out_ref, one_ref, two_ref):
    rows = own_ref.shape[0]
    lay_ring(one_ref, own_ref[...], even_ref, odd_ref, margin)
    diffuse(one_ref, two_ref, coef_ref, rows, margin)
    out_ref[...] = one_ref[:rows]


def result_kernel(response_ref, control_ref, own_ref, other_ref, out_ref):
    for v in range(control_ref.shape[0]):
        mine, theirs = (response_ref[i, v][:1, :1] for i in range(2))
        out_ref[v] = control_ref[v] + mine * own_ref[...] + theirs * other_ref[...]


def swap(values, axis, bit):
    count = lax.axis_size(axis)
    return lax.ppermute(values, axis, [(i, i ^ bit) for i in range(count)])


def swap_edges(even, odd):
    tiles, members = lax.axis_size("tile"), lax.axis_size("var")
    pairs = []
    for t in range(tiles):
        other = t + 1 if t % 2 else t - 1
        for q in range(members):
            to = other * members + q if 0 <= other < tiles else t * members + (q ^ 1)
            pairs.append((t * members + q, to))
    return swap(even, "tile", 1), lax.ppermute(odd, ("tile", "var"), pairs)


def combine(values, members, first):
    bit = first
    while 2 * bit < members:
        values = values + swap(values, "var", bit)
        bit *= 2
    return values, swap(values, "var", bit)


def local(control, diffusivity, land_mask, panel_tile, panel_row, panel_cols, obs_values,
          obs_weights, panel_sensor, sensitivity, cross_factor):
    rows, width = control.shape[1:]
    var_dev = control.shape[0]
    tiles, members = lax.axis_size("tile"), lax.axis_size("var")
    panels, panel_width = panel_cols.shape
    slots = panels // tiles
    blocks = width // LANES
    margin = PASSES
    total = ring_rows(rows, margin)
    field = jax.ShapeDtypeStruct((rows, width), F32)
    field2 = jax.ShapeDtypeStruct((2, rows, width), F32)
    edge = jax.ShapeDtypeStruct((margin * blocks, LANES), F32)
    edge3 = jax.ShapeDtypeStruct((3, margin * blocks, LANES), F32)
    chunks = jax.ShapeDtypeStruct((tiles, 3 * slots + 8, panel_width), F32)
    ints = pltpu.SMEM((panels,), jnp.int32)

    own, other, responses, kappa = call(
        first_kernel,
        [field, field, jax.ShapeDtypeStruct((2, var_dev, 8, LANES), F32), field2],
        [HBM] * 4,
        [
            pltpu.SMEM(sensitivity.shape, F32),
            pltpu.SMEM(cross_factor.shape, F32),
            pltpu.VMEM(control.shape, F32),
            pltpu.SemaphoreType.DMA((4,)),
        ],
        cost=cost(2000),
    )(*(in_hbm(x) for x in (sensitivity, cross_factor, control, diffusivity)))
    (send,) = call(
        functools.partial(pack_kernel, slots),
        [chunks],
        [AFTER] + [HBM] * 6,
        [
            ints, ints, ints,
            pltpu.VMEM(obs_values.shape, F32),
            pltpu.VMEM(obs_weights.shape, F32),
            pltpu.VMEM(panel_cols.shape, jnp.int32),
            pltpu.SMEM((tiles,), jnp.int32),
            pltpu.SemaphoreType.DMA((6,)),
        ],
        cost=cost(3000),
    )(responses, *(in_hbm(x) for x in (panel_tile.reshape(-1), panel_row, panel_sensor, obs_values,
                                       obs_weights, panel_cols)))
    part = own + swap(other, "var", 1)
    (send,) = call(relay_kernel, [chunks], [AFTER, VMEM], cost=cost(100))(part, send)
    got = lax.all_to_all(send, "tile", split_axis=0, concat_axis=0, tiled=True)
    part, more = combine(part, members, 2)
    smooth_in, even, odd = call(
        functools.partial(edges_kernel, margin),
        [field, edge3, edge3],
        [VMEM] * 3,
        cost=cost(500),
    )(part, more, kappa)
    even, odd = swap_edges(even, odd)
    sums, sums_other = call(
        functools.partial(scatter_kernel, slots),
        [field2, field2],
        [AFTER, VMEM],
        [
            pltpu.VMEM((2 * rows * 2 * blocks, LANES), F32),
            pltpu.SMEM((8 * tiles, LANES), F32),
            pltpu.SemaphoreType.DMA((tiles,)),
        ],
        cost=cost(100000),
    )(smooth_in, got)

    ring = pltpu.VMEM((total, width), F32)
    coef, sums_other = call(
        functools.partial(faces_kernel, margin),
        [jax.ShapeDtypeStruct((5, total, width), F32), field2],
        [VMEM] * 4,
        [ring, ring],
        cost=cost(1000),
    )(even, odd, kappa, sums_other)
    more_sums = swap(sums_other, "var", 1)
    (smooth,) = call(
        functools.partial(smooth_kernel, margin),
        [field],
        [VMEM] * 4,
        [ring, ring],
        cost=cost(4000),
    )(smooth_in, even, odd, coef)
    adjoint, even, odd = call(
        functools.partial(adjoint_kernel, margin), [field, edge, edge], [VMEM] * 4, cost=cost(500)
    )(smooth, land_mask, sums, more_sums)
    even, odd = swap_edges(even, odd)
    (mine,) = call(
        functools.partial(spread_kernel, margin),
        [field],
        [VMEM] * 4,
        [ring, ring],
        cost=cost(4000),
    )(adjoint, even, odd, coef)
    (out,) = call(
        result_kernel,
        [jax.ShapeDtypeStruct(control.shape, F32)],
        [VMEM] * 4,
        cost=cost(1000),
    )(responses, control, mine, swap(mine, "var", 1))
    return out


def solution(mesh):
    return jax.shard_map(
        local,
        mesh=mesh,
        in_specs=(
            P("var", ("grp", "tile"), None),
            P(None, ("grp", "tile"), None),
            P(("grp", "tile"), None),
            P(("grp", "tile"), None),
            P(("grp", "tile")),
            P(("grp", "tile"), None),
            P(("grp", "tile"), None),
            P(("grp", "tile"), None),
            P(("grp", "tile")),
            P(),
            P(),
        ),
        out_specs=P("var", ("grp", "tile"), None),
        check_vma=False,
    )
```

```python
import functools

import jax
import jax.numpy as jnp
from jax import lax
from jax.experimental import pallas as pl
from jax.experimental.pallas import tpu as pltpu
from jax.sharding import PartitionSpec as P

PASSES = 10
LANES = 128
GROUP = 16
VMEM = pl.BlockSpec(memory_space=pltpu.VMEM)
SMEM = pl.BlockSpec(memory_space=pltpu.SMEM)
HBM = pl.BlockSpec(memory_space=pltpu.HBM)
AFTER = pl.BlockSpec(memory_space=pl.ANY)
F32 = jnp.float32


def in_hbm(values):
    return pltpu.with_memory_space_constraint(values, pltpu.HBM)


def call(body, outs, ins, scratch=(), limit=16, cost=None):
    return pl.pallas_call(
        body,
        out_shape=outs,
        in_specs=ins,
        out_specs=[VMEM] * len(outs),
        scratch_shapes=list(scratch),
        compiler_params=pltpu.CompilerParams(vmem_limit_bytes=limit << 20),
        cost_estimate=cost,
    )


def cost(cycles):
    return pl.CostEstimate(flops=cycles * 4096, bytes_accessed=cycles * 1024, transcendentals=0)


def response(sens_ref, factor_ref, sensor, variable):
    total = sens_ref[sensor, 0] * factor_ref[0, variable]
    for u in range(1, factor_ref.shape[0]):
        total = total + sens_ref[sensor, u] * factor_ref[u, variable]
    return total


def fetch(pairs, sems):
    copies = [pltpu.make_async_copy(src, dst, sems.at[i]) for i, (src, dst) in enumerate(pairs)]
    for copy in copies:
        copy.start()
    return copies


def window_of(chip, chips, blocks):
    own = blocks // chips
    size = min(own + 2, own + chips - 1)
    return jnp.clip(chip * own - 1, 0, blocks - size), size


def my_chip():
    return lax.axis_index("var") // 2


def chip_count():
    return lax.axis_size("var") // 2


def lanes(start, size):
    return pl.ds(pl.multiple_of(start * LANES, LANES), size * LANES)


def first_kernel(slots, sens_hbm, factor_hbm, control_hbm, kappa_hbm, tile_hbm, row_hbm, sensor_hbm,
                 value_hbm, weight_hbm, cols_hbm, own_ref, other_ref, response_ref, kappa_ref, *refs):
    chunk_refs = refs[:-12]
    (sens_ref, factor_ref, control_ref, tile_ref, row_ref, sensor_ref, value_ref, weight_ref, cols_ref,
     send_ref, count_ref, sems) = refs[-12:]
    window = lanes(*window_of(my_chip(), chip_count(), own_ref.shape[1] // LANES))
    pairs = (
        (sens_hbm, sens_ref), (factor_hbm, factor_ref), (control_hbm, control_ref),
        (kappa_hbm.at[:, :, window], kappa_ref), (tile_hbm, tile_ref), (row_hbm, row_ref), (sensor_hbm, sensor_ref),
        (value_hbm, value_ref), (weight_hbm, weight_ref), (cols_hbm, cols_ref),
    )
    copies = [pltpu.make_async_copy(src, dst, sems.at[i]) for i, (src, dst) in enumerate(pairs)]
    for copy in copies:
        copy.start()
    send_ref[...] = jnp.zeros(send_ref.shape, F32)
    turns = len(chunk_refs)
    for turn in range(turns):
        count_ref[turn] = 0
    for copy in copies:
        copy.wait()

    member, mine = lax.axis_index("var"), lax.axis_index("tile")
    core = member % 2
    var_dev = control_ref.shape[0]
    for which, (sensor, out_ref) in enumerate(((core, own_ref), (1 - core, other_ref))):
        total = None
        for v in range(var_dev):
            scale = response(sens_ref, factor_ref, sensor, member * var_dev + v)
            response_ref[which, v] = jnp.full(response_ref.shape[2:], scale, F32)
            term = scale * control_ref[v]
            total = term if total is None else total + term
        out_ref[...] = total

    panels = value_ref.shape[0]
    sub = lax.broadcasted_iota(jnp.int32, (8 * turns, LANES), 0)
    lane = lax.broadcasted_iota(jnp.int32, (8 * turns, LANES), 1)
    trash = 3 * slots + 7

    def place(p, meta):
        turn = (tile_ref[p] ^ mine) - core * turns
        keep = (turn >= 0) & (turn < turns)
        turn = jnp.where(keep, turn, 0)
        slot = count_ref[turn]
        count_ref[turn] = slot + keep.astype(jnp.int32)
        rows = (value_ref[pl.ds(p, 1), :], weight_ref[pl.ds(p, 1), :], cols_ref[pl.ds(p, 1), :].astype(F32))
        for part, row in enumerate(rows):
            send_ref[turn, pl.ds(jnp.where(keep, part * slots + slot, trash), 1), :] = row
        facts = jnp.where(sub == 8 * turn, row_ref[p], sensor_ref[p]).astype(F32)
        here = (lane == jnp.where(keep, slot, LANES)) & (sub // 8 == turn)
        return jnp.where(here, facts, meta)

    meta = lax.fori_loop(0, panels, place, jnp.zeros((8 * turns, LANES), F32), unroll=8)
    for turn, chunk_ref in enumerate(chunk_refs):
        chunk_ref[: 3 * slots] = send_ref[turn, : 3 * slots]
        facts = meta[8 * turn : 8 * turn + 8]
        chunk_ref[3 * slots :] = jnp.where(lane[:8] == slots, count_ref[turn].astype(F32), facts)


def pieces(values):
    top = values.astype(jnp.bfloat16).astype(F32)
    return top, values - top


def scatter_kernel(slots, blocks_all, after_ref, home_ref, *refs):
    got_refs, (own_ref, other_ref, first_ref, acc_ref, meta_ref, sems) = refs[:-6], refs[-6:]
    core = lax.axis_index("var") % 2
    first_ref[...] = jnp.where(core == 0, home_ref[...], got_refs[0][...])
    got_refs = (first_ref, *got_refs[1:])
    copies = [
        pltpu.make_async_copy(ref.at[pl.ds(3 * slots, 8)], meta_ref.at[pl.ds(8 * s, 8)], sems.at[s])
        for s, ref in enumerate(got_refs)
    ]
    for copy in copies:
        copy.start()
    rows = own_ref.shape[1]
    start, size = window_of(my_chip(), chip_count(), blocks_all)
    per_kind = padded_blocks(size)
    tall = 2 * per_kind
    acc_ref[...] = jnp.zeros(acc_ref.shape, F32)
    place = lax.broadcasted_iota(jnp.int32, (tall, LANES), 0)
    is_weight = place < per_kind
    place = jnp.where(is_weight, place, place - per_kind) + start
    lane_ids = lax.broadcasted_iota(jnp.int32, (LANES, LANES), 0).astype(F32).astype(jnp.bfloat16)
    one, zero = jnp.bfloat16(1), jnp.bfloat16(0)
    sub = lax.broadcasted_iota(jnp.int32, (GROUP, LANES), 0)
    blank = jnp.zeros((2 * tall, LANES), jnp.bfloat16)
    for copy in copies:
        copy.wait()

    def source(s, got_ref):
        count = meta_ref[8 * s, slots].astype(jnp.int32)

        def group(g, carry):
            base = pl.multiple_of(g * GROUP, GROUP)
            value = got_ref[pl.ds(base, GROUP), :]
            weight = got_ref[pl.ds(slots + base, GROUP), :]
            cell = got_ref[pl.ds(2 * slots + base, GROUP), :].astype(jnp.int32)
            weight = jnp.where(sub + base < count, weight, 0.0)
            parts = (pieces(weight), pieces(weight * value))
            low = (cell % LANES).astype(F32)
            high = cell // LANES
            for k in range(0, GROUP, 2):
                left, right = [], []
                for i in (k, k + 1):
                    here = place == high[i : i + 1]
                    rows_of = [
                        jnp.where(here, jnp.where(is_weight, w[i : i + 1], v[i : i + 1]), 0.0)
                        for w, v in zip(*parts)
                    ]
                    left.append(jnp.concatenate(rows_of, axis=0).astype(jnp.bfloat16))
                    column = jnp.broadcast_to(low[i : i + 1], (16, LANES)).astype(jnp.bfloat16)
                    column = jnp.concatenate([column] * (LANES // 16), axis=0)
                    right.append(jnp.where(lane_ids == column, one, zero))
                left = jnp.concatenate(
                    [
                        jnp.concatenate([left[0], blank], axis=1),
                        jnp.concatenate([blank, left[1]], axis=1),
                    ],
                    axis=0,
                )
                both = lax.dot_general(
                    left, jnp.concatenate(right, axis=1), (((1,), (1,)), ((), ())),
                    preferred_element_type=F32,
                )
                for i in (0, 1):
                    row = meta_ref[8 * s, base + k + i].astype(jnp.int32)
                    sensor = meta_ref[8 * s + 1, base + k + i].astype(jnp.int32)
                    at = pl.multiple_of((sensor * rows + row) * tall, 8)
                    mine = both[2 * i * tall : 2 * (i + 1) * tall]
                    acc_ref[pl.ds(at, tall), :] += mine[:tall] + mine[tall:]
            return carry

        lax.fori_loop(0, (count + GROUP - 1) // GROUP, group, 0)

    for s, got_ref in enumerate(got_refs):
        source(s, got_ref)
    for sensor, out_ref in ((core, own_ref), (1 - core, other_ref)):
        begin = sensor * rows * tall
        for kind in range(2):
            for b in range(size):
                out_ref[kind, :, b * LANES : (b + 1) * LANES] = acc_ref[
                    pl.ds(begin + kind * per_kind + b, rows, stride=tall), :
                ]


def padded_blocks(size):
    return -(-size // 4) * 4


def even_tile():
    return lax.axis_index("tile") % 2 == 0


def has_above():
    return lax.axis_index("tile") > 0


def has_below():
    return lax.axis_index("tile") + 1 < lax.axis_size("tile")


def pack_edges(even_ref, odd_ref, rows_value, margin):
    rows, width = rows_value.shape
    even = even_tile()
    for b in range(width // LANES):
        at = slice(b * LANES, (b + 1) * LANES)
        head, tail = rows_value[:margin, at], rows_value[rows - margin :, at]
        even_ref[b * margin : (b + 1) * margin] = jnp.where(even, tail, head)
        odd_ref[b * margin : (b + 1) * margin] = jnp.where(even, head, tail)


def cut_kernel(first_ref, second_ref, mine_ref, *out_refs):
    chip, chips, blocks = my_chip(), chip_count(), first_ref.shape[1] // LANES
    for d, out_ref in enumerate((mine_ref, *out_refs)):
        window = lanes(*window_of(chip ^ d, chips, blocks))
        out_ref[...] = first_ref[:, window] + second_ref[:, window]


def edges_kernel(margin, chips, kappa_ref, *refs):
    terms, (total_ref, even_ref, odd_ref) = refs[:chips], refs[-3:]
    total = terms[0][...]
    for term in terms[1:]:
        total = total + term[...]
    total_ref[...] = total
    for i, field in enumerate((total, kappa_ref[0], kappa_ref[1])):
        pack_edges(even_ref.at[i], odd_ref.at[i], field, margin)


def ring_rows(rows, margin):
    return -(-(rows + 2 * margin) // 8) * 8


def lay_ring(ref, own, from_even, from_odd, margin):
    rows, total = own.shape[0], ref.shape[0]
    even = even_tile()
    ref[rows:total] = jnp.zeros((total - rows, ref.shape[1]), F32)
    ref[:rows] = own
    for b in range(ref.shape[1] // LANES):
        at = slice(b * LANES, (b + 1) * LANES)
        one, two = (m[b * margin : (b + 1) * margin] for m in (from_even, from_odd))
        ref[rows : rows + margin, at] = jnp.where(has_below(), jnp.where(even, one, two), 0.0)
        ref[total - margin :, at] = jnp.where(has_above(), jnp.where(even, two, one), 0.0)


def block(ref, j):
    return ref[:, j * LANES : (j + 1) * LANES]


def sideways(blocks):
    shape = blocks[0].shape
    lane = lax.broadcasted_iota(jnp.int32, shape, 1)
    zero = jnp.zeros(shape, F32)
    ahead = [pltpu.roll(x, 1, 1) for x in blocks]
    back = [pltpu.roll(x, LANES - 1, 1) for x in blocks]
    for j, here in enumerate(blocks):
        before = ahead[j - 1] if j else zero
        after = back[j + 1] if j + 1 < len(blocks) else zero
        yield here, jnp.where(lane == 0, before, ahead[j]), jnp.where(lane == LANES - 1, after, back[j])


def face_weights(coef_ref, row_ref, col_ref, rows, margin):
    total, width = row_ref.shape
    blocks = width // LANES
    r = lax.broadcasted_iota(jnp.int32, (total, LANES), 0)
    inside = (
        (r < rows)
        | ((r < rows + margin) & has_below())
        | ((r >= total - margin) & has_above())
    )
    scale = jnp.where(inside, 0.125, 0.0)
    unit = jnp.where(inside, 1.0, 0.0)
    columns = [block(col_ref, j) for j in range(blocks)]
    for j, (k_col, k_left, k_right) in enumerate(sideways(columns)):
        at = slice(j * LANES, (j + 1) * LANES)
        k_row = block(row_ref, j)
        up = scale * (k_row + pltpu.roll(k_row, 1, 0))
        down = scale * (k_row + pltpu.roll(k_row, total - 1, 0))
        left = scale * (k_col + k_left)
        right = scale * (k_col + k_right)
        coef_ref[0, :, at] = unit - up - down - left - right
        coef_ref[1, :, at] = up
        coef_ref[2, :, at] = down
        coef_ref[3, :, at] = left
        coef_ref[4, :, at] = right


def one_pass(source_ref, target_ref, coef_ref, spans, keep):
    width = source_ref.shape[1]

    def read(ref, *lead, at):
        got = [ref[(*lead, span, at)] for span in spans]
        return jnp.concatenate(got, axis=0) if len(got) > 1 else got[0]

    sections = [slice(j * LANES, (j + 1) * LANES) for j in range(width // LANES)]
    fields = [read(source_ref, at=at) for at in sections]
    total = fields[0].shape[0]
    for at, (here, left, right) in zip(sections, sideways(fields)):
        new = (
            read(coef_ref, 0, at=at) * here
            + read(coef_ref, 1, at=at) * pltpu.roll(here, 1, 0)
            + read(coef_ref, 2, at=at) * pltpu.roll(here, total - 1, 0)
            + read(coef_ref, 3, at=at) * left
            + read(coef_ref, 4, at=at) * right
        )
        start = 0
        for span in spans[:keep]:
            size = span.stop - span.start
            target_ref[span, at] = new[start : start + size]
            start += size


def diffuse(one_ref, two_ref, coef_ref, rows, margin):
    total = one_ref.shape[0]
    wide = [slice(0, total)]
    inner = margin // 8 * 8
    narrow = [slice(0, rows), slice(rows, rows + inner), slice(total - inner, total)]
    first = (margin - inner + 1) // 2

    def twice(spans, index, carry):
        one_pass(one_ref, two_ref, coef_ref, spans, len(spans))
        one_pass(two_ref, one_ref, coef_ref, spans, len(spans))
        return carry

    for i in range(first):
        twice(wide, i, 0)
    lax.fori_loop(0, PASSES // 2 - first - 1, functools.partial(twice, narrow), 0)
    one_pass(one_ref, two_ref, coef_ref, narrow, 3)
    one_pass(two_ref, one_ref, coef_ref, narrow, 1)


def faces_kernel(margin, even_ref, odd_ref, kappa_ref, sums_ref, coef_ref, sums_out, one_ref, two_ref):
    sums_out[...] = sums_ref[...]
    rows = kappa_ref.shape[1]
    lay_ring(one_ref, kappa_ref[0], even_ref.at[1], odd_ref.at[1], margin)
    lay_ring(two_ref, kappa_ref[1], even_ref.at[2], odd_ref.at[2], margin)
    face_weights(coef_ref, one_ref, two_ref, rows, margin)


def smooth_kernel(margin, own_ref, even_ref, odd_ref, coef_ref, out_ref, one_ref, two_ref):
    rows = own_ref.shape[0]
    lay_ring(one_ref, own_ref[...], even_ref.at[0], odd_ref.at[0], margin)
    diffuse(one_ref, two_ref, coef_ref, rows, margin)
    out_ref[...] = one_ref[:rows]


def adjoint_kernel(margin, smooth_ref, mask_ref, sums_ref, more_ref, adjoint_ref, even_ref, odd_ref):
    weight = sums_ref[0] + more_ref[0]
    value = sums_ref[1] + more_ref[1]
    window = lanes(*window_of(my_chip(), chip_count(), mask_ref.shape[1] // LANES))
    adjoint = mask_ref[:, window].astype(F32) * (weight * smooth_ref[...] - value)
    adjoint_ref[...] = adjoint
    pack_edges(even_ref, odd_ref, adjoint, margin)


def spread_kernel(margin, own_ref, even_ref, odd_ref, coef_ref, out_ref, one_ref, two_ref):
    rows = own_ref.shape[0]
    lay_ring(one_ref, own_ref[...], even_ref, odd_ref, margin)
    diffuse(one_ref, two_ref, coef_ref, rows, margin)
    own = out_ref.shape[1] // LANES
    start = window_of(my_chip(), chip_count(), own * chip_count())[0]
    out_ref[...] = one_ref[:rows, lanes(my_chip() * own - start, own)]


def join_kernel(*refs):
    out_ref = refs[-1]
    for d, ref in enumerate(refs[:-1]):
        own = ref.shape[1] // LANES
        out_ref[:, lanes((my_chip() ^ d) * own, own)] = ref[...]


def result_kernel(response_ref, control_ref, own_ref, other_ref, out_ref):
    for v in range(control_ref.shape[0]):
        mine, theirs = (response_ref[i, v][:1, :1] for i in range(2))
        out_ref[v] = control_ref[v] + mine * own_ref[...] + theirs * other_ref[...]


def swap(values, axis, bit):
    count = lax.axis_size(axis)
    return lax.ppermute(values, axis, [(i, i ^ bit) for i in range(count)])


def swap_edges(even, odd):
    tiles, members = lax.axis_size("tile"), lax.axis_size("var")
    pairs = []
    for t in range(tiles):
        other = t + 1 if t % 2 else t - 1
        for q in range(members):
            to = other * members + q if 0 <= other < tiles else t * members + (q ^ 1)
            pairs.append((t * members + q, to))
    return swap(even, "tile", 1), lax.ppermute(odd, ("tile", "var"), pairs)


def deliver(chunk, turn):
    tiles, members = lax.axis_size("tile"), lax.axis_size("var")
    pairs = []
    for t in range(tiles):
        for q in range(members):
            offset = (q % 2) * (tiles // 2) + turn
            pairs.append((t * members + q, (t ^ max(offset, 1)) * members + q))
    return lax.ppermute(chunk, ("tile", "var"), pairs)


def local(control, diffusivity, land_mask, panel_tile, panel_row, panel_cols, obs_values,
          obs_weights, panel_sensor, sensitivity, cross_factor):
    rows, width = control.shape[1:]
    var_dev = control.shape[0]
    tiles, members = lax.axis_size("tile"), lax.axis_size("var")
    panels, panel_width = panel_cols.shape
    slots = 2 * panels // tiles
    turns = tiles // 2
    blocks = width // LANES
    margin = PASSES
    total = ring_rows(rows, margin)
    chips = members // 2
    size = window_of(0, chips, blocks)[1]
    field = jax.ShapeDtypeStruct((rows, width), F32)
    share = jax.ShapeDtypeStruct((rows, width // chips), F32)
    view = jax.ShapeDtypeStruct((rows, size * LANES), F32)
    view2 = jax.ShapeDtypeStruct((2, *view.shape), F32)
    edge = jax.ShapeDtypeStruct((margin * size, LANES), F32)
    edge3 = jax.ShapeDtypeStruct((3, *edge.shape), F32)
    chunk = jax.ShapeDtypeStruct((3 * slots + 8, panel_width), F32)
    ints = pltpu.SMEM((panels,), jnp.int32)

    own, other, responses, kappa, *chunks = call(
        functools.partial(first_kernel, slots),
        [field, field, jax.ShapeDtypeStruct((2, var_dev, 8, LANES), F32), view2] + [chunk] * turns,
        [HBM] * 10,
        [
            pltpu.SMEM(sensitivity.shape, F32),
            pltpu.SMEM(cross_factor.shape, F32),
            pltpu.VMEM(control.shape, F32),
            ints, ints, ints,
            pltpu.VMEM(obs_values.shape, F32),
            pltpu.VMEM(obs_weights.shape, F32),
            pltpu.VMEM(panel_cols.shape, jnp.int32),
            pltpu.VMEM((turns, *chunk.shape), F32),
            pltpu.SMEM((turns,), jnp.int32),
            pltpu.SemaphoreType.DMA((10,)),
        ],
        cost=cost(3000),
    )(*(in_hbm(x) for x in (sensitivity, cross_factor, control, diffusivity, panel_tile.reshape(-1),
                            panel_row, panel_sensor, obs_values, obs_weights, panel_cols)))

    got = [deliver(c, turn) for turn, c in enumerate(chunks)]
    part, *parts = call(cut_kernel, [view] * chips, [VMEM] * 2, cost=cost(200))(
        own, swap(other, "var", 1)
    )
    parts = [swap(p, "var", 2 * (d + 1)) for d, p in enumerate(parts)]
    smooth_in, even, odd = call(
        functools.partial(edges_kernel, margin, chips),
        [view, edge3, edge3],
        [VMEM] * (1 + chips) + [AFTER] * turns,
        cost=cost(500),
    )(kappa, part, *parts, *got)
    even, odd = swap_edges(even, odd)
    sums, sums_other = call(
        functools.partial(scatter_kernel, slots, blocks),
        [view2, view2],
        [AFTER] + [VMEM] * (turns + 1),
        [
            pltpu.VMEM(chunk.shape, F32),
            pltpu.VMEM((2 * rows * 2 * padded_blocks(size), LANES), F32),
            pltpu.SMEM((8 * turns, LANES), F32),
            pltpu.SemaphoreType.DMA((turns,)),
        ],
        cost=cost(10000),
    )(smooth_in, chunks[0], *got)
    ring = pltpu.VMEM((total, size * LANES), F32)
    coef, sums_other = call(
        functools.partial(faces_kernel, margin),
        [jax.ShapeDtypeStruct((5, total, size * LANES), F32), view2],
        [VMEM] * 4,
        [ring, ring],
        cost=cost(1000),
    )(even, odd, kappa, sums_other)
    more_sums = swap(sums_other, "var", 1)
    (smooth,) = call(
        functools.partial(smooth_kernel, margin),
        [view],
        [VMEM] * 4,
        [ring, ring],
        cost=cost(4000),
    )(smooth_in, even, odd, coef)
    adjoint, even, odd = call(
        functools.partial(adjoint_kernel, margin), [view, edge, edge], [VMEM] * 4, cost=cost(500)
    )(smooth, land_mask, sums, more_sums)
    even, odd = swap_edges(even, odd)
    (mine,) = call(
        functools.partial(spread_kernel, margin),
        [share],
        [VMEM] * 4,
        [ring, ring],
        cost=cost(4000),
    )(adjoint, even, odd, coef)
    shares = [mine] + [swap(mine, "var", 2 * d) for d in range(1, chips)]
    (mine,) = call(join_kernel, [field], [VMEM] * chips, cost=cost(200))(*shares)
    (out,) = call(
        result_kernel,
        [jax.ShapeDtypeStruct(control.shape, F32)],
        [VMEM] * 4,
        cost=cost(1000),
    )(responses, control, mine, swap(mine, "var", 1))
    return out


def solution(mesh):
    return jax.shard_map(
        local,
        mesh=mesh,
        in_specs=(
            P("var", ("grp", "tile"), None),
            P(None, ("grp", "tile"), None),
            P(("grp", "tile"), None),
            P(("grp", "tile"), None),
            P(("grp", "tile")),
            P(("grp", "tile"), None),
            P(("grp", "tile"), None),
            P(("grp", "tile"), None),
            P(("grp", "tile")),
            P(),
            P(),
        ),
        out_specs=P("var", ("grp", "tile"), None),
        check_vma=False,
    )
```

```python
import functools

import jax
import jax.numpy as jnp
from jax import lax
from jax.experimental import pallas as pl
from jax.experimental.pallas import tpu as pltpu
from jax.sharding import PartitionSpec as P

PASSES = 10
LANES = 128
GROUP = 16
VMEM = pl.BlockSpec(memory_space=pltpu.VMEM)
SMEM = pl.BlockSpec(memory_space=pltpu.SMEM)
HBM = pl.BlockSpec(memory_space=pltpu.HBM)
AFTER = pl.BlockSpec(memory_space=pl.ANY)
F32 = jnp.float32


def in_hbm(values):
    return pltpu.with_memory_space_constraint(values, pltpu.HBM)


def call(body, outs, ins, scratch=(), limit=16, cost=None):
    return pl.pallas_call(
        body,
        out_shape=outs,
        in_specs=ins,
        out_specs=[VMEM] * len(outs),
        scratch_shapes=list(scratch),
        compiler_params=pltpu.CompilerParams(vmem_limit_bytes=limit << 20),
        cost_estimate=cost,
    )


def cost(cycles):
    return pl.CostEstimate(flops=cycles * 4096, bytes_accessed=cycles * 1024, transcendentals=0)


def response(sens_ref, factor_ref, sensor, variable):
    total = sens_ref[sensor, 0] * factor_ref[0, variable]
    for u in range(1, factor_ref.shape[0]):
        total = total + sens_ref[sensor, u] * factor_ref[u, variable]
    return total


def fetch(pairs, sems):
    copies = [pltpu.make_async_copy(src, dst, sems.at[i]) for i, (src, dst) in enumerate(pairs)]
    for copy in copies:
        copy.start()
    return copies


def window_of(chip, chips, blocks):
    own = blocks // chips
    size = min(own + 2, own + chips - 1)
    return jnp.clip(chip * own - 1, 0, blocks - size), size


def my_chip():
    return lax.axis_index("var") // 2


def chip_count():
    return lax.axis_size("var") // 2


def lanes(start, size):
    return pl.ds(pl.multiple_of(start * LANES, LANES), size * LANES)


def first_kernel(slots, margin, sens_hbm, factor_hbm, control_hbm, kappa_hbm, tile_hbm, row_hbm, sensor_hbm,
                 value_hbm, weight_hbm, cols_hbm, own_ref, other_ref, response_ref, kappa_ref, even_ref,
                 odd_ref, *refs):
    chunk_refs = refs[:-12]
    (sens_ref, factor_ref, control_ref, tile_ref, row_ref, sensor_ref, value_ref, weight_ref, cols_ref,
     send_ref, count_ref, sems) = refs[-12:]
    window = lanes(*window_of(my_chip(), chip_count(), own_ref.shape[1] // LANES))
    pairs = (
        (sens_hbm, sens_ref), (factor_hbm, factor_ref), (control_hbm, control_ref),
        (kappa_hbm.at[:, :, window], kappa_ref), (tile_hbm, tile_ref), (row_hbm, row_ref), (sensor_hbm, sensor_ref),
        (value_hbm, value_ref), (weight_hbm, weight_ref), (cols_hbm, cols_ref),
    )
    copies = [pltpu.make_async_copy(src, dst, sems.at[i]) for i, (src, dst) in enumerate(pairs)]
    for copy in copies:
        copy.start()
    send_ref[...] = jnp.zeros(send_ref.shape, F32)
    turns = len(chunk_refs)
    for turn in range(turns):
        count_ref[turn] = 0
    for copy in copies:
        copy.wait()

    member, mine = lax.axis_index("var"), lax.axis_index("tile")
    core = member % 2
    var_dev = control_ref.shape[0]
    for which, (sensor, out_ref) in enumerate(((core, own_ref), (1 - core, other_ref))):
        total = None
        for v in range(var_dev):
            scale = response(sens_ref, factor_ref, sensor, member * var_dev + v)
            response_ref[which, v] = jnp.full(response_ref.shape[2:], scale, F32)
            term = scale * control_ref[v]
            total = term if total is None else total + term
        out_ref[...] = total

    for i in range(2):
        pack_edges(even_ref.at[i], odd_ref.at[i], kappa_ref[i], margin)

    panels = value_ref.shape[0]
    sub = lax.broadcasted_iota(jnp.int32, (8 * turns, LANES), 0)
    lane = lax.broadcasted_iota(jnp.int32, (8 * turns, LANES), 1)
    trash = 3 * slots + 7

    def place(p, meta):
        turn = (tile_ref[p] ^ mine) - core * turns
        keep = (turn >= 0) & (turn < turns)
        turn = jnp.where(keep, turn, 0)
        slot = count_ref[turn]
        count_ref[turn] = slot + keep.astype(jnp.int32)
        rows = (value_ref[pl.ds(p, 1), :], weight_ref[pl.ds(p, 1), :], cols_ref[pl.ds(p, 1), :].astype(F32))
        for part, row in enumerate(rows):
            send_ref[turn, pl.ds(jnp.where(keep, part * slots + slot, trash), 1), :] = row
        facts = jnp.where(sub == 8 * turn, row_ref[p], sensor_ref[p]).astype(F32)
        here = (lane == jnp.where(keep, slot, LANES)) & (sub // 8 == turn)
        return jnp.where(here, facts, meta)

    meta = lax.fori_loop(0, panels, place, jnp.zeros((8 * turns, LANES), F32), unroll=8)
    for turn, chunk_ref in enumerate(chunk_refs):
        chunk_ref[: 3 * slots] = send_ref[turn, : 3 * slots]
        facts = meta[8 * turn : 8 * turn + 8]
        chunk_ref[3 * slots :] = jnp.where(lane[:8] == slots, count_ref[turn].astype(F32), facts)


def pieces(values):
    top = values.astype(jnp.bfloat16).astype(F32)
    return top, values - top


def scatter_kernel(slots, blocks_all, after_ref, home_ref, *refs):
    got_refs, (own_ref, other_ref, first_ref, acc_ref, meta_ref, sems) = refs[:-6], refs[-6:]
    core = lax.axis_index("var") % 2
    first_ref[...] = jnp.where(core == 0, home_ref[...], got_refs[0][...])
    got_refs = (first_ref, *got_refs[1:])
    copies = [
        pltpu.make_async_copy(ref.at[pl.ds(3 * slots, 8)], meta_ref.at[pl.ds(8 * s, 8)], sems.at[s])
        for s, ref in enumerate(got_refs)
    ]
    for copy in copies:
        copy.start()
    rows = own_ref.shape[1]
    start, size = window_of(my_chip(), chip_count(), blocks_all)
    per_kind = padded_blocks(size)
    tall = 2 * per_kind
    acc_ref[...] = jnp.zeros(acc_ref.shape, F32)
    place = lax.broadcasted_iota(jnp.int32, (tall, LANES), 0)
    is_weight = place < per_kind
    place = jnp.where(is_weight, place, place - per_kind) + start
    lane_ids = lax.broadcasted_iota(jnp.int32, (LANES, LANES), 0).astype(F32).astype(jnp.bfloat16)
    one, zero = jnp.bfloat16(1), jnp.bfloat16(0)
    sub = lax.broadcasted_iota(jnp.int32, (GROUP, LANES), 0)
    blank = jnp.zeros((2 * tall, LANES), jnp.bfloat16)
    for copy in copies:
        copy.wait()

    def source(s, got_ref):
        count = meta_ref[8 * s, slots].astype(jnp.int32)

        def group(g, carry):
            base = pl.multiple_of(g * GROUP, GROUP)
            value = got_ref[pl.ds(base, GROUP), :]
            weight = got_ref[pl.ds(slots + base, GROUP), :]
            cell = got_ref[pl.ds(2 * slots + base, GROUP), :].astype(jnp.int32)
            weight = jnp.where(sub + base < count, weight, 0.0)
            parts = (pieces(weight), pieces(weight * value))
            low = (cell % LANES).astype(F32)
            high = cell // LANES
            for k in range(0, GROUP, 2):
                left, right = [], []
                for i in (k, k + 1):
                    here = place == high[i : i + 1]
                    rows_of = [
                        jnp.where(here, jnp.where(is_weight, w[i : i + 1], v[i : i + 1]), 0.0)
                        for w, v in zip(*parts)
                    ]
                    left.append(jnp.concatenate(rows_of, axis=0).astype(jnp.bfloat16))
                    column = jnp.broadcast_to(low[i : i + 1], (16, LANES)).astype(jnp.bfloat16)
                    column = jnp.concatenate([column] * (LANES // 16), axis=0)
                    right.append(jnp.where(lane_ids == column, one, zero))
                left = jnp.concatenate(
                    [
                        jnp.concatenate([left[0], blank], axis=1),
                        jnp.concatenate([blank, left[1]], axis=1),
                    ],
                    axis=0,
                )
                both = lax.dot_general(
                    left, jnp.concatenate(right, axis=1), (((1,), (1,)), ((), ())),
                    preferred_element_type=F32,
                )
                for i in (0, 1):
                    row = meta_ref[8 * s, base + k + i].astype(jnp.int32)
                    sensor = meta_ref[8 * s + 1, base + k + i].astype(jnp.int32)
                    at = pl.multiple_of((sensor * rows + row) * tall, 8)
                    mine = both[2 * i * tall : 2 * (i + 1) * tall]
                    acc_ref[pl.ds(at, tall), :] += mine[:tall] + mine[tall:]
            return carry

        lax.fori_loop(0, (count + GROUP - 1) // GROUP, group, 0)

    for s, got_ref in enumerate(got_refs):
        source(s, got_ref)
    for sensor, out_ref in ((core, own_ref), (1 - core, other_ref)):
        begin = sensor * rows * tall
        for kind in range(2):
            for b in range(size):
                out_ref[kind, :, b * LANES : (b + 1) * LANES] = acc_ref[
                    pl.ds(begin + kind * per_kind + b, rows, stride=tall), :
                ]


def padded_blocks(size):
    return -(-size // 4) * 4


def even_tile():
    return lax.axis_index("tile") % 2 == 0


def has_above():
    return lax.axis_index("tile") > 0


def has_below():
    return lax.axis_index("tile") + 1 < lax.axis_size("tile")


def pack_edges(even_ref, odd_ref, rows_value, margin):
    rows, width = rows_value.shape
    even = even_tile()
    for b in range(width // LANES):
        at = slice(b * LANES, (b + 1) * LANES)
        head, tail = rows_value[:margin, at], rows_value[rows - margin :, at]
        even_ref[b * margin : (b + 1) * margin] = jnp.where(even, tail, head)
        odd_ref[b * margin : (b + 1) * margin] = jnp.where(even, head, tail)


def cut_kernel(first_ref, second_ref, mine_ref, *out_refs):
    chip, chips, blocks = my_chip(), chip_count(), first_ref.shape[1] // LANES
    for d, out_ref in enumerate((mine_ref, *out_refs)):
        window = lanes(*window_of(chip ^ d, chips, blocks))
        out_ref[...] = first_ref[:, window] + second_ref[:, window]


def edges_kernel(margin, *refs):
    terms, (total_ref, even_ref, odd_ref) = refs[:-3], refs[-3:]
    total = terms[0][...]
    for term in terms[1:]:
        total = total + term[...]
    total_ref[...] = total
    pack_edges(even_ref, odd_ref, total, margin)


def ring_rows(rows, margin):
    return -(-(rows + 2 * margin) // 8) * 8


def lay_ring(ref, own, from_even, from_odd, margin):
    rows, total = own.shape[0], ref.shape[0]
    even = even_tile()
    ref[rows:total] = jnp.zeros((total - rows, ref.shape[1]), F32)
    ref[:rows] = own
    for b in range(ref.shape[1] // LANES):
        at = slice(b * LANES, (b + 1) * LANES)
        one, two = (m[b * margin : (b + 1) * margin] for m in (from_even, from_odd))
        ref[rows : rows + margin, at] = jnp.where(has_below(), jnp.where(even, one, two), 0.0)
        ref[total - margin :, at] = jnp.where(has_above(), jnp.where(even, two, one), 0.0)


def block(ref, j):
    return ref[:, j * LANES : (j + 1) * LANES]


def sideways(blocks):
    shape = blocks[0].shape
    lane = lax.broadcasted_iota(jnp.int32, shape, 1)
    zero = jnp.zeros(shape, F32)
    ahead = [pltpu.roll(x, 1, 1) for x in blocks]
    back = [pltpu.roll(x, LANES - 1, 1) for x in blocks]
    for j, here in enumerate(blocks):
        before = ahead[j - 1] if j else zero
        after = back[j + 1] if j + 1 < len(blocks) else zero
        yield here, jnp.where(lane == 0, before, ahead[j]), jnp.where(lane == LANES - 1, after, back[j])


def face_weights(coef_ref, row_ref, col_ref, rows, margin):
    total, width = row_ref.shape
    blocks = width // LANES
    r = lax.broadcasted_iota(jnp.int32, (total, LANES), 0)
    inside = (
        (r < rows)
        | ((r < rows + margin) & has_below())
        | ((r >= total - margin) & has_above())
    )
    scale = jnp.where(inside, 0.125, 0.0)
    unit = jnp.where(inside, 1.0, 0.0)
    columns = [block(col_ref, j) for j in range(blocks)]
    for j, (k_col, k_left, k_right) in enumerate(sideways(columns)):
        at = slice(j * LANES, (j + 1) * LANES)
        k_row = block(row_ref, j)
        up = scale * (k_row + pltpu.roll(k_row, 1, 0))
        down = scale * (k_row + pltpu.roll(k_row, total - 1, 0))
        left = scale * (k_col + k_left)
        right = scale * (k_col + k_right)
        coef_ref[0, :, at] = unit - up - down - left - right
        coef_ref[1, :, at] = up
        coef_ref[2, :, at] = down
        coef_ref[3, :, at] = left
        coef_ref[4, :, at] = right


def one_pass(source_ref, target_ref, coef_ref, spans, keep):
    width = source_ref.shape[1]

    def read(ref, *lead, at):
        got = [ref[(*lead, span, at)] for span in spans]
        return jnp.concatenate(got, axis=0) if len(got) > 1 else got[0]

    sections = [slice(j * LANES, (j + 1) * LANES) for j in range(width // LANES)]
    fields = [read(source_ref, at=at) for at in sections]
    total = fields[0].shape[0]
    for at, (here, left, right) in zip(sections, sideways(fields)):
        new = (
            read(coef_ref, 0, at=at) * here
            + read(coef_ref, 1, at=at) * pltpu.roll(here, 1, 0)
            + read(coef_ref, 2, at=at) * pltpu.roll(here, total - 1, 0)
            + read(coef_ref, 3, at=at) * left
            + read(coef_ref, 4, at=at) * right
        )
        start = 0
        for span in spans[:keep]:
            size = span.stop - span.start
            target_ref[span, at] = new[start : start + size]
            start += size


def diffuse(one_ref, two_ref, coef_ref, rows, margin):
    total = one_ref.shape[0]
    wide = [slice(0, total)]
    inner = margin // 8 * 8
    narrow = [slice(0, rows), slice(rows, rows + inner), slice(total - inner, total)]
    first = (margin - inner + 1) // 2

    def twice(spans, index, carry):
        one_pass(one_ref, two_ref, coef_ref, spans, len(spans))
        one_pass(two_ref, one_ref, coef_ref, spans, len(spans))
        return carry

    for i in range(first):
        twice(wide, i, 0)
    lax.fori_loop(0, PASSES // 2 - first - 1, functools.partial(twice, narrow), 0)
    one_pass(one_ref, two_ref, coef_ref, narrow, 3)
    one_pass(two_ref, one_ref, coef_ref, narrow, 1)


def faces_kernel(margin, even_ref, odd_ref, kappa_ref, sums_ref, *refs):
    coef_ref, sums_out, one_ref, two_ref = refs[-4:]
    sums_out[...] = sums_ref[...]
    rows = kappa_ref.shape[1]
    lay_ring(one_ref, kappa_ref[0], even_ref.at[0], odd_ref.at[0], margin)
    lay_ring(two_ref, kappa_ref[1], even_ref.at[1], odd_ref.at[1], margin)
    face_weights(coef_ref, one_ref, two_ref, rows, margin)


def smooth_kernel(margin, own_ref, even_ref, odd_ref, coef_ref, out_ref, one_ref, two_ref):
    rows = own_ref.shape[0]
    lay_ring(one_ref, own_ref[...], even_ref, odd_ref, margin)
    diffuse(one_ref, two_ref, coef_ref, rows, margin)
    out_ref[...] = one_ref[:rows]


def adjoint_kernel(margin, smooth_ref, mask_ref, sums_ref, more_ref, adjoint_ref, even_ref, odd_ref):
    weight = sums_ref[0] + more_ref[0]
    value = sums_ref[1] + more_ref[1]
    window = lanes(*window_of(my_chip(), chip_count(), mask_ref.shape[1] // LANES))
    adjoint = mask_ref[:, window].astype(F32) * (weight * smooth_ref[...] - value)
    adjoint_ref[...] = adjoint
    pack_edges(even_ref, odd_ref, adjoint, margin)


def spread_kernel(margin, own_ref, even_ref, odd_ref, coef_ref, out_ref, one_ref, two_ref):
    rows = own_ref.shape[0]
    lay_ring(one_ref, own_ref[...], even_ref, odd_ref, margin)
    diffuse(one_ref, two_ref, coef_ref, rows, margin)
    own = out_ref.shape[1] // LANES
    start = window_of(my_chip(), chip_count(), own * chip_count())[0]
    out_ref[...] = one_ref[:rows, lanes(my_chip() * own - start, own)]


def result_kernel(response_ref, control_ref, *refs):
    own, out_ref = refs[0].shape[1] // LANES, refs[-1]
    for d in range(len(refs) // 2):
        window = lanes((my_chip() ^ d) * own, own)
        for v in range(control_ref.shape[0]):
            mine, theirs = (response_ref[i, v][:1, :1] for i in range(2))
            out_ref[v, :, window] = (
                control_ref[v, :, window] + mine * refs[2 * d][...] + theirs * refs[2 * d + 1][...]
            )


def swap(values, axis, bit):
    count = lax.axis_size(axis)
    return lax.ppermute(values, axis, [(i, i ^ bit) for i in range(count)])


def swap_edges(even, odd):
    tiles, members = lax.axis_size("tile"), lax.axis_size("var")
    pairs = []
    for t in range(tiles):
        other = t + 1 if t % 2 else t - 1
        for q in range(members):
            to = other * members + q if 0 <= other < tiles else t * members + (q ^ 1)
            pairs.append((t * members + q, to))
    return swap(even, "tile", 1), lax.ppermute(odd, ("tile", "var"), pairs)


def deliver(chunk, turn):
    tiles, members = lax.axis_size("tile"), lax.axis_size("var")
    pairs = []
    for t in range(tiles):
        for q in range(members):
            offset = (q % 2) * (tiles // 2) + turn
            pairs.append((t * members + q, (t ^ max(offset, 1)) * members + q))
    return lax.ppermute(chunk, ("tile", "var"), pairs)


def local(control, diffusivity, land_mask, panel_tile, panel_row, panel_cols, obs_values,
          obs_weights, panel_sensor, sensitivity, cross_factor):
    rows, width = control.shape[1:]
    var_dev = control.shape[0]
    tiles, members = lax.axis_size("tile"), lax.axis_size("var")
    panels, panel_width = panel_cols.shape
    slots = 2 * panels // tiles
    turns = tiles // 2
    blocks = width // LANES
    margin = PASSES
    total = ring_rows(rows, margin)
    chips = members // 2
    size = window_of(0, chips, blocks)[1]
    field = jax.ShapeDtypeStruct((rows, width), F32)
    share = jax.ShapeDtypeStruct((rows, width // chips), F32)
    view = jax.ShapeDtypeStruct((rows, size * LANES), F32)
    view2 = jax.ShapeDtypeStruct((2, *view.shape), F32)
    edge = jax.ShapeDtypeStruct((margin * size, LANES), F32)
    edge2 = jax.ShapeDtypeStruct((2, *edge.shape), F32)
    chunk = jax.ShapeDtypeStruct((3 * slots + 8, panel_width), F32)
    ints = pltpu.SMEM((panels,), jnp.int32)

    own, other, responses, kappa, kappa_even, kappa_odd, *chunks = call(
        functools.partial(first_kernel, slots, margin),
        [field, field, jax.ShapeDtypeStruct((2, var_dev, 8, LANES), F32), view2, edge2, edge2]
        + [chunk] * turns,
        [HBM] * 10,
        [
            pltpu.SMEM(sensitivity.shape, F32),
            pltpu.SMEM(cross_factor.shape, F32),
            pltpu.VMEM(control.shape, F32),
            ints, ints, ints,
            pltpu.VMEM(obs_values.shape, F32),
            pltpu.VMEM(obs_weights.shape, F32),
            pltpu.VMEM(panel_cols.shape, jnp.int32),
            pltpu.VMEM((turns, *chunk.shape), F32),
            pltpu.SMEM((turns,), jnp.int32),
            pltpu.SemaphoreType.DMA((10,)),
        ],
        cost=cost(3000),
    )(*(in_hbm(x) for x in (sensitivity, cross_factor, control, diffusivity, panel_tile.reshape(-1),
                            panel_row, panel_sensor, obs_values, obs_weights, panel_cols)))

    got = [deliver(c, turn) for turn, c in enumerate(chunks)]
    part, *parts = call(cut_kernel, [view] * chips, [VMEM] * 2, cost=cost(200))(
        own, swap(other, "var", 1)
    )
    parts = [swap(p, "var", 2 * (d + 1)) for d, p in enumerate(parts)]
    kappa_even, kappa_odd = swap_edges(kappa_even, kappa_odd)
    smooth_in, even, odd = call(
        functools.partial(edges_kernel, margin), [view, edge, edge], [VMEM] * chips, cost=cost(500)
    )(part, *parts)
    even, odd = swap_edges(even, odd)
    sums, sums_other = call(
        functools.partial(scatter_kernel, slots, blocks),
        [view2, view2],
        [AFTER] + [VMEM] * (turns + 1),
        [
            pltpu.VMEM(chunk.shape, F32),
            pltpu.VMEM((2 * rows * 2 * padded_blocks(size), LANES), F32),
            pltpu.SMEM((8 * turns, LANES), F32),
            pltpu.SemaphoreType.DMA((turns,)),
        ],
        cost=cost(100000),
    )(smooth_in, chunks[0], *got)
    ring = pltpu.VMEM((total, size * LANES), F32)
    coef, sums_other = call(
        functools.partial(faces_kernel, margin),
        [jax.ShapeDtypeStruct((5, total, size * LANES), F32), view2],
        [VMEM] * 4 + [AFTER] * 2,
        [ring, ring],
        cost=cost(1000),
    )(kappa_even, kappa_odd, kappa, sums_other, even, odd)
    more_sums = swap(sums_other, "var", 1)
    (smooth,) = call(
        functools.partial(smooth_kernel, margin),
        [view],
        [VMEM] * 4,
        [ring, ring],
        cost=cost(4000),
    )(smooth_in, even, odd, coef)
    adjoint, even, odd = call(
        functools.partial(adjoint_kernel, margin), [view, edge, edge], [VMEM] * 4, cost=cost(500)
    )(smooth, land_mask, sums, more_sums)
    even, odd = swap_edges(even, odd)
    (mine,) = call(
        functools.partial(spread_kernel, margin),
        [share],
        [VMEM] * 4,
        [ring, ring],
        cost=cost(4000),
    )(adjoint, even, odd, coef)
    shares = [mine] + [swap(mine, "var", d) for d in range(1, members)]
    (out,) = call(
        result_kernel,
        [jax.ShapeDtypeStruct(control.shape, F32)],
        [VMEM] * (2 + members),
        cost=cost(1000),
    )(responses, control, *shares)
    return out


def solution(mesh):
    return jax.shard_map(
        local,
        mesh=mesh,
        in_specs=(
            P("var", ("grp", "tile"), None),
            P(None, ("grp", "tile"), None),
            P(("grp", "tile"), None),
            P(("grp", "tile"), None),
            P(("grp", "tile")),
            P(("grp", "tile"), None),
            P(("grp", "tile"), None),
            P(("grp", "tile"), None),
            P(("grp", "tile")),
            P(),
            P(),
        ),
        out_specs=P("var", ("grp", "tile"), None),
        check_vma=False,
    )
```

```python
import functools

import jax
import jax.numpy as jnp
from jax import lax
from jax.experimental import pallas as pl
from jax.experimental.pallas import tpu as pltpu
from jax.sharding import PartitionSpec as P

PASSES = 10
LANES = 128
GROUP = 16
VMEM = pl.BlockSpec(memory_space=pltpu.VMEM)
SMEM = pl.BlockSpec(memory_space=pltpu.SMEM)
HBM = pl.BlockSpec(memory_space=pltpu.HBM)
AFTER = pl.BlockSpec(memory_space=pl.ANY)
F32 = jnp.float32


def in_hbm(values):
    return pltpu.with_memory_space_constraint(values, pltpu.HBM)


def call(body, outs, ins, scratch=(), limit=16, cost=None):
    return pl.pallas_call(
        body,
        out_shape=outs,
        in_specs=ins,
        out_specs=[VMEM] * len(outs),
        scratch_shapes=list(scratch),
        compiler_params=pltpu.CompilerParams(vmem_limit_bytes=limit << 20),
        cost_estimate=cost,
    )


def cost(cycles):
    return pl.CostEstimate(flops=cycles * 4096, bytes_accessed=cycles * 1024, transcendentals=0)


def response(sens_ref, factor_ref, sensor, variable):
    total = sens_ref[sensor, 0] * factor_ref[0, variable]
    for u in range(1, factor_ref.shape[0]):
        total = total + sens_ref[sensor, u] * factor_ref[u, variable]
    return total


def fetch(pairs, sems):
    copies = [pltpu.make_async_copy(src, dst, sems.at[i]) for i, (src, dst) in enumerate(pairs)]
    for copy in copies:
        copy.start()
    return copies


def window_of(chip, chips, blocks):
    own = blocks // chips
    size = min(own + 2, own + chips - 1)
    return jnp.clip(chip * own - 1, 0, blocks - size), size


def my_chip():
    return lax.axis_index("var") // 2


def chip_count():
    return lax.axis_size("var") // 2


def lanes(start, size):
    return pl.ds(pl.multiple_of(start * LANES, LANES), size * LANES)


def first_kernel(slots, margin, sens_hbm, factor_hbm, control_hbm, kappa_hbm, tile_hbm, row_hbm, sensor_hbm,
                 value_hbm, weight_hbm, cols_hbm, own_ref, other_ref, response_ref, kappa_ref, even_ref,
                 odd_ref, *refs):
    chunk_refs = refs[:-11]
    (sens_ref, factor_ref, control_ref, tile_ref, row_ref, sensor_ref, value_ref, weight_ref, cols_ref,
     send_ref, sems) = refs[-11:]
    window = lanes(*window_of(my_chip(), chip_count(), own_ref.shape[1] // LANES))
    pairs = (
        (sens_hbm, sens_ref), (factor_hbm, factor_ref), (control_hbm, control_ref),
        (kappa_hbm.at[:, :, window], kappa_ref), (tile_hbm, tile_ref), (row_hbm, row_ref), (sensor_hbm, sensor_ref),
        (value_hbm, value_ref), (weight_hbm, weight_ref), (cols_hbm, cols_ref),
    )
    copies = [pltpu.make_async_copy(src, dst, sems.at[i]) for i, (src, dst) in enumerate(pairs)]
    for copy in copies:
        copy.start()
    send_ref[...] = jnp.zeros(send_ref.shape, F32)
    turns = len(chunk_refs)
    for copy in copies:
        copy.wait()

    member, mine = lax.axis_index("var"), lax.axis_index("tile")
    core = member % 2
    var_dev = control_ref.shape[0]
    for which, (sensor, out_ref) in enumerate(((core, own_ref), (1 - core, other_ref))):
        total = None
        for v in range(var_dev):
            scale = response(sens_ref, factor_ref, sensor, member * var_dev + v)
            response_ref[which, v] = jnp.full(response_ref.shape[2:], scale, F32)
            term = scale * control_ref[v]
            total = term if total is None else total + term
        out_ref[...] = total

    for i in range(2):
        pack_edges(even_ref.at[i], odd_ref.at[i], kappa_ref[i], margin)

    panels = value_ref.shape[0]
    sub = lax.broadcasted_iota(jnp.int32, (8 * turns, LANES), 0)
    lane = lax.broadcasted_iota(jnp.int32, (8 * turns, LANES), 1)
    trash = 3 * slots + 7

    def place(p, carry):
        meta, counts = carry
        turn = (tile_ref[p] ^ mine) - core * turns
        keep = (turn >= 0) & (turn < turns)
        turn = jnp.where(keep, turn, 0)
        slot = counts[0]
        for i in range(1, turns):
            slot = jnp.where(turn == i, counts[i], slot)
        counts = [c + (keep & (turn == i)).astype(jnp.int32) for i, c in enumerate(counts)]
        rows = (value_ref[pl.ds(p, 1), :], weight_ref[pl.ds(p, 1), :], cols_ref[pl.ds(p, 1), :].astype(F32))
        for part, row in enumerate(rows):
            send_ref[turn, pl.ds(jnp.where(keep, part * slots + slot, trash), 1), :] = row
        facts = jnp.where(sub == 8 * turn, row_ref[p], sensor_ref[p]).astype(F32)
        here = (lane == jnp.where(keep, slot, LANES)) & (sub // 8 == turn)
        return jnp.where(here, facts, meta), counts

    none = jnp.zeros((8 * turns, LANES), F32), [jnp.int32(0)] * turns
    meta, counts = lax.fori_loop(0, panels, place, none, unroll=8)
    for turn, chunk_ref in enumerate(chunk_refs):
        chunk_ref[: 3 * slots] = send_ref[turn, : 3 * slots]
        facts = meta[8 * turn : 8 * turn + 8]
        chunk_ref[3 * slots :] = jnp.where(lane[:8] == slots, counts[turn].astype(F32), facts)


def pieces(values):
    top = values.astype(jnp.bfloat16).astype(F32)
    return top, values - top


def scatter_kernel(slots, blocks_all, after_ref, home_ref, *refs):
    got_refs, (own_ref, other_ref, first_ref, acc_ref, meta_ref, sems) = refs[:-6], refs[-6:]
    core = lax.axis_index("var") % 2
    first_ref[...] = jnp.where(core == 0, home_ref[...], got_refs[0][...])
    got_refs = (first_ref, *got_refs[1:])
    copies = [
        pltpu.make_async_copy(ref.at[pl.ds(3 * slots, 8)], meta_ref.at[pl.ds(8 * s, 8)], sems.at[s])
        for s, ref in enumerate(got_refs)
    ]
    for copy in copies:
        copy.start()
    rows = own_ref.shape[1]
    start, size = window_of(my_chip(), chip_count(), blocks_all)
    per_kind = padded_blocks(size)
    tall = 2 * per_kind
    acc_ref[...] = jnp.zeros(acc_ref.shape, F32)
    place = lax.broadcasted_iota(jnp.int32, (tall, LANES), 0)
    is_weight = place < per_kind
    place = jnp.where(is_weight, place, place - per_kind) + start
    lane_ids = lax.broadcasted_iota(jnp.int32, (LANES, LANES), 0).astype(F32).astype(jnp.bfloat16)
    one, zero = jnp.bfloat16(1), jnp.bfloat16(0)
    sub = lax.broadcasted_iota(jnp.int32, (GROUP, LANES), 0)
    blank = jnp.zeros((2 * tall, LANES), jnp.bfloat16)
    for copy in copies:
        copy.wait()

    def load(s, base):
        got_ref = got_refs[s]
        count = meta_ref[8 * s, slots].astype(jnp.int32)
        value = got_ref[pl.ds(base, GROUP), :]
        weight = got_ref[pl.ds(slots + base, GROUP), :]
        cell = got_ref[pl.ds(2 * slots + base, GROUP), :].astype(jnp.int32)
        weight = jnp.where(sub + base < count, weight, 0.0)
        return pieces(weight), pieces(weight * value), (cell % LANES).astype(F32), cell // LANES

    def one_hots(loaded, i):
        weights, values, low, high = loaded
        here = place == high[i : i + 1]
        rows_of = [
            jnp.where(here, jnp.where(is_weight, w[i : i + 1], v[i : i + 1]), 0.0)
            for w, v in zip(weights, values)
        ]
        left = jnp.concatenate(rows_of, axis=0).astype(jnp.bfloat16)
        column = jnp.broadcast_to(low[i : i + 1], (16, LANES)).astype(jnp.bfloat16)
        column = jnp.concatenate([column] * (LANES // 16), axis=0)
        return left, jnp.where(lane_ids == column, one, zero)

    def pair(s, g, carry):
        base = pl.multiple_of(g * GROUP, GROUP)
        loaded = [load(s + i, base) for i in (0, 1)]
        for k in range(GROUP):
            hots = [one_hots(loaded[i], k) for i in (0, 1)]
            left = jnp.concatenate(
                [
                    jnp.concatenate([hots[0][0], blank], axis=1),
                    jnp.concatenate([blank, hots[1][0]], axis=1),
                ],
                axis=0,
            )
            both = lax.dot_general(
                left, jnp.concatenate([hots[0][1], hots[1][1]], axis=1), (((1,), (1,)), ((), ())),
                preferred_element_type=F32,
            )
            for i in (0, 1):
                row = meta_ref[8 * (s + i), base + k].astype(jnp.int32)
                sensor = meta_ref[8 * (s + i) + 1, base + k].astype(jnp.int32)
                at = pl.multiple_of((sensor * rows + row) * tall, 8)
                mine = both[2 * i * tall : 2 * (i + 1) * tall]
                acc_ref[pl.ds(at, tall), :] += mine[:tall] + mine[tall:]
        return carry

    for s in range(0, len(got_refs), 2):
        most = jnp.maximum(meta_ref[8 * s, slots], meta_ref[8 * s + 8, slots]).astype(jnp.int32)
        lax.fori_loop(0, (most + GROUP - 1) // GROUP, functools.partial(pair, s), 0)
    for sensor, out_ref in ((core, own_ref), (1 - core, other_ref)):
        begin = sensor * rows * tall
        for kind in range(2):
            for b in range(size):
                out_ref[kind, :, b * LANES : (b + 1) * LANES] = acc_ref[
                    pl.ds(begin + kind * per_kind + b, rows, stride=tall), :
                ]


def padded_blocks(size):
    return -(-size // 4) * 4


def even_tile():
    return lax.axis_index("tile") % 2 == 0


def has_above():
    return lax.axis_index("tile") > 0


def has_below():
    return lax.axis_index("tile") + 1 < lax.axis_size("tile")


def pack_edges(even_ref, odd_ref, rows_value, margin):
    rows, width = rows_value.shape
    even = even_tile()
    for b in range(width // LANES):
        at = slice(b * LANES, (b + 1) * LANES)
        head, tail = rows_value[:margin, at], rows_value[rows - margin :, at]
        even_ref[b * margin : (b + 1) * margin] = jnp.where(even, tail, head)
        odd_ref[b * margin : (b + 1) * margin] = jnp.where(even, head, tail)


def cut_kernel(first_ref, second_ref, mine_ref, *out_refs):
    chip, chips, blocks = my_chip(), chip_count(), first_ref.shape[1] // LANES
    for d, out_ref in enumerate((mine_ref, *out_refs)):
        window = lanes(*window_of(chip ^ d, chips, blocks))
        out_ref[...] = first_ref[:, window] + second_ref[:, window]


def edges_kernel(margin, *refs):
    terms, (total_ref, even_ref, odd_ref) = refs[:-3], refs[-3:]
    total = terms[0][...]
    for term in terms[1:]:
        total = total + term[...]
    total_ref[...] = total
    pack_edges(even_ref, odd_ref, total, margin)


def ring_rows(rows, margin):
    return -(-(rows + 2 * margin) // 8) * 8


def lay_ring(ref, own, from_even, from_odd, margin):
    rows, total = own.shape[0], ref.shape[0]
    even = even_tile()
    ref[rows:total] = jnp.zeros((total - rows, ref.shape[1]), F32)
    ref[:rows] = own
    for b in range(ref.shape[1] // LANES):
        at = slice(b * LANES, (b + 1) * LANES)
        one, two = (m[b * margin : (b + 1) * margin] for m in (from_even, from_odd))
        ref[rows : rows + margin, at] = jnp.where(has_below(), jnp.where(even, one, two), 0.0)
        ref[total - margin :, at] = jnp.where(has_above(), jnp.where(even, two, one), 0.0)


def block(ref, j):
    return ref[:, j * LANES : (j + 1) * LANES]


def sideways(blocks):
    shape = blocks[0].shape
    lane = lax.broadcasted_iota(jnp.int32, shape, 1)
    zero = jnp.zeros(shape, F32)
    ahead = [pltpu.roll(x, 1, 1) for x in blocks]
    back = [pltpu.roll(x, LANES - 1, 1) for x in blocks]
    for j, here in enumerate(blocks):
        before = ahead[j - 1] if j else zero
        after = back[j + 1] if j + 1 < len(blocks) else zero
        yield here, jnp.where(lane == 0, before, ahead[j]), jnp.where(lane == LANES - 1, after, back[j])


def face_weights(coef_ref, row_ref, col_ref, rows, margin):
    total, width = row_ref.shape
    blocks = width // LANES
    r = lax.broadcasted_iota(jnp.int32, (total, LANES), 0)
    inside = (
        (r < rows)
        | ((r < rows + margin) & has_below())
        | ((r >= total - margin) & has_above())
    )
    scale = jnp.where(inside, 0.125, 0.0)
    unit = jnp.where(inside, 1.0, 0.0)
    columns = [block(col_ref, j) for j in range(blocks)]
    for j, (k_col, k_left, k_right) in enumerate(sideways(columns)):
        at = slice(j * LANES, (j + 1) * LANES)
        k_row = block(row_ref, j)
        up = scale * (k_row + pltpu.roll(k_row, 1, 0))
        down = scale * (k_row + pltpu.roll(k_row, total - 1, 0))
        left = scale * (k_col + k_left)
        right = scale * (k_col + k_right)
        coef_ref[0, :, at] = unit - up - down - left - right
        coef_ref[1, :, at] = up
        coef_ref[2, :, at] = down
        coef_ref[3, :, at] = left
        coef_ref[4, :, at] = right


def one_pass(fields, coef_ref, spans):
    def weights(i, at):
        got = [coef_ref[i, span, at] for span in spans]
        return jnp.concatenate(got, axis=0) if len(got) > 1 else got[0]

    total = fields[0].shape[0]
    out = []
    for j, (here, left, right) in enumerate(sideways(fields)):
        at = slice(j * LANES, (j + 1) * LANES)
        out.append(
            weights(0, at) * here
            + weights(1, at) * pltpu.roll(here, 1, 0)
            + weights(2, at) * pltpu.roll(here, total - 1, 0)
            + weights(3, at) * left
            + weights(4, at) * right
        )
    return out


def diffuse(ring_ref, coef_ref, rows, margin):
    total, width = ring_ref.shape
    inner = margin // 8 * 8
    wide = [slice(0, total)]
    narrow = [slice(0, rows + inner), slice(total - inner, total)]
    fields = [block(ring_ref, j) for j in range(width // LANES)]
    for _ in range(margin - inner):
        fields = one_pass(fields, coef_ref, wide)
    fields = [jnp.concatenate([f[span] for span in narrow], axis=0) for f in fields]
    for _ in range(inner):
        fields = one_pass(fields, coef_ref, narrow)
    return [f[:rows] for f in fields]


def faces_kernel(margin, even_ref, odd_ref, kappa_ref, sums_ref, *refs):
    coef_ref, sums_out, one_ref, two_ref = refs[-4:]
    sums_out[...] = sums_ref[...]
    rows = kappa_ref.shape[1]
    lay_ring(one_ref, kappa_ref[0], even_ref.at[0], odd_ref.at[0], margin)
    lay_ring(two_ref, kappa_ref[1], even_ref.at[1], odd_ref.at[1], margin)
    face_weights(coef_ref, one_ref, two_ref, rows, margin)


def smooth_kernel(margin, own_ref, even_ref, odd_ref, coef_ref, out_ref, ring_ref):
    rows = own_ref.shape[0]
    lay_ring(ring_ref, own_ref[...], even_ref, odd_ref, margin)
    for j, field in enumerate(diffuse(ring_ref, coef_ref, rows, margin)):
        out_ref[:, j * LANES : (j + 1) * LANES] = field


def adjoint_kernel(margin, smooth_ref, mask_ref, sums_ref, more_ref, adjoint_ref, even_ref, odd_ref):
    weight = sums_ref[0] + more_ref[0]
    value = sums_ref[1] + more_ref[1]
    window = lanes(*window_of(my_chip(), chip_count(), mask_ref.shape[1] // LANES))
    adjoint = mask_ref[:, window].astype(F32) * (weight * smooth_ref[...] - value)
    adjoint_ref[...] = adjoint
    pack_edges(even_ref, odd_ref, adjoint, margin)


def spread_kernel(margin, own_ref, even_ref, odd_ref, coef_ref, out_ref, ring_ref):
    rows = own_ref.shape[0]
    lay_ring(ring_ref, own_ref[...], even_ref, odd_ref, margin)
    for j, field in enumerate(diffuse(ring_ref, coef_ref, rows, margin)):
        ring_ref[:rows, j * LANES : (j + 1) * LANES] = field
    own = out_ref.shape[1] // LANES
    start = window_of(my_chip(), chip_count(), own * chip_count())[0]
    out_ref[...] = ring_ref[:rows, lanes(my_chip() * own - start, own)]


def result_kernel(response_ref, control_ref, *refs):
    own, out_ref = refs[0].shape[1] // LANES, refs[-1]
    for d in range(len(refs) // 2):
        window = lanes((my_chip() ^ d) * own, own)
        for v in range(control_ref.shape[0]):
            mine, theirs = (response_ref[i, v][:1, :1] for i in range(2))
            out_ref[v, :, window] = (
                control_ref[v, :, window] + mine * refs[2 * d][...] + theirs * refs[2 * d + 1][...]
            )


def swap(values, axis, bit):
    count = lax.axis_size(axis)
    return lax.ppermute(values, axis, [(i, i ^ bit) for i in range(count)])


def swap_edges(even, odd):
    tiles, members = lax.axis_size("tile"), lax.axis_size("var")
    pairs = []
    for t in range(tiles):
        other = t + 1 if t % 2 else t - 1
        for q in range(members):
            to = other * members + q if 0 <= other < tiles else t * members + (q ^ 1)
            pairs.append((t * members + q, to))
    return swap(even, "tile", 1), lax.ppermute(odd, ("tile", "var"), pairs)


def deliver(chunk, turn):
    tiles, members = lax.axis_size("tile"), lax.axis_size("var")
    pairs = []
    for t in range(tiles):
        for q in range(members):
            offset = (q % 2) * (tiles // 2) + turn
            to = (t ^ offset) * members + (q if offset else q ^ 2)
            pairs.append((t * members + q, to))
    return lax.ppermute(chunk, ("tile", "var"), pairs)


def local(control, diffusivity, land_mask, panel_tile, panel_row, panel_cols, obs_values,
          obs_weights, panel_sensor, sensitivity, cross_factor):
    rows, width = control.shape[1:]
    var_dev = control.shape[0]
    tiles, members = lax.axis_size("tile"), lax.axis_size("var")
    panels, panel_width = panel_cols.shape
    slots = 2 * panels // tiles
    turns = tiles // 2
    blocks = width // LANES
    margin = PASSES
    total = ring_rows(rows, margin)
    chips = members // 2
    size = window_of(0, chips, blocks)[1]
    field = jax.ShapeDtypeStruct((rows, width), F32)
    share = jax.ShapeDtypeStruct((rows, width // chips), F32)
    view = jax.ShapeDtypeStruct((rows, size * LANES), F32)
    view2 = jax.ShapeDtypeStruct((2, *view.shape), F32)
    edge = jax.ShapeDtypeStruct((margin * size, LANES), F32)
    edge2 = jax.ShapeDtypeStruct((2, *edge.shape), F32)
    chunk = jax.ShapeDtypeStruct((3 * slots + 8, panel_width), F32)
    ints = pltpu.SMEM((panels,), jnp.int32)

    own, other, responses, kappa, kappa_even, kappa_odd, *chunks = call(
        functools.partial(first_kernel, slots, margin),
        [field, field, jax.ShapeDtypeStruct((2, var_dev, 8, LANES), F32), view2, edge2, edge2]
        + [chunk] * turns,
        [HBM] * 10,
        [
            pltpu.SMEM(sensitivity.shape, F32),
            pltpu.SMEM(cross_factor.shape, F32),
            pltpu.VMEM(control.shape, F32),
            ints, ints, ints,
            pltpu.VMEM(obs_values.shape, F32),
            pltpu.VMEM(obs_weights.shape, F32),
            pltpu.VMEM(panel_cols.shape, jnp.int32),
            pltpu.VMEM((turns, *chunk.shape), F32),
            pltpu.SemaphoreType.DMA((10,)),
        ],
        cost=cost(3000),
    )(*(in_hbm(x) for x in (sensitivity, cross_factor, control, diffusivity, panel_tile.reshape(-1),
                            panel_row, panel_sensor, obs_values, obs_weights, panel_cols)))

    got = [deliver(c, turn) for turn, c in enumerate(chunks)]
    part, *parts = call(cut_kernel, [view] * chips, [VMEM] * 2, cost=cost(200))(
        own, swap(other, "var", 1)
    )
    parts = [swap(p, "var", 2 * (d + 1)) for d, p in enumerate(parts)]
    kappa_even, kappa_odd = swap_edges(kappa_even, kappa_odd)
    smooth_in, even, odd = call(
        functools.partial(edges_kernel, margin), [view, edge, edge], [VMEM] * chips, cost=cost(500)
    )(part, *parts)
    even, odd = swap_edges(even, odd)
    sums, sums_other = call(
        functools.partial(scatter_kernel, slots, blocks),
        [view2, view2],
        [AFTER] + [VMEM] * (turns + 1),
        [
            pltpu.VMEM(chunk.shape, F32),
            pltpu.VMEM((2 * rows * 2 * padded_blocks(size), LANES), F32),
            pltpu.SMEM((8 * turns, LANES), F32),
            pltpu.SemaphoreType.DMA((turns,)),
        ],
        cost=cost(100000),
    )(smooth_in, chunks[0], *got)
    ring = pltpu.VMEM((total, size * LANES), F32)
    coef, sums_other = call(
        functools.partial(faces_kernel, margin),
        [jax.ShapeDtypeStruct((5, total, size * LANES), F32), view2],
        [VMEM] * 4 + [AFTER] * 2,
        [ring, ring],
        cost=cost(1000),
    )(kappa_even, kappa_odd, kappa, sums_other, even, odd)
    more_sums = swap(sums_other, "var", 1)
    (smooth,) = call(
        functools.partial(smooth_kernel, margin),
        [view],
        [VMEM] * 4,
        [ring],
        cost=cost(4000),
    )(smooth_in, even, odd, coef)
    adjoint, even, odd = call(
        functools.partial(adjoint_kernel, margin), [view, edge, edge], [VMEM] * 4, cost=cost(500)
    )(smooth, land_mask, sums, more_sums)
    even, odd = swap_edges(even, odd)
    (mine,) = call(
        functools.partial(spread_kernel, margin),
        [share],
        [VMEM] * 4,
        [ring],
        cost=cost(4000),
    )(adjoint, even, odd, coef)
    shares = [mine] + [swap(mine, "var", d) for d in range(1, members)]
    (out,) = call(
        result_kernel,
        [jax.ShapeDtypeStruct(control.shape, F32)],
        [VMEM] * (2 + members),
        cost=cost(1000),
    )(responses, control, *shares)
    return out


def solution(mesh):
    return jax.shard_map(
        local,
        mesh=mesh,
        in_specs=(
            P("var", ("grp", "tile"), None),
            P(None, ("grp", "tile"), None),
            P(("grp", "tile"), None),
            P(("grp", "tile"), None),
            P(("grp", "tile")),
            P(("grp", "tile"), None),
            P(("grp", "tile"), None),
            P(("grp", "tile"), None),
            P(("grp", "tile")),
            P(),
            P(),
        ),
        out_specs=P("var", ("grp", "tile"), None),
        check_vma=False,
    )
```

```python
import functools

import jax
import jax.numpy as jnp
from jax import lax
from jax.experimental import pallas as pl
from jax.experimental.pallas import tpu as pltpu
from jax.sharding import PartitionSpec as P

PASSES = 10
LANES = 128
GROUP = 16
VMEM = pl.BlockSpec(memory_space=pltpu.VMEM)
SMEM = pl.BlockSpec(memory_space=pltpu.SMEM)
HBM = pl.BlockSpec(memory_space=pltpu.HBM)
AFTER = pl.BlockSpec(memory_space=pl.ANY)
F32 = jnp.float32


def in_hbm(values):
    return pltpu.with_memory_space_constraint(values, pltpu.HBM)


def call(body, outs, ins, scratch=(), limit=16, cost=None):
    return pl.pallas_call(
        body,
        out_shape=outs,
        in_specs=ins,
        out_specs=[VMEM] * len(outs),
        scratch_shapes=list(scratch),
        compiler_params=pltpu.CompilerParams(vmem_limit_bytes=limit << 20),
        cost_estimate=cost,
    )


def cost(cycles):
    return pl.CostEstimate(flops=cycles * 4096, bytes_accessed=cycles * 1024, transcendentals=0)


def response(sens_ref, factor_ref, sensor, variable):
    total = sens_ref[sensor, 0] * factor_ref[0, variable]
    for u in range(1, factor_ref.shape[0]):
        total = total + sens_ref[sensor, u] * factor_ref[u, variable]
    return total


def fetch(pairs, sems):
    copies = [pltpu.make_async_copy(src, dst, sems.at[i]) for i, (src, dst) in enumerate(pairs)]
    for copy in copies:
        copy.start()
    return copies


def window_of(chip, chips, blocks):
    own = blocks // chips
    size = min(own + 2, own + chips - 1)
    return jnp.clip(chip * own - 1, 0, blocks - size), size


def my_chip():
    return lax.axis_index("var") // 2


def chip_count():
    return lax.axis_size("var") // 2


def lanes(start, size):
    return pl.ds(pl.multiple_of(start * LANES, LANES), size * LANES)


def first_kernel(slots, margin, sens_hbm, factor_hbm, control_hbm, kappa_hbm, tile_hbm, row_hbm, sensor_hbm,
                 value_hbm, weight_hbm, cols_hbm, own_ref, other_ref, response_ref, kappa_ref, even_ref,
                 odd_ref, *refs):
    chunk_refs = refs[:-12]
    (sens_ref, factor_ref, control_ref, tile_ref, row_ref, sensor_ref, value_ref, weight_ref, cols_ref,
     send_ref, count_ref, sems) = refs[-12:]
    window = lanes(*window_of(my_chip(), chip_count(), own_ref.shape[1] // LANES))
    pairs = (
        (sens_hbm, sens_ref), (factor_hbm, factor_ref), (control_hbm, control_ref),
        (kappa_hbm.at[:, :, window], kappa_ref), (tile_hbm, tile_ref), (row_hbm, row_ref), (sensor_hbm, sensor_ref),
        (value_hbm, value_ref), (weight_hbm, weight_ref), (cols_hbm, cols_ref),
    )
    copies = [pltpu.make_async_copy(src, dst, sems.at[i]) for i, (src, dst) in enumerate(pairs)]
    for copy in copies:
        copy.start()
    send_ref[...] = jnp.zeros(send_ref.shape, F32)
    turns = len(chunk_refs)
    for turn in range(turns):
        count_ref[turn] = 0
    for copy in copies:
        copy.wait()

    member, mine = lax.axis_index("var"), lax.axis_index("tile")
    core = member % 2
    var_dev = control_ref.shape[0]
    for which, (sensor, out_ref) in enumerate(((core, own_ref), (1 - core, other_ref))):
        total = None
        for v in range(var_dev):
            scale = response(sens_ref, factor_ref, sensor, member * var_dev + v)
            response_ref[which, v] = jnp.full(response_ref.shape[2:], scale, F32)
            term = scale * control_ref[v]
            total = term if total is None else total + term
        out_ref[...] = total

    for i in range(2):
        pack_edges(even_ref.at[i], odd_ref.at[i], kappa_ref[i], margin)

    panels = value_ref.shape[0]
    sub = lax.broadcasted_iota(jnp.int32, (8 * turns, LANES), 0)
    lane = lax.broadcasted_iota(jnp.int32, (8 * turns, LANES), 1)
    trash = 3 * slots + 7

    def place(p, meta):
        turn = (tile_ref[p] ^ mine) - core * turns
        keep = (turn >= 0) & (turn < turns)
        turn = jnp.where(keep, turn, 0)
        slot = count_ref[turn]
        count_ref[turn] = slot + keep.astype(jnp.int32)
        rows = (value_ref[pl.ds(p, 1), :], weight_ref[pl.ds(p, 1), :], cols_ref[pl.ds(p, 1), :].astype(F32))
        for part, row in enumerate(rows):
            send_ref[turn, pl.ds(jnp.where(keep, part * slots + slot, trash), 1), :] = row
        facts = jnp.where(sub == 8 * turn, row_ref[p], sensor_ref[p]).astype(F32)
        here = (lane == jnp.where(keep, slot, LANES)) & (sub // 8 == turn)
        return jnp.where(here, facts, meta)

    meta = lax.fori_loop(0, panels, place, jnp.zeros((8 * turns, LANES), F32), unroll=8)
    for turn, chunk_ref in enumerate(chunk_refs):
        chunk_ref[: 3 * slots] = send_ref[turn, : 3 * slots]
        facts = meta[8 * turn : 8 * turn + 8]
        chunk_ref[3 * slots :] = jnp.where(lane[:8] == slots, count_ref[turn].astype(F32), facts)


def pieces(values):
    top = values.astype(jnp.bfloat16).astype(F32)
    return top, values - top


def scatter_kernel(slots, blocks_all, after_ref, home_ref, *refs):
    got_refs, (own_ref, other_ref, first_ref, acc_ref, meta_ref, sems) = refs[:-6], refs[-6:]
    core = lax.axis_index("var") % 2
    first_ref[...] = jnp.where(core == 0, home_ref[...], got_refs[0][...])
    got_refs = (first_ref, *got_refs[1:])
    copies = [
        pltpu.make_async_copy(ref.at[pl.ds(3 * slots, 8)], meta_ref.at[pl.ds(8 * s, 8)], sems.at[s])
        for s, ref in enumerate(got_refs)
    ]
    for copy in copies:
        copy.start()
    rows = own_ref.shape[1]
    start, size = window_of(my_chip(), chip_count(), blocks_all)
    per_kind = padded_blocks(size)
    tall = 2 * per_kind
    acc_ref[...] = jnp.zeros(acc_ref.shape, F32)
    place = lax.broadcasted_iota(jnp.int32, (tall, LANES), 0)
    is_weight = place < per_kind
    place = jnp.where(is_weight, place, place - per_kind) + start
    lane_ids = lax.broadcasted_iota(jnp.int32, (LANES, LANES), 0).astype(F32).astype(jnp.bfloat16)
    one, zero = jnp.bfloat16(1), jnp.bfloat16(0)
    sub = lax.broadcasted_iota(jnp.int32, (GROUP, LANES), 0)
    blank = jnp.zeros((2 * tall, LANES), jnp.bfloat16)
    for copy in copies:
        copy.wait()

    def load(s, base):
        got_ref = got_refs[s]
        count = meta_ref[8 * s, slots].astype(jnp.int32)
        value = got_ref[pl.ds(base, GROUP), :]
        weight = got_ref[pl.ds(slots + base, GROUP), :]
        cell = got_ref[pl.ds(2 * slots + base, GROUP), :].astype(jnp.int32)
        weight = jnp.where(sub + base < count, weight, 0.0)
        return pieces(weight), pieces(weight * value), (cell % LANES).astype(F32), cell // LANES

    def one_hots(loaded, i):
        weights, values, low, high = loaded
        here = place == high[i : i + 1]
        rows_of = [
            jnp.where(here, jnp.where(is_weight, w[i : i + 1], v[i : i + 1]), 0.0)
            for w, v in zip(weights, values)
        ]
        left = jnp.concatenate(rows_of, axis=0).astype(jnp.bfloat16)
        column = jnp.broadcast_to(low[i : i + 1], (16, LANES)).astype(jnp.bfloat16)
        column = jnp.concatenate([column] * (LANES // 16), axis=0)
        return left, jnp.where(lane_ids == column, one, zero)

    def pair(s, g, carry):
        base = pl.multiple_of(g * GROUP, GROUP)
        loaded = [load(s + i, base) for i in (0, 1)]
        for k in range(GROUP):
            hots = [one_hots(loaded[i], k) for i in (0, 1)]
            left = jnp.concatenate(
                [
                    jnp.concatenate([hots[0][0], blank], axis=1),
                    jnp.concatenate([blank, hots[1][0]], axis=1),
                ],
                axis=0,
            )
            both = lax.dot_general(
                left, jnp.concatenate([hots[0][1], hots[1][1]], axis=1), (((1,), (1,)), ((), ())),
                preferred_element_type=F32,
            )
            for i in (0, 1):
                row = meta_ref[8 * (s + i), base + k].astype(jnp.int32)
                sensor = meta_ref[8 * (s + i) + 1, base + k].astype(jnp.int32)
                at = pl.multiple_of((sensor * rows + row) * tall, 8)
                mine = both[2 * i * tall : 2 * (i + 1) * tall]
                acc_ref[pl.ds(at, tall), :] += mine[:tall] + mine[tall:]
        return carry

    for s in range(0, len(got_refs), 2):
        most = jnp.maximum(meta_ref[8 * s, slots], meta_ref[8 * s + 8, slots]).astype(jnp.int32)
        lax.fori_loop(0, (most + GROUP - 1) // GROUP, functools.partial(pair, s), 0)
    for sensor, out_ref in ((core, own_ref), (1 - core, other_ref)):
        begin = sensor * rows * tall
        for kind in range(2):
            for b in range(size):
                out_ref[kind, :, b * LANES : (b + 1) * LANES] = acc_ref[
                    pl.ds(begin + kind * per_kind + b, rows, stride=tall), :
                ]


def padded_blocks(size):
    return -(-size // 4) * 4


def even_tile():
    return lax.axis_index("tile") % 2 == 0


def has_above():
    return lax.axis_index("tile") > 0


def has_below():
    return lax.axis_index("tile") + 1 < lax.axis_size("tile")


def pack_edges(even_ref, odd_ref, rows_value, margin):
    rows, width = rows_value.shape
    even = even_tile()
    for b in range(width // LANES):
        at = slice(b * LANES, (b + 1) * LANES)
        head, tail = rows_value[:margin, at], rows_value[rows - margin :, at]
        even_ref[b * margin : (b + 1) * margin] = jnp.where(even, tail, head)
        odd_ref[b * margin : (b + 1) * margin] = jnp.where(even, head, tail)


def cut_kernel(first_ref, second_ref, mine_ref, *out_refs):
    chip, chips, blocks = my_chip(), chip_count(), first_ref.shape[1] // LANES
    for d, out_ref in enumerate((mine_ref, *out_refs)):
        window = lanes(*window_of(chip ^ d, chips, blocks))
        out_ref[...] = first_ref[:, window] + second_ref[:, window]


def edges_kernel(margin, *refs):
    terms, (total_ref, even_ref, odd_ref) = refs[:-3], refs[-3:]
    total = terms[0][...]
    for term in terms[1:]:
        total = total + term[...]
    total_ref[...] = total
    pack_edges(even_ref, odd_ref, total, margin)


def ring_rows(rows, margin):
    return -(-(rows + 2 * margin) // 8) * 8


def lay_ring(ref, own, from_even, from_odd, margin):
    rows, total = own.shape[0], ref.shape[0]
    even = even_tile()
    ref[rows:total] = jnp.zeros((total - rows, ref.shape[1]), F32)
    ref[:rows] = own
    for b in range(ref.shape[1] // LANES):
        at = slice(b * LANES, (b + 1) * LANES)
        one, two = (m[b * margin : (b + 1) * margin] for m in (from_even, from_odd))
        ref[rows : rows + margin, at] = jnp.where(has_below(), jnp.where(even, one, two), 0.0)
        ref[total - margin :, at] = jnp.where(has_above(), jnp.where(even, two, one), 0.0)


def block(ref, j):
    return ref[:, j * LANES : (j + 1) * LANES]


def sideways(blocks):
    shape = blocks[0].shape
    lane = lax.broadcasted_iota(jnp.int32, shape, 1)
    zero = jnp.zeros(shape, F32)
    ahead = [pltpu.roll(x, 1, 1) for x in blocks]
    back = [pltpu.roll(x, LANES - 1, 1) for x in blocks]
    for j, here in enumerate(blocks):
        before = ahead[j - 1] if j else zero
        after = back[j + 1] if j + 1 < len(blocks) else zero
        yield here, jnp.where(lane == 0, before, ahead[j]), jnp.where(lane == LANES - 1, after, back[j])


def face_weights(coef_ref, row_ref, col_ref, rows, margin):
    total, width = row_ref.shape
    blocks = width // LANES
    r = lax.broadcasted_iota(jnp.int32, (total, LANES), 0)
    inside = (
        (r < rows)
        | ((r < rows + margin) & has_below())
        | ((r >= total - margin) & has_above())
    )
    scale = jnp.where(inside, 0.125, 0.0)
    unit = jnp.where(inside, 1.0, 0.0)
    columns = [block(col_ref, j) for j in range(blocks)]
    for j, (k_col, k_left, k_right) in enumerate(sideways(columns)):
        at = slice(j * LANES, (j + 1) * LANES)
        k_row = block(row_ref, j)
        up = scale * (k_row + pltpu.roll(k_row, 1, 0))
        down = scale * (k_row + pltpu.roll(k_row, total - 1, 0))
        left = scale * (k_col + k_left)
        right = scale * (k_col + k_right)
        coef_ref[0, :, at] = unit - up - down - left - right
        coef_ref[1, :, at] = up
        coef_ref[2, :, at] = down
        coef_ref[3, :, at] = left
        coef_ref[4, :, at] = right


def one_pass(fields, coef_ref, spans):
    def weights(i, at):
        got = [coef_ref[i, span, at] for span in spans]
        return jnp.concatenate(got, axis=0) if len(got) > 1 else got[0]

    total = fields[0].shape[0]
    out = []
    for j, (here, left, right) in enumerate(sideways(fields)):
        at = slice(j * LANES, (j + 1) * LANES)
        out.append(
            weights(0, at) * here
            + weights(1, at) * pltpu.roll(here, 1, 0)
            + weights(2, at) * pltpu.roll(here, total - 1, 0)
            + weights(3, at) * left
            + weights(4, at) * right
        )
    return out


def diffuse(ring_ref, coef_ref, rows, margin):
    total, width = ring_ref.shape
    inner = margin // 8 * 8
    wide = [slice(0, total)]
    narrow = [slice(0, rows + inner), slice(total - inner, total)]
    fields = [block(ring_ref, j) for j in range(width // LANES)]
    for _ in range(margin - inner):
        fields = one_pass(fields, coef_ref, wide)
    fields = [jnp.concatenate([f[span] for span in narrow], axis=0) for f in fields]
    for _ in range(inner):
        fields = one_pass(fields, coef_ref, narrow)
    return [f[:rows] for f in fields]


def faces_kernel(margin, even_ref, odd_ref, kappa_ref, sums_ref, *refs):
    coef_ref, sums_out, one_ref, two_ref = refs[-4:]
    sums_out[...] = sums_ref[...]
    rows = kappa_ref.shape[1]
    lay_ring(one_ref, kappa_ref[0], even_ref.at[0], odd_ref.at[0], margin)
    lay_ring(two_ref, kappa_ref[1], even_ref.at[1], odd_ref.at[1], margin)
    face_weights(coef_ref, one_ref, two_ref, rows, margin)


def smooth_kernel(margin, own_ref, even_ref, odd_ref, coef_ref, out_ref, ring_ref):
    rows = own_ref.shape[0]
    lay_ring(ring_ref, own_ref[...], even_ref, odd_ref, margin)
    for j, field in enumerate(diffuse(ring_ref, coef_ref, rows, margin)):
        out_ref[:, j * LANES : (j + 1) * LANES] = field


def adjoint_kernel(margin, smooth_ref, mask_ref, sums_ref, more_ref, adjoint_ref, even_ref, odd_ref):
    weight = sums_ref[0] + more_ref[0]
    value = sums_ref[1] + more_ref[1]
    window = lanes(*window_of(my_chip(), chip_count(), mask_ref.shape[1] // LANES))
    adjoint = mask_ref[:, window].astype(F32) * (weight * smooth_ref[...] - value)
    adjoint_ref[...] = adjoint
    pack_edges(even_ref, odd_ref, adjoint, margin)


def spread_kernel(margin, own_ref, even_ref, odd_ref, coef_ref, out_ref, ring_ref):
    rows = own_ref.shape[0]
    lay_ring(ring_ref, own_ref[...], even_ref, odd_ref, margin)
    for j, field in enumerate(diffuse(ring_ref, coef_ref, rows, margin)):
        ring_ref[:rows, j * LANES : (j + 1) * LANES] = field
    own = out_ref.shape[1] // LANES
    start = window_of(my_chip(), chip_count(), own * chip_count())[0]
    out_ref[...] = ring_ref[:rows, lanes(my_chip() * own - start, own)]


def result_kernel(response_ref, control_ref, *refs):
    own, out_ref = refs[0].shape[1] // LANES, refs[-1]
    for d in range(len(refs) // 2):
        window = lanes((my_chip() ^ d) * own, own)
        for v in range(control_ref.shape[0]):
            mine, theirs = (response_ref[i, v][:1, :1] for i in range(2))
            out_ref[v, :, window] = (
                control_ref[v, :, window] + mine * refs[2 * d][...] + theirs * refs[2 * d + 1][...]
            )


def swap(values, axis, bit):
    count = lax.axis_size(axis)
    return lax.ppermute(values, axis, [(i, i ^ bit) for i in range(count)])


def swap_edges(even, odd):
    tiles, members = lax.axis_size("tile"), lax.axis_size("var")
    pairs = []
    for t in range(tiles):
        other = t + 1 if t % 2 else t - 1
        for q in range(members):
            to = other * members + q if 0 <= other < tiles else t * members + (q ^ 1)
            pairs.append((t * members + q, to))
    return swap(even, "tile", 1), lax.ppermute(odd, ("tile", "var"), pairs)


def deliver(chunk, turn):
    tiles, members = lax.axis_size("tile"), lax.axis_size("var")
    pairs = []
    for t in range(tiles):
        for q in range(members):
            offset = (q % 2) * (tiles // 2) + turn
            pairs.append((t * members + q, (t ^ max(offset, 1)) * members + q))
    return lax.ppermute(chunk, ("tile", "var"), pairs)


def local(control, diffusivity, land_mask, panel_tile, panel_row, panel_cols, obs_values,
          obs_weights, panel_sensor, sensitivity, cross_factor):
    rows, width = control.shape[1:]
    var_dev = control.shape[0]
    tiles, members = lax.axis_size("tile"), lax.axis_size("var")
    panels, panel_width = panel_cols.shape
    slots = 2 * panels // tiles
    turns = tiles // 2
    blocks = width // LANES
    margin = PASSES
    total = ring_rows(rows, margin)
    chips = members // 2
    size = window_of(0, chips, blocks)[1]
    field = jax.ShapeDtypeStruct((rows, width), F32)
    share = jax.ShapeDtypeStruct((rows, width // chips), F32)
    view = jax.ShapeDtypeStruct((rows, size * LANES), F32)
    view2 = jax.ShapeDtypeStruct((2, *view.shape), F32)
    edge = jax.ShapeDtypeStruct((margin * size, LANES), F32)
    edge2 = jax.ShapeDtypeStruct((2, *edge.shape), F32)
    chunk = jax.ShapeDtypeStruct((3 * slots + 8, panel_width), F32)
    ints = pltpu.SMEM((panels,), jnp.int32)

    own, other, responses, kappa, kappa_even, kappa_odd, *chunks = call(
        functools.partial(first_kernel, slots, margin),
        [field, field, jax.ShapeDtypeStruct((2, var_dev, 8, LANES), F32), view2, edge2, edge2]
        + [chunk] * turns,
        [HBM] * 10,
        [
            pltpu.SMEM(sensitivity.shape, F32),
            pltpu.SMEM(cross_factor.shape, F32),
            pltpu.VMEM(control.shape, F32),
            ints, ints, ints,
            pltpu.VMEM(obs_values.shape, F32),
            pltpu.VMEM(obs_weights.shape, F32),
            pltpu.VMEM(panel_cols.shape, jnp.int32),
            pltpu.VMEM((turns, *chunk.shape), F32),
            pltpu.SMEM((turns,), jnp.int32),
            pltpu.SemaphoreType.DMA((10,)),
        ],
        cost=cost(3000),
    )(*(in_hbm(x) for x in (sensitivity, cross_factor, control, diffusivity, panel_tile.reshape(-1),
                            panel_row, panel_sensor, obs_values, obs_weights, panel_cols)))

    got = [deliver(c, turn) for turn, c in enumerate(chunks)]
    part, *parts = call(cut_kernel, [view] * chips, [VMEM] * 2, cost=cost(200))(
        own, swap(other, "var", 1)
    )
    parts = [swap(p, "var", 2 * (d + 1)) for d, p in enumerate(parts)]
    kappa_even, kappa_odd = swap_edges(kappa_even, kappa_odd)
    smooth_in, even, odd = call(
        functools.partial(edges_kernel, margin), [view, edge, edge], [VMEM] * chips, cost=cost(500)
    )(part, *parts)
    even, odd = swap_edges(even, odd)
    sums, sums_other = call(
        functools.partial(scatter_kernel, slots, blocks),
        [view2, view2],
        [AFTER] + [VMEM] * (turns + 1),
        [
            pltpu.VMEM(chunk.shape, F32),
            pltpu.VMEM((2 * rows * 2 * padded_blocks(size), LANES), F32),
            pltpu.SMEM((8 * turns, LANES), F32),
            pltpu.SemaphoreType.DMA((turns,)),
        ],
        cost=cost(100000),
    )(smooth_in, chunks[0], *got)
    ring = pltpu.VMEM((total, size * LANES), F32)
    coef, sums_other = call(
        functools.partial(faces_kernel, margin),
        [jax.ShapeDtypeStruct((5, total, size * LANES), F32), view2],
        [VMEM] * 4 + [AFTER] * 2,
        [ring, ring],
        cost=cost(1000),
    )(kappa_even, kappa_odd, kappa, sums_other, even, odd)
    more_sums = swap(sums_other, "var", 1)
    (smooth,) = call(
        functools.partial(smooth_kernel, margin),
        [view],
        [VMEM] * 4,
        [ring],
        cost=cost(4000),
    )(smooth_in, even, odd, coef)
    adjoint, even, odd = call(
        functools.partial(adjoint_kernel, margin), [view, edge, edge], [VMEM] * 4, cost=cost(500)
    )(smooth, land_mask, sums, more_sums)
    even, odd = swap_edges(even, odd)
    (mine,) = call(
        functools.partial(spread_kernel, margin),
        [share],
        [VMEM] * 4,
        [ring],
        cost=cost(4000),
    )(adjoint, even, odd, coef)
    shares = [mine] + [swap(mine, "var", d) for d in range(1, members)]
    (out,) = call(
        result_kernel,
        [jax.ShapeDtypeStruct(control.shape, F32)],
        [VMEM] * (2 + members),
        cost=cost(1000),
    )(responses, control, *shares)
    return out


def solution(mesh):
    return jax.shard_map(
        local,
        mesh=mesh,
        in_specs=(
            P("var", ("grp", "tile"), None),
            P(None, ("grp", "tile"), None),
            P(("grp", "tile"), None),
            P(("grp", "tile"), None),
            P(("grp", "tile")),
            P(("grp", "tile"), None),
            P(("grp", "tile"), None),
            P(("grp", "tile"), None),
            P(("grp", "tile")),
            P(),
            P(),
        ),
        out_specs=P("var", ("grp", "tile"), None),
        check_vma=False,
    )
```

```python
import functools

import jax
import jax.numpy as jnp
from jax import lax
from jax.experimental import pallas as pl
from jax.experimental.pallas import tpu as pltpu
from jax.sharding import PartitionSpec as P

PASSES = 10
LANES = 128
GROUP = 16
VMEM = pl.BlockSpec(memory_space=pltpu.VMEM)
SMEM = pl.BlockSpec(memory_space=pltpu.SMEM)
HBM = pl.BlockSpec(memory_space=pltpu.HBM)
AFTER = pl.BlockSpec(memory_space=pl.ANY)
F32 = jnp.float32


def in_hbm(values):
    return pltpu.with_memory_space_constraint(values, pltpu.HBM)


def call(body, outs, ins, scratch=(), limit=16, cost=None):
    return pl.pallas_call(
        body,
        out_shape=outs,
        in_specs=ins,
        out_specs=[VMEM] * len(outs),
        scratch_shapes=list(scratch),
        compiler_params=pltpu.CompilerParams(vmem_limit_bytes=limit << 20),
        cost_estimate=cost,
    )


def cost(cycles):
    return pl.CostEstimate(flops=cycles * 4096, bytes_accessed=cycles * 1024, transcendentals=0)


def response(sens_ref, factor_ref, sensor, variable):
    total = sens_ref[sensor, 0] * factor_ref[0, variable]
    for u in range(1, factor_ref.shape[0]):
        total = total + sens_ref[sensor, u] * factor_ref[u, variable]
    return total


def fetch(pairs, sems):
    copies = [pltpu.make_async_copy(src, dst, sems.at[i]) for i, (src, dst) in enumerate(pairs)]
    for copy in copies:
        copy.start()
    return copies


def window_of(chip, chips, blocks):
    own = blocks // chips
    size = min(own + 2, own + chips - 1)
    return jnp.clip(chip * own - 1, 0, blocks - size), size


def my_chip():
    return lax.axis_index("var") // 2


def chip_count():
    return lax.axis_size("var") // 2


def lanes(start, size):
    return pl.ds(pl.multiple_of(start * LANES, LANES), size * LANES)


def first_kernel(slots, margin, sens_hbm, factor_hbm, control_hbm, kappa_hbm, tile_hbm, row_hbm, sensor_hbm,
                 value_hbm, weight_hbm, cols_hbm, own_ref, other_ref, response_ref, kappa_ref, even_ref,
                 odd_ref, *refs):
    chunk_refs = refs[:-12]
    (sens_ref, factor_ref, control_ref, tile_ref, row_ref, sensor_ref, value_ref, weight_ref, cols_ref,
     send_ref, count_ref, sems) = refs[-12:]
    window = lanes(*window_of(my_chip(), chip_count(), own_ref.shape[1] // LANES))
    pairs = (
        (sens_hbm, sens_ref), (factor_hbm, factor_ref), (control_hbm, control_ref),
        (kappa_hbm.at[:, :, window], kappa_ref), (tile_hbm, tile_ref), (row_hbm, row_ref), (sensor_hbm, sensor_ref),
        (value_hbm, value_ref), (weight_hbm, weight_ref), (cols_hbm, cols_ref),
    )
    copies = [pltpu.make_async_copy(src, dst, sems.at[i]) for i, (src, dst) in enumerate(pairs)]
    for copy in copies:
        copy.start()
    send_ref[...] = jnp.zeros(send_ref.shape, F32)
    turns = len(chunk_refs)
    for turn in range(turns):
        count_ref[turn] = 0
    for copy in copies:
        copy.wait()

    member, mine = lax.axis_index("var"), lax.axis_index("tile")
    core = member % 2
    var_dev = control_ref.shape[0]
    for which, (sensor, out_ref) in enumerate(((core, own_ref), (1 - core, other_ref))):
        total = None
        for v in range(var_dev):
            scale = response(sens_ref, factor_ref, sensor, member * var_dev + v)
            response_ref[which, v] = jnp.full(response_ref.shape[2:], scale, F32)
            term = scale * control_ref[v]
            total = term if total is None else total + term
        out_ref[...] = total

    for i in range(2):
        pack_edges(even_ref.at[i], odd_ref.at[i], kappa_ref[i], margin)

    panels = value_ref.shape[0]
    sub = lax.broadcasted_iota(jnp.int32, (8 * turns, LANES), 0)
    lane = lax.broadcasted_iota(jnp.int32, (8 * turns, LANES), 1)
    trash = 3 * slots + 7

    def place(p, meta):
        turn = (tile_ref[p] ^ mine) - core * turns
        keep = (turn >= 0) & (turn < turns)
        turn = jnp.where(keep, turn, 0)
        slot = count_ref[turn]
        count_ref[turn] = slot + keep.astype(jnp.int32)
        rows = (value_ref[pl.ds(p, 1), :], weight_ref[pl.ds(p, 1), :], cols_ref[pl.ds(p, 1), :].astype(F32))
        for part, row in enumerate(rows):
            send_ref[turn, pl.ds(jnp.where(keep, part * slots + slot, trash), 1), :] = row
        facts = jnp.where(sub == 8 * turn, row_ref[p], sensor_ref[p]).astype(F32)
        here = (lane == jnp.where(keep, slot, LANES)) & (sub // 8 == turn)
        return jnp.where(here, facts, meta)

    meta = lax.fori_loop(0, panels, place, jnp.zeros((8 * turns, LANES), F32), unroll=8)
    for turn, chunk_ref in enumerate(chunk_refs):
        chunk_ref[: 3 * slots] = send_ref[turn, : 3 * slots]
        facts = meta[8 * turn : 8 * turn + 8]
        chunk_ref[3 * slots :] = jnp.where(lane[:8] == slots, count_ref[turn].astype(F32), facts)


def pieces(values):
    top = values.astype(jnp.bfloat16).astype(F32)
    return top, values - top


def scatter_kernel(slots, blocks_all, after_ref, home_ref, *refs):
    got_refs, (own_ref, other_ref, first_ref, acc_ref, meta_ref, sems) = refs[:-6], refs[-6:]
    core = lax.axis_index("var") % 2
    first_ref[...] = jnp.where(core == 0, home_ref[...], got_refs[0][...])
    got_refs = (first_ref, *got_refs[1:])
    copies = [
        pltpu.make_async_copy(ref.at[pl.ds(3 * slots, 8)], meta_ref.at[pl.ds(8 * s, 8)], sems.at[s])
        for s, ref in enumerate(got_refs)
    ]
    for copy in copies:
        copy.start()
    rows = own_ref.shape[1]
    start, size = window_of(my_chip(), chip_count(), blocks_all)
    per_kind = padded_blocks(size)
    tall = 2 * per_kind
    acc_ref[...] = jnp.zeros(acc_ref.shape, F32)
    place = lax.broadcasted_iota(jnp.int32, (tall, LANES), 0)
    is_weight = place < per_kind
    place = jnp.where(is_weight, place, place - per_kind) + start
    lane_ids = lax.broadcasted_iota(jnp.int32, (LANES, LANES), 0).astype(F32).astype(jnp.bfloat16)
    one, zero = jnp.bfloat16(1), jnp.bfloat16(0)
    sub = lax.broadcasted_iota(jnp.int32, (GROUP, LANES), 0)
    blank = jnp.zeros((2 * tall, LANES), jnp.bfloat16)
    for copy in copies:
        copy.wait()

    def load(s, base):
        got_ref = got_refs[s]
        count = meta_ref[8 * s, slots].astype(jnp.int32)
        value = got_ref[pl.ds(base, GROUP), :]
        weight = got_ref[pl.ds(slots + base, GROUP), :]
        cell = got_ref[pl.ds(2 * slots + base, GROUP), :].astype(jnp.int32)
        weight = jnp.where(sub + base < count, weight, 0.0)
        return pieces(weight), pieces(weight * value), (cell % LANES).astype(F32), cell // LANES

    def one_hots(loaded, i):
        weights, values, low, high = loaded
        here = place == high[i : i + 1]
        rows_of = [
            jnp.where(here, jnp.where(is_weight, w[i : i + 1], v[i : i + 1]), 0.0)
            for w, v in zip(weights, values)
        ]
        left = jnp.concatenate(rows_of, axis=0).astype(jnp.bfloat16)
        column = jnp.broadcast_to(low[i : i + 1], (16, LANES)).astype(jnp.bfloat16)
        column = jnp.concatenate([column] * (LANES // 16), axis=0)
        return left, jnp.where(lane_ids == column, one, zero)

    def pair(s, g, carry):
        base = pl.multiple_of(g * GROUP, GROUP)
        loaded = [load(s + i, base) for i in (0, 1)]
        for k in range(GROUP):
            hots = [one_hots(loaded[i], k) for i in (0, 1)]
            left = jnp.concatenate(
                [
                    jnp.concatenate([hots[0][0], blank], axis=1),
                    jnp.concatenate([blank, hots[1][0]], axis=1),
                ],
                axis=0,
            )
            both = lax.dot_general(
                left, jnp.concatenate([hots[0][1], hots[1][1]], axis=1), (((1,), (1,)), ((), ())),
                preferred_element_type=F32,
            )
            for i in (0, 1):
                row = meta_ref[8 * (s + i), base + k].astype(jnp.int32)
                sensor = meta_ref[8 * (s + i) + 1, base + k].astype(jnp.int32)
                at = pl.multiple_of((sensor * rows + row) * tall, 8)
                mine = both[2 * i * tall : 2 * (i + 1) * tall]
                acc_ref[pl.ds(at, tall), :] += mine[:tall] + mine[tall:]
        return carry

    for s in range(0, len(got_refs), 2):
        most = jnp.maximum(meta_ref[8 * s, slots], meta_ref[8 * s + 8, slots]).astype(jnp.int32)
        lax.fori_loop(0, (most + GROUP - 1) // GROUP, functools.partial(pair, s), 0)
    for sensor, out_ref in ((core, own_ref), (1 - core, other_ref)):
        begin = sensor * rows * tall
        for kind in range(2):
            for b in range(size):
                out_ref[kind, :, b * LANES : (b + 1) * LANES] = acc_ref[
                    pl.ds(begin + kind * per_kind + b, rows, stride=tall), :
                ]


def padded_blocks(size):
    return -(-size // 4) * 4


def even_tile():
    return lax.axis_index("tile") % 2 == 0


def has_above():
    return lax.axis_index("tile") > 0


def has_below():
    return lax.axis_index("tile") + 1 < lax.axis_size("tile")


def pack_edges(even_ref, odd_ref, rows_value, margin):
    rows, width = rows_value.shape
    even = even_tile()
    for b in range(width // LANES):
        at = slice(b * LANES, (b + 1) * LANES)
        head, tail = rows_value[:margin, at], rows_value[rows - margin :, at]
        even_ref[b * margin : (b + 1) * margin] = jnp.where(even, tail, head)
        odd_ref[b * margin : (b + 1) * margin] = jnp.where(even, head, tail)


def cut_kernel(first_ref, second_ref, mine_ref, *out_refs):
    chip, chips, blocks = my_chip(), chip_count(), first_ref.shape[1] // LANES
    for d, out_ref in enumerate((mine_ref, *out_refs)):
        window = lanes(*window_of(chip ^ d, chips, blocks))
        out_ref[...] = first_ref[:, window] + second_ref[:, window]


def edges_kernel(margin, *refs):
    terms, (total_ref, even_ref, odd_ref) = refs[:-3], refs[-3:]
    total = terms[0][...]
    for term in terms[1:]:
        total = total + term[...]
    total_ref[...] = total
    pack_edges(even_ref, odd_ref, total, margin)


def ring_rows(rows, margin):
    return -(-(rows + 2 * margin) // 8) * 8


def lay_ring(ref, own, from_even, from_odd, margin):
    rows, total = own.shape[0], ref.shape[0]
    even = even_tile()
    ref[rows:total] = jnp.zeros((total - rows, ref.shape[1]), F32)
    ref[:rows] = own
    for b in range(ref.shape[1] // LANES):
        at = slice(b * LANES, (b + 1) * LANES)
        one, two = (m[b * margin : (b + 1) * margin] for m in (from_even, from_odd))
        ref[rows : rows + margin, at] = jnp.where(has_below(), jnp.where(even, one, two), 0.0)
        ref[total - margin :, at] = jnp.where(has_above(), jnp.where(even, two, one), 0.0)


def block(ref, j):
    return ref[:, j * LANES : (j + 1) * LANES]


def sideways(blocks):
    shape = blocks[0].shape
    lane = lax.broadcasted_iota(jnp.int32, shape, 1)
    zero = jnp.zeros(shape, F32)
    ahead = [pltpu.roll(x, 1, 1) for x in blocks]
    back = [pltpu.roll(x, LANES - 1, 1) for x in blocks]
    for j, here in enumerate(blocks):
        before = ahead[j - 1] if j else zero
        after = back[j + 1] if j + 1 < len(blocks) else zero
        yield here, jnp.where(lane == 0, before, ahead[j]), jnp.where(lane == LANES - 1, after, back[j])


def face_weights(coef_ref, row_ref, col_ref, rows, margin):
    total, width = row_ref.shape
    blocks = width // LANES
    r = lax.broadcasted_iota(jnp.int32, (total, LANES), 0)
    inside = (
        (r < rows)
        | ((r < rows + margin) & has_below())
        | ((r >= total - margin) & has_above())
    )
    scale = jnp.where(inside, 0.125, 0.0)
    unit = jnp.where(inside, 1.0, 0.0)
    columns = [block(col_ref, j) for j in range(blocks)]
    for j, (k_col, k_left, k_right) in enumerate(sideways(columns)):
        at = slice(j * LANES, (j + 1) * LANES)
        k_row = block(row_ref, j)
        up = scale * (k_row + pltpu.roll(k_row, 1, 0))
        down = scale * (k_row + pltpu.roll(k_row, total - 1, 0))
        left = scale * (k_col + k_left)
        right = scale * (k_col + k_right)
        coef_ref[0, :, at] = unit - up - down - left - right
        coef_ref[1, :, at] = up
        coef_ref[2, :, at] = down
        coef_ref[3, :, at] = left
        coef_ref[4, :, at] = right


def one_pass(fields, coef_ref, spans):
    def weights(i, at):
        got = [coef_ref[i, span, at] for span in spans]
        return jnp.concatenate(got, axis=0) if len(got) > 1 else got[0]

    total = fields[0].shape[0]
    out = []
    for j, (here, left, right) in enumerate(sideways(fields)):
        at = slice(j * LANES, (j + 1) * LANES)
        out.append(
            weights(0, at) * here
            + weights(1, at) * pltpu.roll(here, 1, 0)
            + weights(2, at) * pltpu.roll(here, total - 1, 0)
            + weights(3, at) * left
            + weights(4, at) * right
        )
    return out


def diffuse(ring_ref, coef_ref, rows, margin):
    total, width = ring_ref.shape
    inner = margin // 8 * 8
    wide = [slice(0, total)]
    narrow = [slice(0, rows + inner), slice(total - inner, total)]
    fields = [block(ring_ref, j) for j in range(width // LANES)]
    for _ in range(margin - inner):
        fields = one_pass(fields, coef_ref, wide)
    fields = [jnp.concatenate([f[span] for span in narrow], axis=0) for f in fields]
    for _ in range(inner):
        fields = one_pass(fields, coef_ref, narrow)
    return [f[:rows] for f in fields]


def faces_kernel(margin, odd_ref, even_ref, kappa_ref, sums_ref, *refs):
    coef_ref, sums_out, one_ref, two_ref = refs[-4:]
    sums_out[...] = sums_ref[...]
    rows = kappa_ref.shape[1]
    lay_ring(one_ref, kappa_ref[0], even_ref.at[0], odd_ref.at[0], margin)
    lay_ring(two_ref, kappa_ref[1], even_ref.at[1], odd_ref.at[1], margin)
    face_weights(coef_ref, one_ref, two_ref, rows, margin)


def smooth_kernel(margin, own_ref, odd_ref, even_ref, coef_ref, out_ref, ring_ref):
    rows = own_ref.shape[0]
    lay_ring(ring_ref, own_ref[...], even_ref, odd_ref, margin)
    for j, field in enumerate(diffuse(ring_ref, coef_ref, rows, margin)):
        out_ref[:, j * LANES : (j + 1) * LANES] = field


def adjoint_kernel(margin, smooth_ref, mask_ref, sums_ref, more_ref, adjoint_ref, even_ref, odd_ref):
    weight = sums_ref[0] + more_ref[0]
    value = sums_ref[1] + more_ref[1]
    window = lanes(*window_of(my_chip(), chip_count(), mask_ref.shape[1] // LANES))
    adjoint = mask_ref[:, window].astype(F32) * (weight * smooth_ref[...] - value)
    adjoint_ref[...] = adjoint
    pack_edges(even_ref, odd_ref, adjoint, margin)


def spread_kernel(margin, own_ref, even_ref, odd_ref, coef_ref, out_ref, ring_ref):
    rows = own_ref.shape[0]
    lay_ring(ring_ref, own_ref[...], even_ref, odd_ref, margin)
    for j, field in enumerate(diffuse(ring_ref, coef_ref, rows, margin)):
        ring_ref[:rows, j * LANES : (j + 1) * LANES] = field
    own = out_ref.shape[1] // LANES
    start = window_of(my_chip(), chip_count(), own * chip_count())[0]
    out_ref[...] = ring_ref[:rows, lanes(my_chip() * own - start, own)]


def result_kernel(response_ref, control_ref, *refs):
    own, out_ref = refs[0].shape[1] // LANES, refs[-1]
    for d in range(len(refs) // 2):
        window = lanes((my_chip() ^ d) * own, own)
        for v in range(control_ref.shape[0]):
            mine, theirs = (response_ref[i, v][:1, :1] for i in range(2))
            out_ref[v, :, window] = (
                control_ref[v, :, window] + mine * refs[2 * d][...] + theirs * refs[2 * d + 1][...]
            )


def swap(values, axis, bit):
    count = lax.axis_size(axis)
    return lax.ppermute(values, axis, [(i, i ^ bit) for i in range(count)])


def swap_edges(even, odd):
    tiles, members = lax.axis_size("tile"), lax.axis_size("var")
    pairs = []
    for t in range(tiles):
        other = t + 1 if t % 2 else t - 1
        for q in range(members):
            to = other * members + q if 0 <= other < tiles else t * members + (q ^ 1)
            pairs.append((t * members + q, to))
    odd = lax.ppermute(odd, ("tile", "var"), pairs)
    return swap(even, "tile", 1), odd


def deliver(chunk, turn):
    tiles, members = lax.axis_size("tile"), lax.axis_size("var")
    pairs = []
    for t in range(tiles):
        for q in range(members):
            offset = (q % 2) * (tiles // 2) + turn
            pairs.append((t * members + q, (t ^ max(offset, 1)) * members + q))
    return lax.ppermute(chunk, ("tile", "var"), pairs)


def local(control, diffusivity, land_mask, panel_tile, panel_row, panel_cols, obs_values,
          obs_weights, panel_sensor, sensitivity, cross_factor):
    rows, width = control.shape[1:]
    var_dev = control.shape[0]
    tiles, members = lax.axis_size("tile"), lax.axis_size("var")
    panels, panel_width = panel_cols.shape
    slots = 2 * panels // tiles
    turns = tiles // 2
    blocks = width // LANES
    margin = PASSES
    total = ring_rows(rows, margin)
    chips = members // 2
    size = window_of(0, chips, blocks)[1]
    field = jax.ShapeDtypeStruct((rows, width), F32)
    share = jax.ShapeDtypeStruct((rows, width // chips), F32)
    view = jax.ShapeDtypeStruct((rows, size * LANES), F32)
    view2 = jax.ShapeDtypeStruct((2, *view.shape), F32)
    edge = jax.ShapeDtypeStruct((margin * size, LANES), F32)
    edge2 = jax.ShapeDtypeStruct((2, *edge.shape), F32)
    chunk = jax.ShapeDtypeStruct((3 * slots + 8, panel_width), F32)
    ints = pltpu.SMEM((panels,), jnp.int32)

    own, other, responses, kappa, kappa_even, kappa_odd, *chunks = call(
        functools.partial(first_kernel, slots, margin),
        [field, field, jax.ShapeDtypeStruct((2, var_dev, 8, LANES), F32), view2, edge2, edge2]
        + [chunk] * turns,
        [HBM] * 10,
        [
            pltpu.SMEM(sensitivity.shape, F32),
            pltpu.SMEM(cross_factor.shape, F32),
            pltpu.VMEM(control.shape, F32),
            ints, ints, ints,
            pltpu.VMEM(obs_values.shape, F32),
            pltpu.VMEM(obs_weights.shape, F32),
            pltpu.VMEM(panel_cols.shape, jnp.int32),
            pltpu.VMEM((turns, *chunk.shape), F32),
            pltpu.SMEM((turns,), jnp.int32),
            pltpu.SemaphoreType.DMA((10,)),
        ],
        cost=cost(3000),
    )(*(in_hbm(x) for x in (sensitivity, cross_factor, control, diffusivity, panel_tile.reshape(-1),
                            panel_row, panel_sensor, obs_values, obs_weights, panel_cols)))

    got = [deliver(c, turn) for turn, c in enumerate(chunks)]
    part, *parts = call(cut_kernel, [view] * chips, [VMEM] * 2, cost=cost(200))(
        own, swap(other, "var", 1)
    )
    parts = [swap(p, "var", 2 * (d + 1)) for d, p in enumerate(parts)]
    kappa_even, kappa_odd = swap_edges(kappa_even, kappa_odd)
    smooth_in, even, odd = call(
        functools.partial(edges_kernel, margin), [view, edge, edge], [VMEM] * chips, cost=cost(500)
    )(part, *parts)
    even, odd = swap_edges(even, odd)
    sums, sums_other = call(
        functools.partial(scatter_kernel, slots, blocks),
        [view2, view2],
        [AFTER] + [VMEM] * (turns + 1),
        [
            pltpu.VMEM(chunk.shape, F32),
            pltpu.VMEM((2 * rows * 2 * padded_blocks(size), LANES), F32),
            pltpu.SMEM((8 * turns, LANES), F32),
            pltpu.SemaphoreType.DMA((turns,)),
        ],
        cost=cost(100000),
    )(smooth_in, chunks[0], *got)
    ring = pltpu.VMEM((total, size * LANES), F32)
    coef, sums_other = call(
        functools.partial(faces_kernel, margin),
        [jax.ShapeDtypeStruct((5, total, size * LANES), F32), view2],
        [VMEM] * 4 + [AFTER] * 2,
        [ring, ring],
        cost=cost(1000),
    )(kappa_odd, kappa_even, kappa, sums_other, odd, even)
    more_sums = swap(sums_other, "var", 1)
    (smooth,) = call(
        functools.partial(smooth_kernel, margin),
        [view],
        [VMEM] * 4,
        [ring],
        cost=cost(4000),
    )(smooth_in, odd, even, coef)
    adjoint, even, odd = call(
        functools.partial(adjoint_kernel, margin), [view, edge, edge], [VMEM] * 4, cost=cost(500)
    )(smooth, land_mask, sums, more_sums)
    even, odd = swap_edges(even, odd)
    (mine,) = call(
        functools.partial(spread_kernel, margin),
        [share],
        [VMEM] * 4,
        [ring],
        cost=cost(4000),
    )(adjoint, even, odd, coef)
    shares = [mine] + [swap(mine, "var", d) for d in range(1, members)]
    (out,) = call(
        result_kernel,
        [jax.ShapeDtypeStruct(control.shape, F32)],
        [VMEM] * (2 + members),
        cost=cost(1000),
    )(responses, control, *shares)
    return out


def solution(mesh):
    return jax.shard_map(
        local,
        mesh=mesh,
        in_specs=(
            P("var", ("grp", "tile"), None),
            P(None, ("grp", "tile"), None),
            P(("grp", "tile"), None),
            P(("grp", "tile"), None),
            P(("grp", "tile")),
            P(("grp", "tile"), None),
            P(("grp", "tile"), None),
            P(("grp", "tile"), None),
            P(("grp", "tile")),
            P(),
            P(),
        ),
        out_specs=P("var", ("grp", "tile"), None),
        check_vma=False,
    )
```

```python
import functools

import jax
import jax.numpy as jnp
from jax import lax
from jax.experimental import pallas as pl
from jax.experimental.pallas import tpu as pltpu
from jax.sharding import PartitionSpec as P

PASSES = 10
LANES = 128
GROUP = 16
VMEM = pl.BlockSpec(memory_space=pltpu.VMEM)
SMEM = pl.BlockSpec(memory_space=pltpu.SMEM)
HBM = pl.BlockSpec(memory_space=pltpu.HBM)
AFTER = pl.BlockSpec(memory_space=pl.ANY)
F32 = jnp.float32


def in_hbm(values):
    return pltpu.with_memory_space_constraint(values, pltpu.HBM)


def call(body, outs, ins, scratch=(), limit=16, cost=None):
    return pl.pallas_call(
        body,
        out_shape=outs,
        in_specs=ins,
        out_specs=[VMEM] * len(outs),
        scratch_shapes=list(scratch),
        compiler_params=pltpu.CompilerParams(vmem_limit_bytes=limit << 20),
        cost_estimate=cost,
    )


def cost(cycles):
    return pl.CostEstimate(flops=cycles * 4096, bytes_accessed=cycles * 1024, transcendentals=0)


def response(sens_ref, factor_ref, sensor, variable):
    total = sens_ref[sensor, 0] * factor_ref[0, variable]
    for u in range(1, factor_ref.shape[0]):
        total = total + sens_ref[sensor, u] * factor_ref[u, variable]
    return total


def fetch(pairs, sems):
    copies = [pltpu.make_async_copy(src, dst, sems.at[i]) for i, (src, dst) in enumerate(pairs)]
    for copy in copies:
        copy.start()
    return copies


def window_of(chip, chips, blocks):
    own = blocks // chips
    size = min(own + 2, own + chips - 1)
    return jnp.clip(chip * own - 1, 0, blocks - size), size


def my_chip():
    return lax.axis_index("var") // 2


def chip_count():
    return lax.axis_size("var") // 2


def lanes(start, size):
    return pl.ds(pl.multiple_of(start * LANES, LANES), size * LANES)


def first_kernel(slots, margin, sens_hbm, factor_hbm, control_hbm, kappa_hbm, tile_hbm, row_hbm, sensor_hbm,
                 value_hbm, weight_hbm, cols_hbm, own_ref, other_ref, response_ref, kappa_ref, even_ref,
                 odd_ref, *refs):
    chunk_refs = refs[:-12]
    (sens_ref, factor_ref, control_ref, tile_ref, row_ref, sensor_ref, value_ref, weight_ref, cols_ref,
     send_ref, count_ref, sems) = refs[-12:]
    window = lanes(*window_of(my_chip(), chip_count(), own_ref.shape[1] // LANES))
    pairs = (
        (sens_hbm, sens_ref), (factor_hbm, factor_ref), (control_hbm, control_ref),
        (kappa_hbm.at[:, :, window], kappa_ref), (tile_hbm, tile_ref), (row_hbm, row_ref), (sensor_hbm, sensor_ref),
        (value_hbm, value_ref), (weight_hbm, weight_ref), (cols_hbm, cols_ref),
    )
    copies = [pltpu.make_async_copy(src, dst, sems.at[i]) for i, (src, dst) in enumerate(pairs)]
    for copy in copies:
        copy.start()
    send_ref[...] = jnp.zeros(send_ref.shape, F32)
    turns = len(chunk_refs)
    for turn in range(turns):
        count_ref[turn] = 0
    for copy in copies:
        copy.wait()

    member, mine = lax.axis_index("var"), lax.axis_index("tile")
    core = member % 2
    var_dev = control_ref.shape[0]
    for which, (sensor, out_ref) in enumerate(((core, own_ref), (1 - core, other_ref))):
        total = None
        for v in range(var_dev):
            scale = response(sens_ref, factor_ref, sensor, member * var_dev + v)
            response_ref[which, v] = jnp.full(response_ref.shape[2:], scale, F32)
            term = scale * control_ref[v]
            total = term if total is None else total + term
        out_ref[...] = total

    for i in range(2):
        pack_edges(even_ref.at[i], odd_ref.at[i], kappa_ref[i], margin)

    panels = value_ref.shape[0]
    sub = lax.broadcasted_iota(jnp.int32, (8 * turns, LANES), 0)
    lane = lax.broadcasted_iota(jnp.int32, (8 * turns, LANES), 1)
    trash = 3 * slots + 7

    def place(p, meta):
        turn = (tile_ref[p] ^ mine) - core * turns
        keep = (turn >= 0) & (turn < turns)
        turn = jnp.where(keep, turn, 0)
        slot = count_ref[turn]
        count_ref[turn] = slot + keep.astype(jnp.int32)
        rows = (value_ref[pl.ds(p, 1), :], weight_ref[pl.ds(p, 1), :], cols_ref[pl.ds(p, 1), :].astype(F32))
        for part, row in enumerate(rows):
            send_ref[turn, pl.ds(jnp.where(keep, part * slots + slot, trash), 1), :] = row
        facts = jnp.where(sub == 8 * turn, row_ref[p], sensor_ref[p]).astype(F32)
        here = (lane == jnp.where(keep, slot, LANES)) & (sub // 8 == turn)
        return jnp.where(here, facts, meta)

    meta = lax.fori_loop(0, panels, place, jnp.zeros((8 * turns, LANES), F32), unroll=8)
    for turn, chunk_ref in enumerate(chunk_refs):
        chunk_ref[: 3 * slots] = send_ref[turn, : 3 * slots]
        facts = meta[8 * turn : 8 * turn + 8]
        chunk_ref[3 * slots :] = jnp.where(lane[:8] == slots, count_ref[turn].astype(F32), facts)


def pieces(values):
    top = values.astype(jnp.bfloat16).astype(F32)
    return top, values - top


def scatter_kernel(slots, blocks_all, after_ref, home_ref, *refs):
    got_refs, (own_ref, other_ref, first_ref, acc_ref, meta_ref, sems) = refs[:-6], refs[-6:]
    core = lax.axis_index("var") % 2
    first_ref[...] = jnp.where(core == 0, home_ref[...], got_refs[0][...])
    got_refs = (first_ref, *got_refs[1:])
    copies = [
        pltpu.make_async_copy(ref.at[pl.ds(3 * slots, 8)], meta_ref.at[pl.ds(8 * s, 8)], sems.at[s])
        for s, ref in enumerate(got_refs)
    ]
    for copy in copies:
        copy.start()
    rows = own_ref.shape[1]
    start, size = window_of(my_chip(), chip_count(), blocks_all)
    per_kind = padded_blocks(size)
    tall = 2 * per_kind
    acc_ref[...] = jnp.zeros(acc_ref.shape, F32)
    place = lax.broadcasted_iota(jnp.int32, (tall, LANES), 0)
    is_weight = place < per_kind
    place = jnp.where(is_weight, place, place - per_kind) + start
    lane_ids = lax.broadcasted_iota(jnp.int32, (LANES, LANES), 0).astype(F32).astype(jnp.bfloat16)
    one, zero = jnp.bfloat16(1), jnp.bfloat16(0)
    sub = lax.broadcasted_iota(jnp.int32, (GROUP, LANES), 0)
    blank = jnp.zeros((2 * tall, LANES), jnp.bfloat16)
    for copy in copies:
        copy.wait()

    def load(s, base):
        got_ref = got_refs[s]
        count = meta_ref[8 * s, slots].astype(jnp.int32)
        value = got_ref[pl.ds(base, GROUP), :]
        weight = got_ref[pl.ds(slots + base, GROUP), :]
        cell = got_ref[pl.ds(2 * slots + base, GROUP), :].astype(jnp.int32)
        weight = jnp.where(sub + base < count, weight, 0.0)
        return pieces(weight), pieces(weight * value), (cell % LANES).astype(F32), cell // LANES

    def one_hots(loaded, i):
        weights, values, low, high = loaded
        here = place == high[i : i + 1]
        rows_of = [
            jnp.where(here, jnp.where(is_weight, w[i : i + 1], v[i : i + 1]), 0.0)
            for w, v in zip(weights, values)
        ]
        left = jnp.concatenate(rows_of, axis=0).astype(jnp.bfloat16)
        column = jnp.broadcast_to(low[i : i + 1], (16, LANES)).astype(jnp.bfloat16)
        column = jnp.concatenate([column] * (LANES // 16), axis=0)
        return left, jnp.where(lane_ids == column, one, zero)

    def pair(s, g, carry):
        base = pl.multiple_of(g * GROUP, GROUP)
        loaded = [load(s + i, base) for i in (0, 1)]
        for k in range(GROUP):
            hots = [one_hots(loaded[i], k) for i in (0, 1)]
            left = jnp.concatenate(
                [
                    jnp.concatenate([hots[0][0], blank], axis=1),
                    jnp.concatenate([blank, hots[1][0]], axis=1),
                ],
                axis=0,
            )
            both = lax.dot_general(
                left, jnp.concatenate([hots[0][1], hots[1][1]], axis=1), (((1,), (1,)), ((), ())),
                preferred_element_type=F32,
            )
            for i in (0, 1):
                row = meta_ref[8 * (s + i), base + k].astype(jnp.int32)
                sensor = meta_ref[8 * (s + i) + 1, base + k].astype(jnp.int32)
                at = pl.multiple_of((sensor * rows + row) * tall, 8)
                mine = both[2 * i * tall : 2 * (i + 1) * tall]
                acc_ref[pl.ds(at, tall), :] += mine[:tall] + mine[tall:]
        return carry

    for s in range(0, len(got_refs), 2):
        most = jnp.maximum(meta_ref[8 * s, slots], meta_ref[8 * s + 8, slots]).astype(jnp.int32)
        lax.fori_loop(0, (most + GROUP - 1) // GROUP, functools.partial(pair, s), 0)
    for sensor, out_ref in ((core, own_ref), (1 - core, other_ref)):
        begin = sensor * rows * tall
        for kind in range(2):
            for b in range(size):
                out_ref[kind, :, b * LANES : (b + 1) * LANES] = acc_ref[
                    pl.ds(begin + kind * per_kind + b, rows, stride=tall), :
                ]


def padded_blocks(size):
    return -(-size // 4) * 4


def even_tile():
    return lax.axis_index("tile") % 2 == 0


def has_above():
    return lax.axis_index("tile") > 0


def has_below():
    return lax.axis_index("tile") + 1 < lax.axis_size("tile")


def pack_edges(even_ref, odd_ref, rows_value, margin):
    rows, width = rows_value.shape
    even = even_tile()
    for b in range(width // LANES):
        at = slice(b * LANES, (b + 1) * LANES)
        head, tail = rows_value[:margin, at], rows_value[rows - margin :, at]
        even_ref[b * margin : (b + 1) * margin] = jnp.where(even, tail, head)
        odd_ref[b * margin : (b + 1) * margin] = jnp.where(even, head, tail)


def cut_kernel(first_ref, second_ref, mine_ref, *out_refs):
    chip, chips, blocks = my_chip(), chip_count(), first_ref.shape[1] // LANES
    for d, out_ref in enumerate((mine_ref, *out_refs)):
        window = lanes(*window_of(chip ^ d, chips, blocks))
        out_ref[...] = first_ref[:, window] + second_ref[:, window]


def edges_kernel(margin, *refs):
    terms, (total_ref, even_ref, odd_ref) = refs[:-3], refs[-3:]
    total = terms[0][...]
    for term in terms[1:]:
        total = total + term[...]
    total_ref[...] = total
    pack_edges(even_ref, odd_ref, total, margin)


def ring_rows(rows, margin):
    return -(-(rows + 2 * margin) // 8) * 8


def lay_ring(ref, own, from_even, from_odd, margin):
    rows, total = own.shape[0], ref.shape[0]
    even = even_tile()
    ref[rows:total] = jnp.zeros((total - rows, ref.shape[1]), F32)
    ref[:rows] = own
    for b in range(ref.shape[1] // LANES):
        at = slice(b * LANES, (b + 1) * LANES)
        one, two = (m[b * margin : (b + 1) * margin] for m in (from_even, from_odd))
        ref[rows : rows + margin, at] = jnp.where(has_below(), jnp.where(even, one, two), 0.0)
        ref[total - margin :, at] = jnp.where(has_above(), jnp.where(even, two, one), 0.0)


def block(ref, j):
    return ref[:, j * LANES : (j + 1) * LANES]


def sideways(blocks):
    shape = blocks[0].shape
    lane = lax.broadcasted_iota(jnp.int32, shape, 1)
    zero = jnp.zeros(shape, F32)
    ahead = [pltpu.roll(x, 1, 1) for x in blocks]
    back = [pltpu.roll(x, LANES - 1, 1) for x in blocks]
    for j, here in enumerate(blocks):
        before = ahead[j - 1] if j else zero
        after = back[j + 1] if j + 1 < len(blocks) else zero
        yield here, jnp.where(lane == 0, before, ahead[j]), jnp.where(lane == LANES - 1, after, back[j])


def face_weights(coef_ref, row_ref, col_ref, rows, margin):
    total, width = row_ref.shape
    blocks = width // LANES
    r = lax.broadcasted_iota(jnp.int32, (total, LANES), 0)
    inside = (
        (r < rows)
        | ((r < rows + margin) & has_below())
        | ((r >= total - margin) & has_above())
    )
    scale = jnp.where(inside, 0.125, 0.0)
    unit = jnp.where(inside, 1.0, 0.0)
    columns = [block(col_ref, j) for j in range(blocks)]
    for j, (k_col, k_left, k_right) in enumerate(sideways(columns)):
        at = slice(j * LANES, (j + 1) * LANES)
        k_row = block(row_ref, j)
        up = scale * (k_row + pltpu.roll(k_row, 1, 0))
        down = scale * (k_row + pltpu.roll(k_row, total - 1, 0))
        left = scale * (k_col + k_left)
        right = scale * (k_col + k_right)
        coef_ref[0, :, at] = unit - up - down - left - right
        coef_ref[1, :, at] = up
        coef_ref[2, :, at] = down
        coef_ref[3, :, at] = left
        coef_ref[4, :, at] = right


def one_pass(fields, coef_ref, spans):
    def weights(i, at):
        got = [coef_ref[i, span, at] for span in spans]
        return jnp.concatenate(got, axis=0) if len(got) > 1 else got[0]

    total = fields[0].shape[0]
    out = []
    for j, (here, left, right) in enumerate(sideways(fields)):
        at = slice(j * LANES, (j + 1) * LANES)
        out.append(
            weights(0, at) * here
            + weights(1, at) * pltpu.roll(here, 1, 0)
            + weights(2, at) * pltpu.roll(here, total - 1, 0)
            + weights(3, at) * left
            + weights(4, at) * right
        )
    return out


def diffuse(ring_ref, coef_ref, rows, margin):
    total, width = ring_ref.shape
    inner = margin // 8 * 8
    wide = [slice(0, total)]
    narrow = [slice(0, rows + inner), slice(total - inner, total)]
    fields = [block(ring_ref, j) for j in range(width // LANES)]
    for _ in range(margin - inner):
        fields = one_pass(fields, coef_ref, wide)
    fields = [jnp.concatenate([f[span] for span in narrow], axis=0) for f in fields]
    for _ in range(inner):
        fields = one_pass(fields, coef_ref, narrow)
    return [f[:rows] for f in fields]


def faces_kernel(margin, odd_ref, even_ref, kappa_ref, sums_ref, *refs):
    coef_ref, sums_out, one_ref, two_ref = refs[-4:]
    sums_out[...] = sums_ref[...]
    rows = kappa_ref.shape[1]
    lay_ring(one_ref, kappa_ref[0], even_ref.at[0], odd_ref.at[0], margin)
    lay_ring(two_ref, kappa_ref[1], even_ref.at[1], odd_ref.at[1], margin)
    face_weights(coef_ref, one_ref, two_ref, rows, margin)


def smooth_kernel(margin, own_ref, odd_ref, even_ref, coef_ref, out_ref, ring_ref):
    rows = own_ref.shape[0]
    lay_ring(ring_ref, own_ref[...], even_ref, odd_ref, margin)
    for j, field in enumerate(diffuse(ring_ref, coef_ref, rows, margin)):
        out_ref[:, j * LANES : (j + 1) * LANES] = field


def adjoint_kernel(margin, smooth_ref, mask_ref, sums_ref, more_ref, adjoint_ref, even_ref, odd_ref):
    weight = sums_ref[0] + more_ref[0]
    value = sums_ref[1] + more_ref[1]
    window = lanes(*window_of(my_chip(), chip_count(), mask_ref.shape[1] // LANES))
    adjoint = mask_ref[:, window].astype(F32) * (weight * smooth_ref[...] - value)
    adjoint_ref[...] = adjoint
    pack_edges(even_ref, odd_ref, adjoint, margin)


def spread_kernel(margin, own_ref, even_ref, odd_ref, coef_ref, out_ref, ring_ref):
    rows = own_ref.shape[0]
    lay_ring(ring_ref, own_ref[...], even_ref, odd_ref, margin)
    for j, field in enumerate(diffuse(ring_ref, coef_ref, rows, margin)):
        ring_ref[:rows, j * LANES : (j + 1) * LANES] = field
    own = out_ref.shape[1] // LANES
    start = window_of(my_chip(), chip_count(), own * chip_count())[0]
    out_ref[...] = ring_ref[:rows, lanes(my_chip() * own - start, own)]


def result_kernel(response_ref, control_ref, *refs):
    own, out_ref = refs[0].shape[1] // LANES, refs[-1]
    for d in range(len(refs) // 2):
        window = lanes((my_chip() ^ d) * own, own)
        for v in range(control_ref.shape[0]):
            mine, theirs = (response_ref[i, v][:1, :1] for i in range(2))
            out_ref[v, :, window] = (
                control_ref[v, :, window] + mine * refs[2 * d][...] + theirs * refs[2 * d + 1][...]
            )


def swap(values, axis, bit):
    count = lax.axis_size(axis)
    return lax.ppermute(values, axis, [(i, i ^ bit) for i in range(count)])


def swap_edges(even, odd):
    tiles, members = lax.axis_size("tile"), lax.axis_size("var")
    pairs = []
    for t in range(tiles):
        other = t + 1 if t % 2 else t - 1
        for q in range(members):
            to = other * members + q if 0 <= other < tiles else t * members + (q ^ 1)
            pairs.append((t * members + q, to))
    odd = lax.ppermute(odd, ("tile", "var"), pairs)
    return swap(even, "tile", 1), odd


def deliver(chunk, turn):
    groups, tiles, members = (lax.axis_size(name) for name in ("grp", "tile", "var"))
    pairs = []
    for g in range(groups):
        for t in range(tiles):
            for q in range(members):
                offset = (q % 2) * (tiles // 2) + turn
                to_group = g if offset else g ^ 1
                pairs.append((
                    (g * tiles + t) * members + q, (to_group * tiles + (t ^ offset)) * members + q
                ))
    return lax.ppermute(chunk, ("grp", "tile", "var"), pairs)


def local(control, diffusivity, land_mask, panel_tile, panel_row, panel_cols, obs_values,
          obs_weights, panel_sensor, sensitivity, cross_factor):
    rows, width = control.shape[1:]
    var_dev = control.shape[0]
    tiles, members = lax.axis_size("tile"), lax.axis_size("var")
    panels, panel_width = panel_cols.shape
    slots = 2 * panels // tiles
    turns = tiles // 2
    blocks = width // LANES
    margin = PASSES
    total = ring_rows(rows, margin)
    chips = members // 2
    size = window_of(0, chips, blocks)[1]
    field = jax.ShapeDtypeStruct((rows, width), F32)
    share = jax.ShapeDtypeStruct((rows, width // chips), F32)
    view = jax.ShapeDtypeStruct((rows, size * LANES), F32)
    view2 = jax.ShapeDtypeStruct((2, *view.shape), F32)
    edge = jax.ShapeDtypeStruct((margin * size, LANES), F32)
    edge2 = jax.ShapeDtypeStruct((2, *edge.shape), F32)
    chunk = jax.ShapeDtypeStruct((3 * slots + 8, panel_width), F32)
    ints = pltpu.SMEM((panels,), jnp.int32)

    own, other, responses, kappa, kappa_even, kappa_odd, *chunks = call(
        functools.partial(first_kernel, slots, margin),
        [field, field, jax.ShapeDtypeStruct((2, var_dev, 8, LANES), F32), view2, edge2, edge2]
        + [chunk] * turns,
        [HBM] * 10,
        [
            pltpu.SMEM(sensitivity.shape, F32),
            pltpu.SMEM(cross_factor.shape, F32),
            pltpu.VMEM(control.shape, F32),
            ints, ints, ints,
            pltpu.VMEM(obs_values.shape, F32),
            pltpu.VMEM(obs_weights.shape, F32),
            pltpu.VMEM(panel_cols.shape, jnp.int32),
            pltpu.VMEM((turns, *chunk.shape), F32),
            pltpu.SMEM((turns,), jnp.int32),
            pltpu.SemaphoreType.DMA((10,)),
        ],
        cost=cost(3000),
    )(*(in_hbm(x) for x in (sensitivity, cross_factor, control, diffusivity, panel_tile.reshape(-1),
                            panel_row, panel_sensor, obs_values, obs_weights, panel_cols)))

    got = [deliver(c, turn) for turn, c in enumerate(chunks)]
    part, *parts = call(cut_kernel, [view] * chips, [VMEM] * 2, cost=cost(200))(
        own, swap(other, "var", 1)
    )
    parts = [swap(p, "var", 2 * (d + 1)) for d, p in enumerate(parts)]
    kappa_even, kappa_odd = swap_edges(kappa_even, kappa_odd)
    smooth_in, even, odd = call(
        functools.partial(edges_kernel, margin), [view, edge, edge], [VMEM] * chips, cost=cost(500)
    )(part, *parts)
    even, odd = swap_edges(even, odd)
    sums, sums_other = call(
        functools.partial(scatter_kernel, slots, blocks),
        [view2, view2],
        [AFTER] + [VMEM] * (turns + 1),
        [
            pltpu.VMEM(chunk.shape, F32),
            pltpu.VMEM((2 * rows * 2 * padded_blocks(size), LANES), F32),
            pltpu.SMEM((8 * turns, LANES), F32),
            pltpu.SemaphoreType.DMA((turns,)),
        ],
        cost=cost(100000),
    )(smooth_in, chunks[0], *got)
    ring = pltpu.VMEM((total, size * LANES), F32)
    coef, sums_other = call(
        functools.partial(faces_kernel, margin),
        [jax.ShapeDtypeStruct((5, total, size * LANES), F32), view2],
        [VMEM] * 4 + [AFTER] * 2,
        [ring, ring],
        cost=cost(1000),
    )(kappa_odd, kappa_even, kappa, sums_other, odd, even)
    more_sums = swap(sums_other, "var", 1)
    (smooth,) = call(
        functools.partial(smooth_kernel, margin),
        [view],
        [VMEM] * 4,
        [ring],
        cost=cost(4000),
    )(smooth_in, odd, even, coef)
    adjoint, even, odd = call(
        functools.partial(adjoint_kernel, margin), [view, edge, edge], [VMEM] * 4, cost=cost(500)
    )(smooth, land_mask, sums, more_sums)
    even, odd = swap_edges(even, odd)
    (mine,) = call(
        functools.partial(spread_kernel, margin),
        [share],
        [VMEM] * 4,
        [ring],
        cost=cost(4000),
    )(adjoint, even, odd, coef)
    shares = [mine] + [swap(mine, "var", d) for d in range(1, members)]
    (out,) = call(
        result_kernel,
        [jax.ShapeDtypeStruct(control.shape, F32)],
        [VMEM] * (2 + members),
        cost=cost(1000),
    )(responses, control, *shares)
    return out


def solution(mesh):
    return jax.shard_map(
        local,
        mesh=mesh,
        in_specs=(
            P("var", ("grp", "tile"), None),
            P(None, ("grp", "tile"), None),
            P(("grp", "tile"), None),
            P(("grp", "tile"), None),
            P(("grp", "tile")),
            P(("grp", "tile"), None),
            P(("grp", "tile"), None),
            P(("grp", "tile"), None),
            P(("grp", "tile")),
            P(),
            P(),
        ),
        out_specs=P("var", ("grp", "tile"), None),
        check_vma=False,
    )
```

```python
import functools

import jax
import jax.numpy as jnp
from jax import lax
from jax.experimental import pallas as pl
from jax.experimental.pallas import tpu as pltpu
from jax.sharding import PartitionSpec as P

PASSES = 10
LANES = 128
GROUP = 16
VMEM = pl.BlockSpec(memory_space=pltpu.VMEM)
SMEM = pl.BlockSpec(memory_space=pltpu.SMEM)
HBM = pl.BlockSpec(memory_space=pltpu.HBM)
AFTER = pl.BlockSpec(memory_space=pl.ANY)
F32 = jnp.float32


def in_hbm(values):
    return pltpu.with_memory_space_constraint(values, pltpu.HBM)


def call(body, outs, ins, scratch=(), limit=16, cost=None):
    return pl.pallas_call(
        body,
        out_shape=outs,
        in_specs=ins,
        out_specs=[VMEM] * len(outs),
        scratch_shapes=list(scratch),
        compiler_params=pltpu.CompilerParams(vmem_limit_bytes=limit << 20),
        cost_estimate=cost,
    )


def cost(cycles):
    return pl.CostEstimate(flops=cycles * 4096, bytes_accessed=cycles * 1024, transcendentals=0)


def response(sens_ref, factor_ref, sensor, variable):
    total = sens_ref[sensor, 0] * factor_ref[0, variable]
    for u in range(1, factor_ref.shape[0]):
        total = total + sens_ref[sensor, u] * factor_ref[u, variable]
    return total


def fetch(pairs, sems):
    copies = [pltpu.make_async_copy(src, dst, sems.at[i]) for i, (src, dst) in enumerate(pairs)]
    for copy in copies:
        copy.start()
    return copies


def window_of(chip, chips, blocks):
    own = blocks // chips
    size = min(own + 2, own + chips - 1)
    return jnp.clip(chip * own - 1, 0, blocks - size), size


def my_chip():
    return lax.axis_index("var") // 2


def chip_count():
    return lax.axis_size("var") // 2


def lanes(start, size):
    return pl.ds(pl.multiple_of(start * LANES, LANES), size * LANES)


def first_kernel(slots, margin, sens_hbm, factor_hbm, control_hbm, kappa_hbm, tile_hbm, row_hbm, sensor_hbm,
                 value_hbm, weight_hbm, cols_hbm, own_ref, other_ref, response_ref, kappa_ref, even_ref,
                 odd_ref, *refs):
    chunk_refs = refs[:-12]
    (sens_ref, factor_ref, control_ref, tile_ref, row_ref, sensor_ref, value_ref, weight_ref, cols_ref,
     send_ref, count_ref, sems) = refs[-12:]
    window = lanes(*window_of(my_chip(), chip_count(), own_ref.shape[1] // LANES))
    pairs = (
        (sens_hbm, sens_ref), (factor_hbm, factor_ref), (control_hbm, control_ref),
        (kappa_hbm.at[:, :, window], kappa_ref), (tile_hbm, tile_ref), (row_hbm, row_ref), (sensor_hbm, sensor_ref),
        (value_hbm, value_ref), (weight_hbm, weight_ref), (cols_hbm, cols_ref),
    )
    copies = [pltpu.make_async_copy(src, dst, sems.at[i]) for i, (src, dst) in enumerate(pairs)]
    for copy in copies:
        copy.start()
    send_ref[...] = jnp.zeros(send_ref.shape, F32)
    for source in range(lax.axis_size("tile")):
        count_ref[source] = 0
    for copy in copies:
        copy.wait()

    member, mine = lax.axis_index("var"), lax.axis_index("tile")
    core = member % 2
    var_dev = control_ref.shape[0]
    for which, (sensor, out_ref) in enumerate(((core, own_ref), (1 - core, other_ref))):
        total = None
        for v in range(var_dev):
            scale = response(sens_ref, factor_ref, sensor, member * var_dev + v)
            response_ref[which, v] = jnp.full(response_ref.shape[2:], scale, F32)
            term = scale * control_ref[v]
            total = term if total is None else total + term
        out_ref[...] = total

    for i in range(2):
        pack_edges(even_ref.at[i], odd_ref.at[i], kappa_ref[i], margin)

    tiles = lax.axis_size("tile")
    full = tiles // 2 - 1
    first = jnp.where(core == 0, 1, tiles // 2)
    panels = value_ref.shape[0]
    sub = lax.broadcasted_iota(jnp.int32, (8, LANES), 0)
    lane = lax.broadcasted_iota(jnp.int32, (8, LANES), 1)
    trash = 3 * slots + 7

    def place(p, meta):
        source = tile_ref[p] ^ mine
        count = count_ref[source]
        count_ref[source] = count + 1
        parity, slot = count % 2, count // 2
        whole = (source >= first) & (source < first + full)
        shared = ((source == 0) | (source == tiles - 1)) & (parity == core)
        keep = whole | shared
        half = jnp.where(whole, 2 * (source - first) + parity, jnp.where(source == 0, tiles - 1, tiles - 2))
        half = jnp.where(keep, half, 0)
        rows = (value_ref[pl.ds(p, 1), :], weight_ref[pl.ds(p, 1), :], cols_ref[pl.ds(p, 1), :].astype(F32))
        for part, row in enumerate(rows):
            send_ref[half, pl.ds(jnp.where(keep, part * slots + slot, trash), 1), :] = row
        facts = jnp.where(sub == 0, row_ref[p], sensor_ref[p]).astype(F32)
        return jnp.where(lane == jnp.where(keep, half * slots + slot, LANES), facts, meta)

    meta = lax.fori_loop(0, panels, place, jnp.zeros((8, LANES), F32), unroll=8)
    for half in range(tiles):
        if half < 2 * full:
            held = (count_ref[first + half // 2] + 1 - half % 2) // 2
        else:
            held = (count_ref[0 if half == tiles - 1 else tiles - 1] + 1 - core) // 2
        meta = jnp.where((sub == 2) & (lane == half), held.astype(F32), meta)
    for half in range(tiles):
        out_ref = chunk_refs[half // 2].at[half % 2] if half < 2 * full else chunk_refs[half - full]
        out_ref[: 3 * slots] = send_ref[half, : 3 * slots]
        out_ref[3 * slots :] = meta


def pieces(values):
    top = values.astype(jnp.bfloat16).astype(F32)
    return top, values - top


def scatter_kernel(slots, blocks_all, after_ref, *refs):
    got_refs, (own_ref, other_ref, acc_ref, meta_ref, sems) = refs[:-5], refs[-5:]
    core = lax.axis_index("var") % 2
    got_refs = [r.at[i] for r in got_refs[:-2] for i in (0, 1)] + list(got_refs[-2:])
    size_of_group = min(GROUP, slots)
    copies = [
        pltpu.make_async_copy(ref.at[pl.ds(3 * slots, 8)], meta_ref.at[pl.ds(8 * s, 8)], sems.at[s])
        for s, ref in enumerate(got_refs)
    ]
    for copy in copies:
        copy.start()
    rows = own_ref.shape[1]
    start, size = window_of(my_chip(), chip_count(), blocks_all)
    per_kind = padded_blocks(size)
    tall = 2 * per_kind
    acc_ref[...] = jnp.zeros(acc_ref.shape, F32)
    place = lax.broadcasted_iota(jnp.int32, (tall, LANES), 0)
    is_weight = place < per_kind
    place = jnp.where(is_weight, place, place - per_kind) + start
    lane_ids = lax.broadcasted_iota(jnp.int32, (LANES, LANES), 0).astype(F32).astype(jnp.bfloat16)
    one, zero = jnp.bfloat16(1), jnp.bfloat16(0)
    sub = lax.broadcasted_iota(jnp.int32, (size_of_group, LANES), 0)
    blank = jnp.zeros((2 * tall, LANES), jnp.bfloat16)
    for copy in copies:
        copy.wait()

    def load(s, base):
        got_ref = got_refs[s]
        count = meta_ref[8 * s + 2, s].astype(jnp.int32)
        value = got_ref[pl.ds(base, size_of_group), :]
        weight = got_ref[pl.ds(slots + base, size_of_group), :]
        cell = got_ref[pl.ds(2 * slots + base, size_of_group), :].astype(jnp.int32)
        weight = jnp.where(sub + base < count, weight, 0.0)
        return pieces(weight), pieces(weight * value), (cell % LANES).astype(F32), cell // LANES

    def one_hots(loaded, i):
        weights, values, low, high = loaded
        here = place == high[i : i + 1]
        rows_of = [
            jnp.where(here, jnp.where(is_weight, w[i : i + 1], v[i : i + 1]), 0.0)
            for w, v in zip(weights, values)
        ]
        left = jnp.concatenate(rows_of, axis=0).astype(jnp.bfloat16)
        column = jnp.broadcast_to(low[i : i + 1], (16, LANES)).astype(jnp.bfloat16)
        column = jnp.concatenate([column] * (LANES // 16), axis=0)
        return left, jnp.where(lane_ids == column, one, zero)

    def pair(s, g, carry):
        base = pl.multiple_of(g * size_of_group, size_of_group)
        loaded = [load(s + i, base) for i in (0, 1)]
        for k in range(size_of_group):
            hots = [one_hots(loaded[i], k) for i in (0, 1)]
            left = jnp.concatenate(
                [
                    jnp.concatenate([hots[0][0], blank], axis=1),
                    jnp.concatenate([blank, hots[1][0]], axis=1),
                ],
                axis=0,
            )
            both = lax.dot_general(
                left, jnp.concatenate([hots[0][1], hots[1][1]], axis=1), (((1,), (1,)), ((), ())),
                preferred_element_type=F32,
            )
            for i in (0, 1):
                row = meta_ref[8 * (s + i), (s + i) * slots + base + k].astype(jnp.int32)
                sensor = meta_ref[8 * (s + i) + 1, (s + i) * slots + base + k].astype(jnp.int32)
                at = pl.multiple_of((sensor * rows + row) * tall, 8)
                mine = both[2 * i * tall : 2 * (i + 1) * tall]
                acc_ref[pl.ds(at, tall), :] += mine[:tall] + mine[tall:]
        return carry

    for s in range(0, len(got_refs), 2):
        most = jnp.maximum(meta_ref[8 * s + 2, s], meta_ref[8 * s + 10, s + 1]).astype(jnp.int32)
        lax.fori_loop(0, (most + size_of_group - 1) // size_of_group, functools.partial(pair, s), 0)
    for sensor, out_ref in ((core, own_ref), (1 - core, other_ref)):
        begin = sensor * rows * tall
        for kind in range(2):
            for b in range(size):
                out_ref[kind, :, b * LANES : (b + 1) * LANES] = acc_ref[
                    pl.ds(begin + kind * per_kind + b, rows, stride=tall), :
                ]


def padded_blocks(size):
    return -(-size // 4) * 4


def even_tile():
    return lax.axis_index("tile") % 2 == 0


def has_above():
    return lax.axis_index("tile") > 0


def has_below():
    return lax.axis_index("tile") + 1 < lax.axis_size("tile")


def pack_edges(even_ref, odd_ref, rows_value, margin):
    rows, width = rows_value.shape
    even = even_tile()
    for b in range(width // LANES):
        at = slice(b * LANES, (b + 1) * LANES)
        head, tail = rows_value[:margin, at], rows_value[rows - margin :, at]
        even_ref[b * margin : (b + 1) * margin] = jnp.where(even, tail, head)
        odd_ref[b * margin : (b + 1) * margin] = jnp.where(even, head, tail)


def cut_kernel(first_ref, second_ref, mine_ref, *out_refs):
    chip, chips, blocks = my_chip(), chip_count(), first_ref.shape[1] // LANES
    for d, out_ref in enumerate((mine_ref, *out_refs)):
        window = lanes(*window_of(chip ^ d, chips, blocks))
        out_ref[...] = first_ref[:, window] + second_ref[:, window]


def edges_kernel(margin, *refs):
    terms, (total_ref, even_ref, odd_ref) = refs[:-3], refs[-3:]
    total = terms[0][...]
    for term in terms[1:]:
        total = total + term[...]
    total_ref[...] = total
    pack_edges(even_ref, odd_ref, total, margin)


def ring_rows(rows, margin):
    return -(-(rows + 2 * margin) // 8) * 8


def lay_ring(ref, own, from_even, from_odd, margin):
    rows, total = own.shape[0], ref.shape[0]
    even = even_tile()
    ref[rows:total] = jnp.zeros((total - rows, ref.shape[1]), F32)
    ref[:rows] = own
    for b in range(ref.shape[1] // LANES):
        at = slice(b * LANES, (b + 1) * LANES)
        one, two = (m[b * margin : (b + 1) * margin] for m in (from_even, from_odd))
        ref[rows : rows + margin, at] = jnp.where(has_below(), jnp.where(even, one, two), 0.0)
        ref[total - margin :, at] = jnp.where(has_above(), jnp.where(even, two, one), 0.0)


def block(ref, j):
    return ref[:, j * LANES : (j + 1) * LANES]


def sideways(blocks):
    shape = blocks[0].shape
    lane = lax.broadcasted_iota(jnp.int32, shape, 1)
    zero = jnp.zeros(shape, F32)
    ahead = [pltpu.roll(x, 1, 1) for x in blocks]
    back = [pltpu.roll(x, LANES - 1, 1) for x in blocks]
    for j, here in enumerate(blocks):
        before = ahead[j - 1] if j else zero
        after = back[j + 1] if j + 1 < len(blocks) else zero
        yield here, jnp.where(lane == 0, before, ahead[j]), jnp.where(lane == LANES - 1, after, back[j])


def face_weights(coef_ref, row_ref, col_ref, rows, margin):
    total, width = row_ref.shape
    blocks = width // LANES
    r = lax.broadcasted_iota(jnp.int32, (total, LANES), 0)
    inside = (
        (r < rows)
        | ((r < rows + margin) & has_below())
        | ((r >= total - margin) & has_above())
    )
    scale = jnp.where(inside, 0.125, 0.0)
    unit = jnp.where(inside, 1.0, 0.0)
    columns = [block(col_ref, j) for j in range(blocks)]
    for j, (k_col, k_left, k_right) in enumerate(sideways(columns)):
        at = slice(j * LANES, (j + 1) * LANES)
        k_row = block(row_ref, j)
        up = scale * (k_row + pltpu.roll(k_row, 1, 0))
        down = scale * (k_row + pltpu.roll(k_row, total - 1, 0))
        left = scale * (k_col + k_left)
        right = scale * (k_col + k_right)
        coef_ref[0, :, at] = unit - up - down - left - right
        coef_ref[1, :, at] = up
        coef_ref[2, :, at] = down
        coef_ref[3, :, at] = left
        coef_ref[4, :, at] = right


def one_pass(fields, coef_ref, spans):
    def weights(i, at):
        got = [coef_ref[i, span, at] for span in spans]
        return jnp.concatenate(got, axis=0) if len(got) > 1 else got[0]

    total = fields[0].shape[0]
    out = []
    for j, (here, left, right) in enumerate(sideways(fields)):
        at = slice(j * LANES, (j + 1) * LANES)
        out.append(
            weights(0, at) * here
            + weights(1, at) * pltpu.roll(here, 1, 0)
            + weights(2, at) * pltpu.roll(here, total - 1, 0)
            + weights(3, at) * left
            + weights(4, at) * right
        )
    return out


def diffuse(ring_ref, coef_ref, rows, margin):
    total, width = ring_ref.shape
    inner = margin // 8 * 8
    wide = [slice(0, total)]
    narrow = [slice(0, rows + inner), slice(total - inner, total)]
    fields = [block(ring_ref, j) for j in range(width // LANES)]
    for _ in range(margin - inner):
        fields = one_pass(fields, coef_ref, wide)
    fields = [jnp.concatenate([f[span] for span in narrow], axis=0) for f in fields]
    for _ in range(inner):
        fields = one_pass(fields, coef_ref, narrow)
    return [f[:rows] for f in fields]


def faces_kernel(margin, even_ref, odd_ref, kappa_ref, sums_ref, *refs):
    coef_ref, sums_out, one_ref, two_ref = refs[-4:]
    sums_out[...] = sums_ref[...]
    rows = kappa_ref.shape[1]
    lay_ring(one_ref, kappa_ref[0], even_ref.at[0], odd_ref.at[0], margin)
    lay_ring(two_ref, kappa_ref[1], even_ref.at[1], odd_ref.at[1], margin)
    face_weights(coef_ref, one_ref, two_ref, rows, margin)


def smooth_kernel(margin, own_ref, even_ref, odd_ref, coef_ref, out_ref, ring_ref):
    rows = own_ref.shape[0]
    lay_ring(ring_ref, own_ref[...], even_ref, odd_ref, margin)
    for j, field in enumerate(diffuse(ring_ref, coef_ref, rows, margin)):
        out_ref[:, j * LANES : (j + 1) * LANES] = field


def adjoint_kernel(margin, smooth_ref, mask_ref, sums_ref, more_ref, adjoint_ref, even_ref, odd_ref):
    weight = sums_ref[0] + more_ref[0]
    value = sums_ref[1] + more_ref[1]
    window = lanes(*window_of(my_chip(), chip_count(), mask_ref.shape[1] // LANES))
    adjoint = mask_ref[:, window].astype(F32) * (weight * smooth_ref[...] - value)
    adjoint_ref[...] = adjoint
    pack_edges(even_ref, odd_ref, adjoint, margin)


def spread_kernel(margin, own_ref, even_ref, odd_ref, coef_ref, out_ref, ring_ref):
    rows = own_ref.shape[0]
    lay_ring(ring_ref, own_ref[...], even_ref, odd_ref, margin)
    for j, field in enumerate(diffuse(ring_ref, coef_ref, rows, margin)):
        ring_ref[:rows, j * LANES : (j + 1) * LANES] = field
    own = out_ref.shape[1] // LANES
    start = window_of(my_chip(), chip_count(), own * chip_count())[0]
    out_ref[...] = ring_ref[:rows, lanes(my_chip() * own - start, own)]


def result_kernel(response_ref, control_ref, *refs):
    own, out_ref = refs[0].shape[1] // LANES, refs[-1]
    for d in range(len(refs) // 2):
        window = lanes((my_chip() ^ d) * own, own)
        for v in range(control_ref.shape[0]):
            mine, theirs = (response_ref[i, v][:1, :1] for i in range(2))
            out_ref[v, :, window] = (
                control_ref[v, :, window] + mine * refs[2 * d][...] + theirs * refs[2 * d + 1][...]
            )


def swap(values, axis, bit):
    count = lax.axis_size(axis)
    return lax.ppermute(values, axis, [(i, i ^ bit) for i in range(count)])


def swap_edges(even, odd):
    tiles, members = lax.axis_size("tile"), lax.axis_size("var")
    pairs = []
    for t in range(tiles):
        other = t + 1 if t % 2 else t - 1
        for q in range(members):
            to = other * members + q if 0 <= other < tiles else t * members + (q ^ 1)
            pairs.append((t * members + q, to))
    return swap(even, "tile", 1), lax.ppermute(odd, ("tile", "var"), pairs)


def deliver(chunks):
    tiles, members = lax.axis_size("tile"), lax.axis_size("var")
    got = []
    for turn, chunk in enumerate(chunks[:-1]):
        pairs = []
        for t in range(tiles):
            for q in range(members):
                offset = tiles - 1 if turn == len(chunks) - 2 else 1 + turn + (q % 2) * (tiles // 2 - 1)
                pairs.append((t * members + q, (t ^ offset) * members + q))
        got.append(lax.ppermute(chunk, ("tile", "var"), pairs))
    return got + [chunks[-1]]


def local(control, diffusivity, land_mask, panel_tile, panel_row, panel_cols, obs_values,
          obs_weights, panel_sensor, sensitivity, cross_factor):
    rows, width = control.shape[1:]
    var_dev = control.shape[0]
    tiles, members = lax.axis_size("tile"), lax.axis_size("var")
    panels, panel_width = panel_cols.shape
    slots = panels // tiles
    blocks = width // LANES
    margin = PASSES
    total = ring_rows(rows, margin)
    chips = members // 2
    size = window_of(0, chips, blocks)[1]
    field = jax.ShapeDtypeStruct((rows, width), F32)
    share = jax.ShapeDtypeStruct((rows, width // chips), F32)
    view = jax.ShapeDtypeStruct((rows, size * LANES), F32)
    view2 = jax.ShapeDtypeStruct((2, *view.shape), F32)
    edge = jax.ShapeDtypeStruct((margin * size, LANES), F32)
    edge2 = jax.ShapeDtypeStruct((2, *edge.shape), F32)
    half = jax.ShapeDtypeStruct((3 * slots + 8, panel_width), F32)
    chunks = [jax.ShapeDtypeStruct((2, *half.shape), F32)] * (tiles // 2 - 1) + [half] * 2
    ints = pltpu.SMEM((panels,), jnp.int32)

    own, other, responses, kappa, kappa_even, kappa_odd, *chunks = call(
        functools.partial(first_kernel, slots, margin),
        [field, field, jax.ShapeDtypeStruct((2, var_dev, 8, LANES), F32), view2, edge2, edge2]
        + chunks,
        [HBM] * 10,
        [
            pltpu.SMEM(sensitivity.shape, F32),
            pltpu.SMEM(cross_factor.shape, F32),
            pltpu.VMEM(control.shape, F32),
            ints, ints, ints,
            pltpu.VMEM(obs_values.shape, F32),
            pltpu.VMEM(obs_weights.shape, F32),
            pltpu.VMEM(panel_cols.shape, jnp.int32),
            pltpu.VMEM((tiles, *half.shape), F32),
            pltpu.SMEM((tiles,), jnp.int32),
            pltpu.SemaphoreType.DMA((10,)),
        ],
        cost=cost(3000),
    )(*(in_hbm(x) for x in (sensitivity, cross_factor, control, diffusivity, panel_tile.reshape(-1),
                            panel_row, panel_sensor, obs_values, obs_weights, panel_cols)))

    got = deliver(chunks)
    part, *parts = call(cut_kernel, [view] * chips, [VMEM] * 2, cost=cost(200))(
        own, swap(other, "var", 1)
    )
    parts = [swap(p, "var", 2 * (d + 1)) for d, p in enumerate(parts)]
    kappa_even, kappa_odd = swap_edges(kappa_even, kappa_odd)
    smooth_in, even, odd = call(
        functools.partial(edges_kernel, margin), [view, edge, edge], [VMEM] * chips, cost=cost(500)
    )(part, *parts)
    even, odd = swap_edges(even, odd)
    sums, sums_other = call(
        functools.partial(scatter_kernel, slots, blocks),
        [view2, view2],
        [AFTER] + [VMEM] * len(got),
        [
            pltpu.VMEM((2 * rows * 2 * padded_blocks(size), LANES), F32),
            pltpu.SMEM((8 * tiles, LANES), F32),
            pltpu.SemaphoreType.DMA((tiles,)),
        ],
        cost=cost(100000),
    )(smooth_in, *got)
    ring = pltpu.VMEM((total, size * LANES), F32)
    coef, sums_other = call(
        functools.partial(faces_kernel, margin),
        [jax.ShapeDtypeStruct((5, total, size * LANES), F32), view2],
        [VMEM] * 4 + [AFTER] * 2,
        [ring, ring],
        cost=cost(1000),
    )(kappa_even, kappa_odd, kappa, sums_other, even, odd)
    more_sums = swap(sums_other, "var", 1)
    (smooth,) = call(
        functools.partial(smooth_kernel, margin),
        [view],
        [VMEM] * 4,
        [ring],
        cost=cost(4000),
    )(smooth_in, even, odd, coef)
    adjoint, even, odd = call(
        functools.partial(adjoint_kernel, margin), [view, edge, edge], [VMEM] * 4, cost=cost(500)
    )(smooth, land_mask, sums, more_sums)
    even, odd = swap_edges(even, odd)
    (mine,) = call(
        functools.partial(spread_kernel, margin),
        [share],
        [VMEM] * 4,
        [ring],
        cost=cost(4000),
    )(adjoint, even, odd, coef)
    shares = [mine] + [swap(mine, "var", d) for d in range(1, members)]
    (out,) = call(
        result_kernel,
        [jax.ShapeDtypeStruct(control.shape, F32)],
        [VMEM] * (2 + members),
        cost=cost(1000),
    )(responses, control, *shares)
    return out


def solution(mesh):
    return jax.shard_map(
        local,
        mesh=mesh,
        in_specs=(
            P("var", ("grp", "tile"), None),
            P(None, ("grp", "tile"), None),
            P(("grp", "tile"), None),
            P(("grp", "tile"), None),
            P(("grp", "tile")),
            P(("grp", "tile"), None),
            P(("grp", "tile"), None),
            P(("grp", "tile"), None),
            P(("grp", "tile")),
            P(),
            P(),
        ),
        out_specs=P("var", ("grp", "tile"), None),
        check_vma=False,
    )
```

```python
import functools

import jax
import jax.numpy as jnp
from jax import lax
from jax.experimental import pallas as pl
from jax.experimental.pallas import tpu as pltpu
from jax.sharding import PartitionSpec as P

PASSES = 10
LANES = 128
GROUP = 16
VMEM = pl.BlockSpec(memory_space=pltpu.VMEM)
SMEM = pl.BlockSpec(memory_space=pltpu.SMEM)
HBM = pl.BlockSpec(memory_space=pltpu.HBM)
AFTER = pl.BlockSpec(memory_space=pl.ANY)
F32 = jnp.float32


def in_hbm(values):
    return pltpu.with_memory_space_constraint(values, pltpu.HBM)


def call(body, outs, ins, scratch=(), limit=16, cost=None):
    return pl.pallas_call(
        body,
        out_shape=outs,
        in_specs=ins,
        out_specs=[VMEM] * len(outs),
        scratch_shapes=list(scratch),
        compiler_params=pltpu.CompilerParams(vmem_limit_bytes=limit << 20),
        cost_estimate=cost,
    )


def cost(cycles):
    return pl.CostEstimate(flops=cycles * 4096, bytes_accessed=cycles * 1024, transcendentals=0)


def response(sens_ref, factor_ref, sensor, variable):
    total = sens_ref[sensor, 0] * factor_ref[0, variable]
    for u in range(1, factor_ref.shape[0]):
        total = total + sens_ref[sensor, u] * factor_ref[u, variable]
    return total


def fetch(pairs, sems):
    copies = [pltpu.make_async_copy(src, dst, sems.at[i]) for i, (src, dst) in enumerate(pairs)]
    for copy in copies:
        copy.start()
    return copies


def window_of(chip, chips, blocks):
    own = blocks // chips
    size = min(own + 2, own + chips - 1)
    return jnp.clip(chip * own - 1, 0, blocks - size), size


def my_chip():
    return lax.axis_index("var") // 2


def chip_count():
    return lax.axis_size("var") // 2


def lanes(start, size):
    return pl.ds(pl.multiple_of(start * LANES, LANES), size * LANES)


def first_kernel(slots, margin, sens_hbm, factor_hbm, control_hbm, kappa_hbm, tile_hbm, row_hbm, sensor_hbm,
                 value_hbm, weight_hbm, cols_hbm, own_ref, other_ref, response_ref, kappa_ref, even_ref,
                 odd_ref, *refs):
    chunk_refs = refs[:-11]
    (sens_ref, factor_ref, control_ref, tile_ref, row_ref, sensor_ref, value_ref, weight_ref, cols_ref,
     before_ref, sems) = refs[-11:]
    window = lanes(*window_of(my_chip(), chip_count(), own_ref.shape[1] // LANES))
    pairs = (
        (sens_hbm, sens_ref), (factor_hbm, factor_ref), (control_hbm, control_ref),
        (kappa_hbm.at[:, :, window], kappa_ref), (tile_hbm, tile_ref), (row_hbm, row_ref), (sensor_hbm, sensor_ref),
        (value_hbm, value_ref), (weight_hbm, weight_ref), (cols_hbm, cols_ref),
    )
    copies = [pltpu.make_async_copy(src, dst, sems.at[i]) for i, (src, dst) in enumerate(pairs)]
    for copy in copies:
        copy.start()
    from_panel = lax.broadcasted_iota(jnp.int32, before_ref.shape, 0)
    to_panel = lax.broadcasted_iota(jnp.int32, before_ref.shape, 1)
    before_ref[...] = jnp.where(from_panel < to_panel, 1.0, 0.0).astype(jnp.bfloat16)
    for copy in copies:
        copy.wait()

    member, mine = lax.axis_index("var"), lax.axis_index("tile")
    core = member % 2
    var_dev = control_ref.shape[0]
    for which, (sensor, out_ref) in enumerate(((core, own_ref), (1 - core, other_ref))):
        total = None
        for v in range(var_dev):
            scale = response(sens_ref, factor_ref, sensor, member * var_dev + v)
            response_ref[which, v] = jnp.full(response_ref.shape[2:], scale, F32)
            term = scale * control_ref[v]
            total = term if total is None else total + term
        out_ref[...] = total

    for i in range(2):
        pack_edges(even_ref.at[i], odd_ref.at[i], kappa_ref[i], margin)

    tiles = lax.axis_size("tile")
    full = tiles // 2 - 1
    first = jnp.where(core == 0, 1, tiles // 2)
    panels = value_ref.shape[0]
    source = tile_ref[...] ^ mine
    names = lax.broadcasted_iota(jnp.int32, (-(-tiles // 8) * 8, panels), 0)
    hits = jnp.where(names == source, 1.0, 0.0)
    ranks = jnp.dot(hits.astype(jnp.bfloat16), before_ref[...], preferred_element_type=F32)
    rank = jnp.sum(hits * ranks, axis=0, keepdims=True).astype(jnp.int32)
    parity, slot = rank % 2, rank // 2
    whole = (source >= first) & (source < first + full)
    home = source == 0
    keep = whole | ((home | (source == tiles - 1)) & (parity == core))
    half = jnp.where(whole, 2 * (source - first) + parity, jnp.where(home, tiles - 1, tiles - 2))
    place = jnp.where(keep, half * slots + slot, -1)
    spots = lax.broadcasted_iota(jnp.int32, (tiles * slots, panels), 0)
    pick = jnp.where(spots == place, 1.0, 0.0).astype(jnp.bfloat16)

    def picked(parts):
        total = None
        for part in parts:
            term = jnp.dot(pick, part.astype(jnp.bfloat16), preferred_element_type=F32)
            total = term if total is None else total + term
        return total

    cols = cols_ref[...]
    sent = (
        picked(thirds(value_ref[...])),
        picked(thirds(weight_ref[...])),
        picked(((cols // LANES * LANES).astype(F32), (cols % LANES).astype(F32))),
    )
    sub = lax.broadcasted_iota(jnp.int32, (8, panels), 0)
    lane = lax.broadcasted_iota(jnp.int32, (8, panels), 1)
    facts = jnp.where(sub == 0, row_ref[...], jnp.where(sub == 1, sensor_ref[...], 0)).astype(F32)
    meta = lax.dot_general(
        facts.astype(jnp.bfloat16), pick, (((1,), (1,)), ((), ())), preferred_element_type=F32
    )
    for i in range(tiles):
        held = jnp.sum(jnp.where(keep & (half == i), 1.0, 0.0), axis=1, keepdims=True)
        meta = jnp.where((sub == 2) & (lane == i), held, meta)
    for i in range(tiles):
        out_ref = chunk_refs[i // 2].at[i % 2] if i < 2 * full else chunk_refs[i - full]
        for part, rows in enumerate(sent):
            out_ref[part * slots : (part + 1) * slots] = rows[i * slots : (i + 1) * slots]
        out_ref[3 * slots :] = meta


def thirds(values):
    top = values.astype(jnp.bfloat16).astype(F32)
    rest = values - top
    middle = rest.astype(jnp.bfloat16).astype(F32)
    return top, middle, rest - middle


def pieces(values):
    top = values.astype(jnp.bfloat16).astype(F32)
    return top, values - top


def scatter_kernel(slots, blocks_all, after_ref, *refs):
    got_refs, (own_ref, other_ref, acc_ref, meta_ref, sems) = refs[:-5], refs[-5:]
    core = lax.axis_index("var") % 2
    got_refs = [r.at[i] for r in got_refs[:-2] for i in (0, 1)] + list(got_refs[-2:])
    size_of_group = min(GROUP, slots)
    copies = [
        pltpu.make_async_copy(ref.at[pl.ds(3 * slots, 8)], meta_ref.at[pl.ds(8 * s, 8)], sems.at[s])
        for s, ref in enumerate(got_refs)
    ]
    for copy in copies:
        copy.start()
    rows = own_ref.shape[1]
    start, size = window_of(my_chip(), chip_count(), blocks_all)
    per_kind = padded_blocks(size)
    tall = 2 * per_kind
    acc_ref[...] = jnp.zeros(acc_ref.shape, F32)
    place = lax.broadcasted_iota(jnp.int32, (tall, LANES), 0)
    is_weight = place < per_kind
    place = jnp.where(is_weight, place, place - per_kind) + start
    lane_ids = lax.broadcasted_iota(jnp.int32, (LANES, LANES), 0).astype(F32).astype(jnp.bfloat16)
    one, zero = jnp.bfloat16(1), jnp.bfloat16(0)
    sub = lax.broadcasted_iota(jnp.int32, (size_of_group, LANES), 0)
    blank = jnp.zeros((2 * tall, LANES), jnp.bfloat16)
    for copy in copies:
        copy.wait()

    def load(s, base):
        got_ref = got_refs[s]
        count = meta_ref[8 * s + 2, s].astype(jnp.int32)
        value = got_ref[pl.ds(base, size_of_group), :]
        weight = got_ref[pl.ds(slots + base, size_of_group), :]
        cell = got_ref[pl.ds(2 * slots + base, size_of_group), :].astype(jnp.int32)
        weight = jnp.where(sub + base < count, weight, 0.0)
        return pieces(weight), pieces(weight * value), (cell % LANES).astype(F32), cell // LANES

    def one_hots(loaded, i):
        weights, values, low, high = loaded
        here = place == high[i : i + 1]
        rows_of = [
            jnp.where(here, jnp.where(is_weight, w[i : i + 1], v[i : i + 1]), 0.0)
            for w, v in zip(weights, values)
        ]
        left = jnp.concatenate(rows_of, axis=0).astype(jnp.bfloat16)
        column = jnp.broadcast_to(low[i : i + 1], (16, LANES)).astype(jnp.bfloat16)
        column = jnp.concatenate([column] * (LANES // 16), axis=0)
        return left, jnp.where(lane_ids == column, one, zero)

    def pair(s, g, carry):
        base = pl.multiple_of(g * size_of_group, size_of_group)
        loaded = [load(s + i, base) for i in (0, 1)]
        for k in range(size_of_group):
            hots = [one_hots(loaded[i], k) for i in (0, 1)]
            left = jnp.concatenate(
                [
                    jnp.concatenate([hots[0][0], blank], axis=1),
                    jnp.concatenate([blank, hots[1][0]], axis=1),
                ],
                axis=0,
            )
            both = lax.dot_general(
                left, jnp.concatenate([hots[0][1], hots[1][1]], axis=1), (((1,), (1,)), ((), ())),
                preferred_element_type=F32,
            )
            for i in (0, 1):
                row = meta_ref[8 * (s + i), (s + i) * slots + base + k].astype(jnp.int32)
                sensor = meta_ref[8 * (s + i) + 1, (s + i) * slots + base + k].astype(jnp.int32)
                at = pl.multiple_of((sensor * rows + row) * tall, 8)
                mine = both[2 * i * tall : 2 * (i + 1) * tall]
                acc_ref[pl.ds(at, tall), :] += mine[:tall] + mine[tall:]
        return carry

    for s in range(0, len(got_refs), 2):
        most = jnp.maximum(meta_ref[8 * s + 2, s], meta_ref[8 * s + 10, s + 1]).astype(jnp.int32)
        lax.fori_loop(0, (most + size_of_group - 1) // size_of_group, functools.partial(pair, s), 0)
    for sensor, out_ref in ((core, own_ref), (1 - core, other_ref)):
        begin = sensor * rows * tall
        for kind in range(2):
            for b in range(size):
                out_ref[kind, :, b * LANES : (b + 1) * LANES] = acc_ref[
                    pl.ds(begin + kind * per_kind + b, rows, stride=tall), :
                ]


def padded_blocks(size):
    return -(-size // 4) * 4


def even_tile():
    return lax.axis_index("tile") % 2 == 0


def has_above():
    return lax.axis_index("tile") > 0


def has_below():
    return lax.axis_index("tile") + 1 < lax.axis_size("tile")


def pack_edges(even_ref, odd_ref, rows_value, margin):
    rows, width = rows_value.shape
    even = even_tile()
    for b in range(width // LANES):
        at = slice(b * LANES, (b + 1) * LANES)
        head, tail = rows_value[:margin, at], rows_value[rows - margin :, at]
        even_ref[b * margin : (b + 1) * margin] = jnp.where(even, tail, head)
        odd_ref[b * margin : (b + 1) * margin] = jnp.where(even, head, tail)


def cut_kernel(first_ref, second_ref, mine_ref, *out_refs):
    chip, chips, blocks = my_chip(), chip_count(), first_ref.shape[1] // LANES
    for d, out_ref in enumerate((mine_ref, *out_refs)):
        window = lanes(*window_of(chip ^ d, chips, blocks))
        out_ref[...] = first_ref[:, window] + second_ref[:, window]


def edges_kernel(margin, *refs):
    terms, (total_ref, even_ref, odd_ref) = refs[:-3], refs[-3:]
    total = terms[0][...]
    for term in terms[1:]:
        total = total + term[...]
    total_ref[...] = total
    pack_edges(even_ref, odd_ref, total, margin)


def ring_rows(rows, margin):
    return -(-(rows + 2 * margin) // 8) * 8


def lay_ring(ref, own, from_even, from_odd, margin):
    rows, total = own.shape[0], ref.shape[0]
    even = even_tile()
    ref[rows:total] = jnp.zeros((total - rows, ref.shape[1]), F32)
    ref[:rows] = own
    for b in range(ref.shape[1] // LANES):
        at = slice(b * LANES, (b + 1) * LANES)
        one, two = (m[b * margin : (b + 1) * margin] for m in (from_even, from_odd))
        ref[rows : rows + margin, at] = jnp.where(has_below(), jnp.where(even, one, two), 0.0)
        ref[total - margin :, at] = jnp.where(has_above(), jnp.where(even, two, one), 0.0)


def block(ref, j):
    return ref[:, j * LANES : (j + 1) * LANES]


def sideways(blocks):
    shape = blocks[0].shape
    lane = lax.broadcasted_iota(jnp.int32, shape, 1)
    zero = jnp.zeros(shape, F32)
    ahead = [pltpu.roll(x, 1, 1) for x in blocks]
    back = [pltpu.roll(x, LANES - 1, 1) for x in blocks]
    for j, here in enumerate(blocks):
        before = ahead[j - 1] if j else zero
        after = back[j + 1] if j + 1 < len(blocks) else zero
        yield here, jnp.where(lane == 0, before, ahead[j]), jnp.where(lane == LANES - 1, after, back[j])


def face_weights(coef_ref, row_ref, col_ref, rows, margin):
    total, width = row_ref.shape
    blocks = width // LANES
    r = lax.broadcasted_iota(jnp.int32, (total, LANES), 0)
    inside = (
        (r < rows)
        | ((r < rows + margin) & has_below())
        | ((r >= total - margin) & has_above())
    )
    scale = jnp.where(inside, 0.125, 0.0)
    unit = jnp.where(inside, 1.0, 0.0)
    columns = [block(col_ref, j) for j in range(blocks)]
    for j, (k_col, k_left, k_right) in enumerate(sideways(columns)):
        at = slice(j * LANES, (j + 1) * LANES)
        k_row = block(row_ref, j)
        up = scale * (k_row + pltpu.roll(k_row, 1, 0))
        down = scale * (k_row + pltpu.roll(k_row, total - 1, 0))
        left = scale * (k_col + k_left)
        right = scale * (k_col + k_right)
        coef_ref[0, :, at] = unit - up - down - left - right
        coef_ref[1, :, at] = up
        coef_ref[2, :, at] = down
        coef_ref[3, :, at] = left
        coef_ref[4, :, at] = right


def one_pass(fields, coef_ref, spans):
    def weights(i, at):
        got = [coef_ref[i, span, at] for span in spans]
        return jnp.concatenate(got, axis=0) if len(got) > 1 else got[0]

    total = fields[0].shape[0]
    out = []
    for j, (here, left, right) in enumerate(sideways(fields)):
        at = slice(j * LANES, (j + 1) * LANES)
        out.append(
            weights(0, at) * here
            + weights(1, at) * pltpu.roll(here, 1, 0)
            + weights(2, at) * pltpu.roll(here, total - 1, 0)
            + weights(3, at) * left
            + weights(4, at) * right
        )
    return out


def diffuse(ring_ref, coef_ref, rows, margin):
    total, width = ring_ref.shape
    inner = margin // 8 * 8
    wide = [slice(0, total)]
    narrow = [slice(0, rows + inner), slice(total - inner, total)]
    fields = [block(ring_ref, j) for j in range(width // LANES)]
    for _ in range(margin - inner):
        fields = one_pass(fields, coef_ref, wide)
    fields = [jnp.concatenate([f[span] for span in narrow], axis=0) for f in fields]
    for _ in range(inner):
        fields = one_pass(fields, coef_ref, narrow)
    return [f[:rows] for f in fields]


def faces_kernel(margin, even_ref, odd_ref, kappa_ref, sums_ref, *refs):
    coef_ref, sums_out, one_ref, two_ref = refs[-4:]
    sums_out[...] = sums_ref[...]
    rows = kappa_ref.shape[1]
    lay_ring(one_ref, kappa_ref[0], even_ref.at[0], odd_ref.at[0], margin)
    lay_ring(two_ref, kappa_ref[1], even_ref.at[1], odd_ref.at[1], margin)
    face_weights(coef_ref, one_ref, two_ref, rows, margin)


def smooth_kernel(margin, own_ref, even_ref, odd_ref, coef_ref, out_ref, ring_ref):
    rows = own_ref.shape[0]
    lay_ring(ring_ref, own_ref[...], even_ref, odd_ref, margin)
    for j, field in enumerate(diffuse(ring_ref, coef_ref, rows, margin)):
        out_ref[:, j * LANES : (j + 1) * LANES] = field


def adjoint_kernel(margin, smooth_ref, mask_ref, sums_ref, more_ref, adjoint_ref, even_ref, odd_ref):
    weight = sums_ref[0] + more_ref[0]
    value = sums_ref[1] + more_ref[1]
    window = lanes(*window_of(my_chip(), chip_count(), mask_ref.shape[1] // LANES))
    adjoint = mask_ref[:, window].astype(F32) * (weight * smooth_ref[...] - value)
    adjoint_ref[...] = adjoint
    pack_edges(even_ref, odd_ref, adjoint, margin)


def spread_kernel(margin, own_ref, even_ref, odd_ref, coef_ref, out_ref, ring_ref):
    rows = own_ref.shape[0]
    lay_ring(ring_ref, own_ref[...], even_ref, odd_ref, margin)
    for j, field in enumerate(diffuse(ring_ref, coef_ref, rows, margin)):
        ring_ref[:rows, j * LANES : (j + 1) * LANES] = field
    own = out_ref.shape[1] // LANES
    start = window_of(my_chip(), chip_count(), own * chip_count())[0]
    out_ref[...] = ring_ref[:rows, lanes(my_chip() * own - start, own)]


def result_kernel(response_ref, control_ref, *refs):
    own, out_ref = refs[0].shape[1] // LANES, refs[-1]
    for d in range(len(refs) // 2):
        window = lanes((my_chip() ^ d) * own, own)
        for v in range(control_ref.shape[0]):
            mine, theirs = (response_ref[i, v][:1, :1] for i in range(2))
            out_ref[v, :, window] = (
                control_ref[v, :, window] + mine * refs[2 * d][...] + theirs * refs[2 * d + 1][...]
            )


def swap(values, axis, bit):
    count = lax.axis_size(axis)
    return lax.ppermute(values, axis, [(i, i ^ bit) for i in range(count)])


def swap_edges(even, odd):
    tiles, members = lax.axis_size("tile"), lax.axis_size("var")
    pairs = []
    for t in range(tiles):
        other = t + 1 if t % 2 else t - 1
        for q in range(members):
            to = other * members + q if 0 <= other < tiles else t * members + (q ^ 1)
            pairs.append((t * members + q, to))
    return swap(even, "tile", 1), lax.ppermute(odd, ("tile", "var"), pairs)


def deliver(chunks):
    tiles, members = lax.axis_size("tile"), lax.axis_size("var")
    got = []
    for turn, chunk in enumerate(chunks[:-1]):
        pairs = []
        for t in range(tiles):
            for q in range(members):
                offset = tiles - 1 if turn == len(chunks) - 2 else 1 + turn + (q % 2) * (tiles // 2 - 1)
                pairs.append((t * members + q, (t ^ offset) * members + q))
        got.append(lax.ppermute(chunk, ("tile", "var"), pairs))
    return got + [chunks[-1]]


def local(control, diffusivity, land_mask, panel_tile, panel_row, panel_cols, obs_values,
          obs_weights, panel_sensor, sensitivity, cross_factor):
    rows, width = control.shape[1:]
    var_dev = control.shape[0]
    tiles, members = lax.axis_size("tile"), lax.axis_size("var")
    panels, panel_width = panel_cols.shape
    slots = panels // tiles
    blocks = width // LANES
    margin = PASSES
    total = ring_rows(rows, margin)
    chips = members // 2
    size = window_of(0, chips, blocks)[1]
    field = jax.ShapeDtypeStruct((rows, width), F32)
    share = jax.ShapeDtypeStruct((rows, width // chips), F32)
    view = jax.ShapeDtypeStruct((rows, size * LANES), F32)
    view2 = jax.ShapeDtypeStruct((2, *view.shape), F32)
    edge = jax.ShapeDtypeStruct((margin * size, LANES), F32)
    edge2 = jax.ShapeDtypeStruct((2, *edge.shape), F32)
    half = jax.ShapeDtypeStruct((3 * slots + 8, panel_width), F32)
    chunks = [jax.ShapeDtypeStruct((2, *half.shape), F32)] * (tiles // 2 - 1) + [half] * 2
    line = pltpu.VMEM((1, panels), jnp.int32)

    own, other, responses, kappa, kappa_even, kappa_odd, *chunks = call(
        functools.partial(first_kernel, slots, margin),
        [field, field, jax.ShapeDtypeStruct((2, var_dev, 8, LANES), F32), view2, edge2, edge2]
        + chunks,
        [HBM] * 10,
        [
            pltpu.SMEM(sensitivity.shape, F32),
            pltpu.SMEM(cross_factor.shape, F32),
            pltpu.VMEM(control.shape, F32),
            line, line, line,
            pltpu.VMEM(obs_values.shape, F32),
            pltpu.VMEM(obs_weights.shape, F32),
            pltpu.VMEM(panel_cols.shape, jnp.int32),
            pltpu.VMEM((panels, panels), jnp.bfloat16),
            pltpu.SemaphoreType.DMA((10,)),
        ],
        cost=cost(3000),
    )(*(in_hbm(x) for x in (sensitivity, cross_factor, control, diffusivity, panel_tile.reshape(1, -1),
                            panel_row.reshape(1, -1), panel_sensor.reshape(1, -1), obs_values,
                            obs_weights, panel_cols)))

    got = deliver(chunks)
    part, *parts = call(cut_kernel, [view] * chips, [VMEM] * 2, cost=cost(200))(
        own, swap(other, "var", 1)
    )
    parts = [swap(p, "var", 2 * (d + 1)) for d, p in enumerate(parts)]
    kappa_even, kappa_odd = swap_edges(kappa_even, kappa_odd)
    smooth_in, even, odd = call(
        functools.partial(edges_kernel, margin), [view, edge, edge], [VMEM] * chips, cost=cost(500)
    )(part, *parts)
    even, odd = swap_edges(even, odd)
    sums, sums_other = call(
        functools.partial(scatter_kernel, slots, blocks),
        [view2, view2],
        [AFTER] + [VMEM] * len(got),
        [
            pltpu.VMEM((2 * rows * 2 * padded_blocks(size), LANES), F32),
            pltpu.SMEM((8 * tiles, LANES), F32),
            pltpu.SemaphoreType.DMA((tiles,)),
        ],
        cost=cost(100000),
    )(smooth_in, *got)
    ring = pltpu.VMEM((total, size * LANES), F32)
    coef, sums_other = call(
        functools.partial(faces_kernel, margin),
        [jax.ShapeDtypeStruct((5, total, size * LANES), F32), view2],
        [VMEM] * 4 + [AFTER] * 2,
        [ring, ring],
        cost=cost(1000),
    )(kappa_even, kappa_odd, kappa, sums_other, even, odd)
    more_sums = swap(sums_other, "var", 1)
    (smooth,) = call(
        functools.partial(smooth_kernel, margin),
        [view],
        [VMEM] * 4,
        [ring],
        cost=cost(4000),
    )(smooth_in, even, odd, coef)
    adjoint, even, odd = call(
        functools.partial(adjoint_kernel, margin), [view, edge, edge], [VMEM] * 4, cost=cost(500)
    )(smooth, land_mask, sums, more_sums)
    even, odd = swap_edges(even, odd)
    (mine,) = call(
        functools.partial(spread_kernel, margin),
        [share],
        [VMEM] * 4,
        [ring],
        cost=cost(4000),
    )(adjoint, even, odd, coef)
    shares = [mine] + [swap(mine, "var", d) for d in range(1, members)]
    (out,) = call(
        result_kernel,
        [jax.ShapeDtypeStruct(control.shape, F32)],
        [VMEM] * (2 + members),
        cost=cost(1000),
    )(responses, control, *shares)
    return out


def solution(mesh):
    return jax.shard_map(
        local,
        mesh=mesh,
        in_specs=(
            P("var", ("grp", "tile"), None),
            P(None, ("grp", "tile"), None),
            P(("grp", "tile"), None),
            P(("grp", "tile"), None),
            P(("grp", "tile")),
            P(("grp", "tile"), None),
            P(("grp", "tile"), None),
            P(("grp", "tile"), None),
            P(("grp", "tile")),
            P(),
            P(),
        ),
        out_specs=P("var", ("grp", "tile"), None),
        check_vma=False,
    )
```

```python
import functools

import jax
import jax.numpy as jnp
from jax import lax
from jax.experimental import pallas as pl
from jax.experimental.pallas import tpu as pltpu
from jax.sharding import PartitionSpec as P

PASSES = 10
LANES = 128
GROUP = 16
VMEM = pl.BlockSpec(memory_space=pltpu.VMEM)
SMEM = pl.BlockSpec(memory_space=pltpu.SMEM)
HBM = pl.BlockSpec(memory_space=pltpu.HBM)
AFTER = pl.BlockSpec(memory_space=pl.ANY)
F32 = jnp.float32


def in_hbm(values):
    return pltpu.with_memory_space_constraint(values, pltpu.HBM)


def call(body, outs, ins, scratch=(), limit=16, cost=None):
    return pl.pallas_call(
        body,
        out_shape=outs,
        in_specs=ins,
        out_specs=[VMEM] * len(outs),
        scratch_shapes=list(scratch),
        compiler_params=pltpu.CompilerParams(vmem_limit_bytes=limit << 20),
        cost_estimate=cost,
    )


def cost(cycles):
    return pl.CostEstimate(flops=cycles * 4096, bytes_accessed=cycles * 1024, transcendentals=0)


def response(sens_ref, factor_ref, sensor, variable):
    total = sens_ref[sensor, 0] * factor_ref[0, variable]
    for u in range(1, factor_ref.shape[0]):
        total = total + sens_ref[sensor, u] * factor_ref[u, variable]
    return total


def fetch(pairs, sems):
    copies = [pltpu.make_async_copy(src, dst, sems.at[i]) for i, (src, dst) in enumerate(pairs)]
    for copy in copies:
        copy.start()
    return copies


def window_of(chip, chips, blocks):
    own = blocks // chips
    size = min(own + 2, own + chips - 1)
    return jnp.clip(chip * own - 1, 0, blocks - size), size


def my_chip():
    return lax.axis_index("var") // 2


def chip_count():
    return lax.axis_size("var") // 2


def lanes(start, size):
    return pl.ds(pl.multiple_of(start * LANES, LANES), size * LANES)


def first_kernel(slots, margin, sens_hbm, factor_hbm, control_hbm, kappa_hbm, tile_hbm, row_hbm, sensor_hbm,
                 value_hbm, weight_hbm, cols_hbm, own_ref, other_ref, response_ref, kappa_ref, even_ref,
                 odd_ref, *refs):
    chunk_refs = refs[:-11]
    (sens_ref, factor_ref, control_ref, tile_ref, row_ref, sensor_ref, value_ref, weight_ref, cols_ref,
     before_ref, sems) = refs[-11:]
    window = lanes(*window_of(my_chip(), chip_count(), own_ref.shape[1] // LANES))
    pairs = (
        (sens_hbm, sens_ref), (factor_hbm, factor_ref), (control_hbm, control_ref),
        (kappa_hbm.at[:, :, window], kappa_ref), (tile_hbm, tile_ref), (row_hbm, row_ref), (sensor_hbm, sensor_ref),
        (value_hbm, value_ref), (weight_hbm, weight_ref), (cols_hbm, cols_ref),
    )
    copies = [pltpu.make_async_copy(src, dst, sems.at[i]) for i, (src, dst) in enumerate(pairs)]
    for copy in copies:
        copy.start()
    from_panel = lax.broadcasted_iota(jnp.int32, before_ref.shape, 0)
    to_panel = lax.broadcasted_iota(jnp.int32, before_ref.shape, 1)
    before_ref[...] = jnp.where(from_panel < to_panel, 1.0, 0.0).astype(jnp.bfloat16)
    for copy in copies:
        copy.wait()

    member, mine = lax.axis_index("var"), lax.axis_index("tile")
    core = member % 2
    var_dev = control_ref.shape[0]
    for which, (sensor, out_ref) in enumerate(((core, own_ref), (1 - core, other_ref))):
        total = None
        for v in range(var_dev):
            scale = response(sens_ref, factor_ref, sensor, member * var_dev + v)
            response_ref[which, v] = jnp.full(response_ref.shape[2:], scale, F32)
            term = scale * control_ref[v]
            total = term if total is None else total + term
        out_ref[...] = total

    for i in range(2):
        pack_edges(even_ref.at[i], odd_ref.at[i], kappa_ref[i], margin)

    tiles = lax.axis_size("tile")
    full = tiles // 2 - 1
    first = jnp.where(core == 0, 1, tiles // 2 + 1)
    panels = value_ref.shape[0]
    source = tile_ref[...] ^ mine
    names = lax.broadcasted_iota(jnp.int32, (-(-tiles // 8) * 8, panels), 0)
    hits = jnp.where(names == source, 1.0, 0.0)
    ranks = jnp.dot(hits.astype(jnp.bfloat16), before_ref[...], preferred_element_type=F32)
    rank = jnp.sum(hits * ranks, axis=0, keepdims=True).astype(jnp.int32)
    parity, slot = rank % 2, rank // 2
    whole = (source >= first) & (source < first + full)
    home = source == 0
    keep = whole | ((home | (source == tiles // 2)) & (parity == core))
    half = jnp.where(whole, 2 * (source - first) + parity, jnp.where(home, tiles - 1, tiles - 2))
    place = jnp.where(keep, half * slots + slot, -1)
    spots = lax.broadcasted_iota(jnp.int32, (tiles * slots, panels), 0)
    pick = jnp.where(spots == place, 1.0, 0.0).astype(jnp.bfloat16)

    def picked(parts):
        total = None
        for part in parts:
            term = jnp.dot(pick, part.astype(jnp.bfloat16), preferred_element_type=F32)
            total = term if total is None else total + term
        return total

    cols = cols_ref[...]
    sent = (
        picked(thirds(value_ref[...])),
        picked(thirds(weight_ref[...])),
        picked(((cols // LANES * LANES).astype(F32), (cols % LANES).astype(F32))),
    )
    sub = lax.broadcasted_iota(jnp.int32, (8, panels), 0)
    lane = lax.broadcasted_iota(jnp.int32, (8, panels), 1)
    facts = jnp.where(sub == 0, row_ref[...], jnp.where(sub == 1, sensor_ref[...], 0)).astype(F32)
    meta = lax.dot_general(
        facts.astype(jnp.bfloat16), pick, (((1,), (1,)), ((), ())), preferred_element_type=F32
    )
    for i in range(tiles):
        held = jnp.sum(jnp.where(keep & (half == i), 1.0, 0.0), axis=1, keepdims=True)
        meta = jnp.where((sub == 2) & (lane == i), held, meta)
    for i in range(tiles):
        out_ref = chunk_refs[i // 2].at[i % 2] if i < 2 * full else chunk_refs[i - full]
        for part, rows in enumerate(sent):
            out_ref[part * slots : (part + 1) * slots] = rows[i * slots : (i + 1) * slots]
        out_ref[3 * slots :] = meta


def thirds(values):
    top = values.astype(jnp.bfloat16).astype(F32)
    rest = values - top
    middle = rest.astype(jnp.bfloat16).astype(F32)
    return top, middle, rest - middle


def pieces(values):
    top = values.astype(jnp.bfloat16).astype(F32)
    return top, values - top


def scatter_kernel(slots, blocks_all, after_ref, *refs):
    got_refs, (own_ref, other_ref, acc_ref, meta_ref, sems) = refs[:-5], refs[-5:]
    core = lax.axis_index("var") % 2
    got_refs = [r.at[i] for r in got_refs[:-2] for i in (0, 1)] + list(got_refs[-2:])
    size_of_group = min(GROUP, slots)
    copies = [
        pltpu.make_async_copy(ref.at[pl.ds(3 * slots, 8)], meta_ref.at[pl.ds(8 * s, 8)], sems.at[s])
        for s, ref in enumerate(got_refs)
    ]
    for copy in copies:
        copy.start()
    rows = own_ref.shape[1]
    start, size = window_of(my_chip(), chip_count(), blocks_all)
    per_kind = padded_blocks(size)
    tall = 2 * per_kind
    acc_ref[...] = jnp.zeros(acc_ref.shape, F32)
    place = lax.broadcasted_iota(jnp.int32, (tall, LANES), 0)
    is_weight = place < per_kind
    place = jnp.where(is_weight, place, place - per_kind) + start
    lane_ids = lax.broadcasted_iota(jnp.int32, (LANES, LANES), 0).astype(F32).astype(jnp.bfloat16)
    one, zero = jnp.bfloat16(1), jnp.bfloat16(0)
    sub = lax.broadcasted_iota(jnp.int32, (size_of_group, LANES), 0)
    blank = jnp.zeros((2 * tall, LANES), jnp.bfloat16)
    for copy in copies:
        copy.wait()

    def load(s, base):
        got_ref = got_refs[s]
        count = meta_ref[8 * s + 2, s].astype(jnp.int32)
        value = got_ref[pl.ds(base, size_of_group), :]
        weight = got_ref[pl.ds(slots + base, size_of_group), :]
        cell = got_ref[pl.ds(2 * slots + base, size_of_group), :].astype(jnp.int32)
        weight = jnp.where(sub + base < count, weight, 0.0)
        return pieces(weight), pieces(weight * value), (cell % LANES).astype(F32), cell // LANES

    def one_hots(loaded, i):
        weights, values, low, high = loaded
        here = place == high[i : i + 1]
        rows_of = [
            jnp.where(here, jnp.where(is_weight, w[i : i + 1], v[i : i + 1]), 0.0)
            for w, v in zip(weights, values)
        ]
        left = jnp.concatenate(rows_of, axis=0).astype(jnp.bfloat16)
        column = jnp.broadcast_to(low[i : i + 1], (16, LANES)).astype(jnp.bfloat16)
        column = jnp.concatenate([column] * (LANES // 16), axis=0)
        return left, jnp.where(lane_ids == column, one, zero)

    def pair(s, g, carry):
        base = pl.multiple_of(g * size_of_group, size_of_group)
        loaded = [load(s + i, base) for i in (0, 1)]
        for k in range(size_of_group):
            hots = [one_hots(loaded[i], k) for i in (0, 1)]
            left = jnp.concatenate(
                [
                    jnp.concatenate([hots[0][0], blank], axis=1),
                    jnp.concatenate([blank, hots[1][0]], axis=1),
                ],
                axis=0,
            )
            both = lax.dot_general(
                left, jnp.concatenate([hots[0][1], hots[1][1]], axis=1), (((1,), (1,)), ((), ())),
                preferred_element_type=F32,
            )
            for i in (0, 1):
                row = meta_ref[8 * (s + i), (s + i) * slots + base + k].astype(jnp.int32)
                sensor = meta_ref[8 * (s + i) + 1, (s + i) * slots + base + k].astype(jnp.int32)
                at = pl.multiple_of((sensor * rows + row) * tall, 8)
                mine = both[2 * i * tall : 2 * (i + 1) * tall]
                acc_ref[pl.ds(at, tall), :] += mine[:tall] + mine[tall:]
        return carry

    for s in range(0, len(got_refs), 2):
        most = jnp.maximum(meta_ref[8 * s + 2, s], meta_ref[8 * s + 10, s + 1]).astype(jnp.int32)
        lax.fori_loop(0, (most + size_of_group - 1) // size_of_group, functools.partial(pair, s), 0)
    for sensor, out_ref in ((core, own_ref), (1 - core, other_ref)):
        begin = sensor * rows * tall
        for kind in range(2):
            for b in range(size):
                out_ref[kind, :, b * LANES : (b + 1) * LANES] = acc_ref[
                    pl.ds(begin + kind * per_kind + b, rows, stride=tall), :
                ]


def padded_blocks(size):
    return -(-size // 4) * 4


def even_tile():
    return lax.axis_index("tile") % 2 == 0


def has_above():
    return lax.axis_index("tile") > 0


def has_below():
    return lax.axis_index("tile") + 1 < lax.axis_size("tile")


def pack_edges(even_ref, odd_ref, rows_value, margin):
    rows, width = rows_value.shape
    even = even_tile()
    for b in range(width // LANES):
        at = slice(b * LANES, (b + 1) * LANES)
        head, tail = rows_value[:margin, at], rows_value[rows - margin :, at]
        even_ref[b * margin : (b + 1) * margin] = jnp.where(even, tail, head)
        odd_ref[b * margin : (b + 1) * margin] = jnp.where(even, head, tail)


def cut_kernel(first_ref, second_ref, mine_ref, *out_refs):
    chip, chips, blocks = my_chip(), chip_count(), first_ref.shape[1] // LANES
    for d, out_ref in enumerate((mine_ref, *out_refs)):
        window = lanes(*window_of(chip ^ d, chips, blocks))
        out_ref[...] = first_ref[:, window] + second_ref[:, window]


def edges_kernel(margin, *refs):
    terms, (total_ref, even_ref, odd_ref) = refs[:-3], refs[-3:]
    total = terms[0][...]
    for term in terms[1:]:
        total = total + term[...]
    total_ref[...] = total
    pack_edges(even_ref, odd_ref, total, margin)


def ring_rows(rows, margin):
    return -(-(rows + 2 * margin) // 8) * 8


def lay_ring(ref, own, from_even, from_odd, margin):
    rows, total = own.shape[0], ref.shape[0]
    even = even_tile()
    ref[rows:total] = jnp.zeros((total - rows, ref.shape[1]), F32)
    ref[:rows] = own
    for b in range(ref.shape[1] // LANES):
        at = slice(b * LANES, (b + 1) * LANES)
        one, two = (m[b * margin : (b + 1) * margin] for m in (from_even, from_odd))
        ref[rows : rows + margin, at] = jnp.where(has_below(), jnp.where(even, one, two), 0.0)
        ref[total - margin :, at] = jnp.where(has_above(), jnp.where(even, two, one), 0.0)


def block(ref, j):
    return ref[:, j * LANES : (j + 1) * LANES]


def sideways(blocks):
    shape = blocks[0].shape
    lane = lax.broadcasted_iota(jnp.int32, shape, 1)
    zero = jnp.zeros(shape, F32)
    ahead = [pltpu.roll(x, 1, 1) for x in blocks]
    back = [pltpu.roll(x, LANES - 1, 1) for x in blocks]
    for j, here in enumerate(blocks):
        before = ahead[j - 1] if j else zero
        after = back[j + 1] if j + 1 < len(blocks) else zero
        yield here, jnp.where(lane == 0, before, ahead[j]), jnp.where(lane == LANES - 1, after, back[j])


def face_weights(coef_ref, row_ref, col_ref, rows, margin):
    total, width = row_ref.shape
    blocks = width // LANES
    r = lax.broadcasted_iota(jnp.int32, (total, LANES), 0)
    inside = (
        (r < rows)
        | ((r < rows + margin) & has_below())
        | ((r >= total - margin) & has_above())
    )
    scale = jnp.where(inside, 0.125, 0.0)
    unit = jnp.where(inside, 1.0, 0.0)
    columns = [block(col_ref, j) for j in range(blocks)]
    for j, (k_col, k_left, k_right) in enumerate(sideways(columns)):
        at = slice(j * LANES, (j + 1) * LANES)
        k_row = block(row_ref, j)
        up = scale * (k_row + pltpu.roll(k_row, 1, 0))
        down = scale * (k_row + pltpu.roll(k_row, total - 1, 0))
        left = scale * (k_col + k_left)
        right = scale * (k_col + k_right)
        coef_ref[0, :, at] = unit - up - down - left - right
        coef_ref[1, :, at] = up
        coef_ref[2, :, at] = down
        coef_ref[3, :, at] = left
        coef_ref[4, :, at] = right


def one_pass(fields, coef_ref, spans):
    def weights(i, at):
        got = [coef_ref[i, span, at] for span in spans]
        return jnp.concatenate(got, axis=0) if len(got) > 1 else got[0]

    total = fields[0].shape[0]
    out = []
    for j, (here, left, right) in enumerate(sideways(fields)):
        at = slice(j * LANES, (j + 1) * LANES)
        out.append(
            weights(0, at) * here
            + weights(1, at) * pltpu.roll(here, 1, 0)
            + weights(2, at) * pltpu.roll(here, total - 1, 0)
            + weights(3, at) * left
            + weights(4, at) * right
        )
    return out


def diffuse(ring_ref, coef_ref, rows, margin):
    total, width = ring_ref.shape
    inner = margin // 8 * 8
    wide = [slice(0, total)]
    narrow = [slice(0, rows + inner), slice(total - inner, total)]
    fields = [block(ring_ref, j) for j in range(width // LANES)]
    for _ in range(margin - inner):
        fields = one_pass(fields, coef_ref, wide)
    fields = [jnp.concatenate([f[span] for span in narrow], axis=0) for f in fields]
    for _ in range(inner):
        fields = one_pass(fields, coef_ref, narrow)
    return [f[:rows] for f in fields]


def faces_kernel(margin, even_ref, odd_ref, kappa_ref, sums_ref, *refs):
    coef_ref, sums_out, one_ref, two_ref = refs[-4:]
    sums_out[...] = sums_ref[...]
    rows = kappa_ref.shape[1]
    lay_ring(one_ref, kappa_ref[0], even_ref.at[0], odd_ref.at[0], margin)
    lay_ring(two_ref, kappa_ref[1], even_ref.at[1], odd_ref.at[1], margin)
    face_weights(coef_ref, one_ref, two_ref, rows, margin)


def smooth_kernel(margin, own_ref, even_ref, odd_ref, coef_ref, out_ref, ring_ref):
    rows = own_ref.shape[0]
    lay_ring(ring_ref, own_ref[...], even_ref, odd_ref, margin)
    for j, field in enumerate(diffuse(ring_ref, coef_ref, rows, margin)):
        out_ref[:, j * LANES : (j + 1) * LANES] = field


def adjoint_kernel(margin, smooth_ref, mask_ref, sums_ref, more_ref, adjoint_ref, even_ref, odd_ref):
    weight = sums_ref[0] + more_ref[0]
    value = sums_ref[1] + more_ref[1]
    window = lanes(*window_of(my_chip(), chip_count(), mask_ref.shape[1] // LANES))
    adjoint = mask_ref[:, window].astype(F32) * (weight * smooth_ref[...] - value)
    adjoint_ref[...] = adjoint
    pack_edges(even_ref, odd_ref, adjoint, margin)


def spread_kernel(margin, own_ref, even_ref, odd_ref, coef_ref, out_ref, ring_ref):
    rows = own_ref.shape[0]
    lay_ring(ring_ref, own_ref[...], even_ref, odd_ref, margin)
    for j, field in enumerate(diffuse(ring_ref, coef_ref, rows, margin)):
        ring_ref[:rows, j * LANES : (j + 1) * LANES] = field
    own = out_ref.shape[1] // LANES
    start = window_of(my_chip(), chip_count(), own * chip_count())[0]
    out_ref[...] = ring_ref[:rows, lanes(my_chip() * own - start, own)]


def sent_last(members):
    return [0, 1] + sorted(range(2, members), key=lambda d: -(d % 2))


def result_kernel(response_ref, control_ref, *refs):
    own, out_ref = refs[0].shape[1] // LANES, refs[-1]
    refs = [refs[sent_last(len(refs) - 1).index(d)] for d in range(len(refs) - 1)]
    for d in range(len(refs) // 2):
        window = lanes((my_chip() ^ d) * own, own)
        for v in range(control_ref.shape[0]):
            mine, theirs = (response_ref[i, v][:1, :1] for i in range(2))
            out_ref[v, :, window] = (
                control_ref[v, :, window] + mine * refs[2 * d][...] + theirs * refs[2 * d + 1][...]
            )


def swap(values, axis, bit):
    count = lax.axis_size(axis)
    return lax.ppermute(values, axis, [(i, i ^ bit) for i in range(count)])


def swap_edges(even, odd):
    tiles, members = lax.axis_size("tile"), lax.axis_size("var")
    pairs = []
    for t in range(tiles):
        other = t + 1 if t % 2 else t - 1
        for q in range(members):
            to = other * members + q if 0 <= other < tiles else t * members + (q ^ 1)
            pairs.append((t * members + q, to))
    return swap(even, "tile", 1), lax.ppermute(odd, ("tile", "var"), pairs)


def deliver(chunks):
    tiles, members = lax.axis_size("tile"), lax.axis_size("var")
    got = []
    for turn, chunk in enumerate(chunks[:-1]):
        pairs = []
        for t in range(tiles):
            for q in range(members):
                offset = tiles // 2 if turn == len(chunks) - 2 else 1 + turn + (q % 2) * (tiles // 2)
                pairs.append((t * members + q, (t ^ offset) * members + q))
        got.append(lax.ppermute(chunk, ("tile", "var"), pairs))
    return got + [chunks[-1]]


def local(control, diffusivity, land_mask, panel_tile, panel_row, panel_cols, obs_values,
          obs_weights, panel_sensor, sensitivity, cross_factor):
    rows, width = control.shape[1:]
    var_dev = control.shape[0]
    tiles, members = lax.axis_size("tile"), lax.axis_size("var")
    panels, panel_width = panel_cols.shape
    slots = panels // tiles
    blocks = width // LANES
    margin = PASSES
    total = ring_rows(rows, margin)
    chips = members // 2
    size = window_of(0, chips, blocks)[1]
    field = jax.ShapeDtypeStruct((rows, width), F32)
    share = jax.ShapeDtypeStruct((rows, width // chips), F32)
    view = jax.ShapeDtypeStruct((rows, size * LANES), F32)
    view2 = jax.ShapeDtypeStruct((2, *view.shape), F32)
    edge = jax.ShapeDtypeStruct((margin * size, LANES), F32)
    edge2 = jax.ShapeDtypeStruct((2, *edge.shape), F32)
    half = jax.ShapeDtypeStruct((3 * slots + 8, panel_width), F32)
    chunks = [jax.ShapeDtypeStruct((2, *half.shape), F32)] * (tiles // 2 - 1) + [half] * 2
    line = pltpu.VMEM((1, panels), jnp.int32)

    own, other, responses, kappa, kappa_even, kappa_odd, *chunks = call(
        functools.partial(first_kernel, slots, margin),
        [field, field, jax.ShapeDtypeStruct((2, var_dev, 8, LANES), F32), view2, edge2, edge2]
        + chunks,
        [HBM] * 10,
        [
            pltpu.SMEM(sensitivity.shape, F32),
            pltpu.SMEM(cross_factor.shape, F32),
            pltpu.VMEM(control.shape, F32),
            line, line, line,
            pltpu.VMEM(obs_values.shape, F32),
            pltpu.VMEM(obs_weights.shape, F32),
            pltpu.VMEM(panel_cols.shape, jnp.int32),
            pltpu.VMEM((panels, panels), jnp.bfloat16),
            pltpu.SemaphoreType.DMA((10,)),
        ],
        cost=cost(3000),
    )(*(in_hbm(x) for x in (sensitivity, cross_factor, control, diffusivity, panel_tile.reshape(1, -1),
                            panel_row.reshape(1, -1), panel_sensor.reshape(1, -1), obs_values,
                            obs_weights, panel_cols)))

    got = deliver(chunks)
    part, *parts = call(cut_kernel, [view] * chips, [VMEM] * 2, cost=cost(200))(
        own, swap(other, "var", 1)
    )
    parts = [swap(p, "var", 2 * (d + 1)) for d, p in enumerate(parts)]
    kappa_even, kappa_odd = swap_edges(kappa_even, kappa_odd)
    smooth_in, even, odd = call(
        functools.partial(edges_kernel, margin), [view, edge, edge], [VMEM] * chips, cost=cost(500)
    )(part, *parts)
    even, odd = swap_edges(even, odd)
    sums, sums_other = call(
        functools.partial(scatter_kernel, slots, blocks),
        [view2, view2],
        [AFTER] + [VMEM] * len(got),
        [
            pltpu.VMEM((2 * rows * 2 * padded_blocks(size), LANES), F32),
            pltpu.SMEM((8 * tiles, LANES), F32),
            pltpu.SemaphoreType.DMA((tiles,)),
        ],
        cost=cost(100000),
    )(smooth_in, *got)
    ring = pltpu.VMEM((total, size * LANES), F32)
    coef, sums_other = call(
        functools.partial(faces_kernel, margin),
        [jax.ShapeDtypeStruct((5, total, size * LANES), F32), view2],
        [VMEM] * 4 + [AFTER] * 2,
        [ring, ring],
        cost=cost(1000),
    )(kappa_even, kappa_odd, kappa, sums_other, even, odd)
    more_sums = swap(sums_other, "var", 1)
    (smooth,) = call(
        functools.partial(smooth_kernel, margin),
        [view],
        [VMEM] * 4,
        [ring],
        cost=cost(4000),
    )(smooth_in, even, odd, coef)
    adjoint, even, odd = call(
        functools.partial(adjoint_kernel, margin), [view, edge, edge], [VMEM] * 4, cost=cost(500)
    )(smooth, land_mask, sums, more_sums)
    even, odd = swap_edges(even, odd)
    (mine,) = call(
        functools.partial(spread_kernel, margin),
        [share],
        [VMEM] * 4,
        [ring],
        cost=cost(4000),
    )(adjoint, even, odd, coef)
    shares = [mine] + [swap(mine, "var", d) for d in sent_last(members)[1:]]
    (out,) = call(
        result_kernel,
        [jax.ShapeDtypeStruct(control.shape, F32)],
        [VMEM] * (2 + members),
        cost=cost(1000),
    )(responses, control, *shares)
    return out


def solution(mesh):
    return jax.shard_map(
        local,
        mesh=mesh,
        in_specs=(
            P("var", ("grp", "tile"), None),
            P(None, ("grp", "tile"), None),
            P(("grp", "tile"), None),
            P(("grp", "tile"), None),
            P(("grp", "tile")),
            P(("grp", "tile"), None),
            P(("grp", "tile"), None),
            P(("grp", "tile"), None),
            P(("grp", "tile")),
            P(),
            P(),
        ),
        out_specs=P("var", ("grp", "tile"), None),
        check_vma=False,
    )
```

```python
import functools

import jax
import jax.numpy as jnp
from jax import lax
from jax.experimental import pallas as pl
from jax.experimental.pallas import tpu as pltpu
from jax.sharding import PartitionSpec as P

PASSES = 10
LANES = 128
GROUP = 16
VMEM = pl.BlockSpec(memory_space=pltpu.VMEM)
SMEM = pl.BlockSpec(memory_space=pltpu.SMEM)
HBM = pl.BlockSpec(memory_space=pltpu.HBM)
AFTER = pl.BlockSpec(memory_space=pl.ANY)
F32 = jnp.float32


def in_hbm(values):
    return pltpu.with_memory_space_constraint(values, pltpu.HBM)


def call(body, outs, ins, scratch=(), limit=16, cost=None):
    return pl.pallas_call(
        body,
        out_shape=outs,
        in_specs=ins,
        out_specs=[VMEM] * len(outs),
        scratch_shapes=list(scratch),
        compiler_params=pltpu.CompilerParams(vmem_limit_bytes=limit << 20),
        cost_estimate=cost,
    )


def cost(cycles):
    return pl.CostEstimate(flops=cycles * 4096, bytes_accessed=cycles * 1024, transcendentals=0)


def response(sens_ref, factor_ref, sensor, variable):
    total = sens_ref[sensor, 0] * factor_ref[0, variable]
    for u in range(1, factor_ref.shape[0]):
        total = total + sens_ref[sensor, u] * factor_ref[u, variable]
    return total


def fetch(pairs, sems):
    copies = [pltpu.make_async_copy(src, dst, sems.at[i]) for i, (src, dst) in enumerate(pairs)]
    for copy in copies:
        copy.start()
    return copies


def window_of(chip, chips, blocks):
    own = blocks // chips
    size = min(own + 2, own + chips - 1)
    return jnp.clip(chip * own - 1, 0, blocks - size), size


def my_chip():
    return lax.axis_index("var") // 2


def chip_count():
    return lax.axis_size("var") // 2


def lanes(start, size):
    return pl.ds(pl.multiple_of(start * LANES, LANES), size * LANES)


def first_kernel(slots, margin, sens_hbm, factor_hbm, control_hbm, kappa_hbm, tile_hbm, row_hbm, sensor_hbm,
                 value_hbm, weight_hbm, cols_hbm, own_ref, other_ref, response_ref, kappa_ref, even_ref,
                 odd_ref, *refs):
    chunk_refs = refs[:-11]
    (sens_ref, factor_ref, control_ref, tile_ref, row_ref, sensor_ref, value_ref, weight_ref, cols_ref,
     before_ref, sems) = refs[-11:]
    window = lanes(*window_of(my_chip(), chip_count(), own_ref.shape[1] // LANES))
    pairs = (
        (sens_hbm, sens_ref), (factor_hbm, factor_ref), (control_hbm, control_ref),
        (kappa_hbm.at[:, :, window], kappa_ref), (tile_hbm, tile_ref), (row_hbm, row_ref), (sensor_hbm, sensor_ref),
        (value_hbm, value_ref), (weight_hbm, weight_ref), (cols_hbm, cols_ref),
    )
    copies = [pltpu.make_async_copy(src, dst, sems.at[i]) for i, (src, dst) in enumerate(pairs)]
    for copy in copies:
        copy.start()
    from_panel = lax.broadcasted_iota(jnp.int32, before_ref.shape, 0)
    to_panel = lax.broadcasted_iota(jnp.int32, before_ref.shape, 1)
    before_ref[...] = jnp.where(from_panel < to_panel, 1.0, 0.0).astype(jnp.bfloat16)
    for copy in copies:
        copy.wait()

    member, mine = lax.axis_index("var"), lax.axis_index("tile")
    core = member % 2
    var_dev = control_ref.shape[0]
    for which, (sensor, out_ref) in enumerate(((core, own_ref), (1 - core, other_ref))):
        total = None
        for v in range(var_dev):
            scale = response(sens_ref, factor_ref, sensor, member * var_dev + v)
            response_ref[which, v] = jnp.full(response_ref.shape[2:], scale, F32)
            term = scale * control_ref[v]
            total = term if total is None else total + term
        out_ref[...] = total

    for i in range(2):
        pack_edges(even_ref.at[i], odd_ref.at[i], kappa_ref[i], margin)

    tiles = lax.axis_size("tile")
    full = tiles // 2 - 1
    first = jnp.where(core == 0, 1, tiles // 2 + 1)
    panels = value_ref.shape[0]
    source = tile_ref[...] ^ mine
    names = lax.broadcasted_iota(jnp.int32, (-(-tiles // 8) * 8, panels), 0)
    hits = jnp.where(names == source, 1.0, 0.0)
    ranks = jnp.dot(hits.astype(jnp.bfloat16), before_ref[...], preferred_element_type=F32)
    rank = jnp.sum(hits * ranks, axis=0, keepdims=True).astype(jnp.int32)
    parity, slot = rank % 2, rank // 2
    whole = (source >= first) & (source < first + full)
    home = source == 0
    keep = whole | ((home | (source == tiles // 2)) & (parity == core))
    half = jnp.where(whole, 2 * (source - first) + parity, jnp.where(home, tiles - 1, tiles - 2))
    place = jnp.where(keep, half * slots + slot, -1)
    spots = lax.broadcasted_iota(jnp.int32, (tiles * slots, panels), 0)
    pick = jnp.where(spots == place, 1.0, 0.0).astype(jnp.bfloat16)

    def picked(parts):
        total = None
        for part in parts:
            term = jnp.dot(pick, part.astype(jnp.bfloat16), preferred_element_type=F32)
            total = term if total is None else total + term
        return total

    cols = cols_ref[...]
    sent = (
        picked(thirds(value_ref[...])),
        picked(thirds(weight_ref[...])),
        picked(((cols // LANES * LANES).astype(F32), (cols % LANES).astype(F32))),
    )
    sub = lax.broadcasted_iota(jnp.int32, (8, panels), 0)
    lane = lax.broadcasted_iota(jnp.int32, (8, panels), 1)
    facts = jnp.where(sub == 0, row_ref[...], jnp.where(sub == 1, sensor_ref[...], 0)).astype(F32)
    meta = lax.dot_general(
        facts.astype(jnp.bfloat16), pick, (((1,), (1,)), ((), ())), preferred_element_type=F32
    )
    for i in range(tiles):
        held = jnp.sum(jnp.where(keep & (half == i), 1.0, 0.0), axis=1, keepdims=True)
        meta = jnp.where((sub == 2) & (lane == i), held, meta)
    for i in range(tiles):
        out_ref = chunk_refs[i // 2].at[i % 2] if i < 2 * full else chunk_refs[i - full]
        for part, rows in enumerate(sent):
            out_ref[part * slots : (part + 1) * slots] = rows[i * slots : (i + 1) * slots]
        out_ref[3 * slots :] = meta


def thirds(values):
    top = values.astype(jnp.bfloat16).astype(F32)
    rest = values - top
    middle = rest.astype(jnp.bfloat16).astype(F32)
    return top, middle, rest - middle


def pieces(values):
    top = values.astype(jnp.bfloat16).astype(F32)
    return top, values - top


def scatter_kernel(slots, blocks_all, after_ref, *refs):
    got_refs, (own_ref, other_ref, acc_ref, meta_ref, sems) = refs[:-5], refs[-5:]
    core = lax.axis_index("var") % 2
    got_refs = [r.at[i] for r in got_refs[1:-1] for i in (0, 1)] + [got_refs[0], got_refs[-1]]
    size_of_group = min(GROUP, slots)
    copies = [
        pltpu.make_async_copy(ref.at[pl.ds(3 * slots, 8)], meta_ref.at[pl.ds(8 * s, 8)], sems.at[s])
        for s, ref in enumerate(got_refs)
    ]
    for copy in copies:
        copy.start()
    rows = own_ref.shape[1]
    start, size = window_of(my_chip(), chip_count(), blocks_all)
    per_kind = padded_blocks(size)
    tall = 2 * per_kind
    acc_ref[...] = jnp.zeros(acc_ref.shape, F32)
    place = lax.broadcasted_iota(jnp.int32, (tall, LANES), 0)
    is_weight = place < per_kind
    place = jnp.where(is_weight, place, place - per_kind) + start
    lane_ids = lax.broadcasted_iota(jnp.int32, (LANES, LANES), 0).astype(F32).astype(jnp.bfloat16)
    one, zero = jnp.bfloat16(1), jnp.bfloat16(0)
    sub = lax.broadcasted_iota(jnp.int32, (size_of_group, LANES), 0)
    blank = jnp.zeros((2 * tall, LANES), jnp.bfloat16)
    for copy in copies:
        copy.wait()

    def load(s, base):
        got_ref = got_refs[s]
        count = meta_ref[8 * s + 2, s].astype(jnp.int32)
        value = got_ref[pl.ds(base, size_of_group), :]
        weight = got_ref[pl.ds(slots + base, size_of_group), :]
        cell = got_ref[pl.ds(2 * slots + base, size_of_group), :].astype(jnp.int32)
        weight = jnp.where(sub + base < count, weight, 0.0)
        return pieces(weight), pieces(weight * value), (cell % LANES).astype(F32), cell // LANES

    def one_hots(loaded, i):
        weights, values, low, high = loaded
        here = place == high[i : i + 1]
        rows_of = [
            jnp.where(here, jnp.where(is_weight, w[i : i + 1], v[i : i + 1]), 0.0)
            for w, v in zip(weights, values)
        ]
        left = jnp.concatenate(rows_of, axis=0).astype(jnp.bfloat16)
        column = jnp.broadcast_to(low[i : i + 1], (16, LANES)).astype(jnp.bfloat16)
        column = jnp.concatenate([column] * (LANES // 16), axis=0)
        return left, jnp.where(lane_ids == column, one, zero)

    def pair(s, g, carry):
        base = pl.multiple_of(g * size_of_group, size_of_group)
        loaded = [load(s + i, base) for i in (0, 1)]
        for k in range(size_of_group):
            hots = [one_hots(loaded[i], k) for i in (0, 1)]
            left = jnp.concatenate(
                [
                    jnp.concatenate([hots[0][0], blank], axis=1),
                    jnp.concatenate([blank, hots[1][0]], axis=1),
                ],
                axis=0,
            )
            both = lax.dot_general(
                left, jnp.concatenate([hots[0][1], hots[1][1]], axis=1), (((1,), (1,)), ((), ())),
                preferred_element_type=F32,
            )
            for i in (0, 1):
                row = meta_ref[8 * (s + i), (s + i) * slots + base + k].astype(jnp.int32)
                sensor = meta_ref[8 * (s + i) + 1, (s + i) * slots + base + k].astype(jnp.int32)
                at = pl.multiple_of((sensor * rows + row) * tall, 8)
                mine = both[2 * i * tall : 2 * (i + 1) * tall]
                acc_ref[pl.ds(at, tall), :] += mine[:tall] + mine[tall:]
        return carry

    for s in range(0, len(got_refs), 2):
        most = jnp.maximum(meta_ref[8 * s + 2, s], meta_ref[8 * s + 10, s + 1]).astype(jnp.int32)
        lax.fori_loop(0, (most + size_of_group - 1) // size_of_group, functools.partial(pair, s), 0)
    for sensor, out_ref in ((core, own_ref), (1 - core, other_ref)):
        begin = sensor * rows * tall
        for kind in range(2):
            for b in range(size):
                out_ref[kind, :, b * LANES : (b + 1) * LANES] = acc_ref[
                    pl.ds(begin + kind * per_kind + b, rows, stride=tall), :
                ]


def padded_blocks(size):
    return -(-size // 4) * 4


def even_tile():
    return lax.axis_index("tile") % 2 == 0


def has_above():
    return lax.axis_index("tile") > 0


def has_below():
    return lax.axis_index("tile") + 1 < lax.axis_size("tile")


def pack_edges(even_ref, odd_ref, rows_value, margin):
    rows, width = rows_value.shape
    even = even_tile()
    for b in range(width // LANES):
        at = slice(b * LANES, (b + 1) * LANES)
        head, tail = rows_value[:margin, at], rows_value[rows - margin :, at]
        even_ref[b * margin : (b + 1) * margin] = jnp.where(even, tail, head)
        odd_ref[b * margin : (b + 1) * margin] = jnp.where(even, head, tail)


def cut_kernel(first_ref, second_ref, mine_ref, *out_refs):
    chip, chips, blocks = my_chip(), chip_count(), first_ref.shape[1] // LANES
    for d, out_ref in enumerate((mine_ref, *out_refs)):
        window = lanes(*window_of(chip ^ d, chips, blocks))
        out_ref[...] = first_ref[:, window] + second_ref[:, window]


def edges_kernel(margin, *refs):
    terms, (total_ref, even_ref, odd_ref) = refs[:-3], refs[-3:]
    total = terms[0][...]
    for term in terms[1:]:
        total = total + term[...]
    total_ref[...] = total
    pack_edges(even_ref, odd_ref, total, margin)


def ring_rows(rows, margin):
    return -(-(rows + 2 * margin) // 8) * 8


def lay_ring(ref, own, from_even, from_odd, margin):
    rows, total = own.shape[0], ref.shape[0]
    even = even_tile()
    ref[rows:total] = jnp.zeros((total - rows, ref.shape[1]), F32)
    ref[:rows] = own
    for b in range(ref.shape[1] // LANES):
        at = slice(b * LANES, (b + 1) * LANES)
        one, two = (m[b * margin : (b + 1) * margin] for m in (from_even, from_odd))
        ref[rows : rows + margin, at] = jnp.where(has_below(), jnp.where(even, one, two), 0.0)
        ref[total - margin :, at] = jnp.where(has_above(), jnp.where(even, two, one), 0.0)


def block(ref, j):
    return ref[:, j * LANES : (j + 1) * LANES]


def sideways(blocks):
    shape = blocks[0].shape
    lane = lax.broadcasted_iota(jnp.int32, shape, 1)
    zero = jnp.zeros(shape, F32)
    ahead = [pltpu.roll(x, 1, 1) for x in blocks]
    back = [pltpu.roll(x, LANES - 1, 1) for x in blocks]
    for j, here in enumerate(blocks):
        before = ahead[j - 1] if j else zero
        after = back[j + 1] if j + 1 < len(blocks) else zero
        yield here, jnp.where(lane == 0, before, ahead[j]), jnp.where(lane == LANES - 1, after, back[j])


def face_weights(coef_ref, row_ref, col_ref, rows, margin):
    total, width = row_ref.shape
    blocks = width // LANES
    r = lax.broadcasted_iota(jnp.int32, (total, LANES), 0)
    inside = (
        (r < rows)
        | ((r < rows + margin) & has_below())
        | ((r >= total - margin) & has_above())
    )
    scale = jnp.where(inside, 0.125, 0.0)
    unit = jnp.where(inside, 1.0, 0.0)
    columns = [block(col_ref, j) for j in range(blocks)]
    for j, (k_col, k_left, k_right) in enumerate(sideways(columns)):
        at = slice(j * LANES, (j + 1) * LANES)
        k_row = block(row_ref, j)
        up = scale * (k_row + pltpu.roll(k_row, 1, 0))
        down = scale * (k_row + pltpu.roll(k_row, total - 1, 0))
        left = scale * (k_col + k_left)
        right = scale * (k_col + k_right)
        coef_ref[0, :, at] = unit - up - down - left - right
        coef_ref[1, :, at] = up
        coef_ref[2, :, at] = down
        coef_ref[3, :, at] = left
        coef_ref[4, :, at] = right


def one_pass(fields, coef_ref, spans):
    def weights(i, at):
        got = [coef_ref[i, span, at] for span in spans]
        return jnp.concatenate(got, axis=0) if len(got) > 1 else got[0]

    total = fields[0].shape[0]
    out = []
    for j, (here, left, right) in enumerate(sideways(fields)):
        at = slice(j * LANES, (j + 1) * LANES)
        out.append(
            weights(0, at) * here
            + weights(1, at) * pltpu.roll(here, 1, 0)
            + weights(2, at) * pltpu.roll(here, total - 1, 0)
            + weights(3, at) * left
            + weights(4, at) * right
        )
    return out


def diffuse(ring_ref, coef_ref, rows, margin):
    total, width = ring_ref.shape
    inner = margin // 8 * 8
    wide = [slice(0, total)]
    narrow = [slice(0, rows + inner), slice(total - inner, total)]
    fields = [block(ring_ref, j) for j in range(width // LANES)]
    for _ in range(margin - inner):
        fields = one_pass(fields, coef_ref, wide)
    fields = [jnp.concatenate([f[span] for span in narrow], axis=0) for f in fields]
    for _ in range(inner):
        fields = one_pass(fields, coef_ref, narrow)
    return [f[:rows] for f in fields]


def faces_kernel(margin, even_ref, odd_ref, kappa_ref, sums_ref, *refs):
    coef_ref, sums_out, one_ref, two_ref = refs[-4:]
    sums_out[...] = sums_ref[...]
    rows = kappa_ref.shape[1]
    lay_ring(one_ref, kappa_ref[0], even_ref.at[0], odd_ref.at[0], margin)
    lay_ring(two_ref, kappa_ref[1], even_ref.at[1], odd_ref.at[1], margin)
    face_weights(coef_ref, one_ref, two_ref, rows, margin)


def smooth_kernel(margin, own_ref, even_ref, odd_ref, coef_ref, out_ref, ring_ref):
    rows = own_ref.shape[0]
    lay_ring(ring_ref, own_ref[...], even_ref, odd_ref, margin)
    for j, field in enumerate(diffuse(ring_ref, coef_ref, rows, margin)):
        out_ref[:, j * LANES : (j + 1) * LANES] = field


def adjoint_kernel(margin, smooth_ref, mask_ref, sums_ref, more_ref, adjoint_ref, even_ref, odd_ref):
    weight = sums_ref[0] + more_ref[0]
    value = sums_ref[1] + more_ref[1]
    window = lanes(*window_of(my_chip(), chip_count(), mask_ref.shape[1] // LANES))
    adjoint = mask_ref[:, window].astype(F32) * (weight * smooth_ref[...] - value)
    adjoint_ref[...] = adjoint
    pack_edges(even_ref, odd_ref, adjoint, margin)


def spread_kernel(margin, own_ref, even_ref, odd_ref, coef_ref, out_ref, ring_ref):
    rows = own_ref.shape[0]
    lay_ring(ring_ref, own_ref[...], even_ref, odd_ref, margin)
    for j, field in enumerate(diffuse(ring_ref, coef_ref, rows, margin)):
        ring_ref[:rows, j * LANES : (j + 1) * LANES] = field
    own = out_ref.shape[1] // LANES
    start = window_of(my_chip(), chip_count(), own * chip_count())[0]
    out_ref[...] = ring_ref[:rows, lanes(my_chip() * own - start, own)]


def sent_last(members):
    return [0, 1] + sorted(range(2, members), key=lambda d: -(d % 2))


def result_kernel(response_ref, control_ref, *refs):
    own, out_ref = refs[0].shape[1] // LANES, refs[-1]
    refs = [refs[sent_last(len(refs) - 1).index(d)] for d in range(len(refs) - 1)]
    for d in range(len(refs) // 2):
        window = lanes((my_chip() ^ d) * own, own)
        for v in range(control_ref.shape[0]):
            mine, theirs = (response_ref[i, v][:1, :1] for i in range(2))
            out_ref[v, :, window] = (
                control_ref[v, :, window] + mine * refs[2 * d][...] + theirs * refs[2 * d + 1][...]
            )


def swap(values, axis, bit):
    count = lax.axis_size(axis)
    return lax.ppermute(values, axis, [(i, i ^ bit) for i in range(count)])


def swap_edges(even, odd):
    tiles, members = lax.axis_size("tile"), lax.axis_size("var")
    pairs = []
    for t in range(tiles):
        other = t + 1 if t % 2 else t - 1
        for q in range(members):
            to = other * members + q if 0 <= other < tiles else t * members + (q ^ 1)
            pairs.append((t * members + q, to))
    return swap(even, "tile", 1), lax.ppermute(odd, ("tile", "var"), pairs)


def deliver(chunks):
    tiles, members = lax.axis_size("tile"), lax.axis_size("var")
    got = []
    for turn, chunk in enumerate(chunks[:-1]):
        pairs = []
        for t in range(tiles):
            for q in range(members):
                offset = tiles // 2 if turn == len(chunks) - 2 else 1 + turn + (q % 2) * (tiles // 2)
                pairs.append((t * members + q, (t ^ offset) * members + q))
        got.append(lax.ppermute(chunk, ("tile", "var"), pairs))
    return got + [chunks[-1]]


def local(control, diffusivity, land_mask, panel_tile, panel_row, panel_cols, obs_values,
          obs_weights, panel_sensor, sensitivity, cross_factor):
    rows, width = control.shape[1:]
    var_dev = control.shape[0]
    tiles, members = lax.axis_size("tile"), lax.axis_size("var")
    panels, panel_width = panel_cols.shape
    slots = panels // tiles
    blocks = width // LANES
    margin = PASSES
    total = ring_rows(rows, margin)
    chips = members // 2
    size = window_of(0, chips, blocks)[1]
    field = jax.ShapeDtypeStruct((rows, width), F32)
    share = jax.ShapeDtypeStruct((rows, width // chips), F32)
    view = jax.ShapeDtypeStruct((rows, size * LANES), F32)
    view2 = jax.ShapeDtypeStruct((2, *view.shape), F32)
    edge = jax.ShapeDtypeStruct((margin * size, LANES), F32)
    edge2 = jax.ShapeDtypeStruct((2, *edge.shape), F32)
    half = jax.ShapeDtypeStruct((3 * slots + 8, panel_width), F32)
    chunks = [jax.ShapeDtypeStruct((2, *half.shape), F32)] * (tiles // 2 - 1) + [half] * 2
    line = pltpu.VMEM((1, panels), jnp.int32)

    own, other, responses, kappa, kappa_even, kappa_odd, *chunks = call(
        functools.partial(first_kernel, slots, margin),
        [field, field, jax.ShapeDtypeStruct((2, var_dev, 8, LANES), F32), view2, edge2, edge2]
        + chunks,
        [HBM] * 10,
        [
            pltpu.SMEM(sensitivity.shape, F32),
            pltpu.SMEM(cross_factor.shape, F32),
            pltpu.VMEM(control.shape, F32),
            line, line, line,
            pltpu.VMEM(obs_values.shape, F32),
            pltpu.VMEM(obs_weights.shape, F32),
            pltpu.VMEM(panel_cols.shape, jnp.int32),
            pltpu.VMEM((panels, panels), jnp.bfloat16),
            pltpu.SemaphoreType.DMA((10,)),
        ],
        cost=cost(3000),
    )(*(in_hbm(x) for x in (sensitivity, cross_factor, control, diffusivity, panel_tile.reshape(1, -1),
                            panel_row.reshape(1, -1), panel_sensor.reshape(1, -1), obs_values,
                            obs_weights, panel_cols)))

    got = deliver(chunks)
    part, *parts = call(cut_kernel, [view] * chips, [VMEM] * 2, cost=cost(200))(
        own, swap(other, "var", 1)
    )
    parts = [swap(p, "var", 2 * (d + 1)) for d, p in enumerate(parts)]
    kappa_even, kappa_odd = swap_edges(kappa_even, kappa_odd)
    smooth_in, even, odd = call(
        functools.partial(edges_kernel, margin), [view, edge, edge], [VMEM] * chips, cost=cost(500)
    )(part, *parts)
    even, odd = swap_edges(even, odd)
    sums, sums_other = call(
        functools.partial(scatter_kernel, slots, blocks),
        [view2, view2],
        [AFTER] + [VMEM] * len(got),
        [
            pltpu.VMEM((2 * rows * 2 * padded_blocks(size), LANES), F32),
            pltpu.SMEM((8 * tiles, LANES), F32),
            pltpu.SemaphoreType.DMA((tiles,)),
        ],
        cost=cost(100000),
    )(smooth_in, got[-2], *got[:-2], got[-1])
    ring = pltpu.VMEM((total, size * LANES), F32)
    coef, sums_other = call(
        functools.partial(faces_kernel, margin),
        [jax.ShapeDtypeStruct((5, total, size * LANES), F32), view2],
        [VMEM] * 4 + [AFTER] * 2,
        [ring, ring],
        cost=cost(1000),
    )(kappa_even, kappa_odd, kappa, sums_other, even, odd)
    more_sums = swap(sums_other, "var", 1)
    (smooth,) = call(
        functools.partial(smooth_kernel, margin),
        [view],
        [VMEM] * 4,
        [ring],
        cost=cost(4000),
    )(smooth_in, even, odd, coef)
    adjoint, even, odd = call(
        functools.partial(adjoint_kernel, margin), [view, edge, edge], [VMEM] * 4, cost=cost(500)
    )(smooth, land_mask, sums, more_sums)
    even, odd = swap_edges(even, odd)
    (mine,) = call(
        functools.partial(spread_kernel, margin),
        [share],
        [VMEM] * 4,
        [ring],
        cost=cost(4000),
    )(adjoint, even, odd, coef)
    shares = [mine] + [swap(mine, "var", d) for d in sent_last(members)[1:]]
    (out,) = call(
        result_kernel,
        [jax.ShapeDtypeStruct(control.shape, F32)],
        [VMEM] * (2 + members),
        cost=cost(1000),
    )(responses, control, *shares)
    return out


def solution(mesh):
    return jax.shard_map(
        local,
        mesh=mesh,
        in_specs=(
            P("var", ("grp", "tile"), None),
            P(None, ("grp", "tile"), None),
            P(("grp", "tile"), None),
            P(("grp", "tile"), None),
            P(("grp", "tile")),
            P(("grp", "tile"), None),
            P(("grp", "tile"), None),
            P(("grp", "tile"), None),
            P(("grp", "tile")),
            P(),
            P(),
        ),
        out_specs=P("var", ("grp", "tile"), None),
        check_vma=False,
    )
```

```python
import functools

import jax
import jax.numpy as jnp
from jax import lax
from jax.experimental import pallas as pl
from jax.experimental.pallas import tpu as pltpu
from jax.sharding import PartitionSpec as P

PASSES = 10
LANES = 128
GROUP = 16
VMEM = pl.BlockSpec(memory_space=pltpu.VMEM)
SMEM = pl.BlockSpec(memory_space=pltpu.SMEM)
HBM = pl.BlockSpec(memory_space=pltpu.HBM)
AFTER = pl.BlockSpec(memory_space=pl.ANY)
F32 = jnp.float32


def in_hbm(values):
    return pltpu.with_memory_space_constraint(values, pltpu.HBM)


def call(body, outs, ins, scratch=(), limit=16, cost=None):
    return pl.pallas_call(
        body,
        out_shape=outs,
        in_specs=ins,
        out_specs=[VMEM] * len(outs),
        scratch_shapes=list(scratch),
        compiler_params=pltpu.CompilerParams(vmem_limit_bytes=limit << 20),
        cost_estimate=cost,
    )


def cost(cycles):
    return pl.CostEstimate(flops=cycles * 4096, bytes_accessed=cycles * 1024, transcendentals=0)


def response(sens_ref, factor_ref, sensor, variable):
    total = sens_ref[sensor, 0] * factor_ref[0, variable]
    for u in range(1, factor_ref.shape[0]):
        total = total + sens_ref[sensor, u] * factor_ref[u, variable]
    return total


def fetch(pairs, sems):
    copies = [pltpu.make_async_copy(src, dst, sems.at[i]) for i, (src, dst) in enumerate(pairs)]
    for copy in copies:
        copy.start()
    return copies


def window_of(chip, chips, blocks):
    own = blocks // chips
    size = min(own + 2, own + chips - 1)
    return jnp.clip(chip * own - 1, 0, blocks - size), size


def my_chip():
    return lax.axis_index("var") // 2


def chip_count():
    return lax.axis_size("var") // 2


def lanes(start, size):
    return pl.ds(pl.multiple_of(start * LANES, LANES), size * LANES)


def first_kernel(slots, margin, sens_hbm, factor_hbm, control_hbm, kappa_hbm, tile_hbm, row_hbm, sensor_hbm,
                 value_hbm, weight_hbm, cols_hbm, own_ref, other_ref, response_ref, kappa_ref, even_ref,
                 odd_ref, *refs):
    chunk_refs = refs[:-11]
    (sens_ref, factor_ref, control_ref, tile_ref, row_ref, sensor_ref, value_ref, weight_ref, cols_ref,
     before_ref, sems) = refs[-11:]
    window = lanes(*window_of(my_chip(), chip_count(), own_ref.shape[1] // LANES))
    pairs = (
        (sens_hbm, sens_ref), (factor_hbm, factor_ref), (control_hbm, control_ref),
        (kappa_hbm.at[:, :, window], kappa_ref), (tile_hbm, tile_ref), (row_hbm, row_ref), (sensor_hbm, sensor_ref),
        (value_hbm, value_ref), (weight_hbm, weight_ref), (cols_hbm, cols_ref),
    )
    copies = [pltpu.make_async_copy(src, dst, sems.at[i]) for i, (src, dst) in enumerate(pairs)]
    for copy in copies:
        copy.start()
    from_panel = lax.broadcasted_iota(jnp.int32, before_ref.shape, 0)
    to_panel = lax.broadcasted_iota(jnp.int32, before_ref.shape, 1)
    before_ref[...] = jnp.where(from_panel < to_panel, 1.0, 0.0).astype(jnp.bfloat16)
    for copy in copies:
        copy.wait()

    member, mine = lax.axis_index("var"), lax.axis_index("tile")
    core = member % 2
    var_dev = control_ref.shape[0]
    for which, (sensor, out_ref) in enumerate(((core, own_ref), (1 - core, other_ref))):
        total = None
        for v in range(var_dev):
            scale = response(sens_ref, factor_ref, sensor, member * var_dev + v)
            response_ref[which, v] = jnp.full(response_ref.shape[2:], scale, F32)
            term = scale * control_ref[v]
            total = term if total is None else total + term
        out_ref[...] = total

    for i in range(2):
        pack_edges(even_ref.at[i], odd_ref.at[i], kappa_ref[i], margin)

    tiles = lax.axis_size("tile")
    full = tiles // 2 - 1
    first = jnp.where(core == 0, 1, tiles // 2 + 1)
    panels = value_ref.shape[0]
    source = tile_ref[...] ^ mine
    names = lax.broadcasted_iota(jnp.int32, (-(-tiles // 8) * 8, panels), 0)
    hits = jnp.where(names == source, 1.0, 0.0)
    ranks = jnp.dot(hits.astype(jnp.bfloat16), before_ref[...], preferred_element_type=F32)
    rank = jnp.sum(hits * ranks, axis=0, keepdims=True).astype(jnp.int32)
    parity, slot = rank % 2, rank // 2
    whole = (source >= first) & (source < first + full)
    home = source == 0
    keep = whole | ((home | (source == tiles // 2)) & (parity == core))
    half = jnp.where(whole, 2 * (source - first) + parity, jnp.where(home, tiles - 1, tiles - 2))
    place = jnp.where(keep, half * slots + slot, -1)
    spots = lax.broadcasted_iota(jnp.int32, (tiles * slots, panels), 0)
    pick = jnp.where(spots == place, 1.0, 0.0).astype(jnp.bfloat16)

    def picked(parts):
        total = None
        for part in parts:
            term = jnp.dot(pick, part.astype(jnp.bfloat16), preferred_element_type=F32)
            total = term if total is None else total + term
        return total

    cols = cols_ref[...]
    sent = (
        picked(thirds(value_ref[...])),
        picked(thirds(weight_ref[...])),
        picked(((cols // LANES * LANES).astype(F32), (cols % LANES).astype(F32))),
    )
    sub = lax.broadcasted_iota(jnp.int32, (8, panels), 0)
    lane = lax.broadcasted_iota(jnp.int32, (8, panels), 1)
    facts = jnp.where(sub == 0, row_ref[...], jnp.where(sub == 1, sensor_ref[...], 0)).astype(F32)
    meta = lax.dot_general(
        facts.astype(jnp.bfloat16), pick, (((1,), (1,)), ((), ())), preferred_element_type=F32
    )
    for i in range(tiles):
        held = jnp.sum(jnp.where(keep & (half == i), 1.0, 0.0), axis=1, keepdims=True)
        meta = jnp.where((sub == 2) & (lane == i), held, meta)
    for i in range(tiles):
        out_ref = chunk_refs[i // 2].at[i % 2] if i < 2 * full else chunk_refs[i - full]
        for part, rows in enumerate(sent):
            out_ref[part * slots : (part + 1) * slots] = rows[i * slots : (i + 1) * slots]
        out_ref[3 * slots :] = meta


def thirds(values):
    top = values.astype(jnp.bfloat16).astype(F32)
    rest = values - top
    middle = rest.astype(jnp.bfloat16).astype(F32)
    return top, middle, rest - middle


def pieces(values):
    top = values.astype(jnp.bfloat16).astype(F32)
    return top, values - top


def scatter_kernel(slots, blocks_all, after_ref, *refs):
    got_refs, (own_ref, other_ref, acc_ref, meta_ref, sems) = refs[:-5], refs[-5:]
    core = lax.axis_index("var") % 2
    got_refs = [r.at[i] for r in got_refs[1:-1] for i in (0, 1)] + [got_refs[0], got_refs[-1]]
    size_of_group = min(GROUP, slots)
    copies = [
        pltpu.make_async_copy(ref.at[pl.ds(3 * slots, 8)], meta_ref.at[pl.ds(8 * s, 8)], sems.at[s])
        for s, ref in enumerate(got_refs)
    ]
    for copy in copies:
        copy.start()
    rows = own_ref.shape[1]
    start, size = window_of(my_chip(), chip_count(), blocks_all)
    per_kind = padded_blocks(size)
    tall = 2 * per_kind
    acc_ref[...] = jnp.zeros(acc_ref.shape, F32)
    place = lax.broadcasted_iota(jnp.int32, (tall, LANES), 0)
    is_weight = place < per_kind
    place = jnp.where(is_weight, place, place - per_kind) + start
    lane_ids = lax.broadcasted_iota(jnp.int32, (LANES, LANES), 0).astype(F32).astype(jnp.bfloat16)
    one, zero = jnp.bfloat16(1), jnp.bfloat16(0)
    sub = lax.broadcasted_iota(jnp.int32, (size_of_group, LANES), 0)
    blank = jnp.zeros((2 * tall, LANES), jnp.bfloat16)
    for copy in copies:
        copy.wait()

    def load(s, base):
        got_ref = got_refs[s]
        count = meta_ref[8 * s + 2, s].astype(jnp.int32)
        value = got_ref[pl.ds(base, size_of_group), :]
        weight = got_ref[pl.ds(slots + base, size_of_group), :]
        cell = got_ref[pl.ds(2 * slots + base, size_of_group), :].astype(jnp.int32)
        weight = jnp.where(sub + base < count, weight, 0.0)
        return pieces(weight), pieces(weight * value), (cell % LANES).astype(F32), cell // LANES

    def one_hots(loaded, i):
        weights, values, low, high = loaded
        here = place == high[i : i + 1]
        rows_of = [
            jnp.where(here, jnp.where(is_weight, w[i : i + 1], v[i : i + 1]), 0.0)
            for w, v in zip(weights, values)
        ]
        left = jnp.concatenate(rows_of, axis=0).astype(jnp.bfloat16)
        column = jnp.broadcast_to(low[i : i + 1], (16, LANES)).astype(jnp.bfloat16)
        column = jnp.concatenate([column] * (LANES // 16), axis=0)
        return left, jnp.where(lane_ids == column, one, zero)

    def pair(s, g, carry):
        base = pl.multiple_of(g * size_of_group, size_of_group)
        loaded = [load(s + i, base) for i in (0, 1)]
        for k in range(size_of_group):
            hots = [one_hots(loaded[i], k) for i in (0, 1)]
            left = jnp.concatenate(
                [
                    jnp.concatenate([hots[0][0], blank], axis=1),
                    jnp.concatenate([blank, hots[1][0]], axis=1),
                ],
                axis=0,
            )
            both = lax.dot_general(
                left, jnp.concatenate([hots[0][1], hots[1][1]], axis=1), (((1,), (1,)), ((), ())),
                preferred_element_type=F32,
            )
            for i in (0, 1):
                row = meta_ref[8 * (s + i), (s + i) * slots + base + k].astype(jnp.int32)
                sensor = meta_ref[8 * (s + i) + 1, (s + i) * slots + base + k].astype(jnp.int32)
                at = pl.multiple_of((sensor * rows + row) * tall, 8)
                mine = both[2 * i * tall : 2 * (i + 1) * tall]
                acc_ref[pl.ds(at, tall), :] += mine[:tall] + mine[tall:]
        return carry

    for s in range(0, len(got_refs), 2):
        most = jnp.maximum(meta_ref[8 * s + 2, s], meta_ref[8 * s + 10, s + 1]).astype(jnp.int32)
        lax.fori_loop(0, (most + size_of_group - 1) // size_of_group, functools.partial(pair, s), 0)
    for sensor, out_ref in ((core, own_ref), (1 - core, other_ref)):
        begin = sensor * rows * tall
        for kind in range(2):
            for b in range(size):
                out_ref[kind, :, b * LANES : (b + 1) * LANES] = acc_ref[
                    pl.ds(begin + kind * per_kind + b, rows, stride=tall), :
                ]


def padded_blocks(size):
    return -(-size // 4) * 4


def even_tile():
    return lax.axis_index("tile") % 2 == 0


def has_above():
    return lax.axis_index("tile") > 0


def has_below():
    return lax.axis_index("tile") + 1 < lax.axis_size("tile")


def pack_edges(even_ref, odd_ref, rows_value, margin):
    rows, width = rows_value.shape
    even = even_tile()
    for b in range(width // LANES):
        at = slice(b * LANES, (b + 1) * LANES)
        head, tail = rows_value[:margin, at], rows_value[rows - margin :, at]
        even_ref[b * margin : (b + 1) * margin] = jnp.where(even, tail, head)
        odd_ref[b * margin : (b + 1) * margin] = jnp.where(even, head, tail)


def cut_kernel(first_ref, second_ref, mine_ref, *out_refs):
    chip, chips, blocks = my_chip(), chip_count(), first_ref.shape[1] // LANES
    for d, out_ref in enumerate((mine_ref, *out_refs)):
        window = lanes(*window_of(chip ^ d, chips, blocks))
        out_ref[...] = first_ref[:, window] + second_ref[:, window]


def edges_kernel(margin, chips, *refs):
    terms, (total_ref, even_ref, odd_ref) = refs[:chips], refs[-3:]
    total = terms[0][...]
    for term in terms[1:]:
        total = total + term[...]
    total_ref[...] = total
    pack_edges(even_ref, odd_ref, total, margin)


def ring_rows(rows, margin):
    return -(-(rows + 2 * margin) // 8) * 8


def lay_ring(ref, own, from_even, from_odd, margin):
    rows, total = own.shape[0], ref.shape[0]
    even = even_tile()
    ref[rows:total] = jnp.zeros((total - rows, ref.shape[1]), F32)
    ref[:rows] = own
    for b in range(ref.shape[1] // LANES):
        at = slice(b * LANES, (b + 1) * LANES)
        one, two = (m[b * margin : (b + 1) * margin] for m in (from_even, from_odd))
        ref[rows : rows + margin, at] = jnp.where(has_below(), jnp.where(even, one, two), 0.0)
        ref[total - margin :, at] = jnp.where(has_above(), jnp.where(even, two, one), 0.0)


def block(ref, j):
    return ref[:, j * LANES : (j + 1) * LANES]


def sideways(blocks):
    shape = blocks[0].shape
    lane = lax.broadcasted_iota(jnp.int32, shape, 1)
    zero = jnp.zeros(shape, F32)
    ahead = [pltpu.roll(x, 1, 1) for x in blocks]
    back = [pltpu.roll(x, LANES - 1, 1) for x in blocks]
    for j, here in enumerate(blocks):
        before = ahead[j - 1] if j else zero
        after = back[j + 1] if j + 1 < len(blocks) else zero
        yield here, jnp.where(lane == 0, before, ahead[j]), jnp.where(lane == LANES - 1, after, back[j])


def face_weights(coef_ref, row_ref, col_ref, rows, margin):
    total, width = row_ref.shape
    blocks = width // LANES
    r = lax.broadcasted_iota(jnp.int32, (total, LANES), 0)
    inside = (
        (r < rows)
        | ((r < rows + margin) & has_below())
        | ((r >= total - margin) & has_above())
    )
    scale = jnp.where(inside, 0.125, 0.0)
    unit = jnp.where(inside, 1.0, 0.0)
    columns = [block(col_ref, j) for j in range(blocks)]
    for j, (k_col, k_left, k_right) in enumerate(sideways(columns)):
        at = slice(j * LANES, (j + 1) * LANES)
        k_row = block(row_ref, j)
        up = scale * (k_row + pltpu.roll(k_row, 1, 0))
        down = scale * (k_row + pltpu.roll(k_row, total - 1, 0))
        left = scale * (k_col + k_left)
        right = scale * (k_col + k_right)
        coef_ref[0, :, at] = unit - up - down - left - right
        coef_ref[1, :, at] = up
        coef_ref[2, :, at] = down
        coef_ref[3, :, at] = left
        coef_ref[4, :, at] = right


def one_pass(fields, coef_ref, spans):
    def weights(i, at):
        got = [coef_ref[i, span, at] for span in spans]
        return jnp.concatenate(got, axis=0) if len(got) > 1 else got[0]

    total = fields[0].shape[0]
    out = []
    for j, (here, left, right) in enumerate(sideways(fields)):
        at = slice(j * LANES, (j + 1) * LANES)
        out.append(
            weights(0, at) * here
            + weights(1, at) * pltpu.roll(here, 1, 0)
            + weights(2, at) * pltpu.roll(here, total - 1, 0)
            + weights(3, at) * left
            + weights(4, at) * right
        )
    return out


def diffuse(ring_ref, coef_ref, rows, margin):
    total, width = ring_ref.shape
    inner = margin // 8 * 8
    wide = [slice(0, total)]
    narrow = [slice(0, rows + inner), slice(total - inner, total)]
    fields = [block(ring_ref, j) for j in range(width // LANES)]
    for _ in range(margin - inner):
        fields = one_pass(fields, coef_ref, wide)
    fields = [jnp.concatenate([f[span] for span in narrow], axis=0) for f in fields]
    for _ in range(inner):
        fields = one_pass(fields, coef_ref, narrow)
    return [f[:rows] for f in fields]


def faces_kernel(margin, even_ref, odd_ref, kappa_ref, sums_ref, *refs):
    coef_ref, sums_out, one_ref, two_ref = refs[-4:]
    sums_out[...] = sums_ref[...]
    rows = kappa_ref.shape[1]
    lay_ring(one_ref, kappa_ref[0], even_ref.at[0], odd_ref.at[0], margin)
    lay_ring(two_ref, kappa_ref[1], even_ref.at[1], odd_ref.at[1], margin)
    face_weights(coef_ref, one_ref, two_ref, rows, margin)


def smooth_kernel(margin, own_ref, even_ref, odd_ref, coef_ref, out_ref, ring_ref):
    rows = own_ref.shape[0]
    lay_ring(ring_ref, own_ref[...], even_ref, odd_ref, margin)
    for j, field in enumerate(diffuse(ring_ref, coef_ref, rows, margin)):
        out_ref[:, j * LANES : (j + 1) * LANES] = field


def adjoint_kernel(margin, smooth_ref, mask_ref, sums_ref, more_ref, adjoint_ref, even_ref, odd_ref):
    weight = sums_ref[0] + more_ref[0]
    value = sums_ref[1] + more_ref[1]
    window = lanes(*window_of(my_chip(), chip_count(), mask_ref.shape[1] // LANES))
    adjoint = mask_ref[:, window].astype(F32) * (weight * smooth_ref[...] - value)
    adjoint_ref[...] = adjoint
    pack_edges(even_ref, odd_ref, adjoint, margin)


def spread_kernel(margin, own_ref, even_ref, odd_ref, coef_ref, out_ref, ring_ref):
    rows = own_ref.shape[0]
    lay_ring(ring_ref, own_ref[...], even_ref, odd_ref, margin)
    for j, field in enumerate(diffuse(ring_ref, coef_ref, rows, margin)):
        ring_ref[:rows, j * LANES : (j + 1) * LANES] = field
    own = out_ref.shape[1] // LANES
    start = window_of(my_chip(), chip_count(), own * chip_count())[0]
    out_ref[...] = ring_ref[:rows, lanes(my_chip() * own - start, own)]


def sent_last(members):
    return [0, 1] + sorted(range(2, members), key=lambda d: -(d % 2))


def result_kernel(response_ref, control_ref, *refs):
    own, out_ref = refs[0].shape[1] // LANES, refs[-1]
    refs = [refs[sent_last(len(refs) - 1).index(d)] for d in range(len(refs) - 1)]
    for d in range(len(refs) // 2):
        window = lanes((my_chip() ^ d) * own, own)
        for v in range(control_ref.shape[0]):
            mine, theirs = (response_ref[i, v][:1, :1] for i in range(2))
            out_ref[v, :, window] = (
                control_ref[v, :, window] + mine * refs[2 * d][...] + theirs * refs[2 * d + 1][...]
            )


def swap(values, axis, bit):
    count = lax.axis_size(axis)
    return lax.ppermute(values, axis, [(i, i ^ bit) for i in range(count)])


def swap_edges(even, odd):
    tiles, members = lax.axis_size("tile"), lax.axis_size("var")
    pairs = []
    for t in range(tiles):
        other = t + 1 if t % 2 else t - 1
        for q in range(members):
            to = other * members + q if 0 <= other < tiles else t * members + (q ^ 1)
            pairs.append((t * members + q, to))
    return swap(even, "tile", 1), lax.ppermute(odd, ("tile", "var"), pairs)


def deliver(chunks):
    tiles, members = lax.axis_size("tile"), lax.axis_size("var")
    got = []
    for turn, chunk in enumerate(chunks[:-1]):
        pairs = []
        for t in range(tiles):
            for q in range(members):
                offset = tiles // 2 if turn == len(chunks) - 2 else 1 + turn + (q % 2) * (tiles // 2)
                pairs.append((t * members + q, (t ^ offset) * members + q))
        got.append(lax.ppermute(chunk, ("tile", "var"), pairs))
    return got + [chunks[-1]]


def local(control, diffusivity, land_mask, panel_tile, panel_row, panel_cols, obs_values,
          obs_weights, panel_sensor, sensitivity, cross_factor):
    rows, width = control.shape[1:]
    var_dev = control.shape[0]
    tiles, members = lax.axis_size("tile"), lax.axis_size("var")
    panels, panel_width = panel_cols.shape
    slots = panels // tiles
    blocks = width // LANES
    margin = PASSES
    total = ring_rows(rows, margin)
    chips = members // 2
    size = window_of(0, chips, blocks)[1]
    field = jax.ShapeDtypeStruct((rows, width), F32)
    share = jax.ShapeDtypeStruct((rows, width // chips), F32)
    view = jax.ShapeDtypeStruct((rows, size * LANES), F32)
    view2 = jax.ShapeDtypeStruct((2, *view.shape), F32)
    edge = jax.ShapeDtypeStruct((margin * size, LANES), F32)
    edge2 = jax.ShapeDtypeStruct((2, *edge.shape), F32)
    half = jax.ShapeDtypeStruct((3 * slots + 8, panel_width), F32)
    chunks = [jax.ShapeDtypeStruct((2, *half.shape), F32)] * (tiles // 2 - 1) + [half] * 2
    line = pltpu.VMEM((1, panels), jnp.int32)

    own, other, responses, kappa, kappa_even, kappa_odd, *chunks = call(
        functools.partial(first_kernel, slots, margin),
        [field, field, jax.ShapeDtypeStruct((2, var_dev, 8, LANES), F32), view2, edge2, edge2]
        + chunks,
        [HBM] * 10,
        [
            pltpu.SMEM(sensitivity.shape, F32),
            pltpu.SMEM(cross_factor.shape, F32),
            pltpu.VMEM(control.shape, F32),
            line, line, line,
            pltpu.VMEM(obs_values.shape, F32),
            pltpu.VMEM(obs_weights.shape, F32),
            pltpu.VMEM(panel_cols.shape, jnp.int32),
            pltpu.VMEM((panels, panels), jnp.bfloat16),
            pltpu.SemaphoreType.DMA((10,)),
        ],
        cost=cost(3000),
    )(*(in_hbm(x) for x in (sensitivity, cross_factor, control, diffusivity, panel_tile.reshape(1, -1),
                            panel_row.reshape(1, -1), panel_sensor.reshape(1, -1), obs_values,
                            obs_weights, panel_cols)))

    got = deliver(chunks)
    part, *parts = call(cut_kernel, [view] * chips, [VMEM] * 2, cost=cost(200))(
        own, swap(other, "var", 1)
    )
    parts = [swap(p, "var", 2 * (d + 1)) for d, p in enumerate(parts)]
    kappa_even, kappa_odd = swap_edges(kappa_even, kappa_odd)
    smooth_in, even, odd = call(
        functools.partial(edges_kernel, margin, chips),
        [view, edge, edge],
        [VMEM] * chips + [AFTER] * len(got[:-2]),
        cost=cost(500),
    )(part, *parts, *got[:-2])
    even, odd = swap_edges(even, odd)
    sums, sums_other = call(
        functools.partial(scatter_kernel, slots, blocks),
        [view2, view2],
        [AFTER] + [VMEM] * len(got),
        [
            pltpu.VMEM((2 * rows * 2 * padded_blocks(size), LANES), F32),
            pltpu.SMEM((8 * tiles, LANES), F32),
            pltpu.SemaphoreType.DMA((tiles,)),
        ],
        cost=cost(100000),
    )(smooth_in, got[-2], *got[:-2], got[-1])
    ring = pltpu.VMEM((total, size * LANES), F32)
    coef, sums_other = call(
        functools.partial(faces_kernel, margin),
        [jax.ShapeDtypeStruct((5, total, size * LANES), F32), view2],
        [VMEM] * 4 + [AFTER] * 2,
        [ring, ring],
        cost=cost(1000),
    )(kappa_even, kappa_odd, kappa, sums_other, even, odd)
    more_sums = swap(sums_other, "var", 1)
    (smooth,) = call(
        functools.partial(smooth_kernel, margin),
        [view],
        [VMEM] * 4,
        [ring],
        cost=cost(4000),
    )(smooth_in, even, odd, coef)
    adjoint, even, odd = call(
        functools.partial(adjoint_kernel, margin), [view, edge, edge], [VMEM] * 4, cost=cost(500)
    )(smooth, land_mask, sums, more_sums)
    even, odd = swap_edges(even, odd)
    (mine,) = call(
        functools.partial(spread_kernel, margin),
        [share],
        [VMEM] * 4,
        [ring],
        cost=cost(4000),
    )(adjoint, even, odd, coef)
    shares = [mine] + [swap(mine, "var", d) for d in sent_last(members)[1:]]
    (out,) = call(
        result_kernel,
        [jax.ShapeDtypeStruct(control.shape, F32)],
        [VMEM] * (2 + members),
        cost=cost(1000),
    )(responses, control, *shares)
    return out


def solution(mesh):
    return jax.shard_map(
        local,
        mesh=mesh,
        in_specs=(
            P("var", ("grp", "tile"), None),
            P(None, ("grp", "tile"), None),
            P(("grp", "tile"), None),
            P(("grp", "tile"), None),
            P(("grp", "tile")),
            P(("grp", "tile"), None),
            P(("grp", "tile"), None),
            P(("grp", "tile"), None),
            P(("grp", "tile")),
            P(),
            P(),
        ),
        out_specs=P("var", ("grp", "tile"), None),
        check_vma=False,
    )
```

```python
import functools

import jax
import jax.numpy as jnp
from jax import lax
from jax.experimental import pallas as pl
from jax.experimental.pallas import tpu as pltpu
from jax.sharding import PartitionSpec as P

PASSES = 10
LANES = 128
GROUP = 16
VMEM = pl.BlockSpec(memory_space=pltpu.VMEM)
SMEM = pl.BlockSpec(memory_space=pltpu.SMEM)
HBM = pl.BlockSpec(memory_space=pltpu.HBM)
AFTER = pl.BlockSpec(memory_space=pl.ANY)
F32 = jnp.float32


def in_hbm(values):
    return pltpu.with_memory_space_constraint(values, pltpu.HBM)


def call(body, outs, ins, scratch=(), limit=16, cost=None):
    return pl.pallas_call(
        body,
        out_shape=outs,
        in_specs=ins,
        out_specs=[VMEM] * len(outs),
        scratch_shapes=list(scratch),
        compiler_params=pltpu.CompilerParams(vmem_limit_bytes=limit << 20),
        cost_estimate=cost,
    )


def cost(cycles):
    return pl.CostEstimate(flops=cycles * 4096, bytes_accessed=cycles * 1024, transcendentals=0)


def response(sens_ref, factor_ref, sensor, variable):
    total = sens_ref[sensor, 0] * factor_ref[0, variable]
    for u in range(1, factor_ref.shape[0]):
        total = total + sens_ref[sensor, u] * factor_ref[u, variable]
    return total


def fetch(pairs, sems):
    copies = [pltpu.make_async_copy(src, dst, sems.at[i]) for i, (src, dst) in enumerate(pairs)]
    for copy in copies:
        copy.start()
    return copies


def window_of(chip, chips, blocks):
    own = blocks // chips
    size = min(own + 2, own + chips - 1)
    return jnp.clip(chip * own - 1, 0, blocks - size), size


def my_chip():
    return lax.axis_index("var") // 2


def chip_count():
    return lax.axis_size("var") // 2


def lanes(start, size):
    return pl.ds(pl.multiple_of(start * LANES, LANES), size * LANES)


def first_kernel(slots, margin, sens_hbm, factor_hbm, control_hbm, kappa_hbm, tile_hbm, row_hbm, sensor_hbm,
                 value_hbm, weight_hbm, cols_hbm, own_ref, other_ref, response_ref, kappa_ref, even_ref,
                 odd_ref, *refs):
    chunk_refs = refs[:-11]
    (sens_ref, factor_ref, control_ref, tile_ref, row_ref, sensor_ref, value_ref, weight_ref, cols_ref,
     before_ref, sems) = refs[-11:]
    window = lanes(*window_of(my_chip(), chip_count(), own_ref.shape[1] // LANES))
    pairs = (
        (sens_hbm, sens_ref), (factor_hbm, factor_ref), (control_hbm, control_ref),
        (kappa_hbm.at[:, :, window], kappa_ref), (tile_hbm, tile_ref), (row_hbm, row_ref), (sensor_hbm, sensor_ref),
        (value_hbm, value_ref), (weight_hbm, weight_ref), (cols_hbm, cols_ref),
    )
    copies = [pltpu.make_async_copy(src, dst, sems.at[i]) for i, (src, dst) in enumerate(pairs)]
    for copy in copies:
        copy.start()
    from_panel = lax.broadcasted_iota(jnp.int32, before_ref.shape, 0)
    to_panel = lax.broadcasted_iota(jnp.int32, before_ref.shape, 1)
    before_ref[...] = jnp.where(from_panel < to_panel, 1.0, 0.0).astype(jnp.bfloat16)
    for copy in copies:
        copy.wait()

    member, mine = lax.axis_index("var"), lax.axis_index("tile")
    core = member % 2
    var_dev = control_ref.shape[0]
    for which, (sensor, out_ref) in enumerate(((core, own_ref), (1 - core, other_ref))):
        total = None
        for v in range(var_dev):
            scale = response(sens_ref, factor_ref, sensor, member * var_dev + v)
            response_ref[which, v] = jnp.full(response_ref.shape[2:], scale, F32)
            term = scale * control_ref[v]
            total = term if total is None else total + term
        out_ref[...] = total

    for i in range(2):
        pack_edges(even_ref.at[i], odd_ref.at[i], kappa_ref[i], margin)

    tiles = lax.axis_size("tile")
    full = tiles // 2 - 1
    first = jnp.where(core == 0, 2, tiles // 2 + 1)
    panels = value_ref.shape[0]
    source = tile_ref[...] ^ mine
    names = lax.broadcasted_iota(jnp.int32, (-(-tiles // 8) * 8, panels), 0)
    hits = jnp.where(names == source, 1.0, 0.0)
    ranks = jnp.dot(hits.astype(jnp.bfloat16), before_ref[...], preferred_element_type=F32)
    rank = jnp.sum(hits * ranks, axis=0, keepdims=True).astype(jnp.int32)
    parity, slot = rank % 2, rank // 2
    whole = (source >= first) & (source < first + full)
    home = source == 0
    keep = whole | ((home | (source == 1)) & (parity == core))
    half = jnp.where(whole, 2 * (source - first) + parity, jnp.where(home, tiles - 1, tiles - 2))
    place = jnp.where(keep, half * slots + slot, -1)
    spots = lax.broadcasted_iota(jnp.int32, (tiles * slots, panels), 0)
    pick = jnp.where(spots == place, 1.0, 0.0).astype(jnp.bfloat16)

    def picked(parts):
        total = None
        for part in parts:
            term = jnp.dot(pick, part.astype(jnp.bfloat16), preferred_element_type=F32)
            total = term if total is None else total + term
        return total

    cols = cols_ref[...]
    sent = (
        picked(thirds(value_ref[...])),
        picked(thirds(weight_ref[...])),
        picked(((cols // LANES * LANES).astype(F32), (cols % LANES).astype(F32))),
    )
    sub = lax.broadcasted_iota(jnp.int32, (8, panels), 0)
    lane = lax.broadcasted_iota(jnp.int32, (8, panels), 1)
    facts = jnp.where(sub == 0, row_ref[...], jnp.where(sub == 1, sensor_ref[...], 0)).astype(F32)
    meta = lax.dot_general(
        facts.astype(jnp.bfloat16), pick, (((1,), (1,)), ((), ())), preferred_element_type=F32
    )
    for i in range(tiles):
        held = jnp.sum(jnp.where(keep & (half == i), 1.0, 0.0), axis=1, keepdims=True)
        meta = jnp.where((sub == 2) & (lane == i), held, meta)
    for i in range(tiles):
        out_ref = chunk_refs[i // 2].at[i % 2] if i < 2 * full else chunk_refs[i - full]
        for part, rows in enumerate(sent):
            out_ref[part * slots : (part + 1) * slots] = rows[i * slots : (i + 1) * slots]
        out_ref[3 * slots :] = meta


def thirds(values):
    top = values.astype(jnp.bfloat16).astype(F32)
    rest = values - top
    middle = rest.astype(jnp.bfloat16).astype(F32)
    return top, middle, rest - middle


def pieces(values):
    top = values.astype(jnp.bfloat16).astype(F32)
    return top, values - top


def scatter_kernel(slots, blocks_all, after_ref, *refs):
    got_refs, (own_ref, other_ref, acc_ref, meta_ref, sems) = refs[:-5], refs[-5:]
    core = lax.axis_index("var") % 2
    got_refs = [r.at[i] for r in got_refs[1:-1] for i in (0, 1)] + [got_refs[0], got_refs[-1]]
    size_of_group = min(GROUP, slots)
    copies = [
        pltpu.make_async_copy(ref.at[pl.ds(3 * slots, 8)], meta_ref.at[pl.ds(8 * s, 8)], sems.at[s])
        for s, ref in enumerate(got_refs)
    ]
    for copy in copies:
        copy.start()
    rows = own_ref.shape[1]
    start, size = window_of(my_chip(), chip_count(), blocks_all)
    per_kind = padded_blocks(size)
    tall = 2 * per_kind
    acc_ref[...] = jnp.zeros(acc_ref.shape, F32)
    place = lax.broadcasted_iota(jnp.int32, (tall, LANES), 0)
    is_weight = place < per_kind
    place = jnp.where(is_weight, place, place - per_kind) + start
    lane_ids = lax.broadcasted_iota(jnp.int32, (LANES, LANES), 0).astype(F32).astype(jnp.bfloat16)
    one, zero = jnp.bfloat16(1), jnp.bfloat16(0)
    sub = lax.broadcasted_iota(jnp.int32, (size_of_group, LANES), 0)
    blank = jnp.zeros((2 * tall, LANES), jnp.bfloat16)
    for copy in copies:
        copy.wait()

    def load(s, base):
        got_ref = got_refs[s]
        count = meta_ref[8 * s + 2, s].astype(jnp.int32)
        value = got_ref[pl.ds(base, size_of_group), :]
        weight = got_ref[pl.ds(slots + base, size_of_group), :]
        cell = got_ref[pl.ds(2 * slots + base, size_of_group), :].astype(jnp.int32)
        weight = jnp.where(sub + base < count, weight, 0.0)
        return pieces(weight), pieces(weight * value), (cell % LANES).astype(F32), cell // LANES

    def one_hots(loaded, i):
        weights, values, low, high = loaded
        here = place == high[i : i + 1]
        rows_of = [
            jnp.where(here, jnp.where(is_weight, w[i : i + 1], v[i : i + 1]), 0.0)
            for w, v in zip(weights, values)
        ]
        left = jnp.concatenate(rows_of, axis=0).astype(jnp.bfloat16)
        column = jnp.broadcast_to(low[i : i + 1], (16, LANES)).astype(jnp.bfloat16)
        column = jnp.concatenate([column] * (LANES // 16), axis=0)
        return left, jnp.where(lane_ids == column, one, zero)

    def step(chosen, g, carry):
        base = pl.multiple_of(g * size_of_group, size_of_group)
        loaded = {s: load(s, base) for s in chosen}
        for k in range(size_of_group):
            for pair in zip(chosen[::2], chosen[1::2]):
                hots = [one_hots(loaded[s], k) for s in pair]
                left = jnp.concatenate(
                    [
                        jnp.concatenate([hots[0][0], blank], axis=1),
                        jnp.concatenate([blank, hots[1][0]], axis=1),
                    ],
                    axis=0,
                )
                both = lax.dot_general(
                    left, jnp.concatenate([hots[0][1], hots[1][1]], axis=1), (((1,), (1,)), ((), ())),
                    preferred_element_type=F32,
                )
                for i, s in enumerate(pair):
                    row = meta_ref[8 * s, s * slots + base + k].astype(jnp.int32)
                    sensor = meta_ref[8 * s + 1, s * slots + base + k].astype(jnp.int32)
                    at = pl.multiple_of((sensor * rows + row) * tall, 8)
                    mine = both[2 * i * tall : 2 * (i + 1) * tall]
                    acc_ref[pl.ds(at, tall), :] += mine[:tall] + mine[tall:]
        return carry

    for s in range(0, len(got_refs), 4):
        chosen = list(range(s, s + 4))
        most = meta_ref[8 * s + 2, s]
        for other in chosen[1:]:
            most = jnp.maximum(most, meta_ref[8 * other + 2, other])
        turns = (most.astype(jnp.int32) + size_of_group - 1) // size_of_group
        lax.fori_loop(0, turns, functools.partial(step, chosen), 0)
    for sensor, out_ref in ((core, own_ref), (1 - core, other_ref)):
        begin = sensor * rows * tall
        for kind in range(2):
            for b in range(size):
                out_ref[kind, :, b * LANES : (b + 1) * LANES] = acc_ref[
                    pl.ds(begin + kind * per_kind + b, rows, stride=tall), :
                ]


def padded_blocks(size):
    return -(-size // 4) * 4


def even_tile():
    return lax.axis_index("tile") % 2 == 0


def has_above():
    return lax.axis_index("tile") > 0


def has_below():
    return lax.axis_index("tile") + 1 < lax.axis_size("tile")


def pack_edges(even_ref, odd_ref, rows_value, margin):
    rows, width = rows_value.shape
    even = even_tile()
    for b in range(width // LANES):
        at = slice(b * LANES, (b + 1) * LANES)
        head, tail = rows_value[:margin, at], rows_value[rows - margin :, at]
        even_ref[b * margin : (b + 1) * margin] = jnp.where(even, tail, head)
        odd_ref[b * margin : (b + 1) * margin] = jnp.where(even, head, tail)


def cut_kernel(first_ref, second_ref, mine_ref, *out_refs):
    chip, chips, blocks = my_chip(), chip_count(), first_ref.shape[1] // LANES
    for d, out_ref in enumerate((mine_ref, *out_refs)):
        window = lanes(*window_of(chip ^ d, chips, blocks))
        out_ref[...] = first_ref[:, window] + second_ref[:, window]


def edges_kernel(margin, *refs):
    terms, (total_ref, even_ref, odd_ref) = refs[:-3], refs[-3:]
    total = terms[0][...]
    for term in terms[1:]:
        total = total + term[...]
    total_ref[...] = total
    pack_edges(even_ref, odd_ref, total, margin)


def ring_rows(rows, margin):
    return -(-(rows + 2 * margin) // 8) * 8


def lay_ring(ref, own, from_even, from_odd, margin):
    rows, total = own.shape[0], ref.shape[0]
    even = even_tile()
    ref[rows:total] = jnp.zeros((total - rows, ref.shape[1]), F32)
    ref[:rows] = own
    for b in range(ref.shape[1] // LANES):
        at = slice(b * LANES, (b + 1) * LANES)
        one, two = (m[b * margin : (b + 1) * margin] for m in (from_even, from_odd))
        ref[rows : rows + margin, at] = jnp.where(has_below(), jnp.where(even, one, two), 0.0)
        ref[total - margin :, at] = jnp.where(has_above(), jnp.where(even, two, one), 0.0)


def block(ref, j):
    return ref[:, j * LANES : (j + 1) * LANES]


def sideways(blocks):
    shape = blocks[0].shape
    lane = lax.broadcasted_iota(jnp.int32, shape, 1)
    zero = jnp.zeros(shape, F32)
    ahead = [pltpu.roll(x, 1, 1) for x in blocks]
    back = [pltpu.roll(x, LANES - 1, 1) for x in blocks]
    for j, here in enumerate(blocks):
        before = ahead[j - 1] if j else zero
        after = back[j + 1] if j + 1 < len(blocks) else zero
        yield here, jnp.where(lane == 0, before, ahead[j]), jnp.where(lane == LANES - 1, after, back[j])


def face_weights(coef_ref, row_ref, col_ref, rows, margin):
    total, width = row_ref.shape
    blocks = width // LANES
    r = lax.broadcasted_iota(jnp.int32, (total, LANES), 0)
    inside = (
        (r < rows)
        | ((r < rows + margin) & has_below())
        | ((r >= total - margin) & has_above())
    )
    scale = jnp.where(inside, 0.125, 0.0)
    unit = jnp.where(inside, 1.0, 0.0)
    columns = [block(col_ref, j) for j in range(blocks)]
    for j, (k_col, k_left, k_right) in enumerate(sideways(columns)):
        at = slice(j * LANES, (j + 1) * LANES)
        k_row = block(row_ref, j)
        up = scale * (k_row + pltpu.roll(k_row, 1, 0))
        down = scale * (k_row + pltpu.roll(k_row, total - 1, 0))
        left = scale * (k_col + k_left)
        right = scale * (k_col + k_right)
        coef_ref[0, :, at] = unit - up - down - left - right
        coef_ref[1, :, at] = up
        coef_ref[2, :, at] = down
        coef_ref[3, :, at] = left
        coef_ref[4, :, at] = right


def one_pass(fields, coef_ref, spans):
    def weights(i, at):
        got = [coef_ref[i, span, at] for span in spans]
        return jnp.concatenate(got, axis=0) if len(got) > 1 else got[0]

    total = fields[0].shape[0]
    out = []
    for j, (here, left, right) in enumerate(sideways(fields)):
        at = slice(j * LANES, (j + 1) * LANES)
        out.append(
            weights(0, at) * here
            + weights(1, at) * pltpu.roll(here, 1, 0)
            + weights(2, at) * pltpu.roll(here, total - 1, 0)
            + weights(3, at) * left
            + weights(4, at) * right
        )
    return out


def diffuse(ring_ref, coef_ref, rows, margin):
    total, width = ring_ref.shape
    inner = margin // 8 * 8
    wide = [slice(0, total)]
    narrow = [slice(0, rows + inner), slice(total - inner, total)]
    fields = [block(ring_ref, j) for j in range(width // LANES)]
    for _ in range(margin - inner):
        fields = one_pass(fields, coef_ref, wide)
    fields = [jnp.concatenate([f[span] for span in narrow], axis=0) for f in fields]
    for _ in range(inner):
        fields = one_pass(fields, coef_ref, narrow)
    return [f[:rows] for f in fields]


def faces_kernel(margin, even_ref, odd_ref, kappa_ref, sums_ref, *refs):
    coef_ref, sums_out, one_ref, two_ref = refs[-4:]
    sums_out[...] = sums_ref[...]
    rows = kappa_ref.shape[1]
    lay_ring(one_ref, kappa_ref[0], even_ref.at[0], odd_ref.at[0], margin)
    lay_ring(two_ref, kappa_ref[1], even_ref.at[1], odd_ref.at[1], margin)
    face_weights(coef_ref, one_ref, two_ref, rows, margin)


def smooth_kernel(margin, own_ref, even_ref, odd_ref, coef_ref, out_ref, ring_ref):
    rows = own_ref.shape[0]
    lay_ring(ring_ref, own_ref[...], even_ref, odd_ref, margin)
    for j, field in enumerate(diffuse(ring_ref, coef_ref, rows, margin)):
        out_ref[:, j * LANES : (j + 1) * LANES] = field


def adjoint_kernel(margin, smooth_ref, mask_ref, sums_ref, more_ref, adjoint_ref, even_ref, odd_ref):
    weight = sums_ref[0] + more_ref[0]
    value = sums_ref[1] + more_ref[1]
    window = lanes(*window_of(my_chip(), chip_count(), mask_ref.shape[1] // LANES))
    adjoint = mask_ref[:, window].astype(F32) * (weight * smooth_ref[...] - value)
    adjoint_ref[...] = adjoint
    pack_edges(even_ref, odd_ref, adjoint, margin)


def spread_kernel(margin, own_ref, even_ref, odd_ref, coef_ref, out_ref, ring_ref):
    rows = own_ref.shape[0]
    lay_ring(ring_ref, own_ref[...], even_ref, odd_ref, margin)
    for j, field in enumerate(diffuse(ring_ref, coef_ref, rows, margin)):
        ring_ref[:rows, j * LANES : (j + 1) * LANES] = field
    own = out_ref.shape[1] // LANES
    start = window_of(my_chip(), chip_count(), own * chip_count())[0]
    out_ref[...] = ring_ref[:rows, lanes(my_chip() * own - start, own)]


def sent_last(members):
    return [0, 1] + sorted(range(2, members), key=lambda d: -(d % 2))


def result_kernel(response_ref, control_ref, *refs):
    own, out_ref = refs[0].shape[1] // LANES, refs[-1]
    refs = [refs[sent_last(len(refs) - 1).index(d)] for d in range(len(refs) - 1)]
    for d in range(len(refs) // 2):
        window = lanes((my_chip() ^ d) * own, own)
        for v in range(control_ref.shape[0]):
            mine, theirs = (response_ref[i, v][:1, :1] for i in range(2))
            out_ref[v, :, window] = (
                control_ref[v, :, window] + mine * refs[2 * d][...] + theirs * refs[2 * d + 1][...]
            )


def swap(values, axis, bit):
    count = lax.axis_size(axis)
    return lax.ppermute(values, axis, [(i, i ^ bit) for i in range(count)])


def swap_edges(even, odd):
    tiles, members = lax.axis_size("tile"), lax.axis_size("var")
    pairs = []
    for t in range(tiles):
        other = t + 1 if t % 2 else t - 1
        for q in range(members):
            to = other * members + q if 0 <= other < tiles else t * members + (q ^ 1)
            pairs.append((t * members + q, to))
    return swap(even, "tile", 1), lax.ppermute(odd, ("tile", "var"), pairs)


def deliver(chunks):
    tiles, members = lax.axis_size("tile"), lax.axis_size("var")
    got = []
    for turn, chunk in enumerate(chunks[:-1]):
        pairs = []
        for t in range(tiles):
            for q in range(members):
                offset = 1 if turn == len(chunks) - 2 else 2 + turn + (q % 2) * (tiles // 2 - 1)
                pairs.append((t * members + q, (t ^ offset) * members + q))
        got.append(lax.ppermute(chunk, ("tile", "var"), pairs))
    return got + [chunks[-1]]


def local(control, diffusivity, land_mask, panel_tile, panel_row, panel_cols, obs_values,
          obs_weights, panel_sensor, sensitivity, cross_factor):
    rows, width = control.shape[1:]
    var_dev = control.shape[0]
    tiles, members = lax.axis_size("tile"), lax.axis_size("var")
    panels, panel_width = panel_cols.shape
    slots = panels // tiles
    blocks = width // LANES
    margin = PASSES
    total = ring_rows(rows, margin)
    chips = members // 2
    size = window_of(0, chips, blocks)[1]
    field = jax.ShapeDtypeStruct((rows, width), F32)
    share = jax.ShapeDtypeStruct((rows, width // chips), F32)
    view = jax.ShapeDtypeStruct((rows, size * LANES), F32)
    view2 = jax.ShapeDtypeStruct((2, *view.shape), F32)
    edge = jax.ShapeDtypeStruct((margin * size, LANES), F32)
    edge2 = jax.ShapeDtypeStruct((2, *edge.shape), F32)
    half = jax.ShapeDtypeStruct((3 * slots + 8, panel_width), F32)
    chunks = [jax.ShapeDtypeStruct((2, *half.shape), F32)] * (tiles // 2 - 1) + [half] * 2
    line = pltpu.VMEM((1, panels), jnp.int32)

    own, other, responses, kappa, kappa_even, kappa_odd, *chunks = call(
        functools.partial(first_kernel, slots, margin),
        [field, field, jax.ShapeDtypeStruct((2, var_dev, 8, LANES), F32), view2, edge2, edge2]
        + chunks,
        [HBM] * 10,
        [
            pltpu.SMEM(sensitivity.shape, F32),
            pltpu.SMEM(cross_factor.shape, F32),
            pltpu.VMEM(control.shape, F32),
            line, line, line,
            pltpu.VMEM(obs_values.shape, F32),
            pltpu.VMEM(obs_weights.shape, F32),
            pltpu.VMEM(panel_cols.shape, jnp.int32),
            pltpu.VMEM((panels, panels), jnp.bfloat16),
            pltpu.SemaphoreType.DMA((10,)),
        ],
        cost=cost(3000),
    )(*(in_hbm(x) for x in (sensitivity, cross_factor, control, diffusivity, panel_tile.reshape(1, -1),
                            panel_row.reshape(1, -1), panel_sensor.reshape(1, -1), obs_values,
                            obs_weights, panel_cols)))

    got = deliver(chunks)
    part, *parts = call(cut_kernel, [view] * chips, [VMEM] * 2, cost=cost(200))(
        own, swap(other, "var", 1)
    )
    parts = [swap(p, "var", 2 * (d + 1)) for d, p in enumerate(parts)]
    kappa_even, kappa_odd = swap_edges(kappa_even, kappa_odd)
    smooth_in, even, odd = call(
        functools.partial(edges_kernel, margin), [view, edge, edge], [VMEM] * chips, cost=cost(500)
    )(part, *parts)
    even, odd = swap_edges(even, odd)
    sums, sums_other = call(
        functools.partial(scatter_kernel, slots, blocks),
        [view2, view2],
        [AFTER] + [VMEM] * len(got),
        [
            pltpu.VMEM((2 * rows * 2 * padded_blocks(size), LANES), F32),
            pltpu.SMEM((8 * tiles, LANES), F32),
            pltpu.SemaphoreType.DMA((tiles,)),
        ],
        cost=cost(100000),
    )(smooth_in, got[-2], *got[:-2], got[-1])
    ring = pltpu.VMEM((total, size * LANES), F32)
    coef, sums_other = call(
        functools.partial(faces_kernel, margin),
        [jax.ShapeDtypeStruct((5, total, size * LANES), F32), view2],
        [VMEM] * 4 + [AFTER] * 2,
        [ring, ring],
        cost=cost(1000),
    )(kappa_even, kappa_odd, kappa, sums_other, even, odd)
    more_sums = swap(sums_other, "var", 1)
    (smooth,) = call(
        functools.partial(smooth_kernel, margin),
        [view],
        [VMEM] * 4,
        [ring],
        cost=cost(4000),
    )(smooth_in, even, odd, coef)
    adjoint, even, odd = call(
        functools.partial(adjoint_kernel, margin), [view, edge, edge], [VMEM] * 4, cost=cost(500)
    )(smooth, land_mask, sums, more_sums)
    even, odd = swap_edges(even, odd)
    (mine,) = call(
        functools.partial(spread_kernel, margin),
        [share],
        [VMEM] * 4,
        [ring],
        cost=cost(4000),
    )(adjoint, even, odd, coef)
    shares = [mine] + [swap(mine, "var", d) for d in sent_last(members)[1:]]
    (out,) = call(
        result_kernel,
        [jax.ShapeDtypeStruct(control.shape, F32)],
        [VMEM] * (2 + members),
        cost=cost(1000),
    )(responses, control, *shares)
    return out


def solution(mesh):
    return jax.shard_map(
        local,
        mesh=mesh,
        in_specs=(
            P("var", ("grp", "tile"), None),
            P(None, ("grp", "tile"), None),
            P(("grp", "tile"), None),
            P(("grp", "tile"), None),
            P(("grp", "tile")),
            P(("grp", "tile"), None),
            P(("grp", "tile"), None),
            P(("grp", "tile"), None),
            P(("grp", "tile")),
            P(),
            P(),
        ),
        out_specs=P("var", ("grp", "tile"), None),
        check_vma=False,
    )
```

```python
import functools

import jax
import jax.numpy as jnp
from jax import lax
from jax.experimental import pallas as pl
from jax.experimental.pallas import tpu as pltpu
from jax.sharding import PartitionSpec as P

PASSES = 10
LANES = 128
GROUP = 16
VMEM = pl.BlockSpec(memory_space=pltpu.VMEM)
SMEM = pl.BlockSpec(memory_space=pltpu.SMEM)
HBM = pl.BlockSpec(memory_space=pltpu.HBM)
AFTER = pl.BlockSpec(memory_space=pl.ANY)
F32 = jnp.float32


def in_hbm(values):
    return pltpu.with_memory_space_constraint(values, pltpu.HBM)


def call(body, outs, ins, scratch=(), limit=16, cost=None):
    return pl.pallas_call(
        body,
        out_shape=outs,
        in_specs=ins,
        out_specs=[VMEM] * len(outs),
        scratch_shapes=list(scratch),
        compiler_params=pltpu.CompilerParams(vmem_limit_bytes=limit << 20),
        cost_estimate=cost,
    )


def cost(cycles):
    return pl.CostEstimate(flops=cycles * 4096, bytes_accessed=cycles * 1024, transcendentals=0)


def response(sens_ref, factor_ref, sensor, variable):
    total = sens_ref[sensor, 0] * factor_ref[0, variable]
    for u in range(1, factor_ref.shape[0]):
        total = total + sens_ref[sensor, u] * factor_ref[u, variable]
    return total


def fetch(pairs, sems):
    copies = [pltpu.make_async_copy(src, dst, sems.at[i]) for i, (src, dst) in enumerate(pairs)]
    for copy in copies:
        copy.start()
    return copies


def window_of(chip, chips, blocks):
    own = blocks // chips
    size = min(own + 2, own + chips - 1)
    return jnp.clip(chip * own - 1, 0, blocks - size), size


def my_chip():
    return lax.axis_index("var") // 2


def chip_count():
    return lax.axis_size("var") // 2


def lanes(start, size):
    return pl.ds(pl.multiple_of(start * LANES, LANES), size * LANES)


def first_kernel(slots, margin, sens_hbm, factor_hbm, control_hbm, kappa_hbm, tile_hbm, row_hbm, sensor_hbm,
                 value_hbm, weight_hbm, cols_hbm, own_ref, other_ref, response_ref, kappa_ref, even_ref,
                 odd_ref, *refs):
    chunk_refs = refs[:-11]
    (sens_ref, factor_ref, control_ref, tile_ref, row_ref, sensor_ref, value_ref, weight_ref, cols_ref,
     before_ref, sems) = refs[-11:]
    window = lanes(*window_of(my_chip(), chip_count(), own_ref.shape[1] // LANES))
    pairs = (
        (sens_hbm, sens_ref), (factor_hbm, factor_ref), (control_hbm, control_ref),
        (kappa_hbm.at[:, :, window], kappa_ref), (tile_hbm, tile_ref), (row_hbm, row_ref), (sensor_hbm, sensor_ref),
        (value_hbm, value_ref), (weight_hbm, weight_ref), (cols_hbm, cols_ref),
    )
    copies = [pltpu.make_async_copy(src, dst, sems.at[i]) for i, (src, dst) in enumerate(pairs)]
    for copy in copies:
        copy.start()
    from_panel = lax.broadcasted_iota(jnp.int32, before_ref.shape, 0)
    to_panel = lax.broadcasted_iota(jnp.int32, before_ref.shape, 1)
    before_ref[...] = jnp.where(from_panel < to_panel, 1.0, 0.0).astype(jnp.bfloat16)
    for copy in copies:
        copy.wait()

    member, mine = lax.axis_index("var"), lax.axis_index("tile")
    core = member % 2
    var_dev = control_ref.shape[0]
    for which, (sensor, out_ref) in enumerate(((core, own_ref), (1 - core, other_ref))):
        total = None
        for v in range(var_dev):
            scale = response(sens_ref, factor_ref, sensor, member * var_dev + v)
            response_ref[which, v] = jnp.full(response_ref.shape[2:], scale, F32)
            term = scale * control_ref[v]
            total = term if total is None else total + term
        out_ref[...] = total

    for i in range(2):
        pack_edges(even_ref.at[i], odd_ref.at[i], kappa_ref[i], margin)

    tiles = lax.axis_size("tile")
    full = tiles // 2 - 1
    first = jnp.where(core == 0, 2, tiles // 2 + 1)
    panels = value_ref.shape[0]
    source = tile_ref[...] ^ mine
    names = lax.broadcasted_iota(jnp.int32, (-(-tiles // 8) * 8, panels), 0)
    hits = jnp.where(names == source, 1.0, 0.0)
    ranks = jnp.dot(hits.astype(jnp.bfloat16), before_ref[...], preferred_element_type=F32)
    rank = jnp.sum(hits * ranks, axis=0, keepdims=True).astype(jnp.int32)
    parity, slot = rank % 2, rank // 2
    whole = (source >= first) & (source < first + full)
    home = source == 0
    keep = whole | ((home | (source == 1)) & (parity == core))
    half = jnp.where(whole, 2 * (source - first) + parity, jnp.where(home, tiles - 1, tiles - 2))
    place = jnp.where(keep, half * slots + slot, -1)
    spots = lax.broadcasted_iota(jnp.int32, (tiles * slots, panels), 0)
    pick = jnp.where(spots == place, 1.0, 0.0).astype(jnp.bfloat16)

    def picked(parts):
        total = None
        for part in parts:
            term = jnp.dot(pick, part.astype(jnp.bfloat16), preferred_element_type=F32)
            total = term if total is None else total + term
        return total

    cols = cols_ref[...]
    sent = (
        picked(thirds(value_ref[...])),
        picked(thirds(weight_ref[...])),
        picked(((cols // LANES * LANES).astype(F32), (cols % LANES).astype(F32))),
    )
    sub = lax.broadcasted_iota(jnp.int32, (8, panels), 0)
    lane = lax.broadcasted_iota(jnp.int32, (8, panels), 1)
    facts = jnp.where(sub == 0, row_ref[...], jnp.where(sub == 1, sensor_ref[...], 0)).astype(F32)
    meta = lax.dot_general(
        facts.astype(jnp.bfloat16), pick, (((1,), (1,)), ((), ())), preferred_element_type=F32
    )
    for i in range(tiles):
        held = jnp.sum(jnp.where(keep & (half == i), 1.0, 0.0), axis=1, keepdims=True)
        meta = jnp.where((sub == 2) & (lane == i), held, meta)
    for i in range(tiles):
        out_ref = chunk_refs[i // 2].at[i % 2] if i < 2 * full else chunk_refs[i - full]
        for part, rows in enumerate(sent):
            out_ref[part * slots : (part + 1) * slots] = rows[i * slots : (i + 1) * slots]
        out_ref[3 * slots :] = meta


def thirds(values):
    top = values.astype(jnp.bfloat16).astype(F32)
    rest = values - top
    middle = rest.astype(jnp.bfloat16).astype(F32)
    return top, middle, rest - middle


def pieces(values):
    top = values.astype(jnp.bfloat16).astype(F32)
    return top, values - top


def scatter_kernel(slots, blocks_all, after_ref, *refs):
    got_refs, (own_ref, other_ref, acc_ref, meta_ref, sems) = refs[:-5], refs[-5:]
    core = lax.axis_index("var") % 2
    got_refs = [r.at[i] for r in got_refs[1:-1] for i in (0, 1)] + [got_refs[0], got_refs[-1]]
    size_of_group = min(GROUP, slots)
    copies = [
        pltpu.make_async_copy(ref.at[pl.ds(3 * slots, 8)], meta_ref.at[pl.ds(8 * s, 8)], sems.at[s])
        for s, ref in enumerate(got_refs)
    ]
    for copy in copies:
        copy.start()
    rows = own_ref.shape[1]
    start, size = window_of(my_chip(), chip_count(), blocks_all)
    per_kind = padded_blocks(size)
    tall = 2 * per_kind
    acc_ref[...] = jnp.zeros(acc_ref.shape, F32)
    place = lax.broadcasted_iota(jnp.int32, (tall, LANES), 0)
    is_weight = place < per_kind
    place = jnp.where(is_weight, place, place - per_kind) + start
    lane_ids = lax.broadcasted_iota(jnp.int32, (LANES, LANES), 0).astype(F32).astype(jnp.bfloat16)
    one, zero = jnp.bfloat16(1), jnp.bfloat16(0)
    sub = lax.broadcasted_iota(jnp.int32, (size_of_group, LANES), 0)
    blank = jnp.zeros((2 * tall, LANES), jnp.bfloat16)
    for copy in copies:
        copy.wait()

    def load(s, base):
        got_ref = got_refs[s]
        count = meta_ref[8 * s + 2, s].astype(jnp.int32)
        value = got_ref[pl.ds(base, size_of_group), :]
        weight = got_ref[pl.ds(slots + base, size_of_group), :]
        cell = got_ref[pl.ds(2 * slots + base, size_of_group), :].astype(jnp.int32)
        weight = jnp.where(sub + base < count, weight, 0.0)
        return pieces(weight), pieces(weight * value), (cell % LANES).astype(F32), cell // LANES

    def one_hots(loaded, i):
        weights, values, low, high = loaded
        here = place == high[i : i + 1]
        rows_of = [
            jnp.where(here, jnp.where(is_weight, w[i : i + 1], v[i : i + 1]), 0.0)
            for w, v in zip(weights, values)
        ]
        left = jnp.concatenate(rows_of, axis=0).astype(jnp.bfloat16)
        column = jnp.broadcast_to(low[i : i + 1], (16, LANES)).astype(jnp.bfloat16)
        column = jnp.concatenate([column] * (LANES // 16), axis=0)
        return left, jnp.where(lane_ids == column, one, zero)

    def step(chosen, g, carry):
        base = pl.multiple_of(g * size_of_group, size_of_group)
        loaded = {s: load(s, base) for s in chosen}
        for k in range(size_of_group):
            for pair in zip(chosen[::2], chosen[1::2]):
                hots = [one_hots(loaded[s], k) for s in pair]
                left = jnp.concatenate(
                    [
                        jnp.concatenate([hots[0][0], blank], axis=1),
                        jnp.concatenate([blank, hots[1][0]], axis=1),
                    ],
                    axis=0,
                )
                both = lax.dot_general(
                    left, jnp.concatenate([hots[0][1], hots[1][1]], axis=1), (((1,), (1,)), ((), ())),
                    preferred_element_type=F32,
                )
                for i, s in enumerate(pair):
                    row = meta_ref[8 * s, s * slots + base + k].astype(jnp.int32)
                    sensor = meta_ref[8 * s + 1, s * slots + base + k].astype(jnp.int32)
                    at = pl.multiple_of((sensor * rows + row) * tall, 8)
                    mine = both[2 * i * tall : 2 * (i + 1) * tall]
                    acc_ref[pl.ds(at, tall), :] += mine[:tall] + mine[tall:]
        return carry

    for s in range(0, len(got_refs), 4):
        chosen = list(range(s, s + 4))
        most = meta_ref[8 * s + 2, s]
        for other in chosen[1:]:
            most = jnp.maximum(most, meta_ref[8 * other + 2, other])
        turns = (most.astype(jnp.int32) + size_of_group - 1) // size_of_group
        lax.fori_loop(0, turns, functools.partial(step, chosen), 0)
    for sensor, out_ref in ((core, own_ref), (1 - core, other_ref)):
        begin = sensor * rows * tall
        for kind in range(2):
            for b in range(size):
                out_ref[kind, :, b * LANES : (b + 1) * LANES] = acc_ref[
                    pl.ds(begin + kind * per_kind + b, rows, stride=tall), :
                ]


def padded_blocks(size):
    return -(-size // 4) * 4


def even_tile():
    return lax.axis_index("tile") % 2 == 0


def has_above():
    return lax.axis_index("tile") > 0


def has_below():
    return lax.axis_index("tile") + 1 < lax.axis_size("tile")


def pack_edges(even_ref, odd_ref, rows_value, margin):
    rows, width = rows_value.shape
    even = even_tile()
    for b in range(width // LANES):
        at = slice(b * LANES, (b + 1) * LANES)
        head, tail = rows_value[:margin, at], rows_value[rows - margin :, at]
        even_ref[b * margin : (b + 1) * margin] = jnp.where(even, tail, head)
        odd_ref[b * margin : (b + 1) * margin] = jnp.where(even, head, tail)


def cut_kernel(first_ref, second_ref, mine_ref, *out_refs):
    chip, chips, blocks = my_chip(), chip_count(), first_ref.shape[1] // LANES
    for d, out_ref in enumerate((mine_ref, *out_refs)):
        window = lanes(*window_of(chip ^ d, chips, blocks))
        out_ref[...] = first_ref[:, window] + second_ref[:, window]


def edges_kernel(margin, *refs):
    terms, (total_ref, even_ref, odd_ref) = refs[:-3], refs[-3:]
    total = terms[0][...]
    for term in terms[1:]:
        total = total + term[...]
    total_ref[...] = total
    pack_edges(even_ref, odd_ref, total, margin)


def ring_rows(rows, margin):
    return -(-(rows + 2 * margin) // 8) * 8


def lay_ring(ref, own, from_even, from_odd, margin):
    rows, total = own.shape[0], ref.shape[0]
    even = even_tile()
    ref[rows:total] = jnp.zeros((total - rows, ref.shape[1]), F32)
    ref[:rows] = own
    for b in range(ref.shape[1] // LANES):
        at = slice(b * LANES, (b + 1) * LANES)
        one, two = (m[b * margin : (b + 1) * margin] for m in (from_even, from_odd))
        ref[rows : rows + margin, at] = jnp.where(has_below(), jnp.where(even, one, two), 0.0)
        ref[total - margin :, at] = jnp.where(has_above(), jnp.where(even, two, one), 0.0)


def block(ref, j):
    return ref[:, j * LANES : (j + 1) * LANES]


def sideways(blocks):
    shape = blocks[0].shape
    lane = lax.broadcasted_iota(jnp.int32, shape, 1)
    zero = jnp.zeros(shape, F32)
    ahead = [pltpu.roll(x, 1, 1) for x in blocks]
    back = [pltpu.roll(x, LANES - 1, 1) for x in blocks]
    for j, here in enumerate(blocks):
        before = ahead[j - 1] if j else zero
        after = back[j + 1] if j + 1 < len(blocks) else zero
        yield here, jnp.where(lane == 0, before, ahead[j]), jnp.where(lane == LANES - 1, after, back[j])


def face_weights(coef_ref, row_ref, col_ref, rows, margin):
    total, width = row_ref.shape
    blocks = width // LANES
    r = lax.broadcasted_iota(jnp.int32, (total, LANES), 0)
    inside = (
        (r < rows)
        | ((r < rows + margin) & has_below())
        | ((r >= total - margin) & has_above())
    )
    scale = jnp.where(inside, 0.125, 0.0)
    unit = jnp.where(inside, 1.0, 0.0)
    columns = [block(col_ref, j) for j in range(blocks)]
    for j, (k_col, k_left, k_right) in enumerate(sideways(columns)):
        at = slice(j * LANES, (j + 1) * LANES)
        k_row = block(row_ref, j)
        up = scale * (k_row + pltpu.roll(k_row, 1, 0))
        down = scale * (k_row + pltpu.roll(k_row, total - 1, 0))
        left = scale * (k_col + k_left)
        right = scale * (k_col + k_right)
        coef_ref[0, :, at] = unit - up - down - left - right
        coef_ref[1, :, at] = up
        coef_ref[2, :, at] = down
        coef_ref[3, :, at] = left
        coef_ref[4, :, at] = right


def one_pass(fields, coef_ref, spans):
    def weights(i, at):
        got = [coef_ref[i, span, at] for span in spans]
        return jnp.concatenate(got, axis=0) if len(got) > 1 else got[0]

    total = fields[0].shape[0]
    out = []
    for j, (here, left, right) in enumerate(sideways(fields)):
        at = slice(j * LANES, (j + 1) * LANES)
        out.append(
            weights(0, at) * here
            + weights(1, at) * pltpu.roll(here, 1, 0)
            + weights(2, at) * pltpu.roll(here, total - 1, 0)
            + weights(3, at) * left
            + weights(4, at) * right
        )
    return out


def diffuse(ring_ref, coef_ref, rows, margin):
    total, width = ring_ref.shape
    inner = margin // 8 * 8
    wide = [slice(0, total)]
    narrow = [slice(0, rows + inner), slice(total - inner, total)]
    fields = [block(ring_ref, j) for j in range(width // LANES)]
    for _ in range(margin - inner):
        fields = one_pass(fields, coef_ref, wide)
    fields = [jnp.concatenate([f[span] for span in narrow], axis=0) for f in fields]
    for _ in range(inner):
        fields = one_pass(fields, coef_ref, narrow)
    return [f[:rows] for f in fields]


def faces_kernel(margin, even_ref, odd_ref, kappa_ref, sums_ref, *refs):
    coef_ref, sums_out, one_ref, two_ref = refs[-4:]
    sums_out[...] = sums_ref[...]
    rows = kappa_ref.shape[1]
    lay_ring(one_ref, kappa_ref[0], even_ref.at[0], odd_ref.at[0], margin)
    lay_ring(two_ref, kappa_ref[1], even_ref.at[1], odd_ref.at[1], margin)
    face_weights(coef_ref, one_ref, two_ref, rows, margin)


def smooth_kernel(margin, own_ref, even_ref, odd_ref, coef_ref, out_ref, ring_ref):
    rows = own_ref.shape[0]
    lay_ring(ring_ref, own_ref[...], even_ref, odd_ref, margin)
    for j, field in enumerate(diffuse(ring_ref, coef_ref, rows, margin)):
        out_ref[:, j * LANES : (j + 1) * LANES] = field


def adjoint_kernel(margin, smooth_ref, mask_ref, sums_ref, more_ref, adjoint_ref, even_ref, odd_ref):
    weight = sums_ref[0] + more_ref[0]
    value = sums_ref[1] + more_ref[1]
    window = lanes(*window_of(my_chip(), chip_count(), mask_ref.shape[1] // LANES))
    adjoint = mask_ref[:, window].astype(F32) * (weight * smooth_ref[...] - value)
    adjoint_ref[...] = adjoint
    pack_edges(even_ref, odd_ref, adjoint, margin)


def spread_kernel(margin, own_ref, even_ref, odd_ref, coef_ref, out_ref, ring_ref):
    rows = own_ref.shape[0]
    lay_ring(ring_ref, own_ref[...], even_ref, odd_ref, margin)
    for j, field in enumerate(diffuse(ring_ref, coef_ref, rows, margin)):
        ring_ref[:rows, j * LANES : (j + 1) * LANES] = field
    own = out_ref.shape[1] // LANES
    start = window_of(my_chip(), chip_count(), own * chip_count())[0]
    out_ref[...] = ring_ref[:rows, lanes(my_chip() * own - start, own)]


def sent_last(members):
    return [0, 1] + sorted(range(2, members), key=lambda d: -(d % 2))


def result_kernel(response_ref, control_ref, *refs):
    own, out_ref = refs[0].shape[1] // LANES, refs[-1]
    refs = [refs[sent_last(len(refs) - 1).index(d)] for d in range(len(refs) - 1)]
    for d in range(len(refs) // 2):
        window = lanes((my_chip() ^ d) * own, own)
        for v in range(control_ref.shape[0]):
            mine, theirs = (response_ref[i, v][:1, :1] for i in range(2))
            out_ref[v, :, window] = (
                control_ref[v, :, window] + mine * refs[2 * d][...] + theirs * refs[2 * d + 1][...]
            )


def swap(values, axis, bit):
    count = lax.axis_size(axis)
    return lax.ppermute(values, axis, [(i, i ^ bit) for i in range(count)])


def swap_edges(even, odd):
    tiles, members = lax.axis_size("tile"), lax.axis_size("var")
    pairs = []
    for t in range(tiles):
        other = t + 1 if t % 2 else t - 1
        for q in range(members):
            to = other * members + q if 0 <= other < tiles else t * members + (q ^ 1)
            pairs.append((t * members + q, to))
    return swap(even, "tile", 1), lax.ppermute(odd, ("tile", "var"), pairs)


def deliver(chunks):
    tiles, members = lax.axis_size("tile"), lax.axis_size("var")
    got = []
    for turn, chunk in enumerate(chunks[:-1]):
        pairs = []
        for t in range(tiles):
            for q in range(members):
                offset = 1 if turn == len(chunks) - 2 else 2 + turn + (q % 2) * (tiles // 2 - 1)
                pairs.append((t * members + q, (t ^ offset) * members + q))
        got.append(lax.ppermute(chunk, ("tile", "var"), pairs))
    return got + [chunks[-1]]


def local(control, diffusivity, land_mask, panel_tile, panel_row, panel_cols, obs_values,
          obs_weights, panel_sensor, sensitivity, cross_factor):
    rows, width = control.shape[1:]
    var_dev = control.shape[0]
    tiles, members = lax.axis_size("tile"), lax.axis_size("var")
    panels, panel_width = panel_cols.shape
    slots = panels // tiles
    blocks = width // LANES
    margin = PASSES
    total = ring_rows(rows, margin)
    chips = members // 2
    size = window_of(0, chips, blocks)[1]
    field = jax.ShapeDtypeStruct((rows, width), F32)
    share = jax.ShapeDtypeStruct((rows, width // chips), F32)
    view = jax.ShapeDtypeStruct((rows, size * LANES), F32)
    view2 = jax.ShapeDtypeStruct((2, *view.shape), F32)
    edge = jax.ShapeDtypeStruct((margin * size, LANES), F32)
    edge2 = jax.ShapeDtypeStruct((2, *edge.shape), F32)
    half = jax.ShapeDtypeStruct((3 * slots + 8, panel_width), F32)
    chunks = [jax.ShapeDtypeStruct((2, *half.shape), F32)] * (tiles // 2 - 1) + [half] * 2
    line = pltpu.VMEM((1, panels), jnp.int32)

    own, other, responses, kappa, kappa_even, kappa_odd, *chunks = call(
        functools.partial(first_kernel, slots, margin),
        [field, field, jax.ShapeDtypeStruct((2, var_dev, 8, LANES), F32), view2, edge2, edge2]
        + chunks,
        [HBM] * 10,
        [
            pltpu.SMEM(sensitivity.shape, F32),
            pltpu.SMEM(cross_factor.shape, F32),
            pltpu.VMEM(control.shape, F32),
            line, line, line,
            pltpu.VMEM(obs_values.shape, F32),
            pltpu.VMEM(obs_weights.shape, F32),
            pltpu.VMEM(panel_cols.shape, jnp.int32),
            pltpu.VMEM((panels, panels), jnp.bfloat16),
            pltpu.SemaphoreType.DMA((10,)),
        ],
        cost=cost(3000),
    )(*(in_hbm(x) for x in (sensitivity, cross_factor, control, diffusivity, panel_tile.reshape(1, -1),
                            panel_row.reshape(1, -1), panel_sensor.reshape(1, -1), obs_values,
                            obs_weights, panel_cols)))

    got = deliver(chunks)
    part, *parts = call(cut_kernel, [view] * chips, [VMEM] * 2, cost=cost(200))(
        own, swap(other, "var", 1)
    )
    parts = [swap(p, "var", 2 * (d + 1)) for d, p in enumerate(parts)]
    kappa_even, kappa_odd = swap_edges(kappa_even, kappa_odd)
    smooth_in, even, odd = call(
        functools.partial(edges_kernel, margin),
        [view, edge, edge],
        [VMEM] * chips,
        cost=cost(150000),
    )(part, *parts)
    even, odd = swap_edges(even, odd)
    sums, sums_other = call(
        functools.partial(scatter_kernel, slots, blocks),
        [view2, view2],
        [AFTER] + [VMEM] * len(got),
        [
            pltpu.VMEM((2 * rows * 2 * padded_blocks(size), LANES), F32),
            pltpu.SMEM((8 * tiles, LANES), F32),
            pltpu.SemaphoreType.DMA((tiles,)),
        ],
        cost=cost(100000),
    )(smooth_in, got[-2], *got[:-2], got[-1])
    ring = pltpu.VMEM((total, size * LANES), F32)
    coef, sums_other = call(
        functools.partial(faces_kernel, margin),
        [jax.ShapeDtypeStruct((5, total, size * LANES), F32), view2],
        [VMEM] * 4 + [AFTER] * 2,
        [ring, ring],
        cost=cost(1000),
    )(kappa_even, kappa_odd, kappa, sums_other, even, odd)
    more_sums = swap(sums_other, "var", 1)
    (smooth,) = call(
        functools.partial(smooth_kernel, margin),
        [view],
        [VMEM] * 4,
        [ring],
        cost=cost(4000),
    )(smooth_in, even, odd, coef)
    adjoint, even, odd = call(
        functools.partial(adjoint_kernel, margin), [view, edge, edge], [VMEM] * 4, cost=cost(500)
    )(smooth, land_mask, sums, more_sums)
    even, odd = swap_edges(even, odd)
    (mine,) = call(
        functools.partial(spread_kernel, margin),
        [share],
        [VMEM] * 4,
        [ring],
        cost=cost(4000),
    )(adjoint, even, odd, coef)
    shares = [mine] + [swap(mine, "var", d) for d in sent_last(members)[1:]]
    (out,) = call(
        result_kernel,
        [jax.ShapeDtypeStruct(control.shape, F32)],
        [VMEM] * (2 + members),
        cost=cost(1000),
    )(responses, control, *shares)
    return out


def solution(mesh):
    return jax.shard_map(
        local,
        mesh=mesh,
        in_specs=(
            P("var", ("grp", "tile"), None),
            P(None, ("grp", "tile"), None),
            P(("grp", "tile"), None),
            P(("grp", "tile"), None),
            P(("grp", "tile")),
            P(("grp", "tile"), None),
            P(("grp", "tile"), None),
            P(("grp", "tile"), None),
            P(("grp", "tile")),
            P(),
            P(),
        ),
        out_specs=P("var", ("grp", "tile"), None),
        check_vma=False,
    )
```

```python
import functools

import jax
import jax.numpy as jnp
from jax import lax
from jax.experimental import pallas as pl
from jax.experimental.pallas import tpu as pltpu
from jax.sharding import PartitionSpec as P

PASSES = 10
LANES = 128
GROUP = 16
VMEM = pl.BlockSpec(memory_space=pltpu.VMEM)
SMEM = pl.BlockSpec(memory_space=pltpu.SMEM)
HBM = pl.BlockSpec(memory_space=pltpu.HBM)
AFTER = pl.BlockSpec(memory_space=pl.ANY)
F32 = jnp.float32


def in_hbm(values):
    return pltpu.with_memory_space_constraint(values, pltpu.HBM)


def call(body, outs, ins, scratch=(), limit=16, cost=None):
    return pl.pallas_call(
        body,
        out_shape=outs,
        in_specs=ins,
        out_specs=[VMEM] * len(outs),
        scratch_shapes=list(scratch),
        compiler_params=pltpu.CompilerParams(vmem_limit_bytes=limit << 20),
        cost_estimate=cost,
    )


def cost(cycles):
    return pl.CostEstimate(flops=cycles * 4096, bytes_accessed=cycles * 1024, transcendentals=0)


def response(sens_ref, factor_ref, sensor, variable):
    total = sens_ref[sensor, 0] * factor_ref[0, variable]
    for u in range(1, factor_ref.shape[0]):
        total = total + sens_ref[sensor, u] * factor_ref[u, variable]
    return total


def fetch(pairs, sems):
    copies = [pltpu.make_async_copy(src, dst, sems.at[i]) for i, (src, dst) in enumerate(pairs)]
    for copy in copies:
        copy.start()
    return copies


def window_of(chip, chips, blocks):
    own = blocks // chips
    size = min(own + 2, own + chips - 1)
    return jnp.clip(chip * own - 1, 0, blocks - size), size


def my_chip():
    return lax.axis_index("var") // 2


def chip_count():
    return lax.axis_size("var") // 2


def lanes(start, size):
    return pl.ds(pl.multiple_of(start * LANES, LANES), size * LANES)


def first_kernel(slots, margin, sens_hbm, factor_hbm, control_hbm, kappa_hbm, tile_hbm, row_hbm, sensor_hbm,
                 value_hbm, weight_hbm, cols_hbm, own_ref, other_ref, response_ref, kappa_ref, odd_ref,
                 *refs):
    chunk_refs = refs[:-11]
    (sens_ref, factor_ref, control_ref, tile_ref, row_ref, sensor_ref, value_ref, weight_ref, cols_ref,
     before_ref, sems) = refs[-11:]
    window = lanes(*window_of(my_chip(), chip_count(), own_ref.shape[1] // LANES))
    pairs = (
        (sens_hbm, sens_ref), (factor_hbm, factor_ref), (control_hbm, control_ref),
        (kappa_hbm.at[:, :, window], kappa_ref), (tile_hbm, tile_ref), (row_hbm, row_ref), (sensor_hbm, sensor_ref),
        (value_hbm, value_ref), (weight_hbm, weight_ref), (cols_hbm, cols_ref),
    )
    copies = [pltpu.make_async_copy(src, dst, sems.at[i]) for i, (src, dst) in enumerate(pairs)]
    for copy in copies:
        copy.start()
    from_panel = lax.broadcasted_iota(jnp.int32, before_ref.shape, 0)
    to_panel = lax.broadcasted_iota(jnp.int32, before_ref.shape, 1)
    before_ref[...] = jnp.where(from_panel < to_panel, 1.0, 0.0).astype(jnp.bfloat16)
    for copy in copies:
        copy.wait()

    member, mine = lax.axis_index("var"), lax.axis_index("tile")
    core = member % 2
    var_dev = control_ref.shape[0]
    for which, (sensor, out_ref) in enumerate(((core, own_ref), (1 - core, other_ref))):
        total = None
        for v in range(var_dev):
            scale = response(sens_ref, factor_ref, sensor, member * var_dev + v)
            response_ref[which, v] = jnp.full(response_ref.shape[2:], scale, F32)
            term = scale * control_ref[v]
            total = term if total is None else total + term
        out_ref[...] = total

    for i in range(2):
        even_ref = even_kappa(chunk_refs[-2], slots, odd_ref.shape[1], i)
        pack_edges(even_ref, odd_ref.at[i], kappa_ref[i], margin)

    tiles = lax.axis_size("tile")
    full = tiles // 2 - 1
    first = jnp.where(core == 0, 2, tiles // 2 + 1)
    panels = value_ref.shape[0]
    source = tile_ref[...] ^ mine
    names = lax.broadcasted_iota(jnp.int32, (-(-tiles // 8) * 8, panels), 0)
    hits = jnp.where(names == source, 1.0, 0.0)
    ranks = jnp.dot(hits.astype(jnp.bfloat16), before_ref[...], preferred_element_type=F32)
    rank = jnp.sum(hits * ranks, axis=0, keepdims=True).astype(jnp.int32)
    parity, slot = rank % 2, rank // 2
    whole = (source >= first) & (source < first + full)
    home = source == 0
    keep = whole | ((home | (source == 1)) & (parity == core))
    half = jnp.where(whole, 2 * (source - first) + parity, jnp.where(home, tiles - 1, tiles - 2))
    place = jnp.where(keep, half * slots + slot, -1)
    spots = lax.broadcasted_iota(jnp.int32, (tiles * slots, panels), 0)
    pick = jnp.where(spots == place, 1.0, 0.0).astype(jnp.bfloat16)

    def picked(parts):
        total = None
        for part in parts:
            term = jnp.dot(pick, part.astype(jnp.bfloat16), preferred_element_type=F32)
            total = term if total is None else total + term
        return total

    cols = cols_ref[...]
    sent = (
        picked(thirds(value_ref[...])),
        picked(thirds(weight_ref[...])),
        picked(((cols // LANES * LANES).astype(F32), (cols % LANES).astype(F32))),
    )
    sub = lax.broadcasted_iota(jnp.int32, (8, panels), 0)
    lane = lax.broadcasted_iota(jnp.int32, (8, panels), 1)
    facts = jnp.where(sub == 0, row_ref[...], jnp.where(sub == 1, sensor_ref[...], 0)).astype(F32)
    meta = lax.dot_general(
        facts.astype(jnp.bfloat16), pick, (((1,), (1,)), ((), ())), preferred_element_type=F32
    )
    for i in range(tiles):
        held = jnp.sum(jnp.where(keep & (half == i), 1.0, 0.0), axis=1, keepdims=True)
        meta = jnp.where((sub == 2) & (lane == i), held, meta)
    for i in range(tiles):
        out_ref = chunk_refs[i // 2].at[i % 2] if i < 2 * full else chunk_refs[i - full]
        for part, rows in enumerate(sent):
            out_ref[part * slots : (part + 1) * slots] = rows[i * slots : (i + 1) * slots]
        out_ref[3 * slots : 3 * slots + 8] = meta


def thirds(values):
    top = values.astype(jnp.bfloat16).astype(F32)
    rest = values - top
    middle = rest.astype(jnp.bfloat16).astype(F32)
    return top, middle, rest - middle


def pieces(values):
    top = values.astype(jnp.bfloat16).astype(F32)
    return top, values - top


def scatter_kernel(slots, blocks_all, after_ref, *refs):
    got_refs, (own_ref, other_ref, acc_ref, meta_ref, sems) = refs[:-5], refs[-5:]
    core = lax.axis_index("var") % 2
    got_refs = [r.at[i] for r in got_refs[1:-1] for i in (0, 1)] + [got_refs[0], got_refs[-1]]
    size_of_group = min(GROUP, slots)
    copies = [
        pltpu.make_async_copy(ref.at[pl.ds(3 * slots, 8)], meta_ref.at[pl.ds(8 * s, 8)], sems.at[s])
        for s, ref in enumerate(got_refs)
    ]
    for copy in copies:
        copy.start()
    rows = own_ref.shape[1]
    start, size = window_of(my_chip(), chip_count(), blocks_all)
    per_kind = padded_blocks(size)
    tall = 2 * per_kind
    acc_ref[...] = jnp.zeros(acc_ref.shape, F32)
    place = lax.broadcasted_iota(jnp.int32, (tall, LANES), 0)
    is_weight = place < per_kind
    place = jnp.where(is_weight, place, place - per_kind) + start
    lane_ids = lax.broadcasted_iota(jnp.int32, (LANES, LANES), 0).astype(F32).astype(jnp.bfloat16)
    one, zero = jnp.bfloat16(1), jnp.bfloat16(0)
    sub = lax.broadcasted_iota(jnp.int32, (size_of_group, LANES), 0)
    blank = jnp.zeros((2 * tall, LANES), jnp.bfloat16)
    for copy in copies:
        copy.wait()

    def load(s, base):
        got_ref = got_refs[s]
        count = meta_ref[8 * s + 2, s].astype(jnp.int32)
        value = got_ref[pl.ds(base, size_of_group), :]
        weight = got_ref[pl.ds(slots + base, size_of_group), :]
        cell = got_ref[pl.ds(2 * slots + base, size_of_group), :].astype(jnp.int32)
        weight = jnp.where(sub + base < count, weight, 0.0)
        return pieces(weight), pieces(weight * value), (cell % LANES).astype(F32), cell // LANES

    def one_hots(loaded, i):
        weights, values, low, high = loaded
        here = place == high[i : i + 1]
        rows_of = [
            jnp.where(here, jnp.where(is_weight, w[i : i + 1], v[i : i + 1]), 0.0)
            for w, v in zip(weights, values)
        ]
        left = jnp.concatenate(rows_of, axis=0).astype(jnp.bfloat16)
        column = jnp.broadcast_to(low[i : i + 1], (16, LANES)).astype(jnp.bfloat16)
        column = jnp.concatenate([column] * (LANES // 16), axis=0)
        return left, jnp.where(lane_ids == column, one, zero)

    def step(chosen, g, carry):
        base = pl.multiple_of(g * size_of_group, size_of_group)
        loaded = {s: load(s, base) for s in chosen}
        for k in range(size_of_group):
            for pair in zip(chosen[::2], chosen[1::2]):
                hots = [one_hots(loaded[s], k) for s in pair]
                left = jnp.concatenate(
                    [
                        jnp.concatenate([hots[0][0], blank], axis=1),
                        jnp.concatenate([blank, hots[1][0]], axis=1),
                    ],
                    axis=0,
                )
                both = lax.dot_general(
                    left, jnp.concatenate([hots[0][1], hots[1][1]], axis=1), (((1,), (1,)), ((), ())),
                    preferred_element_type=F32,
                )
                for i, s in enumerate(pair):
                    row = meta_ref[8 * s, s * slots + base + k].astype(jnp.int32)
                    sensor = meta_ref[8 * s + 1, s * slots + base + k].astype(jnp.int32)
                    at = pl.multiple_of((sensor * rows + row) * tall, 8)
                    mine = both[2 * i * tall : 2 * (i + 1) * tall]
                    acc_ref[pl.ds(at, tall), :] += mine[:tall] + mine[tall:]
        return carry

    for s in range(0, len(got_refs), 4):
        chosen = list(range(s, s + 4))
        most = meta_ref[8 * s + 2, s]
        for other in chosen[1:]:
            most = jnp.maximum(most, meta_ref[8 * other + 2, other])
        turns = (most.astype(jnp.int32) + size_of_group - 1) // size_of_group
        lax.fori_loop(0, turns, functools.partial(step, chosen), 0)
    for sensor, out_ref in ((core, own_ref), (1 - core, other_ref)):
        begin = sensor * rows * tall
        for kind in range(2):
            for b in range(size):
                out_ref[kind, :, b * LANES : (b + 1) * LANES] = acc_ref[
                    pl.ds(begin + kind * per_kind + b, rows, stride=tall), :
                ]


def padded_blocks(size):
    return -(-size // 4) * 4


def even_tile():
    return lax.axis_index("tile") % 2 == 0


def has_above():
    return lax.axis_index("tile") > 0


def has_below():
    return lax.axis_index("tile") + 1 < lax.axis_size("tile")


def pack_edges(even_ref, odd_ref, rows_value, margin):
    rows, width = rows_value.shape
    even = even_tile()
    for b in range(width // LANES):
        at = slice(b * LANES, (b + 1) * LANES)
        head, tail = rows_value[:margin, at], rows_value[rows - margin :, at]
        even_ref[b * margin : (b + 1) * margin] = jnp.where(even, tail, head)
        odd_ref[b * margin : (b + 1) * margin] = jnp.where(even, head, tail)


def even_kappa(ref, slots, edge_rows, i):
    return ref.at[pl.ds(3 * slots + 8 + i * (-(-edge_rows // 8) * 8), edge_rows)]


def cut_kernel(first_ref, second_ref, mine_ref, *out_refs):
    chip, chips, blocks = my_chip(), chip_count(), first_ref.shape[1] // LANES
    for d, out_ref in enumerate((mine_ref, *out_refs)):
        window = lanes(*window_of(chip ^ d, chips, blocks))
        out_ref[...] = first_ref[:, window] + second_ref[:, window]


def edges_kernel(margin, *refs):
    terms, (total_ref, even_ref, odd_ref) = refs[:-3], refs[-3:]
    total = terms[0][...]
    for term in terms[1:]:
        total = total + term[...]
    total_ref[...] = total
    pack_edges(even_ref, odd_ref, total, margin)


def ring_rows(rows, margin):
    return -(-(rows + 2 * margin) // 8) * 8


def lay_ring(ref, own, from_even, from_odd, margin):
    rows, total = own.shape[0], ref.shape[0]
    even = even_tile()
    ref[rows:total] = jnp.zeros((total - rows, ref.shape[1]), F32)
    ref[:rows] = own
    for b in range(ref.shape[1] // LANES):
        at = slice(b * LANES, (b + 1) * LANES)
        one, two = (m[b * margin : (b + 1) * margin] for m in (from_even, from_odd))
        ref[rows : rows + margin, at] = jnp.where(has_below(), jnp.where(even, one, two), 0.0)
        ref[total - margin :, at] = jnp.where(has_above(), jnp.where(even, two, one), 0.0)


def block(ref, j):
    return ref[:, j * LANES : (j + 1) * LANES]


def sideways(blocks):
    shape = blocks[0].shape
    lane = lax.broadcasted_iota(jnp.int32, shape, 1)
    zero = jnp.zeros(shape, F32)
    ahead = [pltpu.roll(x, 1, 1) for x in blocks]
    back = [pltpu.roll(x, LANES - 1, 1) for x in blocks]
    for j, here in enumerate(blocks):
        before = ahead[j - 1] if j else zero
        after = back[j + 1] if j + 1 < len(blocks) else zero
        yield here, jnp.where(lane == 0, before, ahead[j]), jnp.where(lane == LANES - 1, after, back[j])


def face_weights(coef_ref, row_ref, col_ref, rows, margin):
    total, width = row_ref.shape
    blocks = width // LANES
    r = lax.broadcasted_iota(jnp.int32, (total, LANES), 0)
    inside = (
        (r < rows)
        | ((r < rows + margin) & has_below())
        | ((r >= total - margin) & has_above())
    )
    scale = jnp.where(inside, 0.125, 0.0)
    unit = jnp.where(inside, 1.0, 0.0)
    columns = [block(col_ref, j) for j in range(blocks)]
    for j, (k_col, k_left, k_right) in enumerate(sideways(columns)):
        at = slice(j * LANES, (j + 1) * LANES)
        k_row = block(row_ref, j)
        up = scale * (k_row + pltpu.roll(k_row, 1, 0))
        down = scale * (k_row + pltpu.roll(k_row, total - 1, 0))
        left = scale * (k_col + k_left)
        right = scale * (k_col + k_right)
        coef_ref[0, :, at] = unit - up - down - left - right
        coef_ref[1, :, at] = up
        coef_ref[2, :, at] = down
        coef_ref[3, :, at] = left
        coef_ref[4, :, at] = right


def one_pass(fields, coef_ref, spans):
    def weights(i, at):
        got = [coef_ref[i, span, at] for span in spans]
        return jnp.concatenate(got, axis=0) if len(got) > 1 else got[0]

    total = fields[0].shape[0]
    out = []
    for j, (here, left, right) in enumerate(sideways(fields)):
        at = slice(j * LANES, (j + 1) * LANES)
        out.append(
            weights(0, at) * here
            + weights(1, at) * pltpu.roll(here, 1, 0)
            + weights(2, at) * pltpu.roll(here, total - 1, 0)
            + weights(3, at) * left
            + weights(4, at) * right
        )
    return out


def diffuse(ring_ref, coef_ref, rows, margin):
    total, width = ring_ref.shape
    inner = margin // 8 * 8
    wide = [slice(0, total)]
    narrow = [slice(0, rows + inner), slice(total - inner, total)]
    fields = [block(ring_ref, j) for j in range(width // LANES)]
    for _ in range(margin - inner):
        fields = one_pass(fields, coef_ref, wide)
    fields = [jnp.concatenate([f[span] for span in narrow], axis=0) for f in fields]
    for _ in range(inner):
        fields = one_pass(fields, coef_ref, narrow)
    return [f[:rows] for f in fields]


def faces_kernel(margin, slots, shared_ref, odd_ref, kappa_ref, sums_ref, *refs):
    coef_ref, sums_out, one_ref, two_ref = refs[-4:]
    sums_out[...] = sums_ref[...]
    rows = kappa_ref.shape[1]
    for i, ring_ref in enumerate((one_ref, two_ref)):
        even_ref = even_kappa(shared_ref, slots, odd_ref.shape[1], i)
        lay_ring(ring_ref, kappa_ref[i], even_ref, odd_ref.at[i], margin)
    face_weights(coef_ref, one_ref, two_ref, rows, margin)


def smooth_kernel(margin, own_ref, even_ref, odd_ref, coef_ref, out_ref, ring_ref):
    rows = own_ref.shape[0]
    lay_ring(ring_ref, own_ref[...], even_ref, odd_ref, margin)
    for j, field in enumerate(diffuse(ring_ref, coef_ref, rows, margin)):
        out_ref[:, j * LANES : (j + 1) * LANES] = field


def adjoint_kernel(margin, smooth_ref, mask_ref, sums_ref, more_ref, adjoint_ref, even_ref, odd_ref):
    weight = sums_ref[0] + more_ref[0]
    value = sums_ref[1] + more_ref[1]
    window = lanes(*window_of(my_chip(), chip_count(), mask_ref.shape[1] // LANES))
    adjoint = mask_ref[:, window].astype(F32) * (weight * smooth_ref[...] - value)
    adjoint_ref[...] = adjoint
    pack_edges(even_ref, odd_ref, adjoint, margin)


def spread_kernel(margin, own_ref, even_ref, odd_ref, coef_ref, out_ref, ring_ref):
    rows = own_ref.shape[0]
    lay_ring(ring_ref, own_ref[...], even_ref, odd_ref, margin)
    for j, field in enumerate(diffuse(ring_ref, coef_ref, rows, margin)):
        ring_ref[:rows, j * LANES : (j + 1) * LANES] = field
    own = out_ref.shape[1] // LANES
    start = window_of(my_chip(), chip_count(), own * chip_count())[0]
    out_ref[...] = ring_ref[:rows, lanes(my_chip() * own - start, own)]


def sent_last(members):
    return [0, 1] + sorted(range(2, members), key=lambda d: -(d % 2))


def result_kernel(response_ref, control_ref, *refs):
    own, out_ref = refs[0].shape[1] // LANES, refs[-1]
    refs = [refs[sent_last(len(refs) - 1).index(d)] for d in range(len(refs) - 1)]
    for d in range(len(refs) // 2):
        window = lanes((my_chip() ^ d) * own, own)
        for v in range(control_ref.shape[0]):
            mine, theirs = (response_ref[i, v][:1, :1] for i in range(2))
            out_ref[v, :, window] = (
                control_ref[v, :, window] + mine * refs[2 * d][...] + theirs * refs[2 * d + 1][...]
            )


def swap(values, axis, bit):
    count = lax.axis_size(axis)
    return lax.ppermute(values, axis, [(i, i ^ bit) for i in range(count)])


def swap_odd(edges):
    tiles, members = lax.axis_size("tile"), lax.axis_size("var")
    pairs = []
    for t in range(tiles):
        other = t + 1 if t % 2 else t - 1
        for q in range(members):
            to = other * members + q if 0 <= other < tiles else t * members + (q ^ 1)
            pairs.append((t * members + q, to))
    return lax.ppermute(edges, ("tile", "var"), pairs)


def swap_edges(even, odd):
    return swap(even, "tile", 1), swap_odd(odd)


def deliver(chunks):
    tiles, members = lax.axis_size("tile"), lax.axis_size("var")
    got = []
    for turn, chunk in enumerate(chunks[:-1]):
        pairs = []
        for t in range(tiles):
            for q in range(members):
                offset = 1 if turn == len(chunks) - 2 else 2 + turn + (q % 2) * (tiles // 2 - 1)
                pairs.append((t * members + q, (t ^ offset) * members + q))
        got.append(lax.ppermute(chunk, ("tile", "var"), pairs))
    return got + [chunks[-1]]


def local(control, diffusivity, land_mask, panel_tile, panel_row, panel_cols, obs_values,
          obs_weights, panel_sensor, sensitivity, cross_factor):
    rows, width = control.shape[1:]
    var_dev = control.shape[0]
    tiles, members = lax.axis_size("tile"), lax.axis_size("var")
    panels, panel_width = panel_cols.shape
    slots = panels // tiles
    blocks = width // LANES
    margin = PASSES
    total = ring_rows(rows, margin)
    chips = members // 2
    size = window_of(0, chips, blocks)[1]
    field = jax.ShapeDtypeStruct((rows, width), F32)
    share = jax.ShapeDtypeStruct((rows, width // chips), F32)
    view = jax.ShapeDtypeStruct((rows, size * LANES), F32)
    view2 = jax.ShapeDtypeStruct((2, *view.shape), F32)
    edge = jax.ShapeDtypeStruct((margin * size, LANES), F32)
    edge2 = jax.ShapeDtypeStruct((2, *edge.shape), F32)
    half = jax.ShapeDtypeStruct((3 * slots + 8, panel_width), F32)
    shared = jax.ShapeDtypeStruct((half.shape[0] + 2 * (-(-edge.shape[0] // 8) * 8), panel_width), F32)
    chunks = [jax.ShapeDtypeStruct((2, *half.shape), F32)] * (tiles // 2 - 1) + [shared, half]
    line = pltpu.VMEM((1, panels), jnp.int32)

    own, other, responses, kappa, kappa_odd, *chunks = call(
        functools.partial(first_kernel, slots, margin),
        [field, field, jax.ShapeDtypeStruct((2, var_dev, 8, LANES), F32), view2, edge2]
        + chunks,
        [HBM] * 10,
        [
            pltpu.SMEM(sensitivity.shape, F32),
            pltpu.SMEM(cross_factor.shape, F32),
            pltpu.VMEM(control.shape, F32),
            line, line, line,
            pltpu.VMEM(obs_values.shape, F32),
            pltpu.VMEM(obs_weights.shape, F32),
            pltpu.VMEM(panel_cols.shape, jnp.int32),
            pltpu.VMEM((panels, panels), jnp.bfloat16),
            pltpu.SemaphoreType.DMA((10,)),
        ],
        cost=cost(3000),
    )(*(in_hbm(x) for x in (sensitivity, cross_factor, control, diffusivity, panel_tile.reshape(1, -1),
                            panel_row.reshape(1, -1), panel_sensor.reshape(1, -1), obs_values,
                            obs_weights, panel_cols)))

    got = deliver(chunks)
    part, *parts = call(cut_kernel, [view] * chips, [VMEM] * 2, cost=cost(200))(
        own, swap(other, "var", 1)
    )
    parts = [swap(p, "var", 2 * (d + 1)) for d, p in enumerate(parts)]
    kappa_odd = swap_odd(kappa_odd)
    smooth_in, even, odd = call(
        functools.partial(edges_kernel, margin), [view, edge, edge], [VMEM] * chips, cost=cost(500)
    )(part, *parts)
    even, odd = swap_edges(even, odd)
    sums, sums_other = call(
        functools.partial(scatter_kernel, slots, blocks),
        [view2, view2],
        [AFTER] + [VMEM] * len(got),
        [
            pltpu.VMEM((2 * rows * 2 * padded_blocks(size), LANES), F32),
            pltpu.SMEM((8 * tiles, LANES), F32),
            pltpu.SemaphoreType.DMA((tiles,)),
        ],
        cost=cost(100000),
    )(smooth_in, got[-2], *got[:-2], got[-1])
    ring = pltpu.VMEM((total, size * LANES), F32)
    coef, sums_other = call(
        functools.partial(faces_kernel, margin, slots),
        [jax.ShapeDtypeStruct((5, total, size * LANES), F32), view2],
        [VMEM] * 4 + [AFTER] * 2,
        [ring, ring],
        cost=cost(1000),
    )(got[-2], kappa_odd, kappa, sums_other, even, odd)
    more_sums = swap(sums_other, "var", 1)
    (smooth,) = call(
        functools.partial(smooth_kernel, margin),
        [view],
        [VMEM] * 4,
        [ring],
        cost=cost(4000),
    )(smooth_in, even, odd, coef)
    adjoint, even, odd = call(
        functools.partial(adjoint_kernel, margin), [view, edge, edge], [VMEM] * 4, cost=cost(500)
    )(smooth, land_mask, sums, more_sums)
    even, odd = swap_edges(even, odd)
    (mine,) = call(
        functools.partial(spread_kernel, margin),
        [share],
        [VMEM] * 4,
        [ring],
        cost=cost(4000),
    )(adjoint, even, odd, coef)
    shares = [mine] + [swap(mine, "var", d) for d in sent_last(members)[1:]]
    (out,) = call(
        result_kernel,
        [jax.ShapeDtypeStruct(control.shape, F32)],
        [VMEM] * (2 + members),
        cost=cost(1000),
    )(responses, control, *shares)
    return out


def solution(mesh):
    return jax.shard_map(
        local,
        mesh=mesh,
        in_specs=(
            P("var", ("grp", "tile"), None),
            P(None, ("grp", "tile"), None),
            P(("grp", "tile"), None),
            P(("grp", "tile"), None),
            P(("grp", "tile")),
            P(("grp", "tile"), None),
            P(("grp", "tile"), None),
            P(("grp", "tile"), None),
            P(("grp", "tile")),
            P(),
            P(),
        ),
        out_specs=P("var", ("grp", "tile"), None),
        check_vma=False,
    )
```

```python
import functools

import jax
import jax.numpy as jnp
from jax import lax
from jax.experimental import pallas as pl
from jax.experimental.pallas import tpu as pltpu
from jax.sharding import PartitionSpec as P

PASSES = 10
LANES = 128
GROUP = 16
VMEM = pl.BlockSpec(memory_space=pltpu.VMEM)
SMEM = pl.BlockSpec(memory_space=pltpu.SMEM)
HBM = pl.BlockSpec(memory_space=pltpu.HBM)
AFTER = pl.BlockSpec(memory_space=pl.ANY)
F32 = jnp.float32


def in_hbm(values):
    return pltpu.with_memory_space_constraint(values, pltpu.HBM)


def call(body, outs, ins, scratch=(), limit=16, cost=None):
    return pl.pallas_call(
        body,
        out_shape=outs,
        in_specs=ins,
        out_specs=[VMEM] * len(outs),
        scratch_shapes=list(scratch),
        compiler_params=pltpu.CompilerParams(vmem_limit_bytes=limit << 20),
        cost_estimate=cost,
    )


def cost(cycles):
    return pl.CostEstimate(flops=cycles * 4096, bytes_accessed=cycles * 1024, transcendentals=0)


def response(sens_ref, factor_ref, sensor, variable):
    total = sens_ref[sensor, 0] * factor_ref[0, variable]
    for u in range(1, factor_ref.shape[0]):
        total = total + sens_ref[sensor, u] * factor_ref[u, variable]
    return total


def fetch(pairs, sems):
    copies = [pltpu.make_async_copy(src, dst, sems.at[i]) for i, (src, dst) in enumerate(pairs)]
    for copy in copies:
        copy.start()
    return copies


def window_of(chip, chips, blocks):
    own = blocks // chips
    size = min(own + 2, own + chips - 1)
    return jnp.clip(chip * own - 1, 0, blocks - size), size


def my_chip():
    return lax.axis_index("var") // 2


def chip_count():
    return lax.axis_size("var") // 2


def lanes(start, size):
    return pl.ds(pl.multiple_of(start * LANES, LANES), size * LANES)


def first_kernel(slots, margin, sens_hbm, factor_hbm, control_hbm, kappa_hbm, tile_hbm, row_hbm, sensor_hbm,
                 value_hbm, weight_hbm, cols_hbm, own_ref, other_ref, response_ref, kappa_ref, odd_ref,
                 *refs):
    chunk_refs = refs[:-11]
    (sens_ref, factor_ref, control_ref, tile_ref, row_ref, sensor_ref, value_ref, weight_ref, cols_ref,
     before_ref, sems) = refs[-11:]
    window = lanes(*window_of(my_chip(), chip_count(), own_ref.shape[1] // LANES))
    pairs = (
        (sens_hbm, sens_ref), (factor_hbm, factor_ref), (control_hbm, control_ref),
        (kappa_hbm.at[:, :, window], kappa_ref), (tile_hbm, tile_ref), (row_hbm, row_ref), (sensor_hbm, sensor_ref),
        (value_hbm, value_ref), (weight_hbm, weight_ref), (cols_hbm, cols_ref),
    )
    copies = [pltpu.make_async_copy(src, dst, sems.at[i]) for i, (src, dst) in enumerate(pairs)]
    for copy in copies:
        copy.start()
    from_panel = lax.broadcasted_iota(jnp.int32, before_ref.shape, 0)
    to_panel = lax.broadcasted_iota(jnp.int32, before_ref.shape, 1)
    before_ref[...] = jnp.where(from_panel < to_panel, 1.0, 0.0).astype(jnp.bfloat16)
    for copy in copies:
        copy.wait()

    member, mine = lax.axis_index("var"), lax.axis_index("tile")
    core = member % 2
    var_dev = control_ref.shape[0]
    for which, (sensor, out_ref) in enumerate(((core, own_ref), (1 - core, other_ref))):
        total = None
        for v in range(var_dev):
            scale = response(sens_ref, factor_ref, sensor, member * var_dev + v)
            response_ref[which, v] = jnp.full(response_ref.shape[2:], scale, F32)
            term = scale * control_ref[v]
            total = term if total is None else total + term
        out_ref[...] = total

    for i in range(2):
        even_ref = even_kappa(chunk_refs[-2], slots, odd_ref.shape[1], i)
        pack_edges(even_ref, odd_ref.at[i], kappa_ref[i], margin)

    tiles = lax.axis_size("tile")
    full = tiles // 2 - 1
    first = jnp.where(core == 0, 2, tiles // 2 + 1)
    panels = value_ref.shape[0]
    source = tile_ref[...] ^ mine
    names = lax.broadcasted_iota(jnp.int32, (-(-tiles // 8) * 8, panels), 0)
    hits = jnp.where(names == source, 1.0, 0.0)
    ranks = jnp.dot(hits.astype(jnp.bfloat16), before_ref[...], preferred_element_type=F32)
    rank = jnp.sum(hits * ranks, axis=0, keepdims=True).astype(jnp.int32)
    parity, slot = rank % 2, rank // 2
    whole = (source >= first) & (source < first + full)
    home = source == 0
    keep = whole | ((home | (source == 1)) & (parity == core))
    half = jnp.where(whole, 2 * (source - first) + parity, jnp.where(home, tiles - 1, tiles - 2))
    place = jnp.where(keep, half * slots + slot, -1)
    spots = lax.broadcasted_iota(jnp.int32, (tiles * slots, panels), 0)
    pick = jnp.where(spots == place, 1.0, 0.0).astype(jnp.bfloat16)

    def picked(parts):
        total = None
        for part in parts:
            term = jnp.dot(pick, part.astype(jnp.bfloat16), preferred_element_type=F32)
            total = term if total is None else total + term
        return total

    cols = cols_ref[...]
    sent = (
        picked(thirds(value_ref[...])),
        picked(thirds(weight_ref[...])),
        picked(((cols // LANES * LANES).astype(F32), (cols % LANES).astype(F32))),
    )
    sub = lax.broadcasted_iota(jnp.int32, (8, panels), 0)
    lane = lax.broadcasted_iota(jnp.int32, (8, panels), 1)
    facts = jnp.where(sub == 0, row_ref[...], jnp.where(sub == 1, sensor_ref[...], 0)).astype(F32)
    meta = lax.dot_general(
        facts.astype(jnp.bfloat16), pick, (((1,), (1,)), ((), ())), preferred_element_type=F32
    )
    for i in range(tiles):
        held = jnp.sum(jnp.where(keep & (half == i), 1.0, 0.0), axis=1, keepdims=True)
        meta = jnp.where((sub == 2) & (lane == i), held, meta)
    for i in range(tiles):
        out_ref = chunk_refs[i // 2].at[i % 2] if i < 2 * full else chunk_refs[i - full]
        for part, rows in enumerate(sent):
            out_ref[part * slots : (part + 1) * slots] = rows[i * slots : (i + 1) * slots]
        out_ref[3 * slots : 3 * slots + 8] = meta


def thirds(values):
    top = values.astype(jnp.bfloat16).astype(F32)
    rest = values - top
    middle = rest.astype(jnp.bfloat16).astype(F32)
    return top, middle, rest - middle


def pieces(values):
    top = values.astype(jnp.bfloat16).astype(F32)
    return top, values - top


def scatter_kernel(slots, blocks_all, after_ref, *refs):
    got_refs, (own_ref, other_ref, acc_ref, meta_ref, sems) = refs[:-5], refs[-5:]
    core = lax.axis_index("var") % 2
    got_refs = [r.at[i] for r in got_refs[1:-1] for i in (0, 1)] + [got_refs[0], got_refs[-1]]
    size_of_group = min(GROUP, slots)
    copies = [
        pltpu.make_async_copy(ref.at[pl.ds(3 * slots, 8)], meta_ref.at[pl.ds(8 * s, 8)], sems.at[s])
        for s, ref in enumerate(got_refs)
    ]
    for copy in copies:
        copy.start()
    rows = own_ref.shape[1]
    start, size = window_of(my_chip(), chip_count(), blocks_all)
    per_kind = padded_blocks(size)
    tall = 2 * per_kind
    acc_ref[...] = jnp.zeros(acc_ref.shape, F32)
    place = lax.broadcasted_iota(jnp.int32, (tall, LANES), 0)
    is_weight = place < per_kind
    place = jnp.where(is_weight, place, place - per_kind) + start
    lane_ids = lax.broadcasted_iota(jnp.int32, (LANES, LANES), 0).astype(F32).astype(jnp.bfloat16)
    one, zero = jnp.bfloat16(1), jnp.bfloat16(0)
    sub = lax.broadcasted_iota(jnp.int32, (size_of_group, LANES), 0)
    blank = jnp.zeros((2 * tall, LANES), jnp.bfloat16)
    for copy in copies:
        copy.wait()

    def load(s, base):
        got_ref = got_refs[s]
        count = meta_ref[8 * s + 2, s].astype(jnp.int32)
        value = got_ref[pl.ds(base, size_of_group), :]
        weight = got_ref[pl.ds(slots + base, size_of_group), :]
        cell = got_ref[pl.ds(2 * slots + base, size_of_group), :].astype(jnp.int32)
        weight = jnp.where(sub + base < count, weight, 0.0)
        return pieces(weight), pieces(weight * value), (cell % LANES).astype(F32), cell // LANES

    def one_hots(loaded, i):
        weights, values, low, high = loaded
        here = place == high[i : i + 1]
        rows_of = [
            jnp.where(here, jnp.where(is_weight, w[i : i + 1], v[i : i + 1]), 0.0)
            for w, v in zip(weights, values)
        ]
        left = jnp.concatenate(rows_of, axis=0).astype(jnp.bfloat16)
        column = jnp.broadcast_to(low[i : i + 1], (16, LANES)).astype(jnp.bfloat16)
        column = jnp.concatenate([column] * (LANES // 16), axis=0)
        return left, jnp.where(lane_ids == column, one, zero)

    def step(chosen, g, carry):
        base = pl.multiple_of(g * size_of_group, size_of_group)
        loaded = {s: load(s, base) for s in chosen}
        for k in range(size_of_group):
            for pair in zip(chosen[::2], chosen[1::2]):
                hots = [one_hots(loaded[s], k) for s in pair]
                left = jnp.concatenate(
                    [
                        jnp.concatenate([hots[0][0], blank], axis=1),
                        jnp.concatenate([blank, hots[1][0]], axis=1),
                    ],
                    axis=0,
                )
                both = lax.dot_general(
                    left, jnp.concatenate([hots[0][1], hots[1][1]], axis=1), (((1,), (1,)), ((), ())),
                    preferred_element_type=F32,
                )
                for i, s in enumerate(pair):
                    row = meta_ref[8 * s, s * slots + base + k].astype(jnp.int32)
                    sensor = meta_ref[8 * s + 1, s * slots + base + k].astype(jnp.int32)
                    at = pl.multiple_of((sensor * rows + row) * tall, 8)
                    mine = both[2 * i * tall : 2 * (i + 1) * tall]
                    acc_ref[pl.ds(at, tall), :] += mine[:tall] + mine[tall:]
        return carry

    for s in range(0, len(got_refs), 4):
        chosen = list(range(s, s + 4))
        most = meta_ref[8 * s + 2, s]
        for other in chosen[1:]:
            most = jnp.maximum(most, meta_ref[8 * other + 2, other])
        turns = (most.astype(jnp.int32) + size_of_group - 1) // size_of_group
        lax.fori_loop(0, turns, functools.partial(step, chosen), 0)
    for sensor, out_ref in ((core, own_ref), (1 - core, other_ref)):
        begin = sensor * rows * tall
        for kind in range(2):
            for b in range(size):
                out_ref[kind, :, b * LANES : (b + 1) * LANES] = acc_ref[
                    pl.ds(begin + kind * per_kind + b, rows, stride=tall), :
                ]


def padded_blocks(size):
    return -(-size // 4) * 4


def even_tile():
    return lax.axis_index("tile") % 2 == 0


def has_above():
    return lax.axis_index("tile") > 0


def has_below():
    return lax.axis_index("tile") + 1 < lax.axis_size("tile")


def pack_edges(even_ref, odd_ref, rows_value, margin):
    rows, width = rows_value.shape
    even = even_tile()
    for b in range(width // LANES):
        at = slice(b * LANES, (b + 1) * LANES)
        head, tail = rows_value[:margin, at], rows_value[rows - margin :, at]
        even_ref[b * margin : (b + 1) * margin] = jnp.where(even, tail, head)
        odd_ref[b * margin : (b + 1) * margin] = jnp.where(even, head, tail)


def even_kappa(ref, slots, edge_rows, i):
    return ref.at[pl.ds(3 * slots + 8 + i * (-(-edge_rows // 8) * 8), edge_rows)]


def cut_kernel(first_ref, second_ref, mine_ref, *out_refs):
    chip, chips, blocks = my_chip(), chip_count(), first_ref.shape[1] // LANES
    for d, out_ref in enumerate((mine_ref, *out_refs)):
        window = lanes(*window_of(chip ^ d, chips, blocks))
        out_ref[...] = first_ref[:, window] + second_ref[:, window]


def edges_kernel(margin, *refs):
    terms, (total_ref, even_ref, odd_ref) = refs[:-3], refs[-3:]
    total = terms[0][...]
    for term in terms[1:]:
        total = total + term[...]
    total_ref[...] = total
    pack_edges(even_ref, odd_ref, total, margin)


def ring_rows(rows, margin):
    return -(-(rows + 2 * margin) // 8) * 8


def lay_ring(ref, own, from_even, from_odd, margin):
    rows, total = own.shape[0], ref.shape[0]
    even = even_tile()
    ref[rows:total] = jnp.zeros((total - rows, ref.shape[1]), F32)
    ref[:rows] = own
    for b in range(ref.shape[1] // LANES):
        at = slice(b * LANES, (b + 1) * LANES)
        one, two = (m[b * margin : (b + 1) * margin] for m in (from_even, from_odd))
        ref[rows : rows + margin, at] = jnp.where(has_below(), jnp.where(even, one, two), 0.0)
        ref[total - margin :, at] = jnp.where(has_above(), jnp.where(even, two, one), 0.0)


def block(ref, j):
    return ref[:, j * LANES : (j + 1) * LANES]


def sideways(blocks):
    shape = blocks[0].shape
    lane = lax.broadcasted_iota(jnp.int32, shape, 1)
    zero = jnp.zeros(shape, F32)
    ahead = [pltpu.roll(x, 1, 1) for x in blocks]
    back = [pltpu.roll(x, LANES - 1, 1) for x in blocks]
    for j, here in enumerate(blocks):
        before = ahead[j - 1] if j else zero
        after = back[j + 1] if j + 1 < len(blocks) else zero
        yield here, jnp.where(lane == 0, before, ahead[j]), jnp.where(lane == LANES - 1, after, back[j])


def face_weights(coef_ref, row_ref, col_ref, rows, margin):
    total, width = row_ref.shape
    blocks = width // LANES
    r = lax.broadcasted_iota(jnp.int32, (total, LANES), 0)
    inside = (
        (r < rows)
        | ((r < rows + margin) & has_below())
        | ((r >= total - margin) & has_above())
    )
    scale = jnp.where(inside, 0.125, 0.0)
    unit = jnp.where(inside, 1.0, 0.0)
    columns = [block(col_ref, j) for j in range(blocks)]
    for j, (k_col, k_left, k_right) in enumerate(sideways(columns)):
        at = slice(j * LANES, (j + 1) * LANES)
        k_row = block(row_ref, j)
        up = scale * (k_row + pltpu.roll(k_row, 1, 0))
        down = scale * (k_row + pltpu.roll(k_row, total - 1, 0))
        left = scale * (k_col + k_left)
        right = scale * (k_col + k_right)
        coef_ref[0, :, at] = unit - up - down - left - right
        coef_ref[1, :, at] = up
        coef_ref[2, :, at] = down
        coef_ref[3, :, at] = left
        coef_ref[4, :, at] = right


def one_pass(fields, coef_ref, spans):
    def weights(i, at):
        got = [coef_ref[i, span, at] for span in spans]
        return jnp.concatenate(got, axis=0) if len(got) > 1 else got[0]

    total = fields[0].shape[0]
    out = []
    for j, (here, left, right) in enumerate(sideways(fields)):
        at = slice(j * LANES, (j + 1) * LANES)
        out.append(
            weights(0, at) * here
            + weights(1, at) * pltpu.roll(here, 1, 0)
            + weights(2, at) * pltpu.roll(here, total - 1, 0)
            + weights(3, at) * left
            + weights(4, at) * right
        )
    return out


def diffuse(ring_ref, coef_ref, rows, margin):
    total, width = ring_ref.shape
    inner = margin // 8 * 8
    wide = [slice(0, total)]
    narrow = [slice(0, rows + inner), slice(total - inner, total)]
    fields = [block(ring_ref, j) for j in range(width // LANES)]
    for _ in range(margin - inner):
        fields = one_pass(fields, coef_ref, wide)
    fields = [jnp.concatenate([f[span] for span in narrow], axis=0) for f in fields]
    for _ in range(inner):
        fields = one_pass(fields, coef_ref, narrow)
    return [f[:rows] for f in fields]


def faces_kernel(margin, slots, shared_ref, odd_ref, kappa_ref, sums_ref, *refs):
    coef_ref, sums_out, one_ref, two_ref = refs[-4:]
    sums_out[...] = sums_ref[...]
    rows = kappa_ref.shape[1]
    for i, ring_ref in enumerate((one_ref, two_ref)):
        even_ref = even_kappa(shared_ref, slots, odd_ref.shape[1], i)
        lay_ring(ring_ref, kappa_ref[i], even_ref, odd_ref.at[i], margin)
    face_weights(coef_ref, one_ref, two_ref, rows, margin)


def smooth_kernel(margin, own_ref, even_ref, odd_ref, coef_ref, out_ref, ring_ref):
    rows = own_ref.shape[0]
    lay_ring(ring_ref, own_ref[...], even_ref, odd_ref, margin)
    for j, field in enumerate(diffuse(ring_ref, coef_ref, rows, margin)):
        out_ref[:, j * LANES : (j + 1) * LANES] = field


def adjoint_kernel(margin, smooth_ref, mask_ref, sums_ref, more_ref, adjoint_ref, even_ref, odd_ref):
    weight = sums_ref[0] + more_ref[0]
    value = sums_ref[1] + more_ref[1]
    window = lanes(*window_of(my_chip(), chip_count(), mask_ref.shape[1] // LANES))
    adjoint = mask_ref[:, window].astype(F32) * (weight * smooth_ref[...] - value)
    adjoint_ref[...] = adjoint
    pack_edges(even_ref, odd_ref, adjoint, margin)


def spread_kernel(margin, own_ref, even_ref, odd_ref, coef_ref, out_ref, ring_ref):
    rows = own_ref.shape[0]
    lay_ring(ring_ref, own_ref[...], even_ref, odd_ref, margin)
    for j, field in enumerate(diffuse(ring_ref, coef_ref, rows, margin)):
        ring_ref[:rows, j * LANES : (j + 1) * LANES] = field
    own = out_ref.shape[1] // LANES
    start = window_of(my_chip(), chip_count(), own * chip_count())[0]
    out_ref[...] = ring_ref[:rows, lanes(my_chip() * own - start, own)]


def sent_last(members):
    return [0, 1] + sorted(range(2, members), key=lambda d: -(d % 2))


def result_kernel(response_ref, control_ref, *refs):
    own, out_ref = refs[0].shape[1] // LANES, refs[-1]
    refs = [refs[sent_last(len(refs) - 1).index(d)] for d in range(len(refs) - 1)]
    for d in range(len(refs) // 2):
        window = lanes((my_chip() ^ d) * own, own)
        for v in range(control_ref.shape[0]):
            mine, theirs = (response_ref[i, v][:1, :1] for i in range(2))
            out_ref[v, :, window] = (
                control_ref[v, :, window] + mine * refs[2 * d][...] + theirs * refs[2 * d + 1][...]
            )


def swap(values, axis, bit):
    count = lax.axis_size(axis)
    return lax.ppermute(values, axis, [(i, i ^ bit) for i in range(count)])


def swap_odd(edges):
    tiles, members = lax.axis_size("tile"), lax.axis_size("var")
    pairs = []
    for t in range(tiles):
        other = t + 1 if t % 2 else t - 1
        for q in range(members):
            to = other * members + q if 0 <= other < tiles else t * members + (q ^ 1)
            pairs.append((t * members + q, to))
    return lax.ppermute(edges, ("tile", "var"), pairs)


def swap_edges(even, odd):
    return swap(even, "tile", 1), swap_odd(odd)


def deliver(chunks):
    tiles, members = lax.axis_size("tile"), lax.axis_size("var")
    got = []
    for turn, chunk in enumerate(chunks[:-1]):
        pairs = []
        for t in range(tiles):
            for q in range(members):
                offset = 1 if turn == len(chunks) - 2 else 2 + turn + (q % 2) * (tiles // 2 - 1)
                pairs.append((t * members + q, (t ^ offset) * members + q))
        got.append(lax.ppermute(chunk, ("tile", "var"), pairs))
    return got + [chunks[-1]]


def local(control, diffusivity, land_mask, panel_tile, panel_row, panel_cols, obs_values,
          obs_weights, panel_sensor, sensitivity, cross_factor):
    rows, width = control.shape[1:]
    var_dev = control.shape[0]
    tiles, members = lax.axis_size("tile"), lax.axis_size("var")
    panels, panel_width = panel_cols.shape
    slots = panels // tiles
    blocks = width // LANES
    margin = PASSES
    total = ring_rows(rows, margin)
    chips = members // 2
    size = window_of(0, chips, blocks)[1]
    field = jax.ShapeDtypeStruct((rows, width), F32)
    share = jax.ShapeDtypeStruct((rows, width // chips), F32)
    view = jax.ShapeDtypeStruct((rows, size * LANES), F32)
    view2 = jax.ShapeDtypeStruct((2, *view.shape), F32)
    edge = jax.ShapeDtypeStruct((margin * size, LANES), F32)
    edge2 = jax.ShapeDtypeStruct((2, *edge.shape), F32)
    half = jax.ShapeDtypeStruct((3 * slots + 8, panel_width), F32)
    shared = jax.ShapeDtypeStruct((half.shape[0] + 2 * (-(-edge.shape[0] // 8) * 8), panel_width), F32)
    chunks = [jax.ShapeDtypeStruct((2, *half.shape), F32)] * (tiles // 2 - 1) + [shared, half]
    line = pltpu.VMEM((1, panels), jnp.int32)

    own, other, responses, kappa, kappa_odd, *chunks = call(
        functools.partial(first_kernel, slots, margin),
        [field, field, jax.ShapeDtypeStruct((2, var_dev, 8, LANES), F32), view2, edge2]
        + chunks,
        [HBM] * 10,
        [
            pltpu.SMEM(sensitivity.shape, F32),
            pltpu.SMEM(cross_factor.shape, F32),
            pltpu.VMEM(control.shape, F32),
            line, line, line,
            pltpu.VMEM(obs_values.shape, F32),
            pltpu.VMEM(obs_weights.shape, F32),
            pltpu.VMEM(panel_cols.shape, jnp.int32),
            pltpu.VMEM((panels, panels), jnp.bfloat16),
            pltpu.SemaphoreType.DMA((10,)),
        ],
        cost=cost(3000),
    )(*(in_hbm(x) for x in (sensitivity, cross_factor, control, diffusivity, panel_tile.reshape(1, -1),
                            panel_row.reshape(1, -1), panel_sensor.reshape(1, -1), obs_values,
                            obs_weights, panel_cols)))

    got = deliver(chunks)
    part, *parts = call(cut_kernel, [view] * chips, [VMEM] * 2, cost=cost(200))(
        own, swap(other, "var", 1)
    )
    parts = [swap(p, "var", 2 * (d + 1)) for d, p in enumerate(parts)]
    kappa_odd = swap_odd(kappa_odd)
    smooth_in, even, odd = call(
        functools.partial(edges_kernel, margin),
        [view, edge, edge],
        [VMEM] * chips,
        cost=cost(130000),
    )(part, *parts)
    even, odd = swap_edges(even, odd)
    sums, sums_other = call(
        functools.partial(scatter_kernel, slots, blocks),
        [view2, view2],
        [AFTER] + [VMEM] * len(got),
        [
            pltpu.VMEM((2 * rows * 2 * padded_blocks(size), LANES), F32),
            pltpu.SMEM((8 * tiles, LANES), F32),
            pltpu.SemaphoreType.DMA((tiles,)),
        ],
        cost=cost(100000),
    )(smooth_in, got[-2], *got[:-2], got[-1])
    ring = pltpu.VMEM((total, size * LANES), F32)
    coef, sums_other = call(
        functools.partial(faces_kernel, margin, slots),
        [jax.ShapeDtypeStruct((5, total, size * LANES), F32), view2],
        [VMEM] * 4 + [AFTER] * 2,
        [ring, ring],
        cost=cost(1000),
    )(got[-2], kappa_odd, kappa, sums_other, even, odd)
    more_sums = swap(sums_other, "var", 1)
    (smooth,) = call(
        functools.partial(smooth_kernel, margin),
        [view],
        [VMEM] * 4,
        [ring],
        cost=cost(4000),
    )(smooth_in, even, odd, coef)
    adjoint, even, odd = call(
        functools.partial(adjoint_kernel, margin), [view, edge, edge], [VMEM] * 4, cost=cost(500)
    )(smooth, land_mask, sums, more_sums)
    even, odd = swap_edges(even, odd)
    (mine,) = call(
        functools.partial(spread_kernel, margin),
        [share],
        [VMEM] * 4,
        [ring],
        cost=cost(4000),
    )(adjoint, even, odd, coef)
    shares = [mine] + [swap(mine, "var", d) for d in sent_last(members)[1:]]
    (out,) = call(
        result_kernel,
        [jax.ShapeDtypeStruct(control.shape, F32)],
        [VMEM] * (2 + members),
        cost=cost(1000),
    )(responses, control, *shares)
    return out


def solution(mesh):
    return jax.shard_map(
        local,
        mesh=mesh,
        in_specs=(
            P("var", ("grp", "tile"), None),
            P(None, ("grp", "tile"), None),
            P(("grp", "tile"), None),
            P(("grp", "tile"), None),
            P(("grp", "tile")),
            P(("grp", "tile"), None),
            P(("grp", "tile"), None),
            P(("grp", "tile"), None),
            P(("grp", "tile")),
            P(),
            P(),
        ),
        out_specs=P("var", ("grp", "tile"), None),
        check_vma=False,
    )
```

```python
import functools

import jax
import jax.numpy as jnp
from jax import lax
from jax.experimental import pallas as pl
from jax.experimental.pallas import tpu as pltpu
from jax.sharding import PartitionSpec as P

PASSES = 10
LANES = 128
GROUP = 16
VMEM = pl.BlockSpec(memory_space=pltpu.VMEM)
SMEM = pl.BlockSpec(memory_space=pltpu.SMEM)
HBM = pl.BlockSpec(memory_space=pltpu.HBM)
AFTER = pl.BlockSpec(memory_space=pl.ANY)
F32 = jnp.float32


def in_hbm(values):
    return pltpu.with_memory_space_constraint(values, pltpu.HBM)


def call(body, outs, ins, scratch=(), limit=16, cost=None, space=None):
    return pl.pallas_call(
        body,
        out_shape=outs,
        in_specs=ins,
        out_specs=[space or VMEM] * len(outs),
        scratch_shapes=list(scratch),
        compiler_params=pltpu.CompilerParams(vmem_limit_bytes=limit << 20),
        cost_estimate=cost,
    )


def cost(cycles):
    return pl.CostEstimate(flops=cycles * 4096, bytes_accessed=cycles * 1024, transcendentals=0)


def response(sens_ref, factor_ref, sensor, variable):
    total = sens_ref[sensor, 0] * factor_ref[0, variable]
    for u in range(1, factor_ref.shape[0]):
        total = total + sens_ref[sensor, u] * factor_ref[u, variable]
    return total


def fetch(pairs, sems):
    copies = [pltpu.make_async_copy(src, dst, sems.at[i]) for i, (src, dst) in enumerate(pairs)]
    for copy in copies:
        copy.start()
    return copies


def window_of(chip, chips, blocks):
    own = blocks // chips
    size = min(own + 2, own + chips - 1)
    return jnp.clip(chip * own - 1, 0, blocks - size), size


def my_chip():
    return lax.axis_index("var") // 2


def chip_count():
    return lax.axis_size("var") // 2


def lanes(start, size):
    return pl.ds(pl.multiple_of(start * LANES, LANES), size * LANES)


def first_kernel(slots, margin, sens_hbm, factor_hbm, control_hbm, kappa_hbm, tile_hbm, row_hbm, sensor_hbm,
                 value_hbm, weight_hbm, cols_hbm, own_ref, other_ref, response_ref, kappa_ref, even_ref,
                 odd_ref, *refs):
    chunk_refs = refs[:-11]
    (sens_ref, factor_ref, control_ref, tile_ref, row_ref, sensor_ref, value_ref, weight_ref, cols_ref,
     before_ref, sems) = refs[-11:]
    window = lanes(*window_of(my_chip(), chip_count(), own_ref.shape[1] // LANES))
    pairs = (
        (sens_hbm, sens_ref), (factor_hbm, factor_ref), (control_hbm, control_ref),
        (kappa_hbm.at[:, :, window], kappa_ref), (tile_hbm, tile_ref), (row_hbm, row_ref), (sensor_hbm, sensor_ref),
        (value_hbm, value_ref), (weight_hbm, weight_ref), (cols_hbm, cols_ref),
    )
    copies = [pltpu.make_async_copy(src, dst, sems.at[i]) for i, (src, dst) in enumerate(pairs)]
    for copy in copies:
        copy.start()
    from_panel = lax.broadcasted_iota(jnp.int32, before_ref.shape, 0)
    to_panel = lax.broadcasted_iota(jnp.int32, before_ref.shape, 1)
    before_ref[...] = jnp.where(from_panel < to_panel, 1.0, 0.0).astype(jnp.bfloat16)
    for copy in copies:
        copy.wait()

    member, mine = lax.axis_index("var"), lax.axis_index("tile")
    core = member % 2
    var_dev = control_ref.shape[0]
    for which, (sensor, out_ref) in enumerate(((core, own_ref), (1 - core, other_ref))):
        total = None
        for v in range(var_dev):
            scale = response(sens_ref, factor_ref, sensor, member * var_dev + v)
            response_ref[which, v] = jnp.full(response_ref.shape[2:], scale, F32)
            term = scale * control_ref[v]
            total = term if total is None else total + term
        out_ref[...] = total

    for i in range(2):
        pack_edges(even_ref.at[i], odd_ref.at[i], kappa_ref[i], margin)

    tiles = lax.axis_size("tile")
    full = tiles // 2 - 1
    first = jnp.where(core == 0, 2, tiles // 2 + 1)
    panels = value_ref.shape[0]
    source = tile_ref[...] ^ mine
    names = lax.broadcasted_iota(jnp.int32, (-(-tiles // 8) * 8, panels), 0)
    hits = jnp.where(names == source, 1.0, 0.0)
    ranks = jnp.dot(hits.astype(jnp.bfloat16), before_ref[...], preferred_element_type=F32)
    rank = jnp.sum(hits * ranks, axis=0, keepdims=True).astype(jnp.int32)
    parity, slot = rank % 2, rank // 2
    whole = (source >= first) & (source < first + full)
    home = source == 0
    keep = whole | ((home | (source == 1)) & (parity == core))
    half = jnp.where(whole, 2 * (source - first) + parity, jnp.where(home, tiles - 1, tiles - 2))
    place = jnp.where(keep, half * slots + slot, -1)
    spots = lax.broadcasted_iota(jnp.int32, (tiles * slots, panels), 0)
    pick = jnp.where(spots == place, 1.0, 0.0).astype(jnp.bfloat16)

    def picked(parts):
        total = None
        for part in parts:
            term = jnp.dot(pick, part.astype(jnp.bfloat16), preferred_element_type=F32)
            total = term if total is None else total + term
        return total

    cols = cols_ref[...]
    sent = (
        picked(thirds(value_ref[...])),
        picked(thirds(weight_ref[...])),
        picked(((cols // LANES * LANES).astype(F32), (cols % LANES).astype(F32))),
    )
    sub = lax.broadcasted_iota(jnp.int32, (8, panels), 0)
    lane = lax.broadcasted_iota(jnp.int32, (8, panels), 1)
    facts = jnp.where(sub == 0, row_ref[...], jnp.where(sub == 1, sensor_ref[...], 0)).astype(F32)
    meta = lax.dot_general(
        facts.astype(jnp.bfloat16), pick, (((1,), (1,)), ((), ())), preferred_element_type=F32
    )
    for i in range(tiles):
        held = jnp.sum(jnp.where(keep & (half == i), 1.0, 0.0), axis=1, keepdims=True)
        meta = jnp.where((sub == 2) & (lane == i), held, meta)
    for i in range(tiles):
        out_ref = chunk_refs[i // 2].at[i % 2] if i < 2 * full else chunk_refs[i - full]
        for part, rows in enumerate(sent):
            out_ref[part * slots : (part + 1) * slots] = rows[i * slots : (i + 1) * slots]
        out_ref[3 * slots :] = meta


def thirds(values):
    top = values.astype(jnp.bfloat16).astype(F32)
    rest = values - top
    middle = rest.astype(jnp.bfloat16).astype(F32)
    return top, middle, rest - middle


def pieces(values):
    top = values.astype(jnp.bfloat16).astype(F32)
    return top, values - top


def scatter_kernel(slots, blocks_all, after_ref, *refs):
    got_refs, (own_ref, other_ref, acc_ref, meta_ref, where_ref, sems) = refs[:-6], refs[-6:]
    core = lax.axis_index("var") % 2
    got_refs = [r.at[i] for r in got_refs[1:-1] for i in (0, 1)] + [got_refs[0], got_refs[-1]]
    size_of_group = min(GROUP, slots)
    rows = own_ref.shape[1]
    start, size = window_of(my_chip(), chip_count(), blocks_all)
    per_kind = padded_blocks(size)
    tall = 2 * per_kind
    line = lax.broadcasted_iota(jnp.int32, (8, LANES), 0)
    for s, ref in enumerate(got_refs):
        facts = ref[3 * slots : 3 * slots + 8].astype(jnp.int32)
        where_ref[8 * s : 8 * s + 8] = jnp.where(line == 0, (facts[1:2] * rows + facts[0:1]) * tall, facts)
    copy = pltpu.make_async_copy(where_ref, meta_ref, sems.at[0])
    copy.start()
    acc_ref[...] = jnp.zeros(acc_ref.shape, F32)
    place = lax.broadcasted_iota(jnp.int32, (tall, LANES), 0)
    is_weight = place < per_kind
    place = jnp.where(is_weight, place, place - per_kind) + start
    lane_ids = lax.broadcasted_iota(jnp.int32, (LANES, LANES), 0).astype(F32).astype(jnp.bfloat16)
    one, zero = jnp.bfloat16(1), jnp.bfloat16(0)
    sub = lax.broadcasted_iota(jnp.int32, (size_of_group, LANES), 0)
    blank = jnp.zeros((2 * tall, LANES), jnp.bfloat16)
    copy.wait()

    def load(s, base):
        got_ref = got_refs[s]
        count = meta_ref[8 * s + 2, s]
        value = got_ref[pl.ds(base, size_of_group), :]
        weight = got_ref[pl.ds(slots + base, size_of_group), :]
        cell = got_ref[pl.ds(2 * slots + base, size_of_group), :].astype(jnp.int32)
        weight = jnp.where(sub + base < count, weight, 0.0)
        return pieces(weight), pieces(weight * value), (cell % LANES).astype(F32), cell // LANES

    def one_hots(loaded, i):
        weights, values, low, high = loaded
        here = place == high[i : i + 1]
        rows_of = [
            jnp.where(here, jnp.where(is_weight, w[i : i + 1], v[i : i + 1]), 0.0)
            for w, v in zip(weights, values)
        ]
        left = jnp.concatenate(rows_of, axis=0).astype(jnp.bfloat16)
        column = jnp.broadcast_to(low[i : i + 1], (16, LANES)).astype(jnp.bfloat16)
        column = jnp.concatenate([column] * (LANES // 16), axis=0)
        return left, jnp.where(lane_ids == column, one, zero)

    def step(chosen, g, carry):
        base = pl.multiple_of(g * size_of_group, size_of_group)
        loaded = {s: load(s, base) for s in chosen}
        for k in range(size_of_group):
            for pair in zip(chosen[::2], chosen[1::2]):
                hots = [one_hots(loaded[s], k) for s in pair]
                left = jnp.concatenate(
                    [
                        jnp.concatenate([hots[0][0], blank], axis=1),
                        jnp.concatenate([blank, hots[1][0]], axis=1),
                    ],
                    axis=0,
                )
                both = lax.dot_general(
                    left, jnp.concatenate([hots[0][1], hots[1][1]], axis=1), (((1,), (1,)), ((), ())),
                    preferred_element_type=F32,
                )
                for i, s in enumerate(pair):
                    at = pl.multiple_of(meta_ref[8 * s, s * slots + base + k], 8)
                    mine = both[2 * i * tall : 2 * (i + 1) * tall]
                    acc_ref[pl.ds(at, tall), :] += mine[:tall] + mine[tall:]
        return carry

    for s in range(0, len(got_refs), 4):
        chosen = list(range(s, s + 4))
        most = meta_ref[8 * s + 2, s]
        for other in chosen[1:]:
            most = jnp.maximum(most, meta_ref[8 * other + 2, other])
        turns = (most + size_of_group - 1) // size_of_group
        lax.fori_loop(0, turns, functools.partial(step, chosen), 0)
    for sensor, out_ref in ((core, own_ref), (1 - core, other_ref)):
        begin = sensor * rows * tall
        for kind in range(2):
            for b in range(size):
                out_ref[kind, :, b * LANES : (b + 1) * LANES] = acc_ref[
                    pl.ds(begin + kind * per_kind + b, rows, stride=tall), :
                ]


def padded_blocks(size):
    return -(-size // 4) * 4


def even_tile():
    return lax.axis_index("tile") % 2 == 0


def has_above():
    return lax.axis_index("tile") > 0


def has_below():
    return lax.axis_index("tile") + 1 < lax.axis_size("tile")


def pack_edges(even_ref, odd_ref, rows_value, margin):
    rows, width = rows_value.shape
    even = even_tile()
    for b in range(width // LANES):
        at = slice(b * LANES, (b + 1) * LANES)
        head, tail = rows_value[:margin, at], rows_value[rows - margin :, at]
        even_ref[b * margin : (b + 1) * margin] = jnp.where(even, tail, head)
        odd_ref[b * margin : (b + 1) * margin] = jnp.where(even, head, tail)


def cut_kernel(first_ref, second_ref, mine_ref, *out_refs):
    chip, chips, blocks = my_chip(), chip_count(), first_ref.shape[1] // LANES
    for d, out_ref in enumerate((mine_ref, *out_refs)):
        window = lanes(*window_of(chip ^ d, chips, blocks))
        out_ref[...] = first_ref[:, window] + second_ref[:, window]


def edges_kernel(margin, *refs):
    terms, (total_ref, even_ref, odd_ref) = refs[:-3], refs[-3:]
    total = terms[0][...]
    for term in terms[1:]:
        total = total + term[...]
    total_ref[...] = total
    pack_edges(even_ref, odd_ref, total, margin)


def ring_rows(rows, margin):
    return -(-(rows + 2 * margin) // 8) * 8


def lay_ring(ref, own, from_even, from_odd, margin):
    rows, total = own.shape[0], ref.shape[0]
    even = even_tile()
    ref[rows:total] = jnp.zeros((total - rows, ref.shape[1]), F32)
    ref[:rows] = own
    for b in range(ref.shape[1] // LANES):
        at = slice(b * LANES, (b + 1) * LANES)
        one, two = (m[b * margin : (b + 1) * margin] for m in (from_even, from_odd))
        ref[rows : rows + margin, at] = jnp.where(has_below(), jnp.where(even, one, two), 0.0)
        ref[total - margin :, at] = jnp.where(has_above(), jnp.where(even, two, one), 0.0)


def block(ref, j):
    return ref[:, j * LANES : (j + 1) * LANES]


def sideways(blocks):
    shape = blocks[0].shape
    lane = lax.broadcasted_iota(jnp.int32, shape, 1)
    zero = jnp.zeros(shape, F32)
    ahead = [pltpu.roll(x, 1, 1) for x in blocks]
    back = [pltpu.roll(x, LANES - 1, 1) for x in blocks]
    for j, here in enumerate(blocks):
        before = ahead[j - 1] if j else zero
        after = back[j + 1] if j + 1 < len(blocks) else zero
        yield here, jnp.where(lane == 0, before, ahead[j]), jnp.where(lane == LANES - 1, after, back[j])


def face_weights(coef_ref, row_ref, col_ref, rows, margin):
    total, width = row_ref.shape
    blocks = width // LANES
    r = lax.broadcasted_iota(jnp.int32, (total, LANES), 0)
    inside = (
        (r < rows)
        | ((r < rows + margin) & has_below())
        | ((r >= total - margin) & has_above())
    )
    scale = jnp.where(inside, 0.125, 0.0)
    unit = jnp.where(inside, 1.0, 0.0)
    columns = [block(col_ref, j) for j in range(blocks)]
    for j, (k_col, k_left, k_right) in enumerate(sideways(columns)):
        at = slice(j * LANES, (j + 1) * LANES)
        k_row = block(row_ref, j)
        up = scale * (k_row + pltpu.roll(k_row, 1, 0))
        down = scale * (k_row + pltpu.roll(k_row, total - 1, 0))
        left = scale * (k_col + k_left)
        right = scale * (k_col + k_right)
        coef_ref[0, :, at] = unit - up - down - left - right
        coef_ref[1, :, at] = up
        coef_ref[2, :, at] = down
        coef_ref[3, :, at] = left
        coef_ref[4, :, at] = right


def one_pass(fields, coef_ref, spans):
    def weights(i, at):
        got = [coef_ref[i, span, at] for span in spans]
        return jnp.concatenate(got, axis=0) if len(got) > 1 else got[0]

    total = fields[0].shape[0]
    out = []
    for j, (here, left, right) in enumerate(sideways(fields)):
        at = slice(j * LANES, (j + 1) * LANES)
        out.append(
            weights(0, at) * here
            + weights(1, at) * pltpu.roll(here, 1, 0)
            + weights(2, at) * pltpu.roll(here, total - 1, 0)
            + weights(3, at) * left
            + weights(4, at) * right
        )
    return out


def diffuse(ring_ref, coef_ref, rows, margin):
    total, width = ring_ref.shape
    inner = margin // 8 * 8
    wide = [slice(0, total)]
    narrow = [slice(0, rows + inner), slice(total - inner, total)]
    fields = [block(ring_ref, j) for j in range(width // LANES)]
    for _ in range(margin - inner):
        fields = one_pass(fields, coef_ref, wide)
    fields = [jnp.concatenate([f[span] for span in narrow], axis=0) for f in fields]
    for _ in range(inner):
        fields = one_pass(fields, coef_ref, narrow)
    return [f[:rows] for f in fields]


def faces_kernel(margin, even_ref, odd_ref, kappa_ref, sums_ref, *refs):
    coef_ref, sums_out, one_ref, two_ref = refs[-4:]
    sums_out[...] = sums_ref[...]
    rows = kappa_ref.shape[1]
    lay_ring(one_ref, kappa_ref[0], even_ref.at[0], odd_ref.at[0], margin)
    lay_ring(two_ref, kappa_ref[1], even_ref.at[1], odd_ref.at[1], margin)
    face_weights(coef_ref, one_ref, two_ref, rows, margin)


def smooth_kernel(margin, own_ref, even_ref, odd_ref, coef_ref, out_ref, ring_ref):
    rows = own_ref.shape[0]
    lay_ring(ring_ref, own_ref[...], even_ref, odd_ref, margin)
    for j, field in enumerate(diffuse(ring_ref, coef_ref, rows, margin)):
        out_ref[:, j * LANES : (j + 1) * LANES] = field


def adjoint_kernel(margin, smooth_ref, mask_ref, sums_ref, more_ref, adjoint_ref, even_ref, odd_ref):
    weight = sums_ref[0] + more_ref[0]
    value = sums_ref[1] + more_ref[1]
    window = lanes(*window_of(my_chip(), chip_count(), mask_ref.shape[1] // LANES))
    adjoint = mask_ref[:, window].astype(F32) * (weight * smooth_ref[...] - value)
    adjoint_ref[...] = adjoint
    pack_edges(even_ref, odd_ref, adjoint, margin)


def spread_kernel(margin, own_ref, even_ref, odd_ref, coef_ref, out_ref, ring_ref):
    rows = own_ref.shape[0]
    lay_ring(ring_ref, own_ref[...], even_ref, odd_ref, margin)
    for j, field in enumerate(diffuse(ring_ref, coef_ref, rows, margin)):
        ring_ref[:rows, j * LANES : (j + 1) * LANES] = field
    own = out_ref.shape[1] // LANES
    start = window_of(my_chip(), chip_count(), own * chip_count())[0]
    out_ref[...] = ring_ref[:rows, lanes(my_chip() * own - start, own)]


def sent_last(members):
    return [0, 1] + sorted(range(2, members), key=lambda d: -(d % 2))


def result_kernel(response_ref, control_ref, *refs):
    refs, (out_ref, line_ref, sems) = refs[:-3], refs[-3:]
    own = refs[0].shape[1] // LANES
    refs = [refs[sent_last(len(refs)).index(d)] for d in range(len(refs))]
    copies = []
    for v in range(control_ref.shape[0]):
        mine, theirs = (response_ref[i, v][:1, :1] for i in range(2))
        for d in range(len(refs) // 2):
            window = lanes((my_chip() ^ d) * own, own)
            line_ref[v, :, window] = (
                control_ref[v, :, window] + mine * refs[2 * d][...] + theirs * refs[2 * d + 1][...]
            )
        copies.append(pltpu.make_async_copy(line_ref.at[v], out_ref.at[v], sems.at[v]))
        copies[-1].start()
    for copy in copies:
        copy.wait()


def swap(values, axis, bit):
    count = lax.axis_size(axis)
    return lax.ppermute(values, axis, [(i, i ^ bit) for i in range(count)])


def swap_edges(even, odd):
    tiles, members = lax.axis_size("tile"), lax.axis_size("var")
    pairs = []
    for t in range(tiles):
        other = t + 1 if t % 2 else t - 1
        for q in range(members):
            to = other * members + q if 0 <= other < tiles else t * members + (q ^ 1)
            pairs.append((t * members + q, to))
    return swap(even, "tile", 1), lax.ppermute(odd, ("tile", "var"), pairs)


def deliver(chunks):
    tiles, members = lax.axis_size("tile"), lax.axis_size("var")
    got = []
    for turn, chunk in enumerate(chunks[:-1]):
        pairs = []
        for t in range(tiles):
            for q in range(members):
                offset = 1 if turn == len(chunks) - 2 else 2 + turn + (q % 2) * (tiles // 2 - 1)
                pairs.append((t * members + q, (t ^ offset) * members + q))
        got.append(lax.ppermute(chunk, ("tile", "var"), pairs))
    return got + [chunks[-1]]


def local(control, diffusivity, land_mask, panel_tile, panel_row, panel_cols, obs_values,
          obs_weights, panel_sensor, sensitivity, cross_factor):
    rows, width = control.shape[1:]
    var_dev = control.shape[0]
    tiles, members = lax.axis_size("tile"), lax.axis_size("var")
    panels, panel_width = panel_cols.shape
    slots = panels // tiles
    blocks = width // LANES
    margin = PASSES
    total = ring_rows(rows, margin)
    chips = members // 2
    size = window_of(0, chips, blocks)[1]
    field = jax.ShapeDtypeStruct((rows, width), F32)
    share = jax.ShapeDtypeStruct((rows, width // chips), F32)
    view = jax.ShapeDtypeStruct((rows, size * LANES), F32)
    view2 = jax.ShapeDtypeStruct((2, *view.shape), F32)
    edge = jax.ShapeDtypeStruct((margin * size, LANES), F32)
    edge2 = jax.ShapeDtypeStruct((2, *edge.shape), F32)
    half = jax.ShapeDtypeStruct((3 * slots + 8, panel_width), F32)
    chunks = [jax.ShapeDtypeStruct((2, *half.shape), F32)] * (tiles // 2 - 1) + [half] * 2
    line = pltpu.VMEM((1, panels), jnp.int32)

    own, other, responses, kappa, kappa_even, kappa_odd, *chunks = call(
        functools.partial(first_kernel, slots, margin),
        [field, field, jax.ShapeDtypeStruct((2, var_dev, 8, LANES), F32), view2, edge2, edge2]
        + chunks,
        [HBM] * 10,
        [
            pltpu.SMEM(sensitivity.shape, F32),
            pltpu.SMEM(cross_factor.shape, F32),
            pltpu.VMEM(control.shape, F32),
            line, line, line,
            pltpu.VMEM(obs_values.shape, F32),
            pltpu.VMEM(obs_weights.shape, F32),
            pltpu.VMEM(panel_cols.shape, jnp.int32),
            pltpu.VMEM((panels, panels), jnp.bfloat16),
            pltpu.SemaphoreType.DMA((10,)),
        ],
        cost=cost(3000),
    )(*(in_hbm(x) for x in (sensitivity, cross_factor, control, diffusivity, panel_tile.reshape(1, -1),
                            panel_row.reshape(1, -1), panel_sensor.reshape(1, -1), obs_values,
                            obs_weights, panel_cols)))

    got = deliver(chunks)
    part, *parts = call(cut_kernel, [view] * chips, [VMEM] * 2, cost=cost(200))(
        own, swap(other, "var", 1)
    )
    parts = [swap(p, "var", 2 * (d + 1)) for d, p in enumerate(parts)]
    kappa_even, kappa_odd = swap_edges(kappa_even, kappa_odd)
    smooth_in, even, odd = call(
        functools.partial(edges_kernel, margin), [view, edge, edge], [VMEM] * chips, cost=cost(500)
    )(part, *parts)
    even, odd = swap_edges(even, odd)
    sums, sums_other = call(
        functools.partial(scatter_kernel, slots, blocks),
        [view2, view2],
        [AFTER] + [VMEM] * len(got),
        [
            pltpu.VMEM((2 * rows * 2 * padded_blocks(size), LANES), F32),
            pltpu.SMEM((8 * tiles, LANES), jnp.int32),
            pltpu.VMEM((8 * tiles, LANES), jnp.int32),
            pltpu.SemaphoreType.DMA((1,)),
        ],
        cost=cost(100000),
    )(smooth_in, got[-2], *got[:-2], got[-1])
    ring = pltpu.VMEM((total, size * LANES), F32)
    coef, sums_other = call(
        functools.partial(faces_kernel, margin),
        [jax.ShapeDtypeStruct((5, total, size * LANES), F32), view2],
        [VMEM] * 4 + [AFTER] * 2,
        [ring, ring],
        cost=cost(1000),
    )(kappa_even, kappa_odd, kappa, sums_other, even, odd)
    more_sums = swap(sums_other, "var", 1)
    (smooth,) = call(
        functools.partial(smooth_kernel, margin),
        [view],
        [VMEM] * 4,
        [ring],
        cost=cost(4000),
    )(smooth_in, even, odd, coef)
    adjoint, even, odd = call(
        functools.partial(adjoint_kernel, margin), [view, edge, edge], [VMEM] * 4, cost=cost(500)
    )(smooth, land_mask, sums, more_sums)
    even, odd = swap_edges(even, odd)
    (mine,) = call(
        functools.partial(spread_kernel, margin),
        [share],
        [VMEM] * 4,
        [ring],
        cost=cost(4000),
    )(adjoint, even, odd, coef)
    shares = [mine] + [swap(mine, "var", d) for d in sent_last(members)[1:]]
    (out,) = call(
        result_kernel,
        [jax.ShapeDtypeStruct(control.shape, F32)],
        [VMEM] * (2 + members),
        [pltpu.VMEM(control.shape, F32), pltpu.SemaphoreType.DMA((var_dev,))],
        cost=cost(1000),
        space=HBM,
    )(responses, control, *shares)
    return out


def solution(mesh):
    return jax.shard_map(
        local,
        mesh=mesh,
        in_specs=(
            P("var", ("grp", "tile"), None),
            P(None, ("grp", "tile"), None),
            P(("grp", "tile"), None),
            P(("grp", "tile"), None),
            P(("grp", "tile")),
            P(("grp", "tile"), None),
            P(("grp", "tile"), None),
            P(("grp", "tile"), None),
            P(("grp", "tile")),
            P(),
            P(),
        ),
        out_specs=P("var", ("grp", "tile"), None),
        check_vma=False,
    )
```

```python
import functools

import jax
import jax.numpy as jnp
from jax import lax
from jax.experimental import pallas as pl
from jax.experimental.pallas import tpu as pltpu
from jax.sharding import PartitionSpec as P

PASSES = 10
LANES = 128
GROUP = 16
VMEM = pl.BlockSpec(memory_space=pltpu.VMEM)
SMEM = pl.BlockSpec(memory_space=pltpu.SMEM)
HBM = pl.BlockSpec(memory_space=pltpu.HBM)
AFTER = pl.BlockSpec(memory_space=pl.ANY)
F32 = jnp.float32


def in_hbm(values):
    return pltpu.with_memory_space_constraint(values, pltpu.HBM)


def call(body, outs, ins, scratch=(), limit=16, cost=None, space=None):
    return pl.pallas_call(
        body,
        out_shape=outs,
        in_specs=ins,
        out_specs=[space or VMEM] * len(outs),
        scratch_shapes=list(scratch),
        compiler_params=pltpu.CompilerParams(vmem_limit_bytes=limit << 20),
        cost_estimate=cost,
    )


def cost(cycles):
    return pl.CostEstimate(flops=cycles * 4096, bytes_accessed=cycles * 1024, transcendentals=0)


def response(sens_ref, factor_ref, sensor, variable):
    total = sens_ref[sensor, 0] * factor_ref[0, variable]
    for u in range(1, factor_ref.shape[0]):
        total = total + sens_ref[sensor, u] * factor_ref[u, variable]
    return total


def fetch(pairs, sems):
    copies = [pltpu.make_async_copy(src, dst, sems.at[i]) for i, (src, dst) in enumerate(pairs)]
    for copy in copies:
        copy.start()
    return copies


def window_of(chip, chips, blocks):
    own = blocks // chips
    size = min(own + 2, own + chips - 1)
    return jnp.clip(chip * own - 1, 0, blocks - size), size


def my_chip():
    return lax.axis_index("var") // 2


def chip_count():
    return lax.axis_size("var") // 2


def lanes(start, size):
    return pl.ds(pl.multiple_of(start * LANES, LANES), size * LANES)


def first_kernel(slots, margin, sens_hbm, factor_hbm, control_hbm, kappa_hbm, tile_hbm, row_hbm, sensor_hbm,
                 value_hbm, weight_hbm, cols_hbm, own_ref, other_ref, response_ref, kappa_ref, odd_ref,
                 *refs):
    chunk_refs = refs[:-11]
    (sens_ref, factor_ref, control_ref, tile_ref, row_ref, sensor_ref, value_ref, weight_ref, cols_ref,
     before_ref, sems) = refs[-11:]
    window = lanes(*window_of(my_chip(), chip_count(), own_ref.shape[1] // LANES))
    pairs = (
        (sens_hbm, sens_ref), (factor_hbm, factor_ref), (control_hbm, control_ref),
        (kappa_hbm.at[:, :, window], kappa_ref), (tile_hbm, tile_ref), (row_hbm, row_ref), (sensor_hbm, sensor_ref),
        (value_hbm, value_ref), (weight_hbm, weight_ref), (cols_hbm, cols_ref),
    )
    copies = [pltpu.make_async_copy(src, dst, sems.at[i]) for i, (src, dst) in enumerate(pairs)]
    for copy in copies:
        copy.start()
    from_panel = lax.broadcasted_iota(jnp.int32, before_ref.shape, 0)
    to_panel = lax.broadcasted_iota(jnp.int32, before_ref.shape, 1)
    before_ref[...] = jnp.where(from_panel < to_panel, 1.0, 0.0).astype(jnp.bfloat16)
    for copy in copies:
        copy.wait()

    member, mine = lax.axis_index("var"), lax.axis_index("tile")
    core = member % 2
    var_dev = control_ref.shape[0]
    for which, (sensor, out_ref) in enumerate(((core, own_ref), (1 - core, other_ref))):
        total = None
        for v in range(var_dev):
            scale = response(sens_ref, factor_ref, sensor, member * var_dev + v)
            response_ref[which, v] = jnp.full(response_ref.shape[2:], scale, F32)
            term = scale * control_ref[v]
            total = term if total is None else total + term
        out_ref[...] = total

    for i in range(2):
        even_ref = even_kappa(chunk_refs[-2], slots, odd_ref.shape[1], i)
        pack_edges(even_ref, odd_ref.at[i], kappa_ref[i], margin)

    tiles = lax.axis_size("tile")
    full = tiles // 2 - 1
    first = jnp.where(core == 0, 2, tiles // 2 + 1)
    panels = value_ref.shape[0]
    source = tile_ref[...] ^ mine
    names = lax.broadcasted_iota(jnp.int32, (-(-tiles // 8) * 8, panels), 0)
    hits = jnp.where(names == source, 1.0, 0.0)
    ranks = jnp.dot(hits.astype(jnp.bfloat16), before_ref[...], preferred_element_type=F32)
    rank = jnp.sum(hits * ranks, axis=0, keepdims=True).astype(jnp.int32)
    parity, slot = rank % 2, rank // 2
    whole = (source >= first) & (source < first + full)
    home = source == 0
    keep = whole | ((home | (source == 1)) & (parity == core))
    half = jnp.where(whole, 2 * (source - first) + parity, jnp.where(home, tiles - 1, tiles - 2))
    place = jnp.where(keep, half * slots + slot, -1)
    spots = lax.broadcasted_iota(jnp.int32, (tiles * slots, panels), 0)
    pick = jnp.where(spots == place, 1.0, 0.0).astype(jnp.bfloat16)

    def picked(parts):
        total = None
        for part in parts:
            term = jnp.dot(pick, part.astype(jnp.bfloat16), preferred_element_type=F32)
            total = term if total is None else total + term
        return total

    cols = cols_ref[...]
    sent = (
        picked(thirds(value_ref[...])),
        picked(thirds(weight_ref[...])),
        picked(((cols // LANES * LANES).astype(F32), (cols % LANES).astype(F32))),
    )
    sub = lax.broadcasted_iota(jnp.int32, (8, panels), 0)
    lane = lax.broadcasted_iota(jnp.int32, (8, panels), 1)
    facts = jnp.where(sub == 0, row_ref[...], jnp.where(sub == 1, sensor_ref[...], 0)).astype(F32)
    meta = lax.dot_general(
        facts.astype(jnp.bfloat16), pick, (((1,), (1,)), ((), ())), preferred_element_type=F32
    )
    for i in range(tiles):
        held = jnp.sum(jnp.where(keep & (half == i), 1.0, 0.0), axis=1, keepdims=True)
        meta = jnp.where((sub == 2) & (lane == i), held, meta)
    for i in range(tiles):
        out_ref = chunk_refs[i // 2].at[i % 2] if i < 2 * full else chunk_refs[i - full]
        for part, rows in enumerate(sent):
            out_ref[part * slots : (part + 1) * slots] = rows[i * slots : (i + 1) * slots]
        out_ref[3 * slots : 3 * slots + 8] = meta


def thirds(values):
    top = values.astype(jnp.bfloat16).astype(F32)
    rest = values - top
    middle = rest.astype(jnp.bfloat16).astype(F32)
    return top, middle, rest - middle


def pieces(values):
    top = values.astype(jnp.bfloat16).astype(F32)
    return top, values - top


def scatter_kernel(slots, blocks_all, after_ref, *refs):
    got_refs, (own_ref, other_ref, acc_ref, meta_ref, where_ref, sems) = refs[:-6], refs[-6:]
    core = lax.axis_index("var") % 2
    got_refs = [r.at[i] for r in got_refs[1:-1] for i in (0, 1)] + [got_refs[0], got_refs[-1]]
    size_of_group = min(GROUP, slots)
    rows = own_ref.shape[1]
    start, size = window_of(my_chip(), chip_count(), blocks_all)
    per_kind = padded_blocks(size)
    tall = 2 * per_kind
    line = lax.broadcasted_iota(jnp.int32, (8, LANES), 0)
    for s, ref in enumerate(got_refs):
        facts = ref[3 * slots : 3 * slots + 8].astype(jnp.int32)
        where_ref[8 * s : 8 * s + 8] = jnp.where(line == 0, (facts[1:2] * rows + facts[0:1]) * tall, facts)
    copy = pltpu.make_async_copy(where_ref, meta_ref, sems.at[0])
    copy.start()
    acc_ref[...] = jnp.zeros(acc_ref.shape, F32)
    place = lax.broadcasted_iota(jnp.int32, (tall, LANES), 0)
    is_weight = place < per_kind
    place = jnp.where(is_weight, place, place - per_kind) + start
    lane_ids = lax.broadcasted_iota(jnp.int32, (LANES, LANES), 0).astype(F32).astype(jnp.bfloat16)
    one, zero = jnp.bfloat16(1), jnp.bfloat16(0)
    sub = lax.broadcasted_iota(jnp.int32, (size_of_group, LANES), 0)
    blank = jnp.zeros((2 * tall, LANES), jnp.bfloat16)
    copy.wait()

    def load(s, base):
        got_ref = got_refs[s]
        count = meta_ref[8 * s + 2, s]
        value = got_ref[pl.ds(base, size_of_group), :]
        weight = got_ref[pl.ds(slots + base, size_of_group), :]
        cell = got_ref[pl.ds(2 * slots + base, size_of_group), :].astype(jnp.int32)
        weight = jnp.where(sub + base < count, weight, 0.0)
        return pieces(weight), pieces(weight * value), (cell % LANES).astype(F32), cell // LANES

    def one_hots(loaded, i):
        weights, values, low, high = loaded
        here = place == high[i : i + 1]
        rows_of = [
            jnp.where(here, jnp.where(is_weight, w[i : i + 1], v[i : i + 1]), 0.0)
            for w, v in zip(weights, values)
        ]
        left = jnp.concatenate(rows_of, axis=0).astype(jnp.bfloat16)
        column = jnp.broadcast_to(low[i : i + 1], (16, LANES)).astype(jnp.bfloat16)
        column = jnp.concatenate([column] * (LANES // 16), axis=0)
        return left, jnp.where(lane_ids == column, one, zero)

    def step(chosen, g, carry):
        base = pl.multiple_of(g * size_of_group, size_of_group)
        loaded = {s: load(s, base) for s in chosen}
        for k in range(size_of_group):
            for pair in zip(chosen[::2], chosen[1::2]):
                hots = [one_hots(loaded[s], k) for s in pair]
                left = jnp.concatenate(
                    [
                        jnp.concatenate([hots[0][0], blank], axis=1),
                        jnp.concatenate([blank, hots[1][0]], axis=1),
                    ],
                    axis=0,
                )
                both = lax.dot_general(
                    left, jnp.concatenate([hots[0][1], hots[1][1]], axis=1), (((1,), (1,)), ((), ())),
                    preferred_element_type=F32,
                )
                for i, s in enumerate(pair):
                    at = pl.multiple_of(meta_ref[8 * s, s * slots + base + k], 8)
                    mine = both[2 * i * tall : 2 * (i + 1) * tall]
                    acc_ref[pl.ds(at, tall), :] += mine[:tall] + mine[tall:]
        return carry

    for s in range(0, len(got_refs), 4):
        chosen = list(range(s, s + 4))
        most = meta_ref[8 * s + 2, s]
        for other in chosen[1:]:
            most = jnp.maximum(most, meta_ref[8 * other + 2, other])
        turns = (most + size_of_group - 1) // size_of_group
        lax.fori_loop(0, turns, functools.partial(step, chosen), 0)
    for sensor, out_ref in ((core, own_ref), (1 - core, other_ref)):
        begin = sensor * rows * tall
        for kind in range(2):
            for b in range(size):
                out_ref[kind, :, b * LANES : (b + 1) * LANES] = acc_ref[
                    pl.ds(begin + kind * per_kind + b, rows, stride=tall), :
                ]


def padded_blocks(size):
    return -(-size // 4) * 4


def even_tile():
    return lax.axis_index("tile") % 2 == 0


def has_above():
    return lax.axis_index("tile") > 0


def has_below():
    return lax.axis_index("tile") + 1 < lax.axis_size("tile")


def pack_edges(even_ref, odd_ref, rows_value, margin):
    rows, width = rows_value.shape
    even = even_tile()
    for b in range(width // LANES):
        at = slice(b * LANES, (b + 1) * LANES)
        head, tail = rows_value[:margin, at], rows_value[rows - margin :, at]
        even_ref[b * margin : (b + 1) * margin] = jnp.where(even, tail, head)
        odd_ref[b * margin : (b + 1) * margin] = jnp.where(even, head, tail)


def even_kappa(ref, slots, edge_rows, i):
    return ref.at[pl.ds(3 * slots + 8 + i * (-(-edge_rows // 8) * 8), edge_rows)]


def relay_kernel(*refs):
    for in_ref, out_ref in zip(refs[: len(refs) // 2], refs[len(refs) // 2 :]):
        out_ref[...] = in_ref[...]


def cut_kernel(first_ref, second_ref, mine_ref, *out_refs):
    chip, chips, blocks = my_chip(), chip_count(), first_ref.shape[1] // LANES
    for d, out_ref in enumerate((mine_ref, *out_refs)):
        window = lanes(*window_of(chip ^ d, chips, blocks))
        out_ref[...] = first_ref[:, window] + second_ref[:, window]


def edges_kernel(margin, *refs):
    terms, (total_ref, even_ref, odd_ref) = refs[:-3], refs[-3:]
    total = terms[0][...]
    for term in terms[1:]:
        total = total + term[...]
    total_ref[...] = total
    pack_edges(even_ref, odd_ref, total, margin)


def ring_rows(rows, margin):
    return -(-(rows + 2 * margin) // 8) * 8


def lay_ring(ref, own, from_even, from_odd, margin):
    rows, total = own.shape[0], ref.shape[0]
    even = even_tile()
    ref[rows:total] = jnp.zeros((total - rows, ref.shape[1]), F32)
    ref[:rows] = own
    for b in range(ref.shape[1] // LANES):
        at = slice(b * LANES, (b + 1) * LANES)
        one, two = (m[b * margin : (b + 1) * margin] for m in (from_even, from_odd))
        ref[rows : rows + margin, at] = jnp.where(has_below(), jnp.where(even, one, two), 0.0)
        ref[total - margin :, at] = jnp.where(has_above(), jnp.where(even, two, one), 0.0)


def block(ref, j):
    return ref[:, j * LANES : (j + 1) * LANES]


def sideways(blocks):
    shape = blocks[0].shape
    lane = lax.broadcasted_iota(jnp.int32, shape, 1)
    zero = jnp.zeros(shape, F32)
    ahead = [pltpu.roll(x, 1, 1) for x in blocks]
    back = [pltpu.roll(x, LANES - 1, 1) for x in blocks]
    for j, here in enumerate(blocks):
        before = ahead[j - 1] if j else zero
        after = back[j + 1] if j + 1 < len(blocks) else zero
        yield here, jnp.where(lane == 0, before, ahead[j]), jnp.where(lane == LANES - 1, after, back[j])


def face_weights(coef_ref, row_ref, col_ref, rows, margin):
    total, width = row_ref.shape
    blocks = width // LANES
    r = lax.broadcasted_iota(jnp.int32, (total, LANES), 0)
    inside = (
        (r < rows)
        | ((r < rows + margin) & has_below())
        | ((r >= total - margin) & has_above())
    )
    scale = jnp.where(inside, 0.125, 0.0)
    unit = jnp.where(inside, 1.0, 0.0)
    columns = [block(col_ref, j) for j in range(blocks)]
    for j, (k_col, k_left, k_right) in enumerate(sideways(columns)):
        at = slice(j * LANES, (j + 1) * LANES)
        k_row = block(row_ref, j)
        up = scale * (k_row + pltpu.roll(k_row, 1, 0))
        down = scale * (k_row + pltpu.roll(k_row, total - 1, 0))
        left = scale * (k_col + k_left)
        right = scale * (k_col + k_right)
        coef_ref[0, :, at] = unit - up - down - left - right
        coef_ref[1, :, at] = up
        coef_ref[2, :, at] = down
        coef_ref[3, :, at] = left
        coef_ref[4, :, at] = right


def one_pass(fields, coef_ref, spans):
    def weights(i, at):
        got = [coef_ref[i, span, at] for span in spans]
        return jnp.concatenate(got, axis=0) if len(got) > 1 else got[0]

    total = fields[0].shape[0]
    out = []
    for j, (here, left, right) in enumerate(sideways(fields)):
        at = slice(j * LANES, (j + 1) * LANES)
        out.append(
            weights(0, at) * here
            + weights(1, at) * pltpu.roll(here, 1, 0)
            + weights(2, at) * pltpu.roll(here, total - 1, 0)
            + weights(3, at) * left
            + weights(4, at) * right
        )
    return out


def diffuse(ring_ref, coef_ref, rows, margin):
    total, width = ring_ref.shape
    inner = margin // 8 * 8
    wide = [slice(0, total)]
    narrow = [slice(0, rows + inner), slice(total - inner, total)]
    fields = [block(ring_ref, j) for j in range(width // LANES)]
    for _ in range(margin - inner):
        fields = one_pass(fields, coef_ref, wide)
    fields = [jnp.concatenate([f[span] for span in narrow], axis=0) for f in fields]
    for _ in range(inner):
        fields = one_pass(fields, coef_ref, narrow)
    return [f[:rows] for f in fields]


def faces_kernel(margin, slots, shared_ref, odd_ref, kappa_ref, sums_ref, *refs):
    coef_ref, sums_out, one_ref, two_ref = refs[-4:]
    sums_out[...] = sums_ref[...]
    rows = kappa_ref.shape[1]
    for i, ring_ref in enumerate((one_ref, two_ref)):
        even_ref = even_kappa(shared_ref, slots, odd_ref.shape[1], i)
        lay_ring(ring_ref, kappa_ref[i], even_ref, odd_ref.at[i], margin)
    face_weights(coef_ref, one_ref, two_ref, rows, margin)


def smooth_kernel(margin, own_ref, even_ref, odd_ref, coef_ref, out_ref, ring_ref):
    rows = own_ref.shape[0]
    lay_ring(ring_ref, own_ref[...], even_ref, odd_ref, margin)
    for j, field in enumerate(diffuse(ring_ref, coef_ref, rows, margin)):
        out_ref[:, j * LANES : (j + 1) * LANES] = field


def adjoint_kernel(margin, smooth_ref, mask_ref, sums_ref, more_ref, adjoint_ref, even_ref, odd_ref):
    weight = sums_ref[0] + more_ref[0]
    value = sums_ref[1] + more_ref[1]
    window = lanes(*window_of(my_chip(), chip_count(), mask_ref.shape[1] // LANES))
    adjoint = mask_ref[:, window].astype(F32) * (weight * smooth_ref[...] - value)
    adjoint_ref[...] = adjoint
    pack_edges(even_ref, odd_ref, adjoint, margin)


def spread_kernel(margin, own_ref, even_ref, odd_ref, coef_ref, out_ref, ring_ref):
    rows = own_ref.shape[0]
    lay_ring(ring_ref, own_ref[...], even_ref, odd_ref, margin)
    for j, field in enumerate(diffuse(ring_ref, coef_ref, rows, margin)):
        ring_ref[:rows, j * LANES : (j + 1) * LANES] = field
    own = out_ref.shape[1] // LANES
    start = window_of(my_chip(), chip_count(), own * chip_count())[0]
    out_ref[...] = ring_ref[:rows, lanes(my_chip() * own - start, own)]


def sent_last(members):
    return [0, 1] + sorted(range(2, members), key=lambda d: d % 2)


def result_kernel(response_ref, control_ref, *refs):
    refs, (out_ref, line_ref, sems) = refs[:-3], refs[-3:]
    own = refs[0].shape[1] // LANES
    refs = [refs[sent_last(len(refs)).index(d)] for d in range(len(refs))]
    copies = []
    for v in range(control_ref.shape[0]):
        mine, theirs = (response_ref[i, v][:1, :1] for i in range(2))
        for d in range(len(refs) // 2):
            window = lanes((my_chip() ^ d) * own, own)
            line_ref[v, :, window] = (
                control_ref[v, :, window] + mine * refs[2 * d][...] + theirs * refs[2 * d + 1][...]
            )
        copies.append(pltpu.make_async_copy(line_ref.at[v], out_ref.at[v], sems.at[v]))
        copies[-1].start()
    for copy in copies:
        copy.wait()


def swap(values, axis, bit):
    count = lax.axis_size(axis)
    return lax.ppermute(values, axis, [(i, i ^ bit) for i in range(count)])


def swap_odd(edges):
    tiles, members = lax.axis_size("tile"), lax.axis_size("var")
    pairs = []
    for t in range(tiles):
        other = t + 1 if t % 2 else t - 1
        for q in range(members):
            to = other * members + q if 0 <= other < tiles else t * members + (q ^ 1)
            pairs.append((t * members + q, to))
    return lax.ppermute(edges, ("tile", "var"), pairs)


def swap_edges(even, odd):
    return swap(even, "tile", 1), swap_odd(odd)


def deliver(chunks):
    tiles, members = lax.axis_size("tile"), lax.axis_size("var")
    got = []
    for turn, chunk in enumerate(chunks[:-1]):
        pairs = []
        for t in range(tiles):
            for q in range(members):
                offset = 1 if turn == len(chunks) - 2 else 2 + turn + (q % 2) * (tiles // 2 - 1)
                pairs.append((t * members + q, (t ^ offset) * members + q))
        got.append(lax.ppermute(chunk, ("tile", "var"), pairs))
    return got + [chunks[-1]]


def local(control, diffusivity, land_mask, panel_tile, panel_row, panel_cols, obs_values,
          obs_weights, panel_sensor, sensitivity, cross_factor):
    rows, width = control.shape[1:]
    var_dev = control.shape[0]
    tiles, members = lax.axis_size("tile"), lax.axis_size("var")
    panels, panel_width = panel_cols.shape
    slots = panels // tiles
    blocks = width // LANES
    margin = PASSES
    total = ring_rows(rows, margin)
    chips = members // 2
    size = window_of(0, chips, blocks)[1]
    field = jax.ShapeDtypeStruct((rows, width), F32)
    share = jax.ShapeDtypeStruct((rows, width // chips), F32)
    view = jax.ShapeDtypeStruct((rows, size * LANES), F32)
    view2 = jax.ShapeDtypeStruct((2, *view.shape), F32)
    edge = jax.ShapeDtypeStruct((margin * size, LANES), F32)
    edge2 = jax.ShapeDtypeStruct((2, *edge.shape), F32)
    half = jax.ShapeDtypeStruct((3 * slots + 8, panel_width), F32)
    shared = jax.ShapeDtypeStruct((half.shape[0] + 2 * (-(-edge.shape[0] // 8) * 8), panel_width), F32)
    chunks_far = [jax.ShapeDtypeStruct((2, *half.shape), F32)] * (tiles // 2 - 1)
    chunks = chunks_far + [shared, half]
    line = pltpu.VMEM((1, panels), jnp.int32)

    own, other, responses, kappa, kappa_odd, *chunks = call(
        functools.partial(first_kernel, slots, margin),
        [field, field, jax.ShapeDtypeStruct((2, var_dev, 8, LANES), F32), view2, edge2]
        + chunks,
        [HBM] * 10,
        [
            pltpu.SMEM(sensitivity.shape, F32),
            pltpu.SMEM(cross_factor.shape, F32),
            pltpu.VMEM(control.shape, F32),
            line, line, line,
            pltpu.VMEM(obs_values.shape, F32),
            pltpu.VMEM(obs_weights.shape, F32),
            pltpu.VMEM(panel_cols.shape, jnp.int32),
            pltpu.VMEM((panels, panels), jnp.bfloat16),
            pltpu.SemaphoreType.DMA((10,)),
        ],
        cost=cost(3000),
    )(*(in_hbm(x) for x in (sensitivity, cross_factor, control, diffusivity, panel_tile.reshape(1, -1),
                            panel_row.reshape(1, -1), panel_sensor.reshape(1, -1), obs_values,
                            obs_weights, panel_cols)))

    got = deliver(chunks)
    part, *parts = call(cut_kernel, [view] * chips, [VMEM] * 2, cost=cost(200))(
        own, swap(other, "var", 1)
    )
    parts = [swap(p, "var", 2 * (d + 1)) for d, p in enumerate(parts)]
    kappa_odd = swap_odd(kappa_odd)
    smooth_in, even, odd = call(
        functools.partial(edges_kernel, margin), [view, edge, edge], [VMEM] * chips, cost=cost(500)
    )(part, *parts)
    even, odd = swap_edges(even, odd)
    far = call(relay_kernel, chunks_far, [VMEM] * len(chunks_far), cost=cost(270000))(*got[:-2])
    sums, sums_other = call(
        functools.partial(scatter_kernel, slots, blocks),
        [view2, view2],
        [AFTER] + [VMEM] * len(got),
        [
            pltpu.VMEM((2 * rows * 2 * padded_blocks(size), LANES), F32),
            pltpu.SMEM((8 * tiles, LANES), jnp.int32),
            pltpu.VMEM((8 * tiles, LANES), jnp.int32),
            pltpu.SemaphoreType.DMA((1,)),
        ],
        cost=cost(100000),
    )(smooth_in, got[-2], *far, got[-1])
    ring = pltpu.VMEM((total, size * LANES), F32)
    coef, sums_other = call(
        functools.partial(faces_kernel, margin, slots),
        [jax.ShapeDtypeStruct((5, total, size * LANES), F32), view2],
        [VMEM] * 4 + [AFTER] * 2,
        [ring, ring],
        cost=cost(1000),
    )(got[-2], kappa_odd, kappa, sums_other, even, odd)
    more_sums = swap(sums_other, "var", 1)
    (smooth,) = call(
        functools.partial(smooth_kernel, margin),
        [view],
        [VMEM] * 4,
        [ring],
        cost=cost(4000),
    )(smooth_in, even, odd, coef)
    adjoint, even, odd = call(
        functools.partial(adjoint_kernel, margin), [view, edge, edge], [VMEM] * 4, cost=cost(500)
    )(smooth, land_mask, sums, more_sums)
    even, odd = swap_edges(even, odd)
    (mine,) = call(
        functools.partial(spread_kernel, margin),
        [share],
        [VMEM] * 4,
        [ring],
        cost=cost(4000),
    )(adjoint, even, odd, coef)
    shares = [mine] + [swap(mine, "var", d) for d in sent_last(members)[1:]]
    (out,) = call(
        result_kernel,
        [jax.ShapeDtypeStruct(control.shape, F32)],
        [VMEM] * (2 + members),
        [pltpu.VMEM(control.shape, F32), pltpu.SemaphoreType.DMA((var_dev,))],
        cost=cost(1000),
        space=HBM,
    )(responses, control, *shares)
    return out


def solution(mesh):
    return jax.shard_map(
        local,
        mesh=mesh,
        in_specs=(
            P("var", ("grp", "tile"), None),
            P(None, ("grp", "tile"), None),
            P(("grp", "tile"), None),
            P(("grp", "tile"), None),
            P(("grp", "tile")),
            P(("grp", "tile"), None),
            P(("grp", "tile"), None),
            P(("grp", "tile"), None),
            P(("grp", "tile")),
            P(),
            P(),
        ),
        out_specs=P("var", ("grp", "tile"), None),
        check_vma=False,
    )
```

```python
import functools

import jax
import jax.numpy as jnp
from jax import lax
from jax.experimental import pallas as pl
from jax.experimental.pallas import tpu as pltpu
from jax.sharding import PartitionSpec as P

PASSES = 10
LANES = 128
GROUP = 16
VMEM = pl.BlockSpec(memory_space=pltpu.VMEM)
SMEM = pl.BlockSpec(memory_space=pltpu.SMEM)
HBM = pl.BlockSpec(memory_space=pltpu.HBM)
AFTER = pl.BlockSpec(memory_space=pl.ANY)
F32 = jnp.float32


def in_hbm(values):
    return pltpu.with_memory_space_constraint(values, pltpu.HBM)


def call(body, outs, ins, scratch=(), limit=16, cost=None, space=None):
    return pl.pallas_call(
        body,
        out_shape=outs,
        in_specs=ins,
        out_specs=[space or VMEM] * len(outs),
        scratch_shapes=list(scratch),
        compiler_params=pltpu.CompilerParams(vmem_limit_bytes=limit << 20),
        cost_estimate=cost,
    )


def cost(cycles):
    return pl.CostEstimate(flops=cycles * 4096, bytes_accessed=cycles * 1024, transcendentals=0)


def response(sens_ref, factor_ref, sensor, variable):
    total = sens_ref[sensor, 0] * factor_ref[0, variable]
    for u in range(1, factor_ref.shape[0]):
        total = total + sens_ref[sensor, u] * factor_ref[u, variable]
    return total


def fetch(pairs, sems):
    copies = [pltpu.make_async_copy(src, dst, sems.at[i]) for i, (src, dst) in enumerate(pairs)]
    for copy in copies:
        copy.start()
    return copies


def window_of(chip, chips, blocks):
    own = blocks // chips
    size = min(own + 2, own + chips - 1)
    return jnp.clip(chip * own - 1, 0, blocks - size), size


def my_chip():
    return lax.axis_index("var") // 2


def chip_count():
    return lax.axis_size("var") // 2


def lanes(start, size):
    return pl.ds(pl.multiple_of(start * LANES, LANES), size * LANES)


def first_kernel(slots, margin, sens_hbm, factor_hbm, control_hbm, kappa_hbm, tile_hbm, row_hbm, sensor_hbm,
                 value_hbm, weight_hbm, cols_hbm, own_ref, other_ref, response_ref, kappa_ref, even_ref,
                 odd_ref, *refs):
    chunk_refs = refs[:-11]
    (sens_ref, factor_ref, control_ref, tile_ref, row_ref, sensor_ref, value_ref, weight_ref, cols_ref,
     before_ref, sems) = refs[-11:]
    window = lanes(*window_of(my_chip(), chip_count(), own_ref.shape[1] // LANES))
    pairs = (
        (sens_hbm, sens_ref), (factor_hbm, factor_ref), (control_hbm, control_ref),
        (kappa_hbm.at[:, :, window], kappa_ref), (tile_hbm, tile_ref), (row_hbm, row_ref), (sensor_hbm, sensor_ref),
        (value_hbm, value_ref), (weight_hbm, weight_ref), (cols_hbm, cols_ref),
    )
    copies = [pltpu.make_async_copy(src, dst, sems.at[i]) for i, (src, dst) in enumerate(pairs)]
    for copy in copies:
        copy.start()
    from_panel = lax.broadcasted_iota(jnp.int32, before_ref.shape, 0)
    to_panel = lax.broadcasted_iota(jnp.int32, before_ref.shape, 1)
    before_ref[...] = jnp.where(from_panel < to_panel, 1.0, 0.0).astype(jnp.bfloat16)
    for copy in copies:
        copy.wait()

    member, mine = lax.axis_index("var"), lax.axis_index("tile")
    core = member % 2
    var_dev = control_ref.shape[0]
    for which, (sensor, out_ref) in enumerate(((core, own_ref), (1 - core, other_ref))):
        total = None
        for v in range(var_dev):
            scale = response(sens_ref, factor_ref, sensor, member * var_dev + v)
            response_ref[which, v] = jnp.full(response_ref.shape[2:], scale, F32)
            term = scale * control_ref[v]
            total = term if total is None else total + term
        out_ref[...] = total

    for i in range(2):
        pack_edges(even_ref.at[i], odd_ref.at[i], kappa_ref[i], margin)

    tiles = lax.axis_size("tile")
    full = tiles // 2 - 1
    first = jnp.where(core == 0, 2, tiles // 2 + 1)
    panels = value_ref.shape[0]
    source = tile_ref[...] ^ mine
    names = lax.broadcasted_iota(jnp.int32, (-(-tiles // 8) * 8, panels), 0)
    hits = jnp.where(names == source, 1.0, 0.0)
    ranks = jnp.dot(hits.astype(jnp.bfloat16), before_ref[...], preferred_element_type=F32)
    rank = jnp.sum(hits * ranks, axis=0, keepdims=True).astype(jnp.int32)
    parity, slot = rank % 2, rank // 2
    whole = (source >= first) & (source < first + full)
    home = source == 0
    keep = whole | ((home | (source == 1)) & (parity == core))
    half = jnp.where(whole, 2 * (source - first) + parity, jnp.where(home, tiles - 1, tiles - 2))
    place = jnp.where(keep, half * slots + slot, -1)
    spots = lax.broadcasted_iota(jnp.int32, (tiles * slots, panels), 0)
    pick = jnp.where(spots == place, 1.0, 0.0).astype(jnp.bfloat16)

    def picked(parts):
        total = None
        for part in parts:
            term = jnp.dot(pick, part.astype(jnp.bfloat16), preferred_element_type=F32)
            total = term if total is None else total + term
        return total

    cols = cols_ref[...]
    sent = (
        picked(thirds(value_ref[...])),
        picked(thirds(weight_ref[...])),
        picked(((cols // LANES * LANES).astype(F32), (cols % LANES).astype(F32))),
    )
    sub = lax.broadcasted_iota(jnp.int32, (8, panels), 0)
    lane = lax.broadcasted_iota(jnp.int32, (8, panels), 1)
    facts = jnp.where(sub == 0, row_ref[...], jnp.where(sub == 1, sensor_ref[...], 0)).astype(F32)
    meta = lax.dot_general(
        facts.astype(jnp.bfloat16), pick, (((1,), (1,)), ((), ())), preferred_element_type=F32
    )
    for i in range(tiles):
        held = jnp.sum(jnp.where(keep & (half == i), 1.0, 0.0), axis=1, keepdims=True)
        meta = jnp.where((sub == 2) & (lane == i), held, meta)
    for i in range(tiles):
        out_ref = chunk_refs[i // 2].at[i % 2] if i < 2 * full else chunk_refs[i - full]
        for part, rows in enumerate(sent):
            out_ref[part * slots : (part + 1) * slots] = rows[i * slots : (i + 1) * slots]
        out_ref[3 * slots :] = meta


def thirds(values):
    top = values.astype(jnp.bfloat16).astype(F32)
    rest = values - top
    middle = rest.astype(jnp.bfloat16).astype(F32)
    return top, middle, rest - middle


def pieces(values):
    top = values.astype(jnp.bfloat16).astype(F32)
    return top, values - top


def scatter_kernel(slots, blocks_all, after_ref, *refs):
    got_refs, (own_ref, other_ref, acc_ref, meta_ref, where_ref, sems) = refs[:-6], refs[-6:]
    core = lax.axis_index("var") % 2
    got_refs = [r.at[i] for r in got_refs[1:-1] for i in (0, 1)] + [got_refs[0], got_refs[-1]]
    size_of_group = min(GROUP, slots)
    rows = own_ref.shape[1]
    start, size = window_of(my_chip(), chip_count(), blocks_all)
    per_kind = padded_blocks(size)
    tall = 2 * per_kind
    line = lax.broadcasted_iota(jnp.int32, (8, LANES), 0)
    for s, ref in enumerate(got_refs):
        facts = ref[3 * slots : 3 * slots + 8].astype(jnp.int32)
        where_ref[8 * s : 8 * s + 8] = jnp.where(line == 0, (facts[1:2] * rows + facts[0:1]) * tall, facts)
    copy = pltpu.make_async_copy(where_ref, meta_ref, sems.at[0])
    copy.start()
    acc_ref[...] = jnp.zeros(acc_ref.shape, F32)
    place = lax.broadcasted_iota(jnp.int32, (tall, LANES), 0)
    is_weight = place < per_kind
    place = jnp.where(is_weight, place, place - per_kind) + start
    lane_ids = lax.broadcasted_iota(jnp.int32, (LANES, LANES), 0).astype(F32).astype(jnp.bfloat16)
    one, zero = jnp.bfloat16(1), jnp.bfloat16(0)
    sub = lax.broadcasted_iota(jnp.int32, (size_of_group, LANES), 0)
    blank = jnp.zeros((2 * tall, LANES), jnp.bfloat16)
    copy.wait()

    def load(s, base):
        got_ref = got_refs[s]
        count = meta_ref[8 * s + 2, s]
        value = got_ref[pl.ds(base, size_of_group), :]
        weight = got_ref[pl.ds(slots + base, size_of_group), :]
        cell = got_ref[pl.ds(2 * slots + base, size_of_group), :].astype(jnp.int32)
        weight = jnp.where(sub + base < count, weight, 0.0)
        return pieces(weight), pieces(weight * value), (cell % LANES).astype(F32), cell // LANES

    def one_hots(loaded, i):
        weights, values, low, high = loaded
        here = place == high[i : i + 1]
        rows_of = [
            jnp.where(here, jnp.where(is_weight, w[i : i + 1], v[i : i + 1]), 0.0)
            for w, v in zip(weights, values)
        ]
        left = jnp.concatenate(rows_of, axis=0).astype(jnp.bfloat16)
        column = jnp.broadcast_to(low[i : i + 1], (16, LANES)).astype(jnp.bfloat16)
        column = jnp.concatenate([column] * (LANES // 16), axis=0)
        return left, jnp.where(lane_ids == column, one, zero)

    def step(chosen, g, carry):
        base = pl.multiple_of(g * size_of_group, size_of_group)
        loaded = {s: load(s, base) for s in chosen}
        for k in range(size_of_group):
            for pair in zip(chosen[::2], chosen[1::2]):
                hots = [one_hots(loaded[s], k) for s in pair]
                left = jnp.concatenate(
                    [
                        jnp.concatenate([hots[0][0], blank], axis=1),
                        jnp.concatenate([blank, hots[1][0]], axis=1),
                    ],
                    axis=0,
                )
                both = lax.dot_general(
                    left, jnp.concatenate([hots[0][1], hots[1][1]], axis=1), (((1,), (1,)), ((), ())),
                    preferred_element_type=F32,
                )
                for i, s in enumerate(pair):
                    at = pl.multiple_of(meta_ref[8 * s, s * slots + base + k], 8)
                    mine = both[2 * i * tall : 2 * (i + 1) * tall]
                    acc_ref[pl.ds(at, tall), :] += mine[:tall] + mine[tall:]
        return carry

    for s in range(0, len(got_refs), 4):
        chosen = list(range(s, s + 4))
        most = meta_ref[8 * s + 2, s]
        for other in chosen[1:]:
            most = jnp.maximum(most, meta_ref[8 * other + 2, other])
        turns = (most + size_of_group - 1) // size_of_group
        lax.fori_loop(0, turns, functools.partial(step, chosen), 0)
    for sensor, out_ref in ((core, own_ref), (1 - core, other_ref)):
        begin = sensor * rows * tall
        for kind in range(2):
            for b in range(size):
                out_ref[kind, :, b * LANES : (b + 1) * LANES] = acc_ref[
                    pl.ds(begin + kind * per_kind + b, rows, stride=tall), :
                ]


def padded_blocks(size):
    return -(-size // 4) * 4


def even_tile():
    return lax.axis_index("tile") % 2 == 0


def has_above():
    return lax.axis_index("tile") > 0


def has_below():
    return lax.axis_index("tile") + 1 < lax.axis_size("tile")


def pack_edges(even_ref, odd_ref, rows_value, margin):
    rows, width = rows_value.shape
    even = even_tile()
    for b in range(width // LANES):
        at = slice(b * LANES, (b + 1) * LANES)
        head, tail = rows_value[:margin, at], rows_value[rows - margin :, at]
        even_ref[b * margin : (b + 1) * margin] = jnp.where(even, tail, head)
        odd_ref[b * margin : (b + 1) * margin] = jnp.where(even, head, tail)


def cut_kernel(first_ref, second_ref, mine_ref, *out_refs):
    chip, chips, blocks = my_chip(), chip_count(), first_ref.shape[1] // LANES
    for d, out_ref in enumerate((mine_ref, *out_refs)):
        window = lanes(*window_of(chip ^ d, chips, blocks))
        out_ref[...] = first_ref[:, window] + second_ref[:, window]


def edges_kernel(margin, *refs):
    terms, (total_ref, even_ref, odd_ref) = refs[:-3], refs[-3:]
    total = terms[0][...]
    for term in terms[1:]:
        total = total + term[...]
    total_ref[...] = total
    pack_edges(even_ref, odd_ref, total, margin)


def ring_rows(rows, margin):
    return -(-(rows + 2 * margin) // 8) * 8


def lay_ring(ref, own, from_even, from_odd, margin):
    rows, total = own.shape[0], ref.shape[0]
    even = even_tile()
    ref[rows:total] = jnp.zeros((total - rows, ref.shape[1]), F32)
    ref[:rows] = own
    for b in range(ref.shape[1] // LANES):
        at = slice(b * LANES, (b + 1) * LANES)
        one, two = (m[b * margin : (b + 1) * margin] for m in (from_even, from_odd))
        ref[rows : rows + margin, at] = jnp.where(has_below(), jnp.where(even, one, two), 0.0)
        ref[total - margin :, at] = jnp.where(has_above(), jnp.where(even, two, one), 0.0)


def block(ref, j):
    return ref[:, j * LANES : (j + 1) * LANES]


def sideways(blocks):
    shape = blocks[0].shape
    lane = lax.broadcasted_iota(jnp.int32, shape, 1)
    zero = jnp.zeros(shape, F32)
    ahead = [pltpu.roll(x, 1, 1) for x in blocks]
    back = [pltpu.roll(x, LANES - 1, 1) for x in blocks]
    for j, here in enumerate(blocks):
        before = ahead[j - 1] if j else zero
        after = back[j + 1] if j + 1 < len(blocks) else zero
        yield here, jnp.where(lane == 0, before, ahead[j]), jnp.where(lane == LANES - 1, after, back[j])


def face_weights(coef_ref, row_ref, col_ref, rows, margin):
    total, width = row_ref.shape
    blocks = width // LANES
    r = lax.broadcasted_iota(jnp.int32, (total, LANES), 0)
    inside = (
        (r < rows)
        | ((r < rows + margin) & has_below())
        | ((r >= total - margin) & has_above())
    )
    scale = jnp.where(inside, 0.125, 0.0)
    unit = jnp.where(inside, 1.0, 0.0)
    columns = [block(col_ref, j) for j in range(blocks)]
    for j, (k_col, k_left, k_right) in enumerate(sideways(columns)):
        at = slice(j * LANES, (j + 1) * LANES)
        k_row = block(row_ref, j)
        up = scale * (k_row + pltpu.roll(k_row, 1, 0))
        down = scale * (k_row + pltpu.roll(k_row, total - 1, 0))
        left = scale * (k_col + k_left)
        right = scale * (k_col + k_right)
        coef_ref[0, :, at] = unit - up - down - left - right
        coef_ref[1, :, at] = up
        coef_ref[2, :, at] = down
        coef_ref[3, :, at] = left
        coef_ref[4, :, at] = right


def one_pass(fields, coef_ref, spans):
    def weights(i, at):
        got = [coef_ref[i, span, at] for span in spans]
        return jnp.concatenate(got, axis=0) if len(got) > 1 else got[0]

    total = fields[0].shape[0]
    out = []
    for j, (here, left, right) in enumerate(sideways(fields)):
        at = slice(j * LANES, (j + 1) * LANES)
        out.append(
            weights(0, at) * here
            + weights(1, at) * pltpu.roll(here, 1, 0)
            + weights(2, at) * pltpu.roll(here, total - 1, 0)
            + weights(3, at) * left
            + weights(4, at) * right
        )
    return out


def diffuse(ring_ref, coef_ref, rows, margin):
    total, width = ring_ref.shape
    inner = margin // 8 * 8
    wide = [slice(0, total)]
    narrow = [slice(0, rows + inner), slice(total - inner, total)]
    fields = [block(ring_ref, j) for j in range(width // LANES)]
    for _ in range(margin - inner):
        fields = one_pass(fields, coef_ref, wide)
    fields = [jnp.concatenate([f[span] for span in narrow], axis=0) for f in fields]
    for _ in range(inner):
        fields = one_pass(fields, coef_ref, narrow)
    return [f[:rows] for f in fields]


def faces_kernel(margin, even_ref, odd_ref, kappa_ref, sums_ref, *refs):
    coef_ref, sums_out, one_ref, two_ref = refs[-4:]
    sums_out[...] = sums_ref[...]
    rows = kappa_ref.shape[1]
    lay_ring(one_ref, kappa_ref[0], even_ref.at[0], odd_ref.at[0], margin)
    lay_ring(two_ref, kappa_ref[1], even_ref.at[1], odd_ref.at[1], margin)
    face_weights(coef_ref, one_ref, two_ref, rows, margin)


def smooth_kernel(margin, own_ref, even_ref, odd_ref, coef_ref, out_ref, ring_ref):
    rows = own_ref.shape[0]
    lay_ring(ring_ref, own_ref[...], even_ref, odd_ref, margin)
    for j, field in enumerate(diffuse(ring_ref, coef_ref, rows, margin)):
        out_ref[:, j * LANES : (j + 1) * LANES] = field


def adjoint_kernel(margin, smooth_ref, mask_ref, sums_ref, more_ref, adjoint_ref, even_ref, odd_ref):
    weight = sums_ref[0] + more_ref[0]
    value = sums_ref[1] + more_ref[1]
    window = lanes(*window_of(my_chip(), chip_count(), mask_ref.shape[1] // LANES))
    adjoint = mask_ref[:, window].astype(F32) * (weight * smooth_ref[...] - value)
    adjoint_ref[...] = adjoint
    pack_edges(even_ref, odd_ref, adjoint, margin)


def spread_kernel(margin, own_ref, even_ref, odd_ref, coef_ref, out_ref, ring_ref):
    rows = own_ref.shape[0]
    lay_ring(ring_ref, own_ref[...], even_ref, odd_ref, margin)
    for j, field in enumerate(diffuse(ring_ref, coef_ref, rows, margin)):
        ring_ref[:rows, j * LANES : (j + 1) * LANES] = field
    own = out_ref.shape[1] // LANES
    start = window_of(my_chip(), chip_count(), own * chip_count())[0]
    out_ref[...] = ring_ref[:rows, lanes(my_chip() * own - start, own)]


def sent_last(members):
    return [0, 1] + sorted(range(2, members), key=lambda d: d % 2)


def result_kernel(response_ref, control_ref, *refs):
    refs, (out_ref, line_ref, sems) = refs[:-3], refs[-3:]
    own = refs[0].shape[1] // LANES
    refs = [refs[sent_last(len(refs)).index(d)] for d in range(len(refs))]
    copies = []
    for v in range(control_ref.shape[0]):
        mine, theirs = (response_ref[i, v][:1, :1] for i in range(2))
        for d in range(len(refs) // 2):
            window = lanes((my_chip() ^ d) * own, own)
            line_ref[v, :, window] = (
                control_ref[v, :, window] + mine * refs[2 * d][...] + theirs * refs[2 * d + 1][...]
            )
        copies.append(pltpu.make_async_copy(line_ref.at[v], out_ref.at[v], sems.at[v]))
        copies[-1].start()
    for copy in copies:
        copy.wait()


def swap(values, axis, bit):
    count = lax.axis_size(axis)
    return lax.ppermute(values, axis, [(i, i ^ bit) for i in range(count)])


def swap_edges(even, odd):
    tiles, members = lax.axis_size("tile"), lax.axis_size("var")
    pairs = []
    for t in range(tiles):
        other = t + 1 if t % 2 else t - 1
        for q in range(members):
            to = other * members + q if 0 <= other < tiles else t * members + (q ^ 1)
            pairs.append((t * members + q, to))
    return swap(even, "tile", 1), lax.ppermute(odd, ("tile", "var"), pairs)


def deliver(chunks):
    tiles, members = lax.axis_size("tile"), lax.axis_size("var")
    got = []
    for turn, chunk in enumerate(chunks[:-1]):
        pairs = []
        for t in range(tiles):
            for q in range(members):
                offset = 1 if turn == len(chunks) - 2 else 2 + turn + (q % 2) * (tiles // 2 - 1)
                pairs.append((t * members + q, (t ^ offset) * members + q))
        got.append(lax.ppermute(chunk, ("tile", "var"), pairs))
    return got + [chunks[-1]]


def local(control, diffusivity, land_mask, panel_tile, panel_row, panel_cols, obs_values,
          obs_weights, panel_sensor, sensitivity, cross_factor):
    rows, width = control.shape[1:]
    var_dev = control.shape[0]
    tiles, members = lax.axis_size("tile"), lax.axis_size("var")
    panels, panel_width = panel_cols.shape
    slots = panels // tiles
    blocks = width // LANES
    margin = PASSES
    total = ring_rows(rows, margin)
    chips = members // 2
    size = window_of(0, chips, blocks)[1]
    field = jax.ShapeDtypeStruct((rows, width), F32)
    share = jax.ShapeDtypeStruct((rows, width // chips), F32)
    view = jax.ShapeDtypeStruct((rows, size * LANES), F32)
    view2 = jax.ShapeDtypeStruct((2, *view.shape), F32)
    edge = jax.ShapeDtypeStruct((margin * size, LANES), F32)
    edge2 = jax.ShapeDtypeStruct((2, *edge.shape), F32)
    half = jax.ShapeDtypeStruct((3 * slots + 8, panel_width), F32)
    chunks = [jax.ShapeDtypeStruct((2, *half.shape), F32)] * (tiles // 2 - 1) + [half] * 2
    line = pltpu.VMEM((1, panels), jnp.int32)

    own, other, responses, kappa, kappa_even, kappa_odd, *chunks = call(
        functools.partial(first_kernel, slots, margin),
        [field, field, jax.ShapeDtypeStruct((2, var_dev, 8, LANES), F32), view2, edge2, edge2]
        + chunks,
        [HBM] * 10,
        [
            pltpu.SMEM(sensitivity.shape, F32),
            pltpu.SMEM(cross_factor.shape, F32),
            pltpu.VMEM(control.shape, F32),
            line, line, line,
            pltpu.VMEM(obs_values.shape, F32),
            pltpu.VMEM(obs_weights.shape, F32),
            pltpu.VMEM(panel_cols.shape, jnp.int32),
            pltpu.VMEM((panels, panels), jnp.bfloat16),
            pltpu.SemaphoreType.DMA((10,)),
        ],
        cost=cost(3000),
    )(*(in_hbm(x) for x in (sensitivity, cross_factor, control, diffusivity, panel_tile.reshape(1, -1),
                            panel_row.reshape(1, -1), panel_sensor.reshape(1, -1), obs_values,
                            obs_weights, panel_cols)))

    got = deliver(chunks)
    part, *parts = call(cut_kernel, [view] * chips, [VMEM] * 2, cost=cost(200))(
        own, swap(other, "var", 1)
    )
    parts = [swap(p, "var", 2 * (d + 1)) for d, p in enumerate(parts)]
    kappa_even, kappa_odd = swap_edges(kappa_even, kappa_odd)
    smooth_in, even, odd = call(
        functools.partial(edges_kernel, margin), [view, edge, edge], [VMEM] * chips, cost=cost(500)
    )(part, *parts)
    even, odd = swap_edges(even, odd)
    sums, sums_other = call(
        functools.partial(scatter_kernel, slots, blocks),
        [view2, view2],
        [AFTER] + [VMEM] * len(got),
        [
            pltpu.VMEM((2 * rows * 2 * padded_blocks(size), LANES), F32),
            pltpu.SMEM((8 * tiles, LANES), jnp.int32),
            pltpu.VMEM((8 * tiles, LANES), jnp.int32),
            pltpu.SemaphoreType.DMA((1,)),
        ],
        cost=cost(100000),
    )(smooth_in, got[-2], *got[:-2], got[-1])
    ring = pltpu.VMEM((total, size * LANES), F32)
    coef, sums_other = call(
        functools.partial(faces_kernel, margin),
        [jax.ShapeDtypeStruct((5, total, size * LANES), F32), view2],
        [VMEM] * 4 + [AFTER] * 2,
        [ring, ring],
        cost=cost(1000),
    )(kappa_even, kappa_odd, kappa, sums_other, even, odd)
    more_sums = swap(sums_other, "var", 1)
    (smooth,) = call(
        functools.partial(smooth_kernel, margin),
        [view],
        [VMEM] * 4,
        [ring],
        cost=cost(4000),
    )(smooth_in, even, odd, coef)
    adjoint, even, odd = call(
        functools.partial(adjoint_kernel, margin), [view, edge, edge], [VMEM] * 4, cost=cost(500)
    )(smooth, land_mask, sums, more_sums)
    even, odd = swap_edges(even, odd)
    (mine,) = call(
        functools.partial(spread_kernel, margin),
        [share],
        [VMEM] * 4,
        [ring],
        cost=cost(4000),
    )(adjoint, even, odd, coef)
    shares = [mine] + [swap(mine, "var", d) for d in sent_last(members)[1:]]
    (out,) = call(
        result_kernel,
        [jax.ShapeDtypeStruct(control.shape, F32)],
        [VMEM] * (2 + members),
        [pltpu.VMEM(control.shape, F32), pltpu.SemaphoreType.DMA((var_dev,))],
        cost=cost(1000),
        space=HBM,
    )(responses, control, *shares)
    return out


def solution(mesh):
    return jax.shard_map(
        local,
        mesh=mesh,
        in_specs=(
            P("var", ("grp", "tile"), None),
            P(None, ("grp", "tile"), None),
            P(("grp", "tile"), None),
            P(("grp", "tile"), None),
            P(("grp", "tile")),
            P(("grp", "tile"), None),
            P(("grp", "tile"), None),
            P(("grp", "tile"), None),
            P(("grp", "tile")),
            P(),
            P(),
        ),
        out_specs=P("var", ("grp", "tile"), None),
        check_vma=False,
    )
```

```python
import functools

import jax
import jax.numpy as jnp
from jax import lax
from jax.experimental import pallas as pl
from jax.experimental.pallas import tpu as pltpu
from jax.sharding import PartitionSpec as P

PASSES = 10
LANES = 128
GROUP = 16
VMEM = pl.BlockSpec(memory_space=pltpu.VMEM)
SMEM = pl.BlockSpec(memory_space=pltpu.SMEM)
HBM = pl.BlockSpec(memory_space=pltpu.HBM)
AFTER = pl.BlockSpec(memory_space=pl.ANY)
F32 = jnp.float32


def in_hbm(values):
    return pltpu.with_memory_space_constraint(values, pltpu.HBM)


def call(body, outs, ins, scratch=(), limit=16, cost=None, space=None):
    return pl.pallas_call(
        body,
        out_shape=outs,
        in_specs=ins,
        out_specs=[space or VMEM] * len(outs),
        scratch_shapes=list(scratch),
        compiler_params=pltpu.CompilerParams(vmem_limit_bytes=limit << 20),
        cost_estimate=cost,
    )


def cost(cycles):
    return pl.CostEstimate(flops=cycles * 4096, bytes_accessed=cycles * 1024, transcendentals=0)


def response(sens_ref, factor_ref, sensor, variable):
    total = sens_ref[sensor, 0] * factor_ref[0, variable]
    for u in range(1, factor_ref.shape[0]):
        total = total + sens_ref[sensor, u] * factor_ref[u, variable]
    return total


def fetch(pairs, sems):
    copies = [pltpu.make_async_copy(src, dst, sems.at[i]) for i, (src, dst) in enumerate(pairs)]
    for copy in copies:
        copy.start()
    return copies


def window_of(chip, chips, blocks):
    own = blocks // chips
    size = min(own + 2, own + chips - 1)
    return jnp.clip(chip * own - 1, 0, blocks - size), size


def my_chip():
    return lax.axis_index("var") // 2


def chip_count():
    return lax.axis_size("var") // 2


def lanes(start, size):
    return pl.ds(pl.multiple_of(start * LANES, LANES), size * LANES)


def first_kernel(slots, margin, sens_hbm, factor_hbm, control_hbm, kappa_hbm, tile_hbm, row_hbm, sensor_hbm,
                 value_hbm, weight_hbm, cols_hbm, own_ref, other_ref, response_ref, kappa_ref, even_ref,
                 odd_ref, *refs):
    chunk_refs = refs[:-11]
    (sens_ref, factor_ref, control_ref, tile_ref, row_ref, sensor_ref, value_ref, weight_ref, cols_ref,
     before_ref, sems) = refs[-11:]
    window = lanes(*window_of(my_chip(), chip_count(), own_ref.shape[1] // LANES))
    pairs = (
        (sens_hbm, sens_ref), (factor_hbm, factor_ref), (control_hbm, control_ref),
        (kappa_hbm.at[:, :, window], kappa_ref), (tile_hbm, tile_ref), (row_hbm, row_ref), (sensor_hbm, sensor_ref),
        (value_hbm, value_ref), (weight_hbm, weight_ref), (cols_hbm, cols_ref),
    )
    copies = [pltpu.make_async_copy(src, dst, sems.at[i]) for i, (src, dst) in enumerate(pairs)]
    for copy in copies:
        copy.start()
    from_panel = lax.broadcasted_iota(jnp.int32, before_ref.shape, 0)
    to_panel = lax.broadcasted_iota(jnp.int32, before_ref.shape, 1)
    before_ref[...] = jnp.where(from_panel < to_panel, 1.0, 0.0).astype(jnp.bfloat16)
    for copy in copies:
        copy.wait()

    member, mine = lax.axis_index("var"), lax.axis_index("tile")
    core = member % 2
    var_dev = control_ref.shape[0]
    for which, (sensor, out_ref) in enumerate(((core, own_ref), (1 - core, other_ref))):
        total = None
        for v in range(var_dev):
            scale = response(sens_ref, factor_ref, sensor, member * var_dev + v)
            response_ref[which, v] = jnp.full(response_ref.shape[2:], scale, F32)
            term = scale * control_ref[v]
            total = term if total is None else total + term
        out_ref[...] = total

    for i in range(2):
        pack_edges(even_ref.at[i], odd_ref.at[i], kappa_ref[i], margin)

    tiles = lax.axis_size("tile")
    full = tiles // 2 - 1
    first = jnp.where(core == 0, 2, tiles // 2 + 1)
    panels = value_ref.shape[0]
    source = tile_ref[...] ^ mine
    names = lax.broadcasted_iota(jnp.int32, (-(-tiles // 8) * 8, panels), 0)
    hits = jnp.where(names == source, 1.0, 0.0)
    ranks = jnp.dot(hits.astype(jnp.bfloat16), before_ref[...], preferred_element_type=F32)
    rank = jnp.sum(hits * ranks, axis=0, keepdims=True).astype(jnp.int32)
    parity, slot = rank % 2, rank // 2
    whole = (source >= first) & (source < first + full)
    home = source == 0
    keep = whole | ((home | (source == 1)) & (parity == core))
    half = jnp.where(whole, 2 * (source - first) + parity, jnp.where(home, tiles - 1, tiles - 2))
    place = jnp.where(keep, half * slots + slot, -1)
    spots = lax.broadcasted_iota(jnp.int32, (tiles * slots, panels), 0)
    pick = jnp.where(spots == place, 1.0, 0.0).astype(jnp.bfloat16)

    def picked(parts):
        total = None
        for part in parts:
            term = jnp.dot(pick, part.astype(jnp.bfloat16), preferred_element_type=F32)
            total = term if total is None else total + term
        return total

    cols = cols_ref[...]
    sent = (
        picked(thirds(value_ref[...])),
        picked(thirds(weight_ref[...])),
        picked(((cols // LANES * LANES).astype(F32), (cols % LANES).astype(F32))),
    )
    sub = lax.broadcasted_iota(jnp.int32, (8, panels), 0)
    lane = lax.broadcasted_iota(jnp.int32, (8, panels), 1)
    facts = jnp.where(sub == 0, row_ref[...], jnp.where(sub == 1, sensor_ref[...], 0)).astype(F32)
    meta = lax.dot_general(
        facts.astype(jnp.bfloat16), pick, (((1,), (1,)), ((), ())), preferred_element_type=F32
    )
    for i in range(tiles):
        held = jnp.sum(jnp.where(keep & (half == i), 1.0, 0.0), axis=1, keepdims=True)
        meta = jnp.where((sub == 2) & (lane == i), held, meta)
    for i in range(tiles):
        out_ref = chunk_refs[i // 2].at[i % 2] if i < 2 * full else chunk_refs[i - full]
        for part, rows in enumerate(sent):
            out_ref[part * slots : (part + 1) * slots] = rows[i * slots : (i + 1) * slots]
        out_ref[3 * slots :] = meta


def thirds(values):
    top = values.astype(jnp.bfloat16).astype(F32)
    rest = values - top
    middle = rest.astype(jnp.bfloat16).astype(F32)
    return top, middle, rest - middle


def pieces(values):
    top = values.astype(jnp.bfloat16).astype(F32)
    return top, values - top


def scatter_kernel(slots, blocks_all, after_ref, *refs):
    got_refs, (own_ref, other_ref, acc_ref, meta_ref, where_ref, sems) = refs[:-6], refs[-6:]
    core = lax.axis_index("var") % 2
    got_refs = [r.at[i] for r in got_refs[1:-1] for i in (0, 1)] + [got_refs[0], got_refs[-1]]
    size_of_group = min(GROUP, slots)
    rows = own_ref.shape[1]
    start, size = window_of(my_chip(), chip_count(), blocks_all)
    per_kind = padded_blocks(size)
    tall = 2 * per_kind
    line = lax.broadcasted_iota(jnp.int32, (8, LANES), 0)
    for s, ref in enumerate(got_refs):
        facts = ref[3 * slots : 3 * slots + 8].astype(jnp.int32)
        where_ref[8 * s : 8 * s + 8] = jnp.where(line == 0, (facts[1:2] * rows + facts[0:1]) * tall, facts)
    copy = pltpu.make_async_copy(where_ref, meta_ref, sems.at[0])
    copy.start()
    acc_ref[...] = jnp.zeros(acc_ref.shape, F32)
    place = lax.broadcasted_iota(jnp.int32, (tall, LANES), 0)
    is_weight = place < per_kind
    place = jnp.where(is_weight, place, place - per_kind) + start
    lane_ids = lax.broadcasted_iota(jnp.int32, (LANES, LANES), 0).astype(F32).astype(jnp.bfloat16)
    one, zero = jnp.bfloat16(1), jnp.bfloat16(0)
    sub = lax.broadcasted_iota(jnp.int32, (size_of_group, LANES), 0)
    blank = jnp.zeros((2 * tall, LANES), jnp.bfloat16)
    copy.wait()

    def load(s, base):
        got_ref = got_refs[s]
        count = meta_ref[8 * s + 2, s]
        value = got_ref[pl.ds(base, size_of_group), :]
        weight = got_ref[pl.ds(slots + base, size_of_group), :]
        cell = got_ref[pl.ds(2 * slots + base, size_of_group), :].astype(jnp.int32)
        weight = jnp.where(sub + base < count, weight, 0.0)
        return pieces(weight), pieces(weight * value), (cell % LANES).astype(F32), cell // LANES

    def one_hots(loaded, i):
        weights, values, low, high = loaded
        here = place == high[i : i + 1]
        rows_of = [
            jnp.where(here, jnp.where(is_weight, w[i : i + 1], v[i : i + 1]), 0.0)
            for w, v in zip(weights, values)
        ]
        left = jnp.concatenate(rows_of, axis=0).astype(jnp.bfloat16)
        column = jnp.broadcast_to(low[i : i + 1], (16, LANES)).astype(jnp.bfloat16)
        column = jnp.concatenate([column] * (LANES // 16), axis=0)
        return left, jnp.where(lane_ids == column, one, zero)

    def step(chosen, g, carry):
        base = pl.multiple_of(g * size_of_group, size_of_group)
        loaded = {s: load(s, base) for s in chosen}
        for k in range(size_of_group):
            for pair in zip(chosen[::2], chosen[1::2]):
                hots = [one_hots(loaded[s], k) for s in pair]
                left = jnp.concatenate(
                    [
                        jnp.concatenate([hots[0][0], blank], axis=1),
                        jnp.concatenate([blank, hots[1][0]], axis=1),
                    ],
                    axis=0,
                )
                both = lax.dot_general(
                    left, jnp.concatenate([hots[0][1], hots[1][1]], axis=1), (((1,), (1,)), ((), ())),
                    preferred_element_type=F32,
                )
                for i, s in enumerate(pair):
                    at = pl.multiple_of(meta_ref[8 * s, s * slots + base + k], 8)
                    mine = both[2 * i * tall : 2 * (i + 1) * tall]
                    acc_ref[pl.ds(at, tall), :] += mine[:tall] + mine[tall:]
        return carry

    for s in range(0, len(got_refs), 4):
        chosen = list(range(s, s + 4))
        most = meta_ref[8 * s + 2, s]
        for other in chosen[1:]:
            most = jnp.maximum(most, meta_ref[8 * other + 2, other])
        turns = (most + size_of_group - 1) // size_of_group
        lax.fori_loop(0, turns, functools.partial(step, chosen), 0)
    for sensor, out_ref in ((core, own_ref), (1 - core, other_ref)):
        begin = sensor * rows * tall
        for kind in range(2):
            for b in range(size):
                out_ref[kind, :, b * LANES : (b + 1) * LANES] = acc_ref[
                    pl.ds(begin + kind * per_kind + b, rows, stride=tall), :
                ]


def padded_blocks(size):
    return -(-size // 4) * 4


def even_tile():
    return lax.axis_index("tile") % 2 == 0


def has_above():
    return lax.axis_index("tile") > 0


def has_below():
    return lax.axis_index("tile") + 1 < lax.axis_size("tile")


def pack_edges(even_ref, odd_ref, rows_value, margin):
    rows, width = rows_value.shape
    even = even_tile()
    for b in range(width // LANES):
        at = slice(b * LANES, (b + 1) * LANES)
        head, tail = rows_value[:margin, at], rows_value[rows - margin :, at]
        even_ref[b * margin : (b + 1) * margin] = jnp.where(even, tail, head)
        odd_ref[b * margin : (b + 1) * margin] = jnp.where(even, head, tail)


def cut_kernel(first_ref, second_ref, mine_ref, *out_refs):
    chip, chips, blocks = my_chip(), chip_count(), first_ref.shape[1] // LANES
    for d, out_ref in enumerate((mine_ref, *out_refs)):
        window = lanes(*window_of(chip ^ d, chips, blocks))
        out_ref[...] = first_ref[:, window] + second_ref[:, window]


def edges_kernel(margin, *refs):
    terms, (total_ref, even_ref, odd_ref) = refs[:-3], refs[-3:]
    total = terms[0][...]
    for term in terms[1:]:
        total = total + term[...]
    total_ref[...] = total
    pack_edges(even_ref, odd_ref, total, margin)


def ring_rows(rows, margin):
    return -(-(rows + 2 * margin) // 8) * 8


def lay_ring(ref, own, from_even, from_odd, margin):
    rows, total = own.shape[0], ref.shape[0]
    even = even_tile()
    ref[rows:total] = jnp.zeros((total - rows, ref.shape[1]), F32)
    ref[:rows] = own
    for b in range(ref.shape[1] // LANES):
        at = slice(b * LANES, (b + 1) * LANES)
        one, two = (m[b * margin : (b + 1) * margin] for m in (from_even, from_odd))
        ref[rows : rows + margin, at] = jnp.where(has_below(), jnp.where(even, one, two), 0.0)
        ref[total - margin :, at] = jnp.where(has_above(), jnp.where(even, two, one), 0.0)


def block(ref, j):
    return ref[:, j * LANES : (j + 1) * LANES]


def sideways(blocks):
    shape = blocks[0].shape
    lane = lax.broadcasted_iota(jnp.int32, shape, 1)
    zero = jnp.zeros(shape, F32)
    ahead = [pltpu.roll(x, 1, 1) for x in blocks]
    back = [pltpu.roll(x, LANES - 1, 1) for x in blocks]
    for j, here in enumerate(blocks):
        before = ahead[j - 1] if j else zero
        after = back[j + 1] if j + 1 < len(blocks) else zero
        yield here, jnp.where(lane == 0, before, ahead[j]), jnp.where(lane == LANES - 1, after, back[j])


def face_weights(coef_ref, row_ref, col_ref, rows, margin):
    total, width = row_ref.shape
    blocks = width // LANES
    r = lax.broadcasted_iota(jnp.int32, (total, LANES), 0)
    inside = (
        (r < rows)
        | ((r < rows + margin) & has_below())
        | ((r >= total - margin) & has_above())
    )
    scale = jnp.where(inside, 0.125, 0.0)
    unit = jnp.where(inside, 1.0, 0.0)
    columns = [block(col_ref, j) for j in range(blocks)]
    for j, (k_col, k_left, k_right) in enumerate(sideways(columns)):
        at = slice(j * LANES, (j + 1) * LANES)
        k_row = block(row_ref, j)
        up = scale * (k_row + pltpu.roll(k_row, 1, 0))
        down = scale * (k_row + pltpu.roll(k_row, total - 1, 0))
        left = scale * (k_col + k_left)
        right = scale * (k_col + k_right)
        coef_ref[0, :, at] = unit - up - down - left - right
        coef_ref[1, :, at] = up
        coef_ref[2, :, at] = down
        coef_ref[3, :, at] = left
        coef_ref[4, :, at] = right


def one_pass(fields, coef_ref, spans):
    def weights(i, at):
        got = [coef_ref[i, span, at] for span in spans]
        return jnp.concatenate(got, axis=0) if len(got) > 1 else got[0]

    total = fields[0].shape[0]
    out = []
    for j, (here, left, right) in enumerate(sideways(fields)):
        at = slice(j * LANES, (j + 1) * LANES)
        out.append(
            weights(0, at) * here
            + weights(1, at) * pltpu.roll(here, 1, 0)
            + weights(2, at) * pltpu.roll(here, total - 1, 0)
            + weights(3, at) * left
            + weights(4, at) * right
        )
    return out


def diffuse(ring_ref, coef_ref, rows, margin):
    total, width = ring_ref.shape
    inner = margin // 8 * 8
    wide = [slice(0, total)]
    narrow = [slice(0, rows + inner), slice(total - inner, total)]
    fields = [block(ring_ref, j) for j in range(width // LANES)]
    for _ in range(margin - inner):
        fields = one_pass(fields, coef_ref, wide)
    fields = [jnp.concatenate([f[span] for span in narrow], axis=0) for f in fields]
    for _ in range(inner):
        fields = one_pass(fields, coef_ref, narrow)
    return [f[:rows] for f in fields]


def faces_kernel(margin, even_ref, odd_ref, kappa_ref, sums_ref, *refs):
    coef_ref, sums_out, one_ref, two_ref = refs[-4:]
    sums_out[...] = sums_ref[...]
    rows = kappa_ref.shape[1]
    lay_ring(one_ref, kappa_ref[0], even_ref.at[0], odd_ref.at[0], margin)
    lay_ring(two_ref, kappa_ref[1], even_ref.at[1], odd_ref.at[1], margin)
    face_weights(coef_ref, one_ref, two_ref, rows, margin)


def smooth_kernel(margin, own_ref, odd_ref, even_ref, coef_ref, out_ref, ring_ref):
    rows = own_ref.shape[0]
    lay_ring(ring_ref, own_ref[...], even_ref, odd_ref, margin)
    for j, field in enumerate(diffuse(ring_ref, coef_ref, rows, margin)):
        out_ref[:, j * LANES : (j + 1) * LANES] = field


def adjoint_kernel(margin, smooth_ref, mask_ref, sums_ref, more_ref, adjoint_ref, even_ref, odd_ref):
    weight = sums_ref[0] + more_ref[0]
    value = sums_ref[1] + more_ref[1]
    window = lanes(*window_of(my_chip(), chip_count(), mask_ref.shape[1] // LANES))
    adjoint = mask_ref[:, window].astype(F32) * (weight * smooth_ref[...] - value)
    adjoint_ref[...] = adjoint
    pack_edges(even_ref, odd_ref, adjoint, margin)


def spread_kernel(margin, own_ref, even_ref, odd_ref, coef_ref, out_ref, ring_ref):
    rows = own_ref.shape[0]
    lay_ring(ring_ref, own_ref[...], even_ref, odd_ref, margin)
    for j, field in enumerate(diffuse(ring_ref, coef_ref, rows, margin)):
        ring_ref[:rows, j * LANES : (j + 1) * LANES] = field
    own = out_ref.shape[1] // LANES
    start = window_of(my_chip(), chip_count(), own * chip_count())[0]
    out_ref[...] = ring_ref[:rows, lanes(my_chip() * own - start, own)]


def sent_last(members):
    return [0, 1] + sorted(range(2, members), key=lambda d: -(d % 2))


def result_kernel(response_ref, control_ref, *refs):
    refs, (out_ref, line_ref, sems) = refs[:-3], refs[-3:]
    own = refs[0].shape[1] // LANES
    refs = [refs[sent_last(len(refs)).index(d)] for d in range(len(refs))]
    copies = []
    for v in range(control_ref.shape[0]):
        mine, theirs = (response_ref[i, v][:1, :1] for i in range(2))
        for d in range(len(refs) // 2):
            window = lanes((my_chip() ^ d) * own, own)
            line_ref[v, :, window] = (
                control_ref[v, :, window] + mine * refs[2 * d][...] + theirs * refs[2 * d + 1][...]
            )
        copies.append(pltpu.make_async_copy(line_ref.at[v], out_ref.at[v], sems.at[v]))
        copies[-1].start()
    for copy in copies:
        copy.wait()


def swap(values, axis, bit):
    count = lax.axis_size(axis)
    return lax.ppermute(values, axis, [(i, i ^ bit) for i in range(count)])


def swap_edges(even, odd):
    tiles, members = lax.axis_size("tile"), lax.axis_size("var")
    pairs = []
    for t in range(tiles):
        other = t + 1 if t % 2 else t - 1
        for q in range(members):
            to = other * members + q if 0 <= other < tiles else t * members + (q ^ 1)
            pairs.append((t * members + q, to))
    return swap(even, "tile", 1), lax.ppermute(odd, ("tile", "var"), pairs)


def deliver(chunks):
    tiles, members = lax.axis_size("tile"), lax.axis_size("var")
    got = []
    for turn, chunk in enumerate(chunks[:-1]):
        pairs = []
        for t in range(tiles):
            for q in range(members):
                offset = 1 if turn == len(chunks) - 2 else 2 + turn + (q % 2) * (tiles // 2 - 1)
                pairs.append((t * members + q, (t ^ offset) * members + q))
        got.append(lax.ppermute(chunk, ("tile", "var"), pairs))
    return got + [chunks[-1]]


def local(control, diffusivity, land_mask, panel_tile, panel_row, panel_cols, obs_values,
          obs_weights, panel_sensor, sensitivity, cross_factor):
    rows, width = control.shape[1:]
    var_dev = control.shape[0]
    tiles, members = lax.axis_size("tile"), lax.axis_size("var")
    panels, panel_width = panel_cols.shape
    slots = panels // tiles
    blocks = width // LANES
    margin = PASSES
    total = ring_rows(rows, margin)
    chips = members // 2
    size = window_of(0, chips, blocks)[1]
    field = jax.ShapeDtypeStruct((rows, width), F32)
    share = jax.ShapeDtypeStruct((rows, width // chips), F32)
    view = jax.ShapeDtypeStruct((rows, size * LANES), F32)
    view2 = jax.ShapeDtypeStruct((2, *view.shape), F32)
    edge = jax.ShapeDtypeStruct((margin * size, LANES), F32)
    edge2 = jax.ShapeDtypeStruct((2, *edge.shape), F32)
    half = jax.ShapeDtypeStruct((3 * slots + 8, panel_width), F32)
    chunks = [jax.ShapeDtypeStruct((2, *half.shape), F32)] * (tiles // 2 - 1) + [half] * 2
    line = pltpu.VMEM((1, panels), jnp.int32)

    own, other, responses, kappa, kappa_even, kappa_odd, *chunks = call(
        functools.partial(first_kernel, slots, margin),
        [field, field, jax.ShapeDtypeStruct((2, var_dev, 8, LANES), F32), view2, edge2, edge2]
        + chunks,
        [HBM] * 10,
        [
            pltpu.SMEM(sensitivity.shape, F32),
            pltpu.SMEM(cross_factor.shape, F32),
            pltpu.VMEM(control.shape, F32),
            line, line, line,
            pltpu.VMEM(obs_values.shape, F32),
            pltpu.VMEM(obs_weights.shape, F32),
            pltpu.VMEM(panel_cols.shape, jnp.int32),
            pltpu.VMEM((panels, panels), jnp.bfloat16),
            pltpu.SemaphoreType.DMA((10,)),
        ],
        cost=cost(3000),
    )(*(in_hbm(x) for x in (sensitivity, cross_factor, control, diffusivity, panel_tile.reshape(1, -1),
                            panel_row.reshape(1, -1), panel_sensor.reshape(1, -1), obs_values,
                            obs_weights, panel_cols)))

    got = deliver(chunks)
    part, *parts = call(cut_kernel, [view] * chips, [VMEM] * 2, cost=cost(200))(
        own, swap(other, "var", 1)
    )
    parts = [swap(p, "var", 2 * (d + 1)) for d, p in enumerate(parts)]
    kappa_even, kappa_odd = swap_edges(kappa_even, kappa_odd)
    smooth_in, even, odd = call(
        functools.partial(edges_kernel, margin), [view, edge, edge], [VMEM] * chips, cost=cost(500)
    )(part, *parts)
    even, odd = swap_edges(even, odd)
    sums, sums_other = call(
        functools.partial(scatter_kernel, slots, blocks),
        [view2, view2],
        [AFTER] + [VMEM] * len(got),
        [
            pltpu.VMEM((2 * rows * 2 * padded_blocks(size), LANES), F32),
            pltpu.SMEM((8 * tiles, LANES), jnp.int32),
            pltpu.VMEM((8 * tiles, LANES), jnp.int32),
            pltpu.SemaphoreType.DMA((1,)),
        ],
        cost=cost(100000),
    )(smooth_in, got[-2], *got[:-2], got[-1])
    ring = pltpu.VMEM((total, size * LANES), F32)
    coef, sums_other = call(
        functools.partial(faces_kernel, margin),
        [jax.ShapeDtypeStruct((5, total, size * LANES), F32), view2],
        [VMEM] * 4 + [AFTER] * 2,
        [ring, ring],
        cost=cost(1000),
    )(kappa_even, kappa_odd, kappa, sums_other, odd, even)
    more_sums = swap(sums_other, "var", 1)
    (smooth,) = call(
        functools.partial(smooth_kernel, margin),
        [view],
        [VMEM] * 4,
        [ring],
        cost=cost(4000),
    )(smooth_in, odd, even, coef)
    adjoint, even, odd = call(
        functools.partial(adjoint_kernel, margin), [view, edge, edge], [VMEM] * 4, cost=cost(500)
    )(smooth, land_mask, sums, more_sums)
    even, odd = swap_edges(even, odd)
    (mine,) = call(
        functools.partial(spread_kernel, margin),
        [share],
        [VMEM] * 4,
        [ring],
        cost=cost(4000),
    )(adjoint, even, odd, coef)
    shares = [mine] + [swap(mine, "var", d) for d in sent_last(members)[1:]]
    (out,) = call(
        result_kernel,
        [jax.ShapeDtypeStruct(control.shape, F32)],
        [VMEM] * (2 + members),
        [pltpu.VMEM(control.shape, F32), pltpu.SemaphoreType.DMA((var_dev,))],
        cost=cost(1000),
        space=HBM,
    )(responses, control, *shares)
    return out


def solution(mesh):
    return jax.shard_map(
        local,
        mesh=mesh,
        in_specs=(
            P("var", ("grp", "tile"), None),
            P(None, ("grp", "tile"), None),
            P(("grp", "tile"), None),
            P(("grp", "tile"), None),
            P(("grp", "tile")),
            P(("grp", "tile"), None),
            P(("grp", "tile"), None),
            P(("grp", "tile"), None),
            P(("grp", "tile")),
            P(),
            P(),
        ),
        out_specs=P("var", ("grp", "tile"), None),
        check_vma=False,
    )
```

```python
import functools

import jax
import jax.numpy as jnp
from jax import lax
from jax.experimental import pallas as pl
from jax.experimental.pallas import tpu as pltpu
from jax.sharding import PartitionSpec as P

PASSES = 10
LANES = 128
GROUP = 16
VMEM = pl.BlockSpec(memory_space=pltpu.VMEM)
SMEM = pl.BlockSpec(memory_space=pltpu.SMEM)
HBM = pl.BlockSpec(memory_space=pltpu.HBM)
AFTER = pl.BlockSpec(memory_space=pl.ANY)
F32 = jnp.float32


def in_hbm(values):
    return pltpu.with_memory_space_constraint(values, pltpu.HBM)


def call(body, outs, ins, scratch=(), limit=16, cost=None, space=None):
    return pl.pallas_call(
        body,
        out_shape=outs,
        in_specs=ins,
        out_specs=[space or VMEM] * len(outs),
        scratch_shapes=list(scratch),
        compiler_params=pltpu.CompilerParams(vmem_limit_bytes=limit << 20),
        cost_estimate=cost,
    )


def cost(cycles):
    return pl.CostEstimate(flops=cycles * 4096, bytes_accessed=cycles * 1024, transcendentals=0)


def response(sens_ref, factor_ref, sensor, variable):
    total = sens_ref[sensor, 0] * factor_ref[0, variable]
    for u in range(1, factor_ref.shape[0]):
        total = total + sens_ref[sensor, u] * factor_ref[u, variable]
    return total


def fetch(pairs, sems):
    copies = [pltpu.make_async_copy(src, dst, sems.at[i]) for i, (src, dst) in enumerate(pairs)]
    for copy in copies:
        copy.start()
    return copies


def window_of(chip, chips, blocks):
    own = blocks // chips
    size = min(own + 2, own + chips - 1)
    return jnp.clip(chip * own - 1, 0, blocks - size), size


def my_chip():
    return lax.axis_index("var") // 2


def chip_count():
    return lax.axis_size("var") // 2


def lanes(start, size):
    return pl.ds(pl.multiple_of(start * LANES, LANES), size * LANES)


def first_kernel(slots, margin, sens_hbm, factor_hbm, control_hbm, kappa_hbm, tile_hbm, row_hbm, sensor_hbm,
                 value_hbm, weight_hbm, cols_hbm, own_ref, other_ref, response_ref, kappa_ref, even_ref,
                 odd_ref, *refs):
    chunk_refs = refs[:-11]
    (sens_ref, factor_ref, control_ref, tile_ref, row_ref, sensor_ref, value_ref, weight_ref, cols_ref,
     before_ref, sems) = refs[-11:]
    window = lanes(*window_of(my_chip(), chip_count(), own_ref.shape[1] // LANES))
    pairs = (
        (sens_hbm, sens_ref), (factor_hbm, factor_ref), (control_hbm, control_ref),
        (kappa_hbm.at[:, :, window], kappa_ref), (tile_hbm, tile_ref), (row_hbm, row_ref), (sensor_hbm, sensor_ref),
        (value_hbm, value_ref), (weight_hbm, weight_ref), (cols_hbm, cols_ref),
    )
    copies = [pltpu.make_async_copy(src, dst, sems.at[i]) for i, (src, dst) in enumerate(pairs)]
    for copy in copies:
        copy.start()
    from_panel = lax.broadcasted_iota(jnp.int32, before_ref.shape, 0)
    to_panel = lax.broadcasted_iota(jnp.int32, before_ref.shape, 1)
    before_ref[...] = jnp.where(from_panel < to_panel, 1.0, 0.0).astype(jnp.bfloat16)
    for copy in copies:
        copy.wait()

    member, mine = lax.axis_index("var"), lax.axis_index("tile")
    core = member % 2
    var_dev = control_ref.shape[0]
    for which, (sensor, out_ref) in enumerate(((core, own_ref), (1 - core, other_ref))):
        total = None
        for v in range(var_dev):
            scale = response(sens_ref, factor_ref, sensor, member * var_dev + v)
            response_ref[which, v] = jnp.full(response_ref.shape[2:], scale, F32)
            term = scale * control_ref[v]
            total = term if total is None else total + term
        out_ref[...] = total

    for i in range(2):
        pack_edges(even_ref.at[i], odd_ref.at[i], kappa_ref[i], margin)

    tiles = lax.axis_size("tile")
    full = tiles // 2 - 1
    first = jnp.where(core == 0, 2, tiles // 2 + 1)
    panels = value_ref.shape[0]
    source = tile_ref[...] ^ mine
    names = lax.broadcasted_iota(jnp.int32, (-(-tiles // 8) * 8, panels), 0)
    hits = jnp.where(names == source, 1.0, 0.0)
    ranks = jnp.dot(hits.astype(jnp.bfloat16), before_ref[...], preferred_element_type=F32)
    rank = jnp.sum(hits * ranks, axis=0, keepdims=True).astype(jnp.int32)
    parity, slot = rank % 2, rank // 2
    whole = (source >= first) & (source < first + full)
    home = source == 0
    keep = whole | ((home | (source == 1)) & (parity == core))
    half = jnp.where(whole, 2 * (source - first) + parity, jnp.where(home, tiles - 1, tiles - 2))
    place = jnp.where(keep, half * slots + slot, -1)
    spots = lax.broadcasted_iota(jnp.int32, (tiles * slots, panels), 0)
    pick = jnp.where(spots == place, 1.0, 0.0).astype(jnp.bfloat16)

    def picked(parts):
        total = None
        for part in parts:
            term = jnp.dot(pick, part.astype(jnp.bfloat16), preferred_element_type=F32)
            total = term if total is None else total + term
        return total

    cols = cols_ref[...]
    sent = (
        picked(thirds(value_ref[...])),
        picked(thirds(weight_ref[...])),
        picked(((cols // LANES * LANES).astype(F32), (cols % LANES).astype(F32))),
    )
    sub = lax.broadcasted_iota(jnp.int32, (8, panels), 0)
    lane = lax.broadcasted_iota(jnp.int32, (8, panels), 1)
    facts = jnp.where(sub == 0, row_ref[...], jnp.where(sub == 1, sensor_ref[...], 0)).astype(F32)
    meta = lax.dot_general(
        facts.astype(jnp.bfloat16), pick, (((1,), (1,)), ((), ())), preferred_element_type=F32
    )
    for i in range(tiles):
        held = jnp.sum(jnp.where(keep & (half == i), 1.0, 0.0), axis=1, keepdims=True)
        meta = jnp.where((sub == 2) & (lane == i), held, meta)
    for i in range(tiles):
        out_ref = chunk_refs[i // 2].at[i % 2] if i < 2 * full else chunk_refs[i - full]
        for part, rows in enumerate(sent):
            out_ref[part * slots : (part + 1) * slots] = rows[i * slots : (i + 1) * slots]
        out_ref[3 * slots :] = meta


def thirds(values):
    top = values.astype(jnp.bfloat16).astype(F32)
    rest = values - top
    middle = rest.astype(jnp.bfloat16).astype(F32)
    return top, middle, rest - middle


def pieces(values):
    top = values.astype(jnp.bfloat16).astype(F32)
    return top, values - top


def scatter_kernel(slots, blocks_all, after_ref, *refs):
    got_refs, (own_ref, other_ref, acc_ref, meta_ref, where_ref, sems) = refs[:-6], refs[-6:]
    core = lax.axis_index("var") % 2
    got_refs = [r.at[i] for r in got_refs[1:-1] for i in (0, 1)] + [got_refs[0], got_refs[-1]]
    size_of_group = min(GROUP, slots)
    rows = own_ref.shape[1]
    start, size = window_of(my_chip(), chip_count(), blocks_all)
    per_kind = padded_blocks(size)
    tall = 2 * per_kind
    line = lax.broadcasted_iota(jnp.int32, (8, LANES), 0)
    for s, ref in enumerate(got_refs):
        facts = ref[3 * slots : 3 * slots + 8].astype(jnp.int32)
        where_ref[8 * s : 8 * s + 8] = jnp.where(line == 0, (facts[1:2] * rows + facts[0:1]) * tall, facts)
    copy = pltpu.make_async_copy(where_ref, meta_ref, sems.at[0])
    copy.start()
    acc_ref[...] = jnp.zeros(acc_ref.shape, F32)
    place = lax.broadcasted_iota(jnp.int32, (tall, LANES), 0)
    is_weight = place < per_kind
    place = jnp.where(is_weight, place, place - per_kind) + start
    lane_ids = lax.broadcasted_iota(jnp.int32, (LANES, LANES), 0).astype(F32).astype(jnp.bfloat16)
    one, zero = jnp.bfloat16(1), jnp.bfloat16(0)
    sub = lax.broadcasted_iota(jnp.int32, (size_of_group, LANES), 0)
    blank = jnp.zeros((2 * tall, LANES), jnp.bfloat16)
    copy.wait()

    def load(s, base):
        got_ref = got_refs[s]
        count = meta_ref[8 * s + 2, s]
        value = got_ref[pl.ds(base, size_of_group), :]
        weight = got_ref[pl.ds(slots + base, size_of_group), :]
        cell = got_ref[pl.ds(2 * slots + base, size_of_group), :].astype(jnp.int32)
        weight = jnp.where(sub + base < count, weight, 0.0)
        return pieces(weight), pieces(weight * value), (cell % LANES).astype(F32), cell // LANES

    def one_hots(loaded, i):
        weights, values, low, high = loaded
        here = place == high[i : i + 1]
        rows_of = [
            jnp.where(here, jnp.where(is_weight, w[i : i + 1], v[i : i + 1]), 0.0)
            for w, v in zip(weights, values)
        ]
        left = jnp.concatenate(rows_of, axis=0).astype(jnp.bfloat16)
        column = jnp.broadcast_to(low[i : i + 1], (16, LANES)).astype(jnp.bfloat16)
        column = jnp.concatenate([column] * (LANES // 16), axis=0)
        return left, jnp.where(lane_ids == column, one, zero)

    def step(chosen, g, carry):
        base = pl.multiple_of(g * size_of_group, size_of_group)
        loaded = {s: load(s, base) for s in chosen}
        for k in range(size_of_group):
            for pair in zip(chosen[::2], chosen[1::2]):
                hots = [one_hots(loaded[s], k) for s in pair]
                left = jnp.concatenate(
                    [
                        jnp.concatenate([hots[0][0], blank], axis=1),
                        jnp.concatenate([blank, hots[1][0]], axis=1),
                    ],
                    axis=0,
                )
                both = lax.dot_general(
                    left, jnp.concatenate([hots[0][1], hots[1][1]], axis=1), (((1,), (1,)), ((), ())),
                    preferred_element_type=F32,
                )
                for i, s in enumerate(pair):
                    at = pl.multiple_of(meta_ref[8 * s, s * slots + base + k], 8)
                    mine = both[2 * i * tall : 2 * (i + 1) * tall]
                    acc_ref[pl.ds(at, tall), :] += mine[:tall] + mine[tall:]
        return carry

    for s in range(0, len(got_refs), 4):
        chosen = list(range(s, s + 4))
        most = meta_ref[8 * s + 2, s]
        for other in chosen[1:]:
            most = jnp.maximum(most, meta_ref[8 * other + 2, other])
        turns = (most + size_of_group - 1) // size_of_group
        lax.fori_loop(0, turns, functools.partial(step, chosen), 0)
    for sensor, out_ref in ((core, own_ref), (1 - core, other_ref)):
        begin = sensor * rows * tall
        for kind in range(2):
            for b in range(size):
                out_ref[kind, :, b * LANES : (b + 1) * LANES] = acc_ref[
                    pl.ds(begin + kind * per_kind + b, rows, stride=tall), :
                ]


def padded_blocks(size):
    return -(-size // 4) * 4


def even_tile():
    return lax.axis_index("tile") % 2 == 0


def has_above():
    return lax.axis_index("tile") > 0


def has_below():
    return lax.axis_index("tile") + 1 < lax.axis_size("tile")


def pack_edges(even_ref, odd_ref, rows_value, margin):
    rows, width = rows_value.shape
    even = even_tile()
    for b in range(width // LANES):
        at = slice(b * LANES, (b + 1) * LANES)
        head, tail = rows_value[:margin, at], rows_value[rows - margin :, at]
        even_ref[b * margin : (b + 1) * margin] = jnp.where(even, tail, head)
        odd_ref[b * margin : (b + 1) * margin] = jnp.where(even, head, tail)


def cut_kernel(first_ref, second_ref, mine_ref, *out_refs):
    chip, chips, blocks = my_chip(), chip_count(), first_ref.shape[1] // LANES
    for d, out_ref in enumerate((mine_ref, *out_refs)):
        window = lanes(*window_of(chip ^ d, chips, blocks))
        out_ref[...] = first_ref[:, window] + second_ref[:, window]


def edges_kernel(margin, *refs):
    terms, (total_ref, even_ref, odd_ref) = refs[:-3], refs[-3:]
    total = terms[0][...]
    for term in terms[1:]:
        total = total + term[...]
    total_ref[...] = total
    pack_edges(even_ref, odd_ref, total, margin)


def ring_rows(rows, margin):
    return -(-(rows + 2 * margin) // 8) * 8


def lay_ring(ref, own, from_even, from_odd, margin):
    rows, total = own.shape[0], ref.shape[0]
    even = even_tile()
    ref[rows:total] = jnp.zeros((total - rows, ref.shape[1]), F32)
    ref[:rows] = own
    for b in range(ref.shape[1] // LANES):
        at = slice(b * LANES, (b + 1) * LANES)
        one, two = (m[b * margin : (b + 1) * margin] for m in (from_even, from_odd))
        ref[rows : rows + margin, at] = jnp.where(has_below(), jnp.where(even, one, two), 0.0)
        ref[total - margin :, at] = jnp.where(has_above(), jnp.where(even, two, one), 0.0)


def block(ref, j):
    return ref[:, j * LANES : (j + 1) * LANES]


def sideways(blocks):
    shape = blocks[0].shape
    lane = lax.broadcasted_iota(jnp.int32, shape, 1)
    zero = jnp.zeros(shape, F32)
    ahead = [pltpu.roll(x, 1, 1) for x in blocks]
    back = [pltpu.roll(x, LANES - 1, 1) for x in blocks]
    for j, here in enumerate(blocks):
        before = ahead[j - 1] if j else zero
        after = back[j + 1] if j + 1 < len(blocks) else zero
        yield here, jnp.where(lane == 0, before, ahead[j]), jnp.where(lane == LANES - 1, after, back[j])


def face_weights(coef_ref, row_ref, col_ref, rows, margin):
    total, width = row_ref.shape
    blocks = width // LANES
    r = lax.broadcasted_iota(jnp.int32, (total, LANES), 0)
    inside = (
        (r < rows)
        | ((r < rows + margin) & has_below())
        | ((r >= total - margin) & has_above())
    )
    scale = jnp.where(inside, 0.125, 0.0)
    unit = jnp.where(inside, 1.0, 0.0)
    columns = [block(col_ref, j) for j in range(blocks)]
    for j, (k_col, k_left, k_right) in enumerate(sideways(columns)):
        at = slice(j * LANES, (j + 1) * LANES)
        k_row = block(row_ref, j)
        up = scale * (k_row + pltpu.roll(k_row, 1, 0))
        down = scale * (k_row + pltpu.roll(k_row, total - 1, 0))
        left = scale * (k_col + k_left)
        right = scale * (k_col + k_right)
        coef_ref[0, :, at] = unit - up - down - left - right
        coef_ref[1, :, at] = up
        coef_ref[2, :, at] = down
        coef_ref[3, :, at] = left
        coef_ref[4, :, at] = right


def one_pass(fields, coef_ref, spans):
    def weights(i, at):
        got = [coef_ref[i, span, at] for span in spans]
        return jnp.concatenate(got, axis=0) if len(got) > 1 else got[0]

    total = fields[0].shape[0]
    out = []
    for j, (here, left, right) in enumerate(sideways(fields)):
        at = slice(j * LANES, (j + 1) * LANES)
        out.append(
            weights(0, at) * here
            + weights(1, at) * pltpu.roll(here, 1, 0)
            + weights(2, at) * pltpu.roll(here, total - 1, 0)
            + weights(3, at) * left
            + weights(4, at) * right
        )
    return out


def diffuse(ring_ref, coef_ref, rows, margin):
    total, width = ring_ref.shape
    inner = margin // 8 * 8
    wide = [slice(0, total)]
    narrow = [slice(0, rows + inner), slice(total - inner, total)]
    fields = [block(ring_ref, j) for j in range(width // LANES)]
    for _ in range(margin - inner):
        fields = one_pass(fields, coef_ref, wide)
    fields = [jnp.concatenate([f[span] for span in narrow], axis=0) for f in fields]
    for _ in range(inner):
        fields = one_pass(fields, coef_ref, narrow)
    return [f[:rows] for f in fields]


def faces_kernel(margin, even_ref, odd_ref, kappa_ref, sums_ref, *refs):
    coef_ref, sums_out, one_ref, two_ref = refs[-4:]
    sums_out[...] = sums_ref[...]
    rows = kappa_ref.shape[1]
    lay_ring(one_ref, kappa_ref[0], even_ref.at[0], odd_ref.at[0], margin)
    lay_ring(two_ref, kappa_ref[1], even_ref.at[1], odd_ref.at[1], margin)
    face_weights(coef_ref, one_ref, two_ref, rows, margin)


def smooth_kernel(margin, own_ref, even_ref, odd_ref, coef_ref, out_ref, ring_ref):
    rows = own_ref.shape[0]
    lay_ring(ring_ref, own_ref[...], even_ref, odd_ref, margin)
    for j, field in enumerate(diffuse(ring_ref, coef_ref, rows, margin)):
        out_ref[:, j * LANES : (j + 1) * LANES] = field


def adjoint_kernel(margin, smooth_ref, mask_ref, sums_ref, more_ref, adjoint_ref, even_ref, odd_ref):
    weight = sums_ref[0] + more_ref[0]
    value = sums_ref[1] + more_ref[1]
    window = lanes(*window_of(my_chip(), chip_count(), mask_ref.shape[1] // LANES))
    adjoint = mask_ref[:, window].astype(F32) * (weight * smooth_ref[...] - value)
    adjoint_ref[...] = adjoint
    pack_edges(even_ref, odd_ref, adjoint, margin)


def spread_kernel(margin, own_ref, even_ref, odd_ref, coef_ref, out_ref, ring_ref):
    rows = own_ref.shape[0]
    lay_ring(ring_ref, own_ref[...], even_ref, odd_ref, margin)
    for j, field in enumerate(diffuse(ring_ref, coef_ref, rows, margin)):
        ring_ref[:rows, j * LANES : (j + 1) * LANES] = field
    own = out_ref.shape[1] // LANES
    start = window_of(my_chip(), chip_count(), own * chip_count())[0]
    out_ref[...] = ring_ref[:rows, lanes(my_chip() * own - start, own)]


def sent_last(members):
    return [0, 1] + sorted(range(2, members), key=lambda d: -(d % 2))


def result_kernel(response_ref, control_ref, *refs):
    refs, (out_ref, line_ref, sems) = refs[:-3], refs[-3:]
    own = refs[0].shape[1] // LANES
    refs = [refs[sent_last(len(refs)).index(d)] for d in range(len(refs))]
    copies = []
    for v in range(control_ref.shape[0]):
        mine, theirs = (response_ref[i, v][:1, :1] for i in range(2))
        for d in range(len(refs) // 2):
            window = lanes((my_chip() ^ d) * own, own)
            line_ref[v, :, window] = (
                control_ref[v, :, window] + mine * refs[2 * d][...] + theirs * refs[2 * d + 1][...]
            )
        copies.append(pltpu.make_async_copy(line_ref.at[v], out_ref.at[v], sems.at[v]))
        copies[-1].start()
    for copy in copies:
        copy.wait()


def swap(values, axis, bit):
    count = lax.axis_size(axis)
    return lax.ppermute(values, axis, [(i, i ^ bit) for i in range(count)])


def swap_edges(even, odd):
    tiles, members = lax.axis_size("tile"), lax.axis_size("var")
    pairs = []
    for t in range(tiles):
        other = t + 1 if t % 2 else t - 1
        for q in range(members):
            to = other * members + q if 0 <= other < tiles else t * members + (q ^ 1)
            pairs.append((t * members + q, to))
    return swap(even, "tile", 1), lax.ppermute(odd, ("tile", "var"), pairs)


def deliver(chunks):
    tiles, members = lax.axis_size("tile"), lax.axis_size("var")
    got = []
    for turn, chunk in enumerate(chunks[:-1]):
        pairs = []
        for t in range(tiles):
            for q in range(members):
                offset = 1 if turn == len(chunks) - 2 else 2 + turn + (q % 2) * (tiles // 2 - 1)
                pairs.append((t * members + q, (t ^ offset) * members + q))
        got.append(lax.ppermute(chunk, ("tile", "var"), pairs))
    return got + [chunks[-1]]


def local(control, diffusivity, land_mask, panel_tile, panel_row, panel_cols, obs_values,
          obs_weights, panel_sensor, sensitivity, cross_factor):
    rows, width = control.shape[1:]
    var_dev = control.shape[0]
    tiles, members = lax.axis_size("tile"), lax.axis_size("var")
    panels, panel_width = panel_cols.shape
    slots = panels // tiles
    blocks = width // LANES
    margin = PASSES
    total = ring_rows(rows, margin)
    chips = members // 2
    size = window_of(0, chips, blocks)[1]
    field = jax.ShapeDtypeStruct((rows, width), F32)
    share = jax.ShapeDtypeStruct((rows, width // chips), F32)
    view = jax.ShapeDtypeStruct((rows, size * LANES), F32)
    view2 = jax.ShapeDtypeStruct((2, *view.shape), F32)
    edge = jax.ShapeDtypeStruct((margin * size, LANES), F32)
    edge2 = jax.ShapeDtypeStruct((2, *edge.shape), F32)
    half = jax.ShapeDtypeStruct((3 * slots + 8, panel_width), F32)
    chunks = [jax.ShapeDtypeStruct((2, *half.shape), F32)] * (tiles // 2 - 1) + [half] * 2
    line = pltpu.VMEM((1, panels), jnp.int32)

    own, other, responses, kappa, kappa_even, kappa_odd, *chunks = call(
        functools.partial(first_kernel, slots, margin),
        [field, field, jax.ShapeDtypeStruct((2, var_dev, 8, LANES), F32), view2, edge2, edge2]
        + chunks,
        [HBM] * 10,
        [
            pltpu.SMEM(sensitivity.shape, F32),
            pltpu.SMEM(cross_factor.shape, F32),
            pltpu.VMEM(control.shape, F32),
            line, line, line,
            pltpu.VMEM(obs_values.shape, F32),
            pltpu.VMEM(obs_weights.shape, F32),
            pltpu.VMEM(panel_cols.shape, jnp.int32),
            pltpu.VMEM((panels, panels), jnp.bfloat16),
            pltpu.SemaphoreType.DMA((10,)),
        ],
        cost=cost(3000),
    )(*(in_hbm(x) for x in (sensitivity, cross_factor, control, diffusivity, panel_tile.reshape(1, -1),
                            panel_row.reshape(1, -1), panel_sensor.reshape(1, -1), obs_values,
                            obs_weights, panel_cols)))

    got = deliver(chunks)
    part, *parts = call(cut_kernel, [view] * chips, [VMEM] * 2, cost=cost(200))(
        own, swap(other, "var", 1)
    )
    parts = [swap(p, "var", 2 * (d + 1)) for d, p in enumerate(parts)]
    kappa_even, kappa_odd = swap_edges(kappa_even, kappa_odd)
    smooth_in, even, odd = call(
        functools.partial(edges_kernel, margin), [view, edge, edge], [VMEM] * chips, cost=cost(500)
    )(part, *parts)
    even, odd = swap_edges(even, odd)
    sums, sums_other = call(
        functools.partial(scatter_kernel, slots, blocks),
        [view2, view2],
        [AFTER] + [VMEM] * len(got),
        [
            pltpu.VMEM(((2 * rows + 1) * 2 * padded_blocks(size), LANES), F32),
            pltpu.SMEM((8 * tiles, LANES), jnp.int32),
            pltpu.VMEM((8 * tiles, LANES), jnp.int32),
            pltpu.SemaphoreType.DMA((1,)),
        ],
        cost=cost(100000),
    )(smooth_in, got[-2], *got[:-2], got[-1])
    ring = pltpu.VMEM((total, size * LANES), F32)
    coef, sums_other = call(
        functools.partial(faces_kernel, margin),
        [jax.ShapeDtypeStruct((5, total, size * LANES), F32), view2],
        [VMEM] * 4 + [AFTER] * 2,
        [ring, ring],
        cost=cost(1000),
    )(kappa_even, kappa_odd, kappa, sums_other, even, odd)
    more_sums = swap(sums_other, "var", 1)
    (smooth,) = call(
        functools.partial(smooth_kernel, margin),
        [view],
        [VMEM] * 4,
        [ring],
        cost=cost(4000),
    )(smooth_in, even, odd, coef)
    adjoint, even, odd = call(
        functools.partial(adjoint_kernel, margin), [view, edge, edge], [VMEM] * 4, cost=cost(500)
    )(smooth, land_mask, sums, more_sums)
    even, odd = swap_edges(even, odd)
    (mine,) = call(
        functools.partial(spread_kernel, margin),
        [share],
        [VMEM] * 4,
        [ring],
        cost=cost(4000),
    )(adjoint, even, odd, coef)
    shares = [mine] + [swap(mine, "var", d) for d in sent_last(members)[1:]]
    (out,) = call(
        result_kernel,
        [jax.ShapeDtypeStruct(control.shape, F32)],
        [VMEM] * (2 + members),
        [pltpu.VMEM(control.shape, F32), pltpu.SemaphoreType.DMA((var_dev,))],
        cost=cost(1000),
        space=HBM,
    )(responses, control, *shares)
    return out


def solution(mesh):
    return jax.shard_map(
        local,
        mesh=mesh,
        in_specs=(
            P("var", ("grp", "tile"), None),
            P(None, ("grp", "tile"), None),
            P(("grp", "tile"), None),
            P(("grp", "tile"), None),
            P(("grp", "tile")),
            P(("grp", "tile"), None),
            P(("grp", "tile"), None),
            P(("grp", "tile"), None),
            P(("grp", "tile")),
            P(),
            P(),
        ),
        out_specs=P("var", ("grp", "tile"), None),
        check_vma=False,
    )
```

```python
import functools

import jax
import jax.numpy as jnp
from jax import lax
from jax.experimental import pallas as pl
from jax.experimental.pallas import tpu as pltpu
from jax.sharding import PartitionSpec as P

PASSES = 10
LANES = 128
GROUP = 16
VMEM = pl.BlockSpec(memory_space=pltpu.VMEM)
SMEM = pl.BlockSpec(memory_space=pltpu.SMEM)
HBM = pl.BlockSpec(memory_space=pltpu.HBM)
AFTER = pl.BlockSpec(memory_space=pl.ANY)
F32 = jnp.float32


def in_hbm(values):
    return pltpu.with_memory_space_constraint(values, pltpu.HBM)


def call(body, outs, ins, scratch=(), limit=16, cost=None, space=None):
    return pl.pallas_call(
        body,
        out_shape=outs,
        in_specs=ins,
        out_specs=[space or VMEM] * len(outs),
        scratch_shapes=list(scratch),
        compiler_params=pltpu.CompilerParams(vmem_limit_bytes=limit << 20),
        cost_estimate=cost,
    )


def cost(cycles):
    return pl.CostEstimate(flops=cycles * 4096, bytes_accessed=cycles * 1024, transcendentals=0)


def response(sens_ref, factor_ref, sensor, variable):
    total = sens_ref[sensor, 0] * factor_ref[0, variable]
    for u in range(1, factor_ref.shape[0]):
        total = total + sens_ref[sensor, u] * factor_ref[u, variable]
    return total


def fetch(pairs, sems):
    copies = [pltpu.make_async_copy(src, dst, sems.at[i]) for i, (src, dst) in enumerate(pairs)]
    for copy in copies:
        copy.start()
    return copies


def window_of(chip, chips, blocks):
    own = blocks // chips
    size = min(own + 2, own + chips - 1)
    return jnp.clip(chip * own - 1, 0, blocks - size), size


def my_chip():
    return lax.axis_index("var") // 2


def chip_count():
    return lax.axis_size("var") // 2


def lanes(start, size):
    return pl.ds(pl.multiple_of(start * LANES, LANES), size * LANES)


def first_kernel(slots, margin, sens_hbm, factor_hbm, control_hbm, kappa_hbm, tile_hbm, row_hbm, sensor_hbm,
                 value_hbm, weight_hbm, cols_hbm, own_ref, other_ref, response_ref, kappa_ref, even_ref,
                 odd_ref, *refs):
    chunk_refs = refs[:-11]
    (sens_ref, factor_ref, control_ref, tile_ref, row_ref, sensor_ref, value_ref, weight_ref, cols_ref,
     before_ref, sems) = refs[-11:]
    window = lanes(*window_of(my_chip(), chip_count(), own_ref.shape[1] // LANES))
    pairs = (
        (sens_hbm, sens_ref), (factor_hbm, factor_ref), (control_hbm, control_ref),
        (kappa_hbm.at[:, :, window], kappa_ref), (tile_hbm, tile_ref), (row_hbm, row_ref), (sensor_hbm, sensor_ref),
        (value_hbm, value_ref), (weight_hbm, weight_ref), (cols_hbm, cols_ref),
    )
    copies = [pltpu.make_async_copy(src, dst, sems.at[i]) for i, (src, dst) in enumerate(pairs)]
    for copy in copies:
        copy.start()
    from_panel = lax.broadcasted_iota(jnp.int32, before_ref.shape, 0)
    to_panel = lax.broadcasted_iota(jnp.int32, before_ref.shape, 1)
    before_ref[...] = jnp.where(from_panel < to_panel, 1.0, 0.0).astype(jnp.bfloat16)
    for copy in copies:
        copy.wait()

    member, mine = lax.axis_index("var"), lax.axis_index("tile")
    core = member % 2
    var_dev = control_ref.shape[0]
    for which, (sensor, out_ref) in enumerate(((core, own_ref), (1 - core, other_ref))):
        total = None
        for v in range(var_dev):
            scale = response(sens_ref, factor_ref, sensor, member * var_dev + v)
            response_ref[which, v] = jnp.full(response_ref.shape[2:], scale, F32)
            term = scale * control_ref[v]
            total = term if total is None else total + term
        out_ref[...] = total

    for i in range(2):
        pack_edges(even_ref.at[i], odd_ref.at[i], kappa_ref[i], margin)

    tiles = lax.axis_size("tile")
    full = tiles // 2 - 1
    first = jnp.where(core == 0, 2, tiles // 2 + 1)
    panels = value_ref.shape[0]
    source = tile_ref[...] ^ mine
    names = lax.broadcasted_iota(jnp.int32, (-(-tiles // 8) * 8, panels), 0)
    hits = jnp.where(names == source, 1.0, 0.0)
    ranks = jnp.dot(hits.astype(jnp.bfloat16), before_ref[...], preferred_element_type=F32)
    rank = jnp.sum(hits * ranks, axis=0, keepdims=True).astype(jnp.int32)
    parity, slot = rank % 2, rank // 2
    whole = (source >= first) & (source < first + full)
    home = source == 0
    keep = whole | ((home | (source == 1)) & (parity == core))
    half = jnp.where(whole, 2 * (source - first) + parity, jnp.where(home, tiles - 1, tiles - 2))
    place = jnp.where(keep, half * slots + slot, -1)
    spots = lax.broadcasted_iota(jnp.int32, (tiles * slots, panels), 0)
    pick = jnp.where(spots == place, 1.0, 0.0).astype(jnp.bfloat16)

    def picked(parts):
        total = None
        for part in parts:
            term = jnp.dot(pick, part.astype(jnp.bfloat16), preferred_element_type=F32)
            total = term if total is None else total + term
        return total

    cols = cols_ref[...]
    sent = (
        picked(thirds(value_ref[...])),
        picked(thirds(weight_ref[...])),
        picked(((cols // LANES * LANES).astype(F32), (cols % LANES).astype(F32))),
    )
    sub = lax.broadcasted_iota(jnp.int32, (8, panels), 0)
    lane = lax.broadcasted_iota(jnp.int32, (8, panels), 1)
    facts = jnp.where(sub == 0, row_ref[...], jnp.where(sub == 1, sensor_ref[...], 0)).astype(F32)
    meta = lax.dot_general(
        facts.astype(jnp.bfloat16), pick, (((1,), (1,)), ((), ())), preferred_element_type=F32
    )
    for i in range(tiles):
        held = jnp.sum(jnp.where(keep & (half == i), 1.0, 0.0), axis=1, keepdims=True)
        meta = jnp.where((sub == 2) & (lane == i), held, meta)
    for i in range(tiles):
        out_ref = chunk_refs[i // 2].at[i % 2] if i < 2 * full else chunk_refs[i - full]
        for part, rows in enumerate(sent):
            out_ref[part * slots : (part + 1) * slots] = rows[i * slots : (i + 1) * slots]
        out_ref[3 * slots :] = meta


def thirds(values):
    top = values.astype(jnp.bfloat16).astype(F32)
    rest = values - top
    middle = rest.astype(jnp.bfloat16).astype(F32)
    return top, middle, rest - middle


def pieces(values):
    top = values.astype(jnp.bfloat16).astype(F32)
    return top, values - top


def scatter_kernel(slots, blocks_all, after_ref, *refs):
    got_refs, (own_ref, other_ref, acc_ref, meta_ref, where_ref, sems) = refs[:-6], refs[-6:]
    core = lax.axis_index("var") % 2
    got_refs = [r.at[i] for r in got_refs[1:-1] for i in (0, 1)] + [got_refs[0], got_refs[-1]]
    size_of_group = min(GROUP, slots)
    rows = own_ref.shape[1]
    start, size = window_of(my_chip(), chip_count(), blocks_all)
    per_kind = padded_blocks(size)
    tall = 2 * per_kind
    line = lax.broadcasted_iota(jnp.int32, (8, LANES), 0)
    for s, ref in enumerate(got_refs):
        facts = ref[3 * slots : 3 * slots + 8].astype(jnp.int32)
        where_ref[8 * s : 8 * s + 8] = jnp.where(line == 0, (facts[1:2] * rows + facts[0:1]) * tall, facts)
    copy = pltpu.make_async_copy(where_ref, meta_ref, sems.at[0])
    copy.start()
    acc_ref[...] = jnp.zeros(acc_ref.shape, F32)
    place = lax.broadcasted_iota(jnp.int32, (tall, LANES), 0)
    is_weight = place < per_kind
    place = jnp.where(is_weight, place, place - per_kind) + start
    lane_ids = lax.broadcasted_iota(jnp.int32, (LANES, LANES), 0).astype(F32).astype(jnp.bfloat16)
    one, zero = jnp.bfloat16(1), jnp.bfloat16(0)
    sub = lax.broadcasted_iota(jnp.int32, (size_of_group, LANES), 0)
    blank = jnp.zeros((2 * tall, LANES), jnp.bfloat16)
    copy.wait()

    def load(s, base):
        got_ref = got_refs[s]
        count = meta_ref[8 * s + 2, s]
        value = got_ref[pl.ds(base, size_of_group), :]
        weight = got_ref[pl.ds(slots + base, size_of_group), :]
        cell = got_ref[pl.ds(2 * slots + base, size_of_group), :].astype(jnp.int32)
        weight = jnp.where(sub + base < count, weight, 0.0)
        return pieces(weight), pieces(weight * value), (cell % LANES).astype(F32), cell // LANES

    def one_hots(loaded, i):
        weights, values, low, high = loaded
        here = place == high[i : i + 1]
        rows_of = [
            jnp.where(here, jnp.where(is_weight, w[i : i + 1], v[i : i + 1]), 0.0)
            for w, v in zip(weights, values)
        ]
        left = jnp.concatenate(rows_of, axis=0).astype(jnp.bfloat16)
        column = jnp.broadcast_to(low[i : i + 1], (16, LANES)).astype(jnp.bfloat16)
        column = jnp.concatenate([column] * (LANES // 16), axis=0)
        return left, jnp.where(lane_ids == column, one, zero)

    def step(chosen, g, carry):
        base = pl.multiple_of(g * size_of_group, size_of_group)
        loaded = {s: load(s, base) for s in chosen}
        for k in range(size_of_group):
            for pair in zip(chosen[::2], chosen[1::2]):
                hots = [one_hots(loaded[s], k) for s in pair]
                left = jnp.concatenate(
                    [
                        jnp.concatenate([hots[0][0], blank], axis=1),
                        jnp.concatenate([blank, hots[1][0]], axis=1),
                    ],
                    axis=0,
                )
                both = lax.dot_general(
                    left, jnp.concatenate([hots[0][1], hots[1][1]], axis=1), (((1,), (1,)), ((), ())),
                    preferred_element_type=F32,
                )
                for i, s in enumerate(pair):
                    at = pl.multiple_of(meta_ref[8 * s, s * slots + base + k], 8)
                    mine = both[2 * i * tall : 2 * (i + 1) * tall]
                    acc_ref[pl.ds(at, tall), :] += mine[:tall] + mine[tall:]
        return carry

    for s in range(0, len(got_refs), 4):
        chosen = list(range(s, s + 4))
        most = meta_ref[8 * s + 2, s]
        for other in chosen[1:]:
            most = jnp.maximum(most, meta_ref[8 * other + 2, other])
        turns = (most + size_of_group - 1) // size_of_group
        lax.fori_loop(0, turns, functools.partial(step, chosen), 0)
    for sensor, out_ref in ((core, own_ref), (1 - core, other_ref)):
        begin = sensor * rows * tall
        for kind in range(2):
            for b in range(size):
                out_ref[kind, :, b * LANES : (b + 1) * LANES] = acc_ref[
                    pl.ds(begin + kind * per_kind + b, rows, stride=tall), :
                ]


def padded_blocks(size):
    return -(-size // 4) * 4


def even_tile():
    return lax.axis_index("tile") % 2 == 0


def has_above():
    return lax.axis_index("tile") > 0


def has_below():
    return lax.axis_index("tile") + 1 < lax.axis_size("tile")


def pack_edges(even_ref, odd_ref, rows_value, margin):
    rows, width = rows_value.shape
    even = even_tile()
    for b in range(width // LANES):
        at = slice(b * LANES, (b + 1) * LANES)
        head, tail = rows_value[:margin, at], rows_value[rows - margin :, at]
        even_ref[b * margin : (b + 1) * margin] = jnp.where(even, tail, head)
        odd_ref[b * margin : (b + 1) * margin] = jnp.where(even, head, tail)


def relay_kernel(*refs):
    for in_ref, out_ref in zip(refs[: len(refs) // 2], refs[len(refs) // 2 :]):
        out_ref[...] = in_ref[...]


def cut_kernel(first_ref, second_ref, mine_ref, *out_refs):
    chip, chips, blocks = my_chip(), chip_count(), first_ref.shape[1] // LANES
    for d, out_ref in enumerate((mine_ref, *out_refs)):
        window = lanes(*window_of(chip ^ d, chips, blocks))
        out_ref[...] = first_ref[:, window] + second_ref[:, window]


def edges_kernel(margin, *refs):
    terms, (total_ref, even_ref, odd_ref) = refs[:-3], refs[-3:]
    total = terms[0][...]
    for term in terms[1:]:
        total = total + term[...]
    total_ref[...] = total
    pack_edges(even_ref, odd_ref, total, margin)


def ring_rows(rows, margin):
    return -(-(rows + 2 * margin) // 8) * 8


def lay_ring(ref, own, from_even, from_odd, margin):
    rows, total = own.shape[0], ref.shape[0]
    even = even_tile()
    ref[rows:total] = jnp.zeros((total - rows, ref.shape[1]), F32)
    ref[:rows] = own
    for b in range(ref.shape[1] // LANES):
        at = slice(b * LANES, (b + 1) * LANES)
        one, two = (m[b * margin : (b + 1) * margin] for m in (from_even, from_odd))
        ref[rows : rows + margin, at] = jnp.where(has_below(), jnp.where(even, one, two), 0.0)
        ref[total - margin :, at] = jnp.where(has_above(), jnp.where(even, two, one), 0.0)


def block(ref, j):
    return ref[:, j * LANES : (j + 1) * LANES]


def sideways(blocks):
    shape = blocks[0].shape
    lane = lax.broadcasted_iota(jnp.int32, shape, 1)
    zero = jnp.zeros(shape, F32)
    ahead = [pltpu.roll(x, 1, 1) for x in blocks]
    back = [pltpu.roll(x, LANES - 1, 1) for x in blocks]
    for j, here in enumerate(blocks):
        before = ahead[j - 1] if j else zero
        after = back[j + 1] if j + 1 < len(blocks) else zero
        yield here, jnp.where(lane == 0, before, ahead[j]), jnp.where(lane == LANES - 1, after, back[j])


def face_weights(coef_ref, row_ref, col_ref, rows, margin):
    total, width = row_ref.shape
    blocks = width // LANES
    r = lax.broadcasted_iota(jnp.int32, (total, LANES), 0)
    inside = (
        (r < rows)
        | ((r < rows + margin) & has_below())
        | ((r >= total - margin) & has_above())
    )
    scale = jnp.where(inside, 0.125, 0.0)
    unit = jnp.where(inside, 1.0, 0.0)
    columns = [block(col_ref, j) for j in range(blocks)]
    for j, (k_col, k_left, k_right) in enumerate(sideways(columns)):
        at = slice(j * LANES, (j + 1) * LANES)
        k_row = block(row_ref, j)
        up = scale * (k_row + pltpu.roll(k_row, 1, 0))
        down = scale * (k_row + pltpu.roll(k_row, total - 1, 0))
        left = scale * (k_col + k_left)
        right = scale * (k_col + k_right)
        coef_ref[0, :, at] = unit - up - down - left - right
        coef_ref[1, :, at] = up
        coef_ref[2, :, at] = down
        coef_ref[3, :, at] = left
        coef_ref[4, :, at] = right


def one_pass(fields, coef_ref, spans):
    def weights(i, at):
        got = [coef_ref[i, span, at] for span in spans]
        return jnp.concatenate(got, axis=0) if len(got) > 1 else got[0]

    total = fields[0].shape[0]
    out = []
    for j, (here, left, right) in enumerate(sideways(fields)):
        at = slice(j * LANES, (j + 1) * LANES)
        out.append(
            weights(0, at) * here
            + weights(1, at) * pltpu.roll(here, 1, 0)
            + weights(2, at) * pltpu.roll(here, total - 1, 0)
            + weights(3, at) * left
            + weights(4, at) * right
        )
    return out


def diffuse(ring_ref, coef_ref, rows, margin):
    total, width = ring_ref.shape
    inner = margin // 8 * 8
    wide = [slice(0, total)]
    narrow = [slice(0, rows + inner), slice(total - inner, total)]
    fields = [block(ring_ref, j) for j in range(width // LANES)]
    for _ in range(margin - inner):
        fields = one_pass(fields, coef_ref, wide)
    fields = [jnp.concatenate([f[span] for span in narrow], axis=0) for f in fields]
    for _ in range(inner):
        fields = one_pass(fields, coef_ref, narrow)
    return [f[:rows] for f in fields]


def faces_kernel(margin, even_ref, odd_ref, kappa_ref, sums_ref, *refs):
    coef_ref, sums_out, one_ref, two_ref = refs[-4:]
    sums_out[...] = sums_ref[...]
    rows = kappa_ref.shape[1]
    lay_ring(one_ref, kappa_ref[0], even_ref.at[0], odd_ref.at[0], margin)
    lay_ring(two_ref, kappa_ref[1], even_ref.at[1], odd_ref.at[1], margin)
    face_weights(coef_ref, one_ref, two_ref, rows, margin)


def smooth_kernel(margin, own_ref, even_ref, odd_ref, coef_ref, out_ref, ring_ref):
    rows = own_ref.shape[0]
    lay_ring(ring_ref, own_ref[...], even_ref, odd_ref, margin)
    for j, field in enumerate(diffuse(ring_ref, coef_ref, rows, margin)):
        out_ref[:, j * LANES : (j + 1) * LANES] = field


def adjoint_kernel(margin, smooth_ref, mask_ref, sums_ref, more_ref, adjoint_ref, even_ref, odd_ref):
    weight = sums_ref[0] + more_ref[0]
    value = sums_ref[1] + more_ref[1]
    window = lanes(*window_of(my_chip(), chip_count(), mask_ref.shape[1] // LANES))
    adjoint = mask_ref[:, window].astype(F32) * (weight * smooth_ref[...] - value)
    adjoint_ref[...] = adjoint
    pack_edges(even_ref, odd_ref, adjoint, margin)


def spread_kernel(margin, own_ref, even_ref, odd_ref, coef_ref, out_ref, ring_ref):
    rows = own_ref.shape[0]
    lay_ring(ring_ref, own_ref[...], even_ref, odd_ref, margin)
    for j, field in enumerate(diffuse(ring_ref, coef_ref, rows, margin)):
        ring_ref[:rows, j * LANES : (j + 1) * LANES] = field
    own = out_ref.shape[1] // LANES
    start = window_of(my_chip(), chip_count(), own * chip_count())[0]
    out_ref[...] = ring_ref[:rows, lanes(my_chip() * own - start, own)]


def sent_last(members):
    return [0, 1] + sorted(range(2, members), key=lambda d: -(d % 2))


def result_kernel(response_ref, control_ref, *refs):
    refs, (out_ref, line_ref, sems) = refs[:-3], refs[-3:]
    own = refs[0].shape[1] // LANES
    refs = [refs[sent_last(len(refs)).index(d)] for d in range(len(refs))]
    copies = []
    for v in range(control_ref.shape[0]):
        mine, theirs = (response_ref[i, v][:1, :1] for i in range(2))
        for d in range(len(refs) // 2):
            window = lanes((my_chip() ^ d) * own, own)
            line_ref[v, :, window] = (
                control_ref[v, :, window] + mine * refs[2 * d][...] + theirs * refs[2 * d + 1][...]
            )
        copies.append(pltpu.make_async_copy(line_ref.at[v], out_ref.at[v], sems.at[v]))
        copies[-1].start()
    for copy in copies:
        copy.wait()


def swap(values, axis, bit):
    count = lax.axis_size(axis)
    return lax.ppermute(values, axis, [(i, i ^ bit) for i in range(count)])


def swap_edges(even, odd):
    tiles, members = lax.axis_size("tile"), lax.axis_size("var")
    pairs = []
    for t in range(tiles):
        other = t + 1 if t % 2 else t - 1
        for q in range(members):
            to = other * members + q if 0 <= other < tiles else t * members + (q ^ 1)
            pairs.append((t * members + q, to))
    return swap(even, "tile", 1), lax.ppermute(odd, ("tile", "var"), pairs)


def deliver(chunks):
    tiles, members = lax.axis_size("tile"), lax.axis_size("var")
    got = []
    for turn, chunk in enumerate(chunks[:-1]):
        pairs = []
        for t in range(tiles):
            for q in range(members):
                offset = 1 if turn == len(chunks) - 2 else 2 + turn + (q % 2) * (tiles // 2 - 1)
                pairs.append((t * members + q, (t ^ offset) * members + q))
        got.append(lax.ppermute(chunk, ("tile", "var"), pairs))
    return got + [chunks[-1]]


def local(control, diffusivity, land_mask, panel_tile, panel_row, panel_cols, obs_values,
          obs_weights, panel_sensor, sensitivity, cross_factor):
    rows, width = control.shape[1:]
    var_dev = control.shape[0]
    tiles, members = lax.axis_size("tile"), lax.axis_size("var")
    panels, panel_width = panel_cols.shape
    slots = panels // tiles
    blocks = width // LANES
    margin = PASSES
    total = ring_rows(rows, margin)
    chips = members // 2
    size = window_of(0, chips, blocks)[1]
    field = jax.ShapeDtypeStruct((rows, width), F32)
    share = jax.ShapeDtypeStruct((rows, width // chips), F32)
    view = jax.ShapeDtypeStruct((rows, size * LANES), F32)
    view2 = jax.ShapeDtypeStruct((2, *view.shape), F32)
    edge = jax.ShapeDtypeStruct((margin * size, LANES), F32)
    edge2 = jax.ShapeDtypeStruct((2, *edge.shape), F32)
    half = jax.ShapeDtypeStruct((3 * slots + 8, panel_width), F32)
    far_shapes = [jax.ShapeDtypeStruct((2, *half.shape), F32)] * (tiles // 2 - 1)
    chunks = far_shapes + [half] * 2
    line = pltpu.VMEM((1, panels), jnp.int32)

    own, other, responses, kappa, kappa_even, kappa_odd, *chunks = call(
        functools.partial(first_kernel, slots, margin),
        [field, field, jax.ShapeDtypeStruct((2, var_dev, 8, LANES), F32), view2, edge2, edge2]
        + chunks,
        [HBM] * 10,
        [
            pltpu.SMEM(sensitivity.shape, F32),
            pltpu.SMEM(cross_factor.shape, F32),
            pltpu.VMEM(control.shape, F32),
            line, line, line,
            pltpu.VMEM(obs_values.shape, F32),
            pltpu.VMEM(obs_weights.shape, F32),
            pltpu.VMEM(panel_cols.shape, jnp.int32),
            pltpu.VMEM((panels, panels), jnp.bfloat16),
            pltpu.SemaphoreType.DMA((10,)),
        ],
        cost=cost(3000),
    )(*(in_hbm(x) for x in (sensitivity, cross_factor, control, diffusivity, panel_tile.reshape(1, -1),
                            panel_row.reshape(1, -1), panel_sensor.reshape(1, -1), obs_values,
                            obs_weights, panel_cols)))

    got = deliver(chunks)
    part, *parts = call(cut_kernel, [view] * chips, [VMEM] * 2, cost=cost(200))(
        own, swap(other, "var", 1)
    )
    parts = [swap(p, "var", 2 * (d + 1)) for d, p in enumerate(parts)]
    kappa_even, kappa_odd = swap_edges(kappa_even, kappa_odd)
    smooth_in, even, odd = call(
        functools.partial(edges_kernel, margin), [view, edge, edge], [VMEM] * chips, cost=cost(500)
    )(part, *parts)
    even, odd = swap_edges(even, odd)
    far = call(relay_kernel, far_shapes, [VMEM] * len(far_shapes), cost=cost(270000))(*got[:-2])
    sums, sums_other = call(
        functools.partial(scatter_kernel, slots, blocks),
        [view2, view2],
        [AFTER] + [VMEM] * len(got),
        [
            pltpu.VMEM(((2 * rows + 1) * 2 * padded_blocks(size), LANES), F32),
            pltpu.SMEM((8 * tiles, LANES), jnp.int32),
            pltpu.VMEM((8 * tiles, LANES), jnp.int32),
            pltpu.SemaphoreType.DMA((1,)),
        ],
        cost=cost(100000),
    )(smooth_in, got[-2], *far, got[-1])
    ring = pltpu.VMEM((total, size * LANES), F32)
    coef, sums_other = call(
        functools.partial(faces_kernel, margin),
        [jax.ShapeDtypeStruct((5, total, size * LANES), F32), view2],
        [VMEM] * 4 + [AFTER] * 2,
        [ring, ring],
        cost=cost(1000),
    )(kappa_even, kappa_odd, kappa, sums_other, even, odd)
    more_sums = swap(sums_other, "var", 1)
    (smooth,) = call(
        functools.partial(smooth_kernel, margin),
        [view],
        [VMEM] * 4,
        [ring],
        cost=cost(4000),
    )(smooth_in, even, odd, coef)
    adjoint, even, odd = call(
        functools.partial(adjoint_kernel, margin), [view, edge, edge], [VMEM] * 4, cost=cost(500)
    )(smooth, land_mask, sums, more_sums)
    even, odd = swap_edges(even, odd)
    (mine,) = call(
        functools.partial(spread_kernel, margin),
        [share],
        [VMEM] * 4,
        [ring],
        cost=cost(4000),
    )(adjoint, even, odd, coef)
    shares = [mine] + [swap(mine, "var", d) for d in sent_last(members)[1:]]
    (out,) = call(
        result_kernel,
        [jax.ShapeDtypeStruct(control.shape, F32)],
        [VMEM] * (2 + members),
        [pltpu.VMEM(control.shape, F32), pltpu.SemaphoreType.DMA((var_dev,))],
        cost=cost(1000),
        space=HBM,
    )(responses, control, *shares)
    return out


def solution(mesh):
    return jax.shard_map(
        local,
        mesh=mesh,
        in_specs=(
            P("var", ("grp", "tile"), None),
            P(None, ("grp", "tile"), None),
            P(("grp", "tile"), None),
            P(("grp", "tile"), None),
            P(("grp", "tile")),
            P(("grp", "tile"), None),
            P(("grp", "tile"), None),
            P(("grp", "tile"), None),
            P(("grp", "tile")),
            P(),
            P(),
        ),
        out_specs=P("var", ("grp", "tile"), None),
        check_vma=False,
    )
```
